32 devices in a mesh: groups: 2 (over x), row: 4 (over y, core), col: 4 (over z).
Axes of the slice: x: 2, y: 2, z: 4, core: 2. Of those that a mesh axis runs over, the one named last changes fastest.
Arguments:
- positions: float32 [3, 32768], P(None, ('groups', 'row', 'col')), parts along dimension 1, may hold values from -6 to 6
- strengths: float32 [3, 32768], P(None, ('groups', 'row', 'col')), parts along dimension 1, may hold values from -6 to 6
- cores: float32 [32768], P(('groups', 'row', 'col')), parts along dimension 0, may hold values from 0.3 to 1
- order: int32 [32768], P(('groups', 'row', 'col')), parts along dimension 0, may hold values from 0 to 1023, as said below
- tile_counts: int32 [256], P(('groups', 'row', 'col')), parts along dimension 0, may hold values from 32 to 128
- pair_slots: int32 [2, 2048], P(None, ('groups', 'row', 'col')), parts along dimension 1, may hold values from 0 to 31, as said below
- pair_count: int32 [32], P(('groups', 'row', 'col')), parts along dimension 0, may hold values from 16 to 64, as said below
Outputs:
- velocity: float32 [3, 32768], P(None, ('groups', 'row', 'col')), parts along dimension 1
- stretching: float32 [3, 32768], P(None, ('groups', 'row', 'col')), parts along dimension 1
The draws below stay inside these ranges and needn't reach their ends.
There are 2 independent parts, one for each index of `groups`. The reference program is written for one: setup_inputs(seed, part) draws one part's arguments, and reference() takes and returns one part's arrays. A program takes and returns all parts, laid end to end along the dimension named above; each array names one. Nothing has to cross between parts.
Inputs may be any that keep to these rules, and one draw needn't show every extreme that they name: `order`: each device's block of 1024 entries is a permutation of 0 to 1023. `pair_slots`: row 0 is below 32, row 1 below 32; the first 8 slots of every device pair each of its own tiles with itself. `pair_count`: some device has all its slots live.
All inputs are finite; a program needn't handle non-finite values.
Results may differ from the reference program's by a relative error of at most 0.0001.
Values sent between devices are 32-bit elements; how exact they have to be, the bound alone decides.
No kernel may reach another device: no remote copies, remote signals or barrier semaphores. Data moves between devices by JAX's collectives and lax.ppermute only.
A program may use at most 64 MiB of HBM per device.

```python
import math
import jax
import jax.numpy as jnp
from jax import lax

TILE = 128
TILES_DEV = 8
PAIRS_DEV = 64
PAIR_BLOCK = 8
GRID = 16
TILES = 128
NPART = 16384
ROW_TILES = 32
COL_TILES = 32
SLOTS = 1024
N_COL = 4


def draw_order(key, part):
    per_dev = TILES_DEV * TILE
    count = NPART // per_dev
    keys = jax.random.split(jax.random.fold_in(key, 11), count)
    perms = jax.vmap(lambda single: jax.random.permutation(single, per_dev))(keys)
    return perms.reshape(-1).astype(jnp.int32)


def draw_pair_slots(key, part):
    ncols = ROW_TILES // TILES_DEV
    slot = jnp.arange(SLOTS, dtype=jnp.int32)
    device = slot // PAIRS_DEV
    within = slot % PAIRS_DEV
    row_index = device // ncols
    col_index = device % ncols
    first = jax.random.randint(jax.random.fold_in(key, 21), (SLOTS,), 0, ROW_TILES, dtype=jnp.int32)
    second = jax.random.randint(jax.random.fold_in(key, 22), (SLOTS,), 0, COL_TILES, dtype=jnp.int32)
    diagonal = within < TILES_DEV
    first = jnp.where(diagonal, col_index * TILES_DEV + within, first)
    second = jnp.where(diagonal, row_index * TILES_DEV + within, second)
    return jnp.stack([first, second]).astype(jnp.int32)


def draw_pair_count(key, part):
    base = jax.random.randint(jax.random.fold_in(key, 31), (GRID,), PAIRS_DEV // 4, PAIRS_DEV // 2 + 1, dtype=jnp.int32)
    dense = jax.random.randint(jax.random.fold_in(key, 32), (GRID,), 0, 8, dtype=jnp.int32) == 0
    chosen = jax.random.randint(jax.random.fold_in(key, 33), (), 0, GRID, dtype=jnp.int32)
    full = dense | (jnp.arange(GRID, dtype=jnp.int32) == chosen)
    return jnp.where(full, PAIRS_DEV, base).astype(jnp.int32)


def place_ends(result, key, low, largest):
    longest = result.shape.index(max(result.shape))
    spots = []
    for shift in (0, 1):
        where = [jax.random.randint(jax.random.fold_in(key, axis), (), 0, length) for axis, length in enumerate(result.shape)]
        where[longest] = (where[longest] + shift) % result.shape[longest]
        spots.append(tuple(where))
    return result.at[spots[0]].set(low).at[spots[1]].set(largest)


def block_scale(rng, extent, cuts, low, high):
    loudness, own = 1.0, jax.random.fold_in(rng, 6)
    for dim, shards_of in cuts:
        steps = jnp.exp(jax.random.uniform(jax.random.fold_in(own, dim), (shards_of,), jnp.float32, low / len(cuts), high / len(cuts)))
        loudness = loudness * jnp.repeat(steps, extent[dim] // shards_of).reshape([-1 if axis == dim else 1 for axis in range(len(extent))])
    return loudness


def bell_draw(stream_key, shape, width, bound, cuts=(), kind=jnp.bfloat16):
    gain = block_scale(stream_key, shape, cuts, -0.22, 0.18) if cuts else 1.0
    result = jax.random.normal(stream_key, shape, jnp.float32) * width * gain
    return jnp.minimum(jnp.maximum(result, -bound), bound).astype(kind)


def setup_inputs(seed: int = 0, part: int = 0) -> dict:
    arg_keys = jax.random.split(jax.random.key(seed), 8)
    part_keys = jax.random.split(jax.random.fold_in(arg_keys[7], part), 8)
    return {
        "positions": bell_draw(part_keys[0], (3, NPART), 1.0, 6.0, ((1, 16),), jnp.float32),
        "strengths": bell_draw(part_keys[1], (3, NPART), 1.0, 6.0, ((1, 16),), jnp.float32),
        "cores": jnp.clip(jnp.exp(math.log(1.0) - 1.2039728 * jax.random.uniform(part_keys[2], (NPART,), jnp.float32) ** block_scale(part_keys[2], (NPART,), ((0, 16),), -0.2, 0.2)), 0.3, 1.0),
        "order": draw_order(jax.random.fold_in(jax.random.fold_in(arg_keys[7], part), 71), part),
        "tile_counts": place_ends(jax.random.randint(part_keys[4], (TILES,), TILE // 4, TILE + 1), jax.random.fold_in(part_keys[4], 1), TILE // 4, TILE).astype(jnp.int32),
        "pair_slots": draw_pair_slots(jax.random.fold_in(jax.random.fold_in(arg_keys[7], part), 71), part),
        "pair_count": draw_pair_count(jax.random.fold_in(jax.random.fold_in(arg_keys[7], part), 71), part),
    }


biot_factor = -1.0 / (4.0 * math.pi)

def cross_product(left, right):
    return jnp.stack([left[1] * right[2] - left[2] * right[1], left[2] * right[0] - left[0] * right[2], left[0] * right[1] - left[1] * right[0]])

def pair_terms(target, source, weight_t, weight_r):
    target_pos = target[0:3, :, :, None]
    source_pos = source[0:3, :, None, :]
    target_str = target[3:6, :, :, None]
    source_str = source[3:6, :, None, :]
    offset = target_pos - source_pos
    sigma_sq = 0.5 * (target[6][:, :, None] ** 2 + source[6][:, None, :] ** 2)
    rho_sq = (offset[0] * offset[0] + offset[1] * offset[1] + offset[2] * offset[2]) / sigma_sq
    inverse = lax.rsqrt(rho_sq + 1.0)
    inverse_sq = inverse * inverse
    inverse_five = inverse_sq * inverse_sq * inverse
    core_cube = sigma_sq * jnp.sqrt(sigma_sq)
    smooth = (rho_sq + 2.5) * inverse_five / core_cube
    gradient = -3.0 * (rho_sq + 3.5) * inverse_five * inverse_sq / (core_cube * sigma_sq)
    cross_src = cross_product(offset, source_str)
    cross_tgt = cross_product(offset, target_str)
    along_tgt = lax.optimization_barrier(jnp.sum(target_str * offset, axis=0))
    along_src = lax.optimization_barrier(jnp.sum(source_str * offset, axis=0))
    smooth_t = smooth * weight_t[:, None, None]
    grad_t = gradient * weight_t[:, None, None]
    vel_target = biot_factor * lax.optimization_barrier(jnp.sum(smooth_t * cross_src, axis=-1))
    mix_target = lax.optimization_barrier(jnp.sum(smooth_t * source_str, axis=-1))
    str_target = biot_factor * (cross_product(target[3:6], mix_target) + lax.optimization_barrier(jnp.sum(grad_t * along_tgt * cross_src, axis=-1)))
    smooth_r = smooth * weight_r[:, None, None]
    grad_r = gradient * weight_r[:, None, None]
    vel_source = -biot_factor * lax.optimization_barrier(jnp.sum(smooth_r * cross_tgt, axis=-2))
    mix_source = lax.optimization_barrier(jnp.sum(smooth_r * target_str, axis=-2))
    str_source = biot_factor * (-cross_product(mix_source, source[3:6]) + lax.optimization_barrier(jnp.sum(grad_r * along_src * cross_tgt, axis=-2)))
    return (jnp.concatenate([vel_target, str_target], axis=0), jnp.concatenate([vel_source, str_source], axis=0))

def reference(positions, strengths, cores, order, tile_counts, pair_slots, pair_count):
    per_dev = TILES_DEV * TILE
    spots = jnp.arange(NPART, dtype=jnp.int32)
    index = order + spots // per_dev * per_dev
    live = (spots % TILE < tile_counts[spots // TILE]).astype(jnp.float32)
    packed = jnp.concatenate([positions[:, index], strengths[:, index] * live, cores[index][None, :]], axis=0)
    tiles = packed.reshape(7, TILES, TILE)
    slot = jnp.arange(SLOTS, dtype=jnp.int32)
    device = slot // PAIRS_DEV
    row_index = device // N_COL
    col_index = device % N_COL
    first = pair_slots[0]
    second = pair_slots[1]
    target_tile = row_index * ROW_TILES + first
    source_tile = (second // TILES_DEV * N_COL + col_index) * TILES_DEV + second % TILES_DEV
    alive = (slot % PAIRS_DEV < pair_count[device]).astype(jnp.float32)
    react = alive * (target_tile != source_tile).astype(jnp.float32)
    blocks = SLOTS // PAIR_BLOCK

    def step(total, items):
        tgt_idx, src_idx, weight_t, weight_r = items
        tgt_terms, src_terms = pair_terms(tiles[:, tgt_idx], tiles[:, src_idx], weight_t, weight_r)
        total = total.at[:, tgt_idx].add(tgt_terms)
        total = total.at[:, src_idx].add(src_terms)
        return (total, None)
    items = (target_tile.reshape(blocks, PAIR_BLOCK), source_tile.reshape(blocks, PAIR_BLOCK), alive.reshape(blocks, PAIR_BLOCK), react.reshape(blocks, PAIR_BLOCK))
    total, _ = lax.scan(step, jnp.zeros((6, TILES, TILE), jnp.float32), items)
    total = total.reshape(6, NPART) * live
    return (total[0:3], total[3:6])
```

```python
import functools
import math

import jax
import jax.numpy as jnp
from jax import lax
from jax.experimental import pallas as pl
from jax.experimental.pallas import tpu as pltpu
from jax.sharding import PartitionSpec as P

TILE = 128
ROWS = 8
UNROLL = 2
VMEM_BYTES = 48 * 1024 * 1024

biot_factor = -1.0 / (4.0 * math.pi)


def row_ids(count=ROWS):
    return lax.broadcasted_iota(jnp.int32, (count, TILE), 0)


def roll_rows(value, shift):
    return pltpu.roll(value, shift % ROWS, 0)


def pack_kernel(counts_ref, pos_ref, str_ref, core_ref, order_ref, out_ref, stored):
    tiles = out_ref.shape[0] // ROWS
    stored[0:3, :] = pos_ref[...]
    stored[3:6, :] = str_ref[...]
    stored[6:7, :] = core_ref[...]
    stored[7:8, :] = jnp.zeros_like(core_ref[...])
    lane = lax.broadcasted_iota(jnp.int32, (ROWS, TILE), 1)
    rows = row_ids()
    is_strength = (rows >= 3) & (rows < 6)
    for tile in range(tiles):
        where_from = jnp.broadcast_to(order_ref[:, tile * TILE : (tile + 1) * TILE], (ROWS, TILE))
        inside = where_from & (TILE - 1)
        block = where_from >> 7
        value = jnp.zeros((ROWS, TILE), jnp.float32)
        for source in range(tiles):
            part = jnp.take_along_axis(stored[:, source * TILE : (source + 1) * TILE], inside, axis=1)
            value = jnp.where(block == source, part, value)
        dead = is_strength & (lane >= counts_ref[tile])
        out_ref[tile * ROWS : (tile + 1) * ROWS, :] = jnp.where(dead, 0.0, value)


def split_three(value):
    first = value.astype(jnp.bfloat16).astype(jnp.float32)
    rest = value - first
    second = rest.astype(jnp.bfloat16).astype(jnp.float32)
    return first, second, rest - second


def split_two(value):
    high = value.astype(jnp.bfloat16)
    return high, (value - high.astype(jnp.float32)).astype(jnp.bfloat16)


def features(tile, rows):
    down1, down2 = roll_rows(tile, 1), roll_rows(tile, 2)
    pos1 = jnp.where(rows == 5, roll_rows(tile, 5), down2)
    pos2 = jnp.where(rows == 3, down1, roll_rows(tile, 4))
    str1 = jnp.where(rows == 5, down2, roll_rows(tile, 7))
    str2 = jnp.where(rows == 3, roll_rows(tile, 6), down1)
    cross = pos1 * str2 - pos2 * str1
    value = jnp.where(rows < 3, roll_rows(tile, 5), jnp.where(rows < 6, cross, 0.0))
    pieces = jnp.concatenate([*split_three(value), jnp.zeros_like(value)], axis=0).astype(jnp.bfloat16)
    return jnp.concatenate([pieces, pieces], axis=1)


def add_pieces(terms):
    return terms[0:ROWS, :] + (terms[ROWS : 2 * ROWS, :] + terms[2 * ROWS : 3 * ROWS, :])


def tile_scalars(tile, rows):
    position = jnp.where(rows < 3, tile, 0.0)
    strength = jnp.where(rows < 3, roll_rows(tile, 5), 0.0)
    half = 0.5 * tile[6:7, :] * tile[6:7, :]
    norm = jnp.sum(position * position, axis=0, keepdims=True) + half
    along = jnp.sum(position * strength, axis=0, keepdims=True)
    return position, strength, half, norm, along


def target_side(tile, rows):
    position, strength, half, norm, along = tile_scalars(tile, rows)
    upper = jnp.where(rows == 3, norm, position)
    upper = jnp.where(rows == 4, along, upper)
    upper = jnp.where(rows == 5, half, upper)
    upper = jnp.where(rows == 6, 1.0, upper)
    first, second, third = split_three(jnp.concatenate([upper, strength], axis=0))
    stacked = jnp.concatenate([first, first, first, second, second, second, third, third], axis=0)
    return stacked.T.astype(jnp.bfloat16)


def source_side(tile, rows):
    position, strength, half, norm, along = tile_scalars(tile, rows)
    zero = jnp.zeros_like(position)
    one = jnp.ones_like(position)
    dist = jnp.where(rows == 6, norm, jnp.where(rows == 3, one, -2.0 * position))
    back = jnp.where(rows == 6, along, -strength)
    core = jnp.where(rows == 6, half, jnp.where(rows == 5, one, zero))
    unit = jnp.where(rows == 4, one, zero)
    blocks = []
    for upper, lower in ((dist, zero), (unit, -position), (back, zero), (core, zero)):
        pieces = [p.astype(jnp.bfloat16) for p in split_three(jnp.concatenate([upper, lower], axis=0))]
        first, second, third = pieces
        blocks.append(jnp.concatenate([first, second, third, first, second, third, first, second], axis=0))
    return jnp.concatenate(blocks, axis=1)


def cycle(value, start, rows):
    one = jnp.where(rows == 2, roll_rows(value, 2 - start), roll_rows(value, -1 - start))
    two = jnp.where(rows == 0, roll_rows(value, -2 - start), roll_rows(value, 1 - start))
    return one, two


def finish_tile(tile, sums, rows):
    smooth, grad = sums[:, :TILE], sums[:, TILE:]
    pos1, pos2 = cycle(tile, 0, rows)
    str1, str2 = cycle(tile, 3, rows)
    smooth1, smooth2 = cycle(smooth, 0, rows)
    grad1, grad2 = cycle(grad, 0, rows)
    velocity = pos1 * smooth2 - pos2 * smooth1 - roll_rows(smooth, -3)
    turn = str1 * smooth2 - str2 * smooth1
    stretch = turn - 3.0 * (pos1 * grad2 - pos2 * grad1 - roll_rows(grad, -3))
    return biot_factor * jnp.where(rows < 3, velocity, roll_rows(stretch, 3))


def pair_kernel(nrows, ncols, tiles, where_ref, slots_ref, count_ref, *refs):
    peers = nrows + ncols - 1
    ins, outs = refs[:peers], refs[peers : peers + nrows + ncols]
    row_blk, col_blk, row_mid, col_mid, left, row_sum, col_sum = refs[peers + nrows + ncols :]
    per = tiles * ROWS
    rows = row_ids()
    for block, middle, sources in (
        (row_blk, row_mid, ins[:ncols]),
        (col_blk, col_mid, (ins[0],) + ins[ncols:]),
    ):
        for k, source in enumerate(sources):
            value = source[...]
            block[k * per : (k + 1) * per, :] = value
            mean = jnp.sum(value, axis=1, keepdims=True) * (1.0 / TILE)
            keep = (lax.broadcasted_iota(jnp.int32, (per, TILE), 0) & (ROWS - 1)) < 3
            middle[k * per : (k + 1) * per, :] = jnp.where(keep, mean, 0.0)
    row_sum[...] = jnp.zeros_like(row_sum)
    col_sum[...] = jnp.zeros_like(col_sum)

    def prepare(tile, carry):
        at = pl.ds(pl.multiple_of(tile * ROWS, ROWS), ROWS)
        to = pl.ds(pl.multiple_of(tile * TILE, TILE), TILE)
        left[to, :] = target_side(row_blk[at, :] - row_mid[at, :], rows)
        return carry

    lax.fori_loop(0, ncols * tiles, prepare, 0, unroll=4)

    my_row, my_col = where_ref[0], where_ref[1]
    count = count_ref[0]

    def one_pair(slot):
        first, second = slots_ref[0, slot], slots_ref[1, slot]
        first_dev, second_dev = first // tiles, second // tiles
        first_in, second_in = first % tiles, second % tiles
        back_col = my_col - first_dev
        back_row = my_row - second_dev
        tgt = jnp.where(back_col < 0, back_col + ncols, back_col) * tiles + first_in
        src = jnp.where(back_row < 0, back_row + nrows, back_row) * tiles + second_in
        own = (first_dev == my_col) & (second_dev == my_row) & (first_in == second_in)
        alive = jnp.where(slot < count, 1.0, 0.0)
        react = jnp.where(own, 0.0, alive)
        tgt_at = pl.ds(pl.multiple_of(tgt * ROWS, ROWS), ROWS)
        src_at = pl.ds(pl.multiple_of(src * ROWS, ROWS), ROWS)
        target = row_blk[tgt_at, :]
        source = col_blk[src_at, :]
        source_here = source - row_mid[tgt_at, :]
        target_there = target - col_mid[src_at, :]
        products = jnp.dot(
            left[pl.ds(pl.multiple_of(tgt * TILE, TILE), TILE), :],
            source_side(source_here, rows),
            preferred_element_type=jnp.float32,
        )
        smooths, fronts, backs = [], [], []
        for start in range(0, TILE, 16):
            part = products[start : start + 16, :]
            dist, front, back, core = (part[:, k * TILE : (k + 1) * TILE] for k in range(4))
            inv = lax.rsqrt(dist)
            inv2 = inv * inv
            inv3 = inv2 * inv
            tail = core * (inv3 * inv2)
            smooth = inv3 + 1.5 * tail
            grad = inv2 * (smooth + tail)
            smooths.append(split_two(smooth))
            fronts.append(split_two(grad * front))
            backs.append(split_two(grad * back))

        def joined(parts, which):
            return jnp.concatenate([p[which] for p in parts], axis=0)

        smooth_hi, smooth_lo = joined(smooths, 0), joined(smooths, 1)
        front_hi, front_lo = joined(fronts, 0), joined(fronts, 1)
        back_hi, back_lo = joined(backs, 0), joined(backs, 1)
        to_target = jnp.concatenate(
            [
                jnp.concatenate([smooth_hi, smooth_lo], axis=1),
                jnp.concatenate([front_hi, front_lo], axis=1),
            ],
            axis=0,
        )
        to_source = jnp.concatenate(
            [
                jnp.concatenate([smooth_hi, back_hi], axis=1),
                jnp.concatenate([smooth_lo, back_lo], axis=1),
            ],
            axis=0,
        )
        tgt_terms = lax.dot_general(
            features(source_here, rows), to_target, (((1,), (1,)), ((), ())), preferred_element_type=jnp.float32
        )
        src_terms = jnp.dot(features(target_there, rows), to_source, preferred_element_type=jnp.float32)
        return tgt, src, alive * add_pieces(tgt_terms), react * add_pieces(src_terms)

    def visit(step, carry):
        done = [one_pair(step * UNROLL + k) for k in range(UNROLL)]
        for tgt, src, tgt_terms, src_terms in done:
            row_sum[tgt] += tgt_terms
            col_sum[src] += src_terms
        return carry

    lax.fori_loop(0, (count + UNROLL - 1) // UNROLL, visit, 0)

    for block, middle, sums, results in (
        (row_blk, row_mid, row_sum, outs[:ncols]),
        (col_blk, col_mid, col_sum, outs[ncols:]),
    ):
        for k, result in enumerate(results):

            def close(tile, carry, k=k, result=result, block=block, middle=middle, sums=sums):
                at = pl.ds(pl.multiple_of((k * tiles + tile) * ROWS, ROWS), ROWS)
                to = pl.ds(pl.multiple_of(tile * ROWS, ROWS), ROWS)
                result[to, :] = finish_tile(block[at, :] - middle[at, :], sums[k * tiles + tile], rows)
                return carry

            lax.fori_loop(0, tiles, close, 0, unroll=True)


def total_kernel(counts_ref, *refs):
    vel_ref, str_ref = refs[-2:]
    tiles = vel_ref.shape[1] // TILE
    lane = lax.broadcasted_iota(jnp.int32, (ROWS, TILE), 1)
    for tile in range(tiles):
        at = slice(tile * ROWS, (tile + 1) * ROWS)
        total = refs[0][at, :]
        for ref in refs[1:-2]:
            total = total + ref[at, :]
        total = jnp.where(lane < counts_ref[tile], total, 0.0)
        vel_ref[:, tile * TILE : (tile + 1) * TILE] = total[0:3, :]
        str_ref[:, tile * TILE : (tile + 1) * TILE] = total[3:6, :]


def shards(positions, strengths, cores, order, tile_counts, pair_slots, pair_count):
    tiles = tile_counts.shape[0]
    per_dev = tiles * TILE
    nrows = lax.axis_size("row")
    ncols = lax.axis_size("col")
    smem = pl.BlockSpec(memory_space=pltpu.SMEM)
    vmem = pl.BlockSpec(memory_space=pltpu.VMEM)
    tile_block = jax.ShapeDtypeStruct((tiles * ROWS, TILE), jnp.float32)
    params = pltpu.CompilerParams(vmem_limit_bytes=VMEM_BYTES)

    packed = pl.pallas_call(
        pack_kernel,
        out_shape=tile_block,
        in_specs=[smem] + [vmem] * 4,
        out_specs=vmem,
        scratch_shapes=[pltpu.VMEM((ROWS, per_dev), jnp.float32)],
        compiler_params=params,
        name="pack",
    )(tile_counts, positions, strengths, cores.reshape(1, per_dev), order.reshape(1, per_dev))

    def shift(value, axis, size, by):
        return lax.ppermute(value, axis, [(d, (d + by) % size) for d in range(size)])

    from_row = [shift(packed, "col", ncols, k) for k in range(1, ncols)]
    from_col = [shift(packed, "row", nrows, k) for k in range(1, nrows)]
    where = jnp.stack([lax.axis_index("row"), lax.axis_index("col")]).astype(jnp.int32)
    sums = pl.pallas_call(
        functools.partial(pair_kernel, nrows, ncols, tiles),
        out_shape=[tile_block] * (nrows + ncols),
        in_specs=[smem] * 3 + [vmem] * (nrows + ncols - 1),
        out_specs=[vmem] * (nrows + ncols),
        scratch_shapes=[
            pltpu.VMEM((ncols * tiles * ROWS, TILE), jnp.float32),
            pltpu.VMEM((nrows * tiles * ROWS, TILE), jnp.float32),
            pltpu.VMEM((ncols * tiles * ROWS, TILE), jnp.float32),
            pltpu.VMEM((nrows * tiles * ROWS, TILE), jnp.float32),
            pltpu.VMEM((ncols * tiles * TILE, TILE), jnp.bfloat16),
            pltpu.VMEM((ncols * tiles, ROWS, 2 * TILE), jnp.float32),
            pltpu.VMEM((nrows * tiles, ROWS, 2 * TILE), jnp.float32),
        ],
        compiler_params=params,
        name="pairs",
    )(where, pair_slots, pair_count, packed, *from_row, *from_col)
    tgt_sums, src_sums = sums[:ncols], sums[ncols:]
    parts = [tgt_sums[0], src_sums[0]]
    parts += [shift(tgt_sums[k], "col", ncols, -k) for k in range(1, ncols)]
    parts += [shift(src_sums[k], "row", nrows, -k) for k in range(1, nrows)]
    velocity, stretching = pl.pallas_call(
        total_kernel,
        out_shape=[jax.ShapeDtypeStruct((3, per_dev), jnp.float32)] * 2,
        in_specs=[smem] + [vmem] * len(parts),
        out_specs=[vmem, vmem],
        compiler_params=params,
        name="totals",
    )(tile_counts, *parts)
    return velocity, stretching


def solution(mesh):
    whole = ("groups", "row", "col")
    in_specs = (P(None, whole), P(None, whole), P(whole), P(whole), P(whole), P(None, whole), P(whole))
    out_specs = (P(None, whole), P(None, whole))
    return jax.shard_map(shards, mesh=mesh, in_specs=in_specs, out_specs=out_specs, check_vma=False)
```

```python
import functools
import math

import jax
import jax.numpy as jnp
from jax import lax
from jax.experimental import pallas as pl
from jax.experimental.pallas import tpu as pltpu
from jax.sharding import PartitionSpec as P

TILE = 128
ROWS = 8
UNROLL = 4
VMEM_BYTES = 48 * 1024 * 1024
PACK_BYTES = 60 * 1024 * 1024

biot_factor = -1.0 / (4.0 * math.pi)


def row_ids(count=ROWS):
    return lax.broadcasted_iota(jnp.int32, (count, TILE), 0)


def roll_rows(value, shift):
    return pltpu.roll(value, shift % ROWS, 0)


def pack_kernel(counts_ref, pos_hbm, str_hbm, core_hbm, order_hbm, row_ref, col_ref, stored, order_ref, arrived):
    tiles = order_ref.shape[1] // TILE
    pairs = (
        (pos_hbm, stored.at[0:3, :]),
        (str_hbm, stored.at[3:6, :]),
        (core_hbm, stored.at[6:7, :]),
        (order_hbm, order_ref),
    )
    copies = [pltpu.make_async_copy(src, dst, arrived.at[k]) for k, (src, dst) in enumerate(pairs)]
    for copy in copies:
        copy.start()
    stored[7:8, :] = jnp.zeros((1, stored.shape[1]), jnp.float32)
    for copy in copies:
        copy.wait()
    lane = lax.broadcasted_iota(jnp.int32, (ROWS, TILE), 1)
    rows = row_ids()
    is_strength = (rows >= 3) & (rows < 6)
    for tile in range(tiles):
        where_from = jnp.broadcast_to(order_ref[:, tile * TILE : (tile + 1) * TILE], (ROWS, TILE))
        inside = where_from & (TILE - 1)
        block = where_from >> 7
        value = jnp.zeros((ROWS, TILE), jnp.float32)
        for source in range(tiles):
            part = jnp.take_along_axis(stored[:, source * TILE : (source + 1) * TILE], inside, axis=1)
            value = jnp.where(block == source, part, value)
        dead = is_strength & (lane >= counts_ref[tile])
        value = jnp.where(dead, 0.0, value)
        for ref in (row_ref, col_ref):
            for start in range(tile * ROWS, ref.shape[0], tiles * ROWS):
                ref[start : start + ROWS, :] = value


def split_three(value):
    first = value.astype(jnp.bfloat16).astype(jnp.float32)
    rest = value - first
    second = rest.astype(jnp.bfloat16).astype(jnp.float32)
    return first, second, rest - second


def split_two(value):
    high = value.astype(jnp.bfloat16)
    return high, (value - high.astype(jnp.float32)).astype(jnp.bfloat16)


def features(tile, rows):
    down1, down2 = roll_rows(tile, 1), roll_rows(tile, 2)
    pos1 = jnp.where(rows == 5, roll_rows(tile, 5), down2)
    pos2 = jnp.where(rows == 3, down1, roll_rows(tile, 4))
    str1 = jnp.where(rows == 5, down2, roll_rows(tile, 7))
    str2 = jnp.where(rows == 3, roll_rows(tile, 6), down1)
    cross = pos1 * str2 - pos2 * str1
    value = jnp.where(rows < 3, roll_rows(tile, 5), jnp.where(rows < 6, cross, 0.0))
    pieces = jnp.concatenate([*split_three(value), jnp.zeros_like(value)], axis=0).astype(jnp.bfloat16)
    return jnp.concatenate([pieces, pieces], axis=1)


def add_pieces(terms):
    return terms[0:ROWS, :] + (terms[ROWS : 2 * ROWS, :] + terms[2 * ROWS : 3 * ROWS, :])


def tile_scalars(tile, rows):
    position = jnp.where(rows < 3, tile, 0.0)
    strength = jnp.where(rows < 3, roll_rows(tile, 5), 0.0)
    half = 0.5 * tile[6:7, :] * tile[6:7, :]
    norm = jnp.sum(position * position, axis=0, keepdims=True) + half
    along = jnp.sum(position * strength, axis=0, keepdims=True)
    return position, strength, half, norm, along


def target_side(tile, rows):
    position, strength, half, norm, along = tile_scalars(tile, rows)
    upper = jnp.where(rows == 3, norm, position)
    upper = jnp.where(rows == 4, along, upper)
    upper = jnp.where(rows == 5, half, upper)
    upper = jnp.where(rows == 6, 1.0, upper)
    first, second, third = split_three(jnp.concatenate([upper, strength], axis=0))
    stacked = jnp.concatenate([first, first, first, second, second, second, third, third], axis=0)
    return stacked.T.astype(jnp.bfloat16)


def source_side(tile, rows):
    position, strength, half, norm, along = tile_scalars(tile, rows)
    zero = jnp.zeros_like(position)
    one = jnp.ones_like(position)
    dist = jnp.where(rows == 6, norm, jnp.where(rows == 3, one, -2.0 * position))
    back = jnp.where(rows == 6, along, -strength)
    core = jnp.where(rows == 6, half, jnp.where(rows == 5, one, zero))
    unit = jnp.where(rows == 4, one, zero)
    back_shift = split_three(-position)
    halves = (
        [jnp.concatenate([p, zero], axis=0) for p in split_three(dist)],
        [jnp.concatenate([u, p], axis=0) for u, p in zip((unit, zero, zero), back_shift)],
        [jnp.concatenate([p, zero], axis=0) for p in split_three(back)],
        [jnp.concatenate([p, zero], axis=0) for p in split_three(core)],
    )
    blocks = []
    for pieces in halves:
        first, second, third = [p.astype(jnp.bfloat16) for p in pieces]
        blocks.append(jnp.concatenate([first, second, third, first, second, third, first, second], axis=0))
    return jnp.concatenate(blocks, axis=1)


def cycle(value, start, rows):
    one = jnp.where(rows == 2, roll_rows(value, 2 - start), roll_rows(value, -1 - start))
    two = jnp.where(rows == 0, roll_rows(value, -2 - start), roll_rows(value, 1 - start))
    return one, two


def finish_tile(tile, sums, rows):
    smooth, grad = sums[:, :TILE], sums[:, TILE:]
    pos1, pos2 = cycle(tile, 0, rows)
    str1, str2 = cycle(tile, 3, rows)
    smooth1, smooth2 = cycle(smooth, 0, rows)
    grad1, grad2 = cycle(grad, 0, rows)
    velocity = pos1 * smooth2 - pos2 * smooth1 - roll_rows(smooth, -3)
    turn = str1 * smooth2 - str2 * smooth1
    stretch = turn - 3.0 * (pos1 * grad2 - pos2 * grad1 - roll_rows(grad, -3))
    return biot_factor * jnp.where(rows < 3, velocity, roll_rows(stretch, 3))


def pair_kernel(tiles, where_ref, slots_ref, count_ref, row_blk, col_blk, row_out, col_out, *scratch):
    row_mid, col_mid, left, row_sum, col_sum = scratch
    row_tiles, col_tiles = row_sum.shape[0], col_sum.shape[0]
    rows = row_ids()
    for block, middle in ((row_blk, row_mid), (col_blk, col_mid)):
        per = tiles * ROWS
        keep = (lax.broadcasted_iota(jnp.int32, (per, TILE), 0) & (ROWS - 1)) < 3
        for start in range(0, block.shape[0], per):
            mean = jnp.sum(block[start : start + per, :], axis=1, keepdims=True) * (1.0 / TILE)
            middle[start : start + per, :] = jnp.where(keep, mean, 0.0)
    row_sum[...] = jnp.zeros_like(row_sum)
    col_sum[...] = jnp.zeros_like(col_sum)

    def prepare(tile, carry):
        at = pl.ds(pl.multiple_of(tile * ROWS, ROWS), ROWS)
        to = pl.ds(pl.multiple_of(tile * TILE, TILE), TILE)
        left[to, :] = target_side(row_blk[at, :] - row_mid[at, :], rows)
        return carry

    lax.fori_loop(0, row_tiles, prepare, 0, unroll=4)

    my_row, my_col = where_ref[0], where_ref[1]
    count = count_ref[0]

    def one_pair(slot):
        tgt, src = slots_ref[0, slot], slots_ref[1, slot]
        own = (tgt // tiles == my_col) & (src // tiles == my_row) & (tgt % tiles == src % tiles)
        alive = jnp.where(slot < count, 1.0, 0.0)
        react = jnp.where(own, 0.0, alive)
        tgt_at = pl.ds(pl.multiple_of(tgt * ROWS, ROWS), ROWS)
        src_at = pl.ds(pl.multiple_of(src * ROWS, ROWS), ROWS)
        target = row_blk[tgt_at, :]
        source = col_blk[src_at, :]
        source_here = source - row_mid[tgt_at, :]
        target_there = target - col_mid[src_at, :]
        products = jnp.dot(
            left[pl.ds(pl.multiple_of(tgt * TILE, TILE), TILE), :],
            source_side(source_here, rows),
            preferred_element_type=jnp.float32,
        )
        smooths, fronts, backs = [], [], []
        for start in range(0, TILE, 16):
            part = products[start : start + 16, :]
            dist, front, back, core = (part[:, k * TILE : (k + 1) * TILE] for k in range(4))
            inv = lax.rsqrt(dist)
            inv2 = inv * inv
            inv3 = inv2 * inv
            tail = core * (inv3 * inv2)
            smooth = inv3 + 1.5 * tail
            grad = inv2 * (smooth + tail)
            smooths.append(split_two(smooth))
            fronts.append(split_two(grad * front))
            backs.append(split_two(grad * back))

        def joined(parts, which):
            return jnp.concatenate([p[which] for p in parts], axis=0)

        smooth_hi, smooth_lo = joined(smooths, 0), joined(smooths, 1)
        front_hi, front_lo = joined(fronts, 0), joined(fronts, 1)
        back_hi, back_lo = joined(backs, 0), joined(backs, 1)
        to_target = jnp.concatenate(
            [
                jnp.concatenate([smooth_hi, smooth_lo], axis=1),
                jnp.concatenate([front_hi, front_lo], axis=1),
            ],
            axis=0,
        )
        to_source = jnp.concatenate(
            [
                jnp.concatenate([smooth_hi, back_hi], axis=1),
                jnp.concatenate([smooth_lo, back_lo], axis=1),
            ],
            axis=0,
        )
        tgt_terms = lax.dot_general(
            features(source_here, rows), to_target, (((1,), (1,)), ((), ())), preferred_element_type=jnp.float32
        )
        src_terms = jnp.dot(features(target_there, rows), to_source, preferred_element_type=jnp.float32)
        return tgt, src, alive * add_pieces(tgt_terms), react * add_pieces(src_terms)

    def visit(step, carry):
        done = [one_pair(step * UNROLL + k) for k in range(UNROLL)]
        for tgt, src, tgt_terms, src_terms in done:
            row_sum[tgt] += tgt_terms
            col_sum[src] += src_terms
        return carry

    lax.fori_loop(0, (count + UNROLL - 1) // UNROLL, visit, 0)

    for block, middle, sums, result in (
        (row_blk, row_mid, row_sum, row_out),
        (col_blk, col_mid, col_sum, col_out),
    ):

        def close(tile, carry, block=block, middle=middle, sums=sums, result=result):
            at = pl.ds(pl.multiple_of(tile * ROWS, ROWS), ROWS)
            result[at, :] = finish_tile(block[at, :] - middle[at, :], sums[tile], rows)
            return carry

        lax.fori_loop(0, sums.shape[0], close, 0, unroll=8)


def total_kernel(counts_ref, row_ref, col_ref, vel_ref, str_ref):
    tiles = vel_ref.shape[1] // TILE
    lane = lax.broadcasted_iota(jnp.int32, (ROWS, TILE), 1)
    for tile in range(tiles):
        total = None
        for ref in (row_ref, col_ref):
            for start in range(tile * ROWS, ref.shape[0], tiles * ROWS):
                part = ref[start : start + ROWS, :]
                total = part if total is None else total + part
        total = jnp.where(lane < counts_ref[tile], total, 0.0)
        vel_ref[:, tile * TILE : (tile + 1) * TILE] = total[0:3, :]
        str_ref[:, tile * TILE : (tile + 1) * TILE] = total[3:6, :]


def shards(positions, strengths, cores, order, tile_counts, pair_slots, pair_count):
    tiles = tile_counts.shape[0]
    per_dev = tiles * TILE
    nrows = lax.axis_size("row")
    ncols = lax.axis_size("col")
    row_tiles, col_tiles = ncols * tiles, nrows * tiles
    smem = pl.BlockSpec(memory_space=pltpu.SMEM)
    vmem = pl.BlockSpec(memory_space=pltpu.VMEM)
    hbm = pl.BlockSpec(memory_space=pltpu.HBM)
    params = pltpu.CompilerParams(vmem_limit_bytes=VMEM_BYTES)

    def block(count):
        return jax.ShapeDtypeStruct((count * ROWS, TILE), jnp.float32)

    row_copies, col_copies = pl.pallas_call(
        pack_kernel,
        out_shape=[block(row_tiles), block(col_tiles)],
        in_specs=[smem] + [hbm] * 4,
        out_specs=[vmem] * 2,
        scratch_shapes=[
            pltpu.VMEM((ROWS, per_dev), jnp.float32),
            pltpu.VMEM((1, per_dev), jnp.int32),
            pltpu.SemaphoreType.DMA((4,)),
        ],
        compiler_params=pltpu.CompilerParams(vmem_limit_bytes=PACK_BYTES),
        name="pack",
    )(tile_counts, positions, strengths, cores.reshape(1, per_dev), order.reshape(1, per_dev))

    row_blk = lax.all_to_all(row_copies, "col", 0, 0, tiled=True)
    col_blk = lax.all_to_all(col_copies, "row", 0, 0, tiled=True)
    where = jnp.stack([lax.axis_index("row"), lax.axis_index("col")]).astype(jnp.int32)
    row_sum, col_sum = pl.pallas_call(
        functools.partial(pair_kernel, tiles),
        out_shape=[block(row_tiles), block(col_tiles)],
        in_specs=[smem] * 3 + [vmem] * 2,
        out_specs=[vmem] * 2,
        scratch_shapes=[
            pltpu.VMEM((row_tiles * ROWS, TILE), jnp.float32),
            pltpu.VMEM((col_tiles * ROWS, TILE), jnp.float32),
            pltpu.VMEM((row_tiles * TILE, TILE), jnp.bfloat16),
            pltpu.VMEM((row_tiles, ROWS, 2 * TILE), jnp.float32),
            pltpu.VMEM((col_tiles, ROWS, 2 * TILE), jnp.float32),
        ],
        compiler_params=params,
        name="pairs",
    )(where, pair_slots, pair_count, row_blk, col_blk)
    row_back = lax.all_to_all(row_sum, "col", 0, 0, tiled=True)
    col_back = lax.all_to_all(col_sum, "row", 0, 0, tiled=True)
    velocity, stretching = pl.pallas_call(
        total_kernel,
        out_shape=[jax.ShapeDtypeStruct((3, per_dev), jnp.float32)] * 2,
        in_specs=[smem] + [vmem] * 2,
        out_specs=[vmem, vmem],
        compiler_params=params,
        name="totals",
    )(tile_counts, row_back, col_back)
    return velocity, stretching


def solution(mesh):
    whole = ("groups", "row", "col")
    in_specs = (P(None, whole), P(None, whole), P(whole), P(whole), P(whole), P(None, whole), P(whole))
    out_specs = (P(None, whole), P(None, whole))
    return jax.shard_map(shards, mesh=mesh, in_specs=in_specs, out_specs=out_specs, check_vma=False)
```

```python
import functools
import math

import jax
import jax.numpy as jnp
from jax import lax
from jax.experimental import pallas as pl
from jax.experimental.pallas import tpu as pltpu
from jax.sharding import PartitionSpec as P

TILE = 128
ROWS = 8
UNROLL = 4
VMEM_BYTES = 48 * 1024 * 1024
PACK_BYTES = 60 * 1024 * 1024

biot_factor = -1.0 / (4.0 * math.pi)


def row_ids(count=ROWS):
    return lax.broadcasted_iota(jnp.int32, (count, TILE), 0)


def roll_rows(value, shift):
    return pltpu.roll(value, shift % ROWS, 0)


def pack_kernel(counts_ref, pos_hbm, str_hbm, core_hbm, order_hbm, out_ref, stored, order_ref, arrived):
    tiles = order_ref.shape[1] // TILE
    pairs = (
        (pos_hbm, stored.at[0:3, :]),
        (str_hbm, stored.at[3:6, :]),
        (core_hbm, stored.at[6:7, :]),
        (order_hbm, order_ref),
    )
    copies = [pltpu.make_async_copy(src, dst, arrived.at[k]) for k, (src, dst) in enumerate(pairs)]
    for copy in copies:
        copy.start()
    stored[7:8, :] = jnp.zeros((1, stored.shape[1]), jnp.float32)
    for copy in copies:
        copy.wait()
    lane = lax.broadcasted_iota(jnp.int32, (ROWS, TILE), 1)
    rows = row_ids()
    is_strength = (rows >= 3) & (rows < 6)
    for tile in range(tiles):
        where_from = jnp.broadcast_to(order_ref[:, tile * TILE : (tile + 1) * TILE], (ROWS, TILE))
        inside = where_from & (TILE - 1)
        block = where_from >> 7
        value = jnp.zeros((ROWS, TILE), jnp.float32)
        for source in range(tiles):
            part = jnp.take_along_axis(stored[:, source * TILE : (source + 1) * TILE], inside, axis=1)
            value = jnp.where(block == source, part, value)
        dead = is_strength & (lane >= counts_ref[tile])
        out_ref[tile * ROWS : (tile + 1) * ROWS, :] = jnp.where(dead, 0.0, value)


def partner(me, k, size):
    assert size & (size - 1) == 0, size
    return me ^ k


def split_three(value):
    first = value.astype(jnp.bfloat16).astype(jnp.float32)
    rest = value - first
    second = rest.astype(jnp.bfloat16).astype(jnp.float32)
    return first, second, rest - second


def split_two(value):
    high = value.astype(jnp.bfloat16)
    return high, (value - high.astype(jnp.float32)).astype(jnp.bfloat16)


def features(tile, rows):
    down1, down2 = roll_rows(tile, 1), roll_rows(tile, 2)
    pos1 = jnp.where(rows == 5, roll_rows(tile, 5), down2)
    pos2 = jnp.where(rows == 3, down1, roll_rows(tile, 4))
    str1 = jnp.where(rows == 5, down2, roll_rows(tile, 7))
    str2 = jnp.where(rows == 3, roll_rows(tile, 6), down1)
    cross = pos1 * str2 - pos2 * str1
    value = jnp.where(rows < 3, roll_rows(tile, 5), jnp.where(rows < 6, cross, 0.0))
    return jnp.concatenate([*split_three(value), jnp.zeros_like(value)], axis=0)


def features_left(tile, rows):
    pieces = features(tile, rows).astype(jnp.bfloat16)
    return jnp.concatenate([pieces, pieces], axis=1)


def features_right(tile, rows):
    pieces = features(tile, rows)
    zero = jnp.zeros_like(pieces)
    smooth = jnp.concatenate([pieces, zero], axis=0).T.astype(jnp.bfloat16)
    grad = jnp.concatenate([zero, pieces], axis=0).T.astype(jnp.bfloat16)
    return jnp.concatenate([smooth, smooth, grad, grad], axis=0)


def add_pieces(terms):
    return terms[0:ROWS, :] + (terms[ROWS : 2 * ROWS, :] + terms[2 * ROWS : 3 * ROWS, :])


def tile_scalars(tile, rows):
    position = jnp.where(rows < 3, tile, 0.0)
    strength = jnp.where(rows < 3, roll_rows(tile, 5), 0.0)
    half = 0.5 * tile[6:7, :] * tile[6:7, :]
    norm = jnp.sum(position * position, axis=0, keepdims=True) + half
    along = jnp.sum(position * strength, axis=0, keepdims=True)
    return position, strength, half, norm, along


def target_side(tile, rows):
    position, strength, half, norm, along = tile_scalars(tile, rows)
    upper = jnp.where(rows == 3, norm, position)
    upper = jnp.where(rows == 4, along, upper)
    upper = jnp.where(rows == 5, 1.0, upper)
    first, second, third = split_three(jnp.concatenate([upper, strength], axis=0))
    stacked = jnp.concatenate([first, first, first, second, second, second, third, third], axis=0)
    return stacked.T.astype(jnp.bfloat16)


def source_side(tile, rows):
    position, strength, half, norm, along = tile_scalars(tile, rows)
    zero = jnp.zeros_like(position)
    one = jnp.ones_like(position)
    dist = jnp.where(rows == 5, norm, jnp.where(rows == 3, one, -2.0 * position))
    back = jnp.where(rows == 5, along, -strength)
    unit = jnp.where(rows == 4, one, zero)
    shift = split_three(-position)
    halves = (
        [jnp.concatenate([p, zero], axis=0) for p in split_three(dist)],
        [jnp.concatenate([u, p], axis=0) for u, p in zip((unit, zero, zero), shift)],
        [jnp.concatenate([p, zero], axis=0) for p in split_three(back)],
    )
    blocks = []
    for pieces in halves:
        first, second, third = [p.astype(jnp.bfloat16) for p in pieces]
        blocks.append(jnp.concatenate([first, second, third, first, second, third, first, second], axis=0))
    return jnp.concatenate(blocks, axis=1)


def cycle(value, start, rows):
    one = jnp.where(rows == 2, roll_rows(value, 2 - start), roll_rows(value, -1 - start))
    two = jnp.where(rows == 0, roll_rows(value, -2 - start), roll_rows(value, 1 - start))
    return one, two


def finish_tile(tile, smooth, grad, rows):
    pos1, pos2 = cycle(tile, 0, rows)
    str1, str2 = cycle(tile, 3, rows)
    smooth1, smooth2 = cycle(smooth, 0, rows)
    grad1, grad2 = cycle(grad, 0, rows)
    velocity = pos1 * smooth2 - pos2 * smooth1 - roll_rows(smooth, -3)
    turn = str1 * smooth2 - str2 * smooth1
    stretch = turn - 3.0 * (pos1 * grad2 - pos2 * grad1 - roll_rows(grad, -3))
    return biot_factor * jnp.where(rows < 3, velocity, roll_rows(stretch, 3))


def pair_kernel(nrows, ncols, tiles, where_ref, slots_ref, count_ref, *refs):
    peers = nrows + ncols - 1
    ins, outs = refs[:peers], refs[peers : peers + nrows + ncols]
    row_blk, col_blk, row_mid, col_mid, left, halves, row_sum, col_sum = refs[peers + nrows + ncols :]
    per = tiles * ROWS
    rows = row_ids()
    my_row, my_col = where_ref[0], where_ref[1]
    count = count_ref[0]
    keep = (lax.broadcasted_iota(jnp.int32, (per, TILE), 0) & (ROWS - 1)) < 3
    for block, middle, me, size, sources in (
        (row_blk, row_mid, my_col, ncols, ins[:ncols]),
        (col_blk, col_mid, my_row, nrows, (ins[0],) + ins[ncols:]),
    ):
        for k, source in enumerate(sources):
            at = pl.ds(pl.multiple_of(partner(me, k, size) * per, per), per)
            value = source[...]
            block[at, :] = value
            mean = jnp.sum(value, axis=1, keepdims=True) * (1.0 / TILE)
            middle[at, :] = jnp.where(keep, mean, 0.0)
    row_sum[...] = jnp.zeros_like(row_sum)
    col_sum[...] = jnp.zeros_like(col_sum)

    def prepare(tile, carry):
        at = pl.ds(pl.multiple_of(tile * ROWS, ROWS), ROWS)
        to = pl.ds(pl.multiple_of(tile * TILE, TILE), TILE)
        here = row_blk[at, :] - row_mid[at, :]
        left[to, :] = target_side(here, rows)
        core = jnp.broadcast_to(here[6:7, :], (TILE, TILE)).T
        halves[to, :] = 0.5 * core * core
        return carry

    lax.fori_loop(0, ncols * tiles, prepare, 0, unroll=4)

    def one_pair(slot):
        tgt, src = slots_ref[0, slot], slots_ref[1, slot]
        own = (tgt // tiles == my_col) & (src // tiles == my_row) & (tgt % tiles == src % tiles)
        alive = jnp.where(slot < count, 1.0, 0.0)
        react = jnp.where(own, 0.0, alive)
        tgt_at = pl.ds(pl.multiple_of(tgt * ROWS, ROWS), ROWS)
        src_at = pl.ds(pl.multiple_of(src * ROWS, ROWS), ROWS)
        wide = pl.ds(pl.multiple_of(tgt * TILE, TILE), TILE)
        target = row_blk[tgt_at, :]
        source = col_blk[src_at, :]
        source_here = source - row_mid[tgt_at, :]
        target_there = target - col_mid[src_at, :]
        products = jnp.dot(left[wide, :], source_side(source_here, rows), preferred_element_type=jnp.float32)
        half_i = halves[wide, :]
        half_j = 0.5 * source[6:7, :] * source[6:7, :]
        smooths, fronts, backs = [], [], []
        for start in range(0, TILE, 16):
            part = products[start : start + 16, :]
            dist, front, back = (part[:, k * TILE : (k + 1) * TILE] for k in range(3))
            core = half_i[start : start + 16, :] + half_j
            inv = lax.rsqrt(dist)
            inv2 = inv * inv
            inv3 = inv2 * inv
            tail = core * (inv3 * inv2)
            smooth = inv3 + 1.5 * tail
            grad = inv2 * (smooth + tail)
            smooths.append(split_two(smooth))
            fronts.append(split_two(grad * front))
            backs.append(split_two(grad * back))

        def joined(parts, which):
            return jnp.concatenate([p[which] for p in parts], axis=0)

        smooth_hi, smooth_lo = joined(smooths, 0), joined(smooths, 1)
        to_target = jnp.concatenate([smooth_hi, smooth_lo, joined(fronts, 0), joined(fronts, 1)], axis=1)
        to_source = jnp.concatenate(
            [
                jnp.concatenate([smooth_hi, joined(backs, 0)], axis=1),
                jnp.concatenate([smooth_lo, joined(backs, 1)], axis=1),
            ],
            axis=0,
        )
        tgt_terms = jnp.dot(to_target, features_right(source_here, rows), preferred_element_type=jnp.float32)
        src_terms = jnp.dot(features_left(target_there, rows), to_source, preferred_element_type=jnp.float32)
        return tgt, src, alive * tgt_terms, react * add_pieces(src_terms)

    def visit(step, carry):
        done = [one_pair(step * UNROLL + k) for k in range(UNROLL)]
        for tgt, src, tgt_terms, src_terms in done:
            row_sum[pl.ds(pl.multiple_of(tgt * TILE, TILE), TILE), :] += tgt_terms
            col_sum[pl.ds(pl.multiple_of(src * ROWS, ROWS), ROWS), :] += src_terms
        return carry

    lax.fori_loop(0, (count + UNROLL - 1) // UNROLL, visit, 0)

    for k in range(ncols):
        base = partner(my_col, k, ncols) * tiles

        def close_row(tile, carry, result=outs[k], base=base):
            at = pl.ds(pl.multiple_of((base + tile) * ROWS, ROWS), ROWS)
            sums = row_sum[pl.ds(pl.multiple_of((base + tile) * TILE, TILE), TILE), :].T
            smooth, grad = add_pieces(sums), add_pieces(sums[4 * ROWS :, :])
            to = pl.ds(pl.multiple_of(tile * ROWS, ROWS), ROWS)
            result[to, :] = finish_tile(row_blk[at, :] - row_mid[at, :], smooth, grad, rows)
            return carry

        lax.fori_loop(0, tiles, close_row, 0, unroll=True)
    for k in range(nrows):
        base = partner(my_row, k, nrows) * tiles

        def close_col(tile, carry, result=outs[ncols + k], base=base):
            at = pl.ds(pl.multiple_of((base + tile) * ROWS, ROWS), ROWS)
            sums = col_sum[at, :]
            to = pl.ds(pl.multiple_of(tile * ROWS, ROWS), ROWS)
            result[to, :] = finish_tile(col_blk[at, :] - col_mid[at, :], sums[:, :TILE], sums[:, TILE:], rows)
            return carry

        lax.fori_loop(0, tiles, close_col, 0, unroll=True)


def total_kernel(counts_ref, *refs):
    vel_ref, str_ref = refs[-2:]
    tiles = vel_ref.shape[1] // TILE
    lane = lax.broadcasted_iota(jnp.int32, (ROWS, TILE), 1)
    for tile in range(tiles):
        at = slice(tile * ROWS, (tile + 1) * ROWS)
        total = refs[0][at, :]
        for ref in refs[1:-2]:
            total = total + ref[at, :]
        total = jnp.where(lane < counts_ref[tile], total, 0.0)
        vel_ref[:, tile * TILE : (tile + 1) * TILE] = total[0:3, :]
        str_ref[:, tile * TILE : (tile + 1) * TILE] = total[3:6, :]


def shards(positions, strengths, cores, order, tile_counts, pair_slots, pair_count):
    tiles = tile_counts.shape[0]
    per_dev = tiles * TILE
    nrows = lax.axis_size("row")
    ncols = lax.axis_size("col")
    row_tiles, col_tiles = ncols * tiles, nrows * tiles
    smem = pl.BlockSpec(memory_space=pltpu.SMEM)
    vmem = pl.BlockSpec(memory_space=pltpu.VMEM)
    hbm = pl.BlockSpec(memory_space=pltpu.HBM)
    block = jax.ShapeDtypeStruct((tiles * ROWS, TILE), jnp.float32)

    packed = pl.pallas_call(
        pack_kernel,
        out_shape=block,
        in_specs=[smem] + [hbm] * 4,
        out_specs=vmem,
        scratch_shapes=[
            pltpu.VMEM((ROWS, per_dev), jnp.float32),
            pltpu.VMEM((1, per_dev), jnp.int32),
            pltpu.SemaphoreType.DMA((4,)),
        ],
        compiler_params=pltpu.CompilerParams(vmem_limit_bytes=PACK_BYTES),
        name="pack",
    )(tile_counts, positions, strengths, cores.reshape(1, per_dev), order.reshape(1, per_dev))

    def swap(value, axis, size, k):
        return lax.ppermute(value, axis, [(d, partner(d, k, size)) for d in range(size)])

    from_row = [swap(packed, "col", ncols, k) for k in range(1, ncols)]
    from_col = [swap(packed, "row", nrows, k) for k in range(1, nrows)]
    where = jnp.stack([lax.axis_index("row"), lax.axis_index("col")]).astype(jnp.int32)
    sums = pl.pallas_call(
        functools.partial(pair_kernel, nrows, ncols, tiles),
        out_shape=[block] * (nrows + ncols),
        in_specs=[smem] * 3 + [vmem] * (nrows + ncols - 1),
        out_specs=[vmem] * (nrows + ncols),
        scratch_shapes=[
            pltpu.VMEM((row_tiles * ROWS, TILE), jnp.float32),
            pltpu.VMEM((col_tiles * ROWS, TILE), jnp.float32),
            pltpu.VMEM((row_tiles * ROWS, TILE), jnp.float32),
            pltpu.VMEM((col_tiles * ROWS, TILE), jnp.float32),
            pltpu.VMEM((row_tiles * TILE, TILE), jnp.bfloat16),
            pltpu.VMEM((row_tiles * TILE, TILE), jnp.float32),
            pltpu.VMEM((row_tiles * TILE, 64), jnp.float32),
            pltpu.VMEM((col_tiles * ROWS, 2 * TILE), jnp.float32),
        ],
        compiler_params=pltpu.CompilerParams(vmem_limit_bytes=VMEM_BYTES),
        name="pairs",
    )(where, pair_slots, pair_count, packed, *from_row, *from_col)
    parts = [sums[0], sums[ncols]]
    parts += [swap(sums[k], "col", ncols, k) for k in range(1, ncols)]
    parts += [swap(sums[ncols + k], "row", nrows, k) for k in range(1, nrows)]
    velocity, stretching = pl.pallas_call(
        total_kernel,
        out_shape=[jax.ShapeDtypeStruct((3, per_dev), jnp.float32)] * 2,
        in_specs=[smem] + [vmem] * len(parts),
        out_specs=[vmem, vmem],
        compiler_params=pltpu.CompilerParams(vmem_limit_bytes=VMEM_BYTES),
        name="totals",
    )(tile_counts, *parts)
    return velocity, stretching


def solution(mesh):
    whole = ("groups", "row", "col")
    in_specs = (P(None, whole), P(None, whole), P(whole), P(whole), P(whole), P(None, whole), P(whole))
    out_specs = (P(None, whole), P(None, whole))
    return jax.shard_map(shards, mesh=mesh, in_specs=in_specs, out_specs=out_specs, check_vma=False)
```

```python
import functools
import math

import jax
import jax.numpy as jnp
from jax import lax
from jax.experimental import pallas as pl
from jax.experimental.pallas import tpu as pltpu
from jax.sharding import PartitionSpec as P

TILE = 128
ROWS = 8
STEPS = 4
VMEM_BYTES = 48 * 1024 * 1024
PACK_BYTES = 60 * 1024 * 1024

biot_factor = -1.0 / (4.0 * math.pi)


def row_ids(count=ROWS):
    return lax.broadcasted_iota(jnp.int32, (count, TILE), 0)


def roll_rows(value, shift):
    return pltpu.roll(value, shift % ROWS, 0)


def pack_kernel(counts_ref, pos_hbm, str_hbm, core_hbm, order_hbm, out_ref, stored, order_ref, arrived):
    tiles = order_ref.shape[1] // TILE
    pairs = (
        (pos_hbm, stored.at[0:3, :]),
        (str_hbm, stored.at[3:6, :]),
        (core_hbm, stored.at[6:7, :]),
        (order_hbm, order_ref),
    )
    copies = [pltpu.make_async_copy(src, dst, arrived.at[k]) for k, (src, dst) in enumerate(pairs)]
    for copy in copies:
        copy.start()
    stored[7:8, :] = jnp.zeros((1, stored.shape[1]), jnp.float32)
    for copy in copies:
        copy.wait()
    lane = lax.broadcasted_iota(jnp.int32, (ROWS, TILE), 1)
    rows = row_ids()
    is_strength = (rows >= 3) & (rows < 6)
    for tile in range(tiles):
        where_from = jnp.broadcast_to(order_ref[:, tile * TILE : (tile + 1) * TILE], (ROWS, TILE))
        inside = where_from & (TILE - 1)
        block = where_from >> 7
        value = jnp.zeros((ROWS, TILE), jnp.float32)
        for source in range(tiles):
            part = jnp.take_along_axis(stored[:, source * TILE : (source + 1) * TILE], inside, axis=1)
            value = jnp.where(block == source, part, value)
        live = lane < counts_ref[tile]
        value = jnp.where(is_strength & ~live, 0.0, value)
        value = jnp.where(rows == 7, live.astype(jnp.float32), value)
        out_ref[tile * ROWS : (tile + 1) * ROWS, :] = value


def partner(me, k, size):
    assert size & (size - 1) == 0, size
    return me ^ k


def split_three(value):
    first = value.astype(jnp.bfloat16).astype(jnp.float32)
    rest = value - first
    second = rest.astype(jnp.bfloat16).astype(jnp.float32)
    return first, second, rest - second


def split_two(value):
    high = value.astype(jnp.bfloat16)
    return high, (value - high.astype(jnp.float32)).astype(jnp.bfloat16)


def features(tile, rows):
    down1, down2 = roll_rows(tile, 1), roll_rows(tile, 2)
    pos1 = jnp.where(rows == 5, roll_rows(tile, 5), down2)
    pos2 = jnp.where(rows == 3, down1, roll_rows(tile, 4))
    str1 = jnp.where(rows == 5, down2, roll_rows(tile, 7))
    str2 = jnp.where(rows == 3, roll_rows(tile, 6), down1)
    cross = pos1 * str2 - pos2 * str1
    value = jnp.where(rows < 3, roll_rows(tile, 5), jnp.where(rows < 6, cross, 0.0))
    return jnp.concatenate([*split_three(value), jnp.zeros_like(value)], axis=0)


def features_right(pieces):
    zero = jnp.zeros_like(pieces)
    return jnp.concatenate([pieces, zero, zero, pieces], axis=0).T


def add_pieces(terms):
    return terms[0:ROWS, :] + (terms[ROWS : 2 * ROWS, :] + terms[2 * ROWS : 3 * ROWS, :])


def tile_scalars(tile, rows):
    position = jnp.where(rows < 3, tile, 0.0)
    strength = jnp.where(rows < 3, roll_rows(tile, 5), 0.0)
    half = 0.5 * tile[6:7, :] * tile[6:7, :]
    norm = jnp.sum(position * position, axis=0, keepdims=True) + half
    along = jnp.sum(position * strength, axis=0, keepdims=True)
    return position, strength, half, norm, along


def target_side(tile, rows):
    position, strength, half, norm, along = tile_scalars(tile, rows)
    upper = jnp.where(rows == 3, norm, position)
    upper = jnp.where(rows == 4, along, upper)
    upper = jnp.where(rows == 5, half, upper)
    upper = jnp.where(rows == 6, 1.0, upper)
    first, second, third = split_three(jnp.concatenate([upper, strength], axis=0))
    stacked = jnp.concatenate([first, first, first, second, second, second, third, third], axis=0)
    return stacked.T.astype(jnp.bfloat16)


def source_side(tile, rows):
    position, strength, half, norm, along = tile_scalars(tile, rows)
    zero = jnp.zeros_like(position)
    one = jnp.ones_like(position)
    dist = jnp.where(rows == 6, norm, jnp.where(rows == 3, one, -2.0 * position))
    back = jnp.where(rows == 6, along, -strength)
    core = jnp.where(rows == 6, half, jnp.where(rows == 5, one, zero))
    unit = jnp.where(rows == 4, one, zero)
    shift = split_three(-position)
    halves = (
        [jnp.concatenate([p, zero], axis=0) for p in split_three(dist)],
        [jnp.concatenate([u, p], axis=0) for u, p in zip((unit, zero, zero), shift)],
        [jnp.concatenate([p, zero], axis=0) for p in split_three(back)],
        [jnp.concatenate([p, zero], axis=0) for p in split_three(core)],
    )
    blocks = []
    for pieces in halves:
        first, second, third = [p.astype(jnp.bfloat16) for p in pieces]
        blocks.append(jnp.concatenate([first, second, third, first, second, third, first, second], axis=0))
    return jnp.concatenate(blocks, axis=1)


def cycle(value, start, rows):
    one = jnp.where(rows == 2, roll_rows(value, 2 - start), roll_rows(value, -1 - start))
    two = jnp.where(rows == 0, roll_rows(value, -2 - start), roll_rows(value, 1 - start))
    return one, two


def finish_tile(tile, smooth, grad, rows):
    pos1, pos2 = cycle(tile, 0, rows)
    str1, str2 = cycle(tile, 3, rows)
    smooth1, smooth2 = cycle(smooth, 0, rows)
    grad1, grad2 = cycle(grad, 0, rows)
    velocity = pos1 * smooth2 - pos2 * smooth1 - roll_rows(smooth, -3)
    turn = str1 * smooth2 - str2 * smooth1
    stretch = turn - 3.0 * (pos1 * grad2 - pos2 * grad1 - roll_rows(grad, -3))
    return biot_factor * jnp.where(rows < 3, velocity, roll_rows(stretch, 3)) * tile[7:8, :]


def evaluate(products, pieces):
    for start in range(0, TILE, 16):
        at = slice(start, start + 16)
        dist, front, back, core = (products[at, k * TILE : (k + 1) * TILE] for k in range(4))
        inv = lax.rsqrt(dist)
        inv2 = inv * inv
        inv3 = inv2 * inv
        tail = core * (inv3 * inv2)
        smooth = inv3 + 1.5 * tail
        grad = inv2 * (smooth + tail)
        for k, value in enumerate((smooth, grad * front, grad * back)):
            high, low = split_two(value)
            pieces[at, 2 * k * TILE : (2 * k + 1) * TILE] = high
            pieces[at, (2 * k + 1) * TILE : (2 * k + 2) * TILE] = low


def pair_kernel(nrows, ncols, tiles, where_ref, slots_ref, count_ref, packed_ref, *refs):
    peers = nrows + ncols - 2
    ins, outs = refs[:peers], refs[peers : peers + nrows + ncols]
    scratch = refs[peers + nrows + ncols :]
    row_blk, col_blk, left, right, row_feat, col_feat, row_sum, col_sum = scratch[:8]
    products, pieces, arrived = scratch[8:10], scratch[10:12], scratch[12]
    per = tiles * ROWS
    rows = row_ids()
    my_row, my_col = where_ref[0], where_ref[1]
    count = count_ref[0]

    def tile_at(tile):
        return pl.ds(pl.multiple_of(tile * ROWS, ROWS), ROWS)

    def wide_at(tile):
        return pl.ds(pl.multiple_of(tile * TILE, TILE), TILE)

    own_copy = pltpu.make_async_copy(packed_ref, row_blk.at[pl.ds(pl.multiple_of(my_col * per, per), per), :], arrived)
    own_copy.start()
    row_sum[...] = jnp.zeros_like(row_sum)
    col_sum[...] = jnp.zeros_like(col_sum)
    pieces[1][...] = jnp.zeros_like(pieces[1])
    total = jnp.zeros((ROWS, TILE), jnp.float32)
    for block, me, size, sources in ((row_blk, my_col, ncols, ins[: ncols - 1]), (col_blk, my_row, nrows, ins[ncols - 1 :])):
        for k, source in enumerate(sources, 1):
            block[pl.ds(pl.multiple_of(partner(me, k, size) * per, per), per), :] = source[...]
            for tile in range(tiles):
                total = total + source[tile * ROWS : (tile + 1) * ROWS, :]
    own_copy.wait()
    col_blk[pl.ds(pl.multiple_of(my_row * per, per), per), :] = row_blk[pl.ds(pl.multiple_of(my_col * per, per), per), :]
    origin = jnp.sum(total, axis=1, keepdims=True) * (1.0 / (peers * tiles * TILE))
    origin = jnp.where(rows < 3, jnp.broadcast_to(origin, (ROWS, TILE)), 0.0)

    def prepare_row(tile, carry):
        here = row_blk[tile_at(tile), :] - origin
        row_blk[tile_at(tile), :] = here
        left[wide_at(tile), :] = target_side(here, rows)
        row_feat[pl.ds(pl.multiple_of(tile * 32, 32), 32), :] = features(here, rows).astype(jnp.bfloat16)
        return carry

    def prepare_col(tile, carry):
        here = col_blk[tile_at(tile), :] - origin
        col_blk[tile_at(tile), :] = here
        right[wide_at(tile), :] = source_side(here, rows)
        col_feat[wide_at(tile), :] = features_right(features(here, rows)).astype(jnp.bfloat16)
        return carry

    lax.fori_loop(0, ncols * tiles, prepare_row, 0, unroll=4)
    lax.fori_loop(0, nrows * tiles, prepare_col, 0, unroll=4)

    last = slots_ref.shape[1] - 1

    def multiply(slot, out):
        slot = jnp.minimum(slot, last)
        tgt, src = slots_ref[0, slot], slots_ref[1, slot]
        out[...] = jnp.dot(left[wide_at(tgt), :], right[wide_at(src), :], preferred_element_type=jnp.float32)

    def add_up(slot, values):
        kept = jnp.clip(slot, 0, last)
        tgt, src = slots_ref[0, kept], slots_ref[1, kept]
        own = (tgt // tiles == my_col) & (src // tiles == my_row) & (tgt % tiles == src % tiles)
        alive = jnp.where((slot >= 0) & (slot < count), 1.0, 0.0)
        react = jnp.where(own, 0.0, alive)
        feat = col_feat[wide_at(src), :]
        smooth, grad = feat[:, :64], feat[:, 64:]
        to_target = jnp.concatenate([smooth, smooth, grad, grad], axis=0)
        row_sum[wide_at(tgt), :] += alive * jnp.dot(values[:, : 4 * TILE], to_target, preferred_element_type=jnp.float32)
        feat = row_feat[pl.ds(pl.multiple_of(tgt * 32, 32), 32), :]
        high = jnp.concatenate([values[:, :TILE], values[:, 4 * TILE : 5 * TILE]], axis=1)
        low = jnp.concatenate([values[:, TILE : 2 * TILE], values[:, 5 * TILE :]], axis=1)
        terms = jnp.dot(
            jnp.concatenate([feat, feat], axis=1), jnp.concatenate([high, low], axis=0), preferred_element_type=jnp.float32
        )
        col_sum[tile_at(src), :] += react * add_pieces(terms)

    multiply(0, products[0])

    def visit(step, carry):
        for k in range(STEPS):
            slot = step * STEPS + k
            multiply(slot + 1, products[(k + 1) % 2])
            evaluate(products[k % 2], pieces[k % 2])
            add_up(slot - 1, pieces[(k + 1) % 2])
        return carry

    lax.fori_loop(0, (count + STEPS) // STEPS, visit, 0)

    for k in range(ncols):
        base = partner(my_col, k, ncols) * tiles
        for tile in range(tiles):
            sums = row_sum[wide_at(base + tile), :].T
            here = row_blk[tile_at(base + tile), :]
            done = finish_tile(here, add_pieces(sums), add_pieces(sums[4 * ROWS :, :]), rows)
            outs[k][tile * ROWS : (tile + 1) * ROWS, :] = done
    for k in range(nrows):
        base = partner(my_row, k, nrows) * tiles
        for tile in range(tiles):
            sums = col_sum[tile_at(base + tile), :]
            done = finish_tile(col_blk[tile_at(base + tile), :], sums[:, :TILE], sums[:, TILE:], rows)
            outs[ncols + k][tile * ROWS : (tile + 1) * ROWS, :] = done


def total_kernel(*refs):
    vel_ref, str_ref = refs[-2:]
    tiles = vel_ref.shape[1] // TILE
    for tile in range(tiles):
        at = slice(tile * ROWS, (tile + 1) * ROWS)
        total = refs[0][at, :]
        for ref in refs[1:-2]:
            total = total + ref[at, :]
        vel_ref[:, tile * TILE : (tile + 1) * TILE] = total[0:3, :]
        str_ref[:, tile * TILE : (tile + 1) * TILE] = total[3:6, :]


def shards(positions, strengths, cores, order, tile_counts, pair_slots, pair_count):
    tiles = tile_counts.shape[0]
    per_dev = tiles * TILE
    nrows = lax.axis_size("row")
    ncols = lax.axis_size("col")
    row_tiles, col_tiles = ncols * tiles, nrows * tiles
    smem = pl.BlockSpec(memory_space=pltpu.SMEM)
    vmem = pl.BlockSpec(memory_space=pltpu.VMEM)
    hbm = pl.BlockSpec(memory_space=pltpu.HBM)
    block = jax.ShapeDtypeStruct((tiles * ROWS, TILE), jnp.float32)

    packed = pl.pallas_call(
        pack_kernel,
        out_shape=block,
        in_specs=[smem] + [hbm] * 4,
        out_specs=vmem,
        scratch_shapes=[
            pltpu.VMEM((ROWS, per_dev), jnp.float32),
            pltpu.VMEM((1, per_dev), jnp.int32),
            pltpu.SemaphoreType.DMA((4,)),
        ],
        compiler_params=pltpu.CompilerParams(vmem_limit_bytes=PACK_BYTES),
        name="pack",
    )(tile_counts, positions, strengths, cores.reshape(1, per_dev), order.reshape(1, per_dev))

    def swap(value, axis, size, k):
        return lax.ppermute(value, axis, [(d, partner(d, k, size)) for d in range(size)])

    from_row = [swap(packed, "col", ncols, k) for k in range(1, ncols)]
    from_col = [swap(packed, "row", nrows, k) for k in range(1, nrows)]
    where = jnp.stack([lax.axis_index("row"), lax.axis_index("col")]).astype(jnp.int32)
    sums = pl.pallas_call(
        functools.partial(pair_kernel, nrows, ncols, tiles),
        out_shape=[block] * (nrows + ncols),
        in_specs=[smem] * 3 + [hbm] + [vmem] * (nrows + ncols - 2),
        out_specs=[vmem] * (nrows + ncols),
        scratch_shapes=[
            pltpu.VMEM((row_tiles * ROWS, TILE), jnp.float32),
            pltpu.VMEM((col_tiles * ROWS, TILE), jnp.float32),
            pltpu.VMEM((row_tiles * TILE, TILE), jnp.bfloat16),
            pltpu.VMEM((col_tiles * TILE, 4 * TILE), jnp.bfloat16),
            pltpu.VMEM((row_tiles * 32, TILE), jnp.bfloat16),
            pltpu.VMEM((col_tiles * TILE, TILE), jnp.bfloat16),
            pltpu.VMEM((row_tiles * TILE, 64), jnp.float32),
            pltpu.VMEM((col_tiles * ROWS, 2 * TILE), jnp.float32),
            pltpu.VMEM((TILE, 4 * TILE), jnp.float32),
            pltpu.VMEM((TILE, 4 * TILE), jnp.float32),
            pltpu.VMEM((TILE, 6 * TILE), jnp.bfloat16),
            pltpu.VMEM((TILE, 6 * TILE), jnp.bfloat16),
            pltpu.SemaphoreType.DMA(()),
        ],
        compiler_params=pltpu.CompilerParams(vmem_limit_bytes=VMEM_BYTES),
        name="pairs",
    )(where, pair_slots, pair_count, packed, *from_row, *from_col)
    parts = [sums[0], sums[ncols]]
    parts += [swap(sums[k], "col", ncols, k) for k in range(1, ncols)]
    parts += [swap(sums[ncols + k], "row", nrows, k) for k in range(1, nrows)]
    velocity, stretching = pl.pallas_call(
        total_kernel,
        out_shape=[jax.ShapeDtypeStruct((3, per_dev), jnp.float32)] * 2,
        in_specs=[vmem] * len(parts),
        out_specs=[vmem, vmem],
        compiler_params=pltpu.CompilerParams(vmem_limit_bytes=VMEM_BYTES),
        name="totals",
    )(*parts)
    return velocity, stretching


def solution(mesh):
    whole = ("groups", "row", "col")
    in_specs = (P(None, whole), P(None, whole), P(whole), P(whole), P(whole), P(None, whole), P(whole))
    out_specs = (P(None, whole), P(None, whole))
    return jax.shard_map(shards, mesh=mesh, in_specs=in_specs, out_specs=out_specs, check_vma=False)
```

```python
import functools
import math

import jax
import jax.numpy as jnp
from jax import lax
from jax.experimental import pallas as pl
from jax.experimental.pallas import tpu as pltpu
from jax.sharding import PartitionSpec as P

TILE = 128
ROWS = 8
STEPS = 4
VMEM_BYTES = 48 * 1024 * 1024
PACK_BYTES = 60 * 1024 * 1024

biot_factor = -1.0 / (4.0 * math.pi)


def row_ids(count=ROWS):
    return lax.broadcasted_iota(jnp.int32, (count, TILE), 0)


def roll_rows(value, shift):
    return pltpu.roll(value, shift % ROWS, 0)


def pack_kernel(counts_ref, pos_hbm, str_hbm, core_hbm, order_hbm, out_ref, stored, order_ref, arrived):
    tiles = order_ref.shape[1] // TILE
    pairs = (
        (pos_hbm, stored.at[0:3, :]),
        (str_hbm, stored.at[3:6, :]),
        (core_hbm, stored.at[6:7, :]),
        (order_hbm, order_ref),
    )
    copies = [pltpu.make_async_copy(src, dst, arrived.at[k]) for k, (src, dst) in enumerate(pairs)]
    for copy in copies:
        copy.start()
    stored[7:8, :] = jnp.zeros((1, stored.shape[1]), jnp.float32)
    for copy in copies:
        copy.wait()
    lane = lax.broadcasted_iota(jnp.int32, (ROWS, TILE), 1)
    rows = row_ids()
    is_strength = (rows >= 3) & (rows < 6)
    for tile in range(tiles):
        where_from = jnp.broadcast_to(order_ref[:, tile * TILE : (tile + 1) * TILE], (ROWS, TILE))
        inside = where_from & (TILE - 1)
        block = where_from >> 7
        value = jnp.zeros((ROWS, TILE), jnp.float32)
        for source in range(tiles):
            part = jnp.take_along_axis(stored[:, source * TILE : (source + 1) * TILE], inside, axis=1)
            value = jnp.where(block == source, part, value)
        live = lane < counts_ref[tile]
        value = jnp.where(is_strength & ~live, 0.0, value)
        value = jnp.where(rows == 7, live.astype(jnp.float32), value)
        out_ref[tile * ROWS : (tile + 1) * ROWS, :] = value


def partner(me, k, size):
    assert size & (size - 1) == 0, size
    return me ^ k


def split_three(value):
    first = value.astype(jnp.bfloat16).astype(jnp.float32)
    rest = value - first
    second = rest.astype(jnp.bfloat16).astype(jnp.float32)
    return first, second, rest - second


def split_two(value):
    high = value.astype(jnp.bfloat16)
    return high, (value - high.astype(jnp.float32)).astype(jnp.bfloat16)


def features(tile, rows):
    down1, down2 = roll_rows(tile, 1), roll_rows(tile, 2)
    pos1 = jnp.where(rows == 5, roll_rows(tile, 5), down2)
    pos2 = jnp.where(rows == 3, down1, roll_rows(tile, 4))
    str1 = jnp.where(rows == 5, down2, roll_rows(tile, 7))
    str2 = jnp.where(rows == 3, roll_rows(tile, 6), down1)
    cross = pos1 * str2 - pos2 * str1
    value = jnp.where(rows < 3, roll_rows(tile, 5), jnp.where(rows < 6, cross, 0.0))
    return jnp.concatenate([*split_three(value), jnp.zeros_like(value)], axis=0)


def add_pieces(terms):
    return terms[0:ROWS, :] + (terms[ROWS : 2 * ROWS, :] + terms[2 * ROWS : 3 * ROWS, :])


def tile_scalars(tile, rows):
    position = jnp.where(rows < 3, tile, 0.0)
    strength = jnp.where(rows < 3, roll_rows(tile, 5), 0.0)
    half = 0.5 * tile[6:7, :] * tile[6:7, :]
    norm = jnp.sum(position * position, axis=0, keepdims=True) + half
    along = jnp.sum(position * strength, axis=0, keepdims=True)
    return position, strength, half, norm, along


def target_side(tile, rows):
    position, strength, half, norm, along = tile_scalars(tile, rows)
    upper = jnp.where(rows == 3, norm, position)
    upper = jnp.where(rows == 4, along, upper)
    upper = jnp.where(rows == 5, half, upper)
    upper = jnp.where(rows == 6, 1.0, upper)
    first, second, third = split_three(jnp.concatenate([upper, strength], axis=0))
    stacked = jnp.concatenate([first, first, first, second, second, second, third, third], axis=0)
    return stacked.astype(jnp.bfloat16).T


def source_side(tile, rows):
    position, strength, half, norm, along = tile_scalars(tile, rows)
    zero = jnp.zeros_like(position)
    one = jnp.ones_like(position)
    dist = jnp.where(rows == 6, norm, jnp.where(rows == 3, one, -2.0 * position))
    back = jnp.where(rows == 6, along, -strength)
    core = jnp.where(rows == 6, half, jnp.where(rows == 5, one, zero))
    unit = jnp.where(rows == 4, one, zero)
    shift = split_three(-position)
    halves = (
        [jnp.concatenate([p, zero], axis=0) for p in split_three(dist)],
        [jnp.concatenate([u, p], axis=0) for u, p in zip((unit, zero, zero), shift)],
        [jnp.concatenate([p, zero], axis=0) for p in split_three(back)],
        [jnp.concatenate([p, zero], axis=0) for p in split_three(core)],
    )
    blocks = []
    for pieces in halves:
        first, second, third = [p.astype(jnp.bfloat16) for p in pieces]
        blocks.append(jnp.concatenate([first, second, third, first, second, third, first, second], axis=0))
    return jnp.concatenate(blocks, axis=1)


def cycle(value, start, rows):
    one = jnp.where(rows == 2, roll_rows(value, 2 - start), roll_rows(value, -1 - start))
    two = jnp.where(rows == 0, roll_rows(value, -2 - start), roll_rows(value, 1 - start))
    return one, two


def finish_tile(tile, smooth, grad, rows):
    pos1, pos2 = cycle(tile, 0, rows)
    str1, str2 = cycle(tile, 3, rows)
    smooth1, smooth2 = cycle(smooth, 0, rows)
    grad1, grad2 = cycle(grad, 0, rows)
    velocity = pos1 * smooth2 - pos2 * smooth1 - roll_rows(smooth, -3)
    turn = str1 * smooth2 - str2 * smooth1
    stretch = turn - 3.0 * (pos1 * grad2 - pos2 * grad1 - roll_rows(grad, -3))
    return biot_factor * jnp.where(rows < 3, velocity, roll_rows(stretch, 3)) * tile[7:8, :]


def evaluate(products, pieces):
    for start in range(0, TILE, 16):
        at = slice(start, start + 16)
        dist, front, back, core = (products[at, k * TILE : (k + 1) * TILE] for k in range(4))
        inv = lax.rsqrt(dist)
        inv2 = inv * inv
        inv3 = inv2 * inv
        tail = core * (inv3 * inv2)
        smooth = inv3 + 1.5 * tail
        grad = inv2 * (smooth + tail)
        for k, value in enumerate((smooth, grad * front, grad * back)):
            high, low = split_two(value)
            pieces[at, 2 * k * TILE : (2 * k + 1) * TILE] = high
            pieces[at, (2 * k + 1) * TILE : (2 * k + 2) * TILE] = low


def pair_kernel(nrows, ncols, tiles, where_ref, slots_ref, count_ref, packed_ref, *refs):
    peers = nrows + ncols - 2
    ins, outs = refs[:peers], refs[peers : peers + nrows + ncols]
    scratch = refs[peers + nrows + ncols :]
    row_blk, col_blk, left, right, row_feat, col_feat, row_sum, col_sum = scratch[:8]
    products, pieces, arrived = scratch[8:10], scratch[10:12], scratch[12]
    per = tiles * ROWS
    rows = row_ids()
    my_row, my_col = where_ref[0], where_ref[1]
    count = count_ref[0]

    def tile_at(tile):
        return pl.ds(pl.multiple_of(tile * ROWS, ROWS), ROWS)

    def wide_at(tile):
        return pl.ds(pl.multiple_of(tile * TILE, TILE), TILE)

    def feat_at(tile):
        return pl.ds(pl.multiple_of(tile * 32, 32), 32)

    own_copy = pltpu.make_async_copy(packed_ref, row_blk.at[pl.ds(pl.multiple_of(my_col * per, per), per), :], arrived)
    own_copy.start()
    row_sum[...] = jnp.zeros_like(row_sum)
    col_sum[...] = jnp.zeros_like(col_sum)
    pieces[1][...] = jnp.zeros_like(pieces[1])
    total = jnp.zeros((ROWS, TILE), jnp.float32)
    for block, me, size, sources in ((row_blk, my_col, ncols, ins[: ncols - 1]), (col_blk, my_row, nrows, ins[ncols - 1 :])):
        for k, source in enumerate(sources, 1):
            block[pl.ds(pl.multiple_of(partner(me, k, size) * per, per), per), :] = source[...]
            for tile in range(tiles):
                total = total + source[tile * ROWS : (tile + 1) * ROWS, :]
    own_copy.wait()
    col_blk[pl.ds(pl.multiple_of(my_row * per, per), per), :] = row_blk[pl.ds(pl.multiple_of(my_col * per, per), per), :]
    origin = jnp.sum(total, axis=1, keepdims=True) * (1.0 / (peers * tiles * TILE))
    origin = jnp.where(rows < 3, jnp.broadcast_to(origin, (ROWS, TILE)), 0.0)

    def prepare_row(tile, carry):
        here = row_blk[tile_at(tile), :] - origin
        row_blk[tile_at(tile), :] = here
        left[wide_at(tile), :] = target_side(here, rows)
        row_feat[feat_at(tile), :] = features(here, rows).astype(jnp.bfloat16)
        return carry

    def prepare_col(tile, carry):
        here = col_blk[tile_at(tile), :] - origin
        col_blk[tile_at(tile), :] = here
        right[wide_at(tile), :] = source_side(here, rows)
        col_feat[feat_at(tile), :] = features(here, rows).astype(jnp.bfloat16)
        return carry

    lax.fori_loop(0, ncols * tiles, prepare_row, 0, unroll=4)
    lax.fori_loop(0, nrows * tiles, prepare_col, 0, unroll=4)

    last = slots_ref.shape[1] - 1

    def multiply(slot, out):
        slot = jnp.minimum(slot, last)
        tgt, src = slots_ref[0, slot], slots_ref[1, slot]
        out[...] = jnp.dot(left[wide_at(tgt), :], right[wide_at(src), :], preferred_element_type=jnp.float32)

    def add_up(slot, values):
        kept = jnp.clip(slot, 0, last)
        tgt, src = slots_ref[0, kept], slots_ref[1, kept]
        own = (tgt // tiles == my_col) & (src // tiles == my_row) & (tgt % tiles == src % tiles)
        alive = jnp.where((slot >= 0) & (slot < count), 1.0, 0.0)
        react = jnp.where(own, 0.0, alive)
        smooth, front = values[:, : 2 * TILE], values[:, 2 * TILE : 4 * TILE]
        feat = col_feat[feat_at(src), :]
        terms = lax.dot_general(
            jnp.concatenate([feat, feat], axis=1),
            jnp.concatenate([smooth, front], axis=0),
            (((1,), (1,)), ((), ())),
            preferred_element_type=jnp.float32,
        )
        row_sum[tile_at(tgt), :] += alive * add_pieces(terms)
        feat = row_feat[feat_at(tgt), :]
        high = jnp.concatenate([values[:, :TILE], values[:, 4 * TILE : 5 * TILE]], axis=1)
        low = jnp.concatenate([values[:, TILE : 2 * TILE], values[:, 5 * TILE :]], axis=1)
        terms = jnp.dot(
            jnp.concatenate([feat, feat], axis=1), jnp.concatenate([high, low], axis=0), preferred_element_type=jnp.float32
        )
        col_sum[tile_at(src), :] += react * add_pieces(terms)

    multiply(0, products[0])

    def visit(step, carry):
        for k in range(STEPS):
            slot = step * STEPS + k
            multiply(slot + 1, products[(k + 1) % 2])
            evaluate(products[k % 2], pieces[k % 2])
            add_up(slot - 1, pieces[(k + 1) % 2])
        return carry

    lax.fori_loop(0, (count + STEPS) // STEPS, visit, 0)

    for block, sums, me, size, results in (
        (row_blk, row_sum, my_col, ncols, outs[:ncols]),
        (col_blk, col_sum, my_row, nrows, outs[ncols:]),
    ):
        for k, result in enumerate(results):
            base = partner(me, k, size) * tiles
            for tile in range(tiles):
                terms = sums[tile_at(base + tile), :]
                here = block[tile_at(base + tile), :]
                done = finish_tile(here, terms[:, :TILE], terms[:, TILE:], rows)
                result[tile * ROWS : (tile + 1) * ROWS, :] = done


def total_kernel(*refs):
    vel_ref, str_ref = refs[-2:]
    tiles = vel_ref.shape[1] // TILE
    for tile in range(tiles):
        at = slice(tile * ROWS, (tile + 1) * ROWS)
        total = refs[0][at, :]
        for ref in refs[1:-2]:
            total = total + ref[at, :]
        vel_ref[:, tile * TILE : (tile + 1) * TILE] = total[0:3, :]
        str_ref[:, tile * TILE : (tile + 1) * TILE] = total[3:6, :]


def shards(positions, strengths, cores, order, tile_counts, pair_slots, pair_count):
    tiles = tile_counts.shape[0]
    per_dev = tiles * TILE
    nrows = lax.axis_size("row")
    ncols = lax.axis_size("col")
    row_tiles, col_tiles = ncols * tiles, nrows * tiles
    smem = pl.BlockSpec(memory_space=pltpu.SMEM)
    vmem = pl.BlockSpec(memory_space=pltpu.VMEM)
    hbm = pl.BlockSpec(memory_space=pltpu.HBM)
    block = jax.ShapeDtypeStruct((tiles * ROWS, TILE), jnp.float32)

    packed = pl.pallas_call(
        pack_kernel,
        out_shape=block,
        in_specs=[smem] + [hbm] * 4,
        out_specs=vmem,
        scratch_shapes=[
            pltpu.VMEM((ROWS, per_dev), jnp.float32),
            pltpu.VMEM((1, per_dev), jnp.int32),
            pltpu.SemaphoreType.DMA((4,)),
        ],
        compiler_params=pltpu.CompilerParams(vmem_limit_bytes=PACK_BYTES),
        name="pack",
    )(tile_counts, positions, strengths, cores.reshape(1, per_dev), order.reshape(1, per_dev))

    def swap(value, axis, size, k):
        return lax.ppermute(value, axis, [(d, partner(d, k, size)) for d in range(size)])

    from_row = [swap(packed, "col", ncols, k) for k in range(1, ncols)]
    from_col = [swap(packed, "row", nrows, k) for k in range(1, nrows)]
    where = jnp.stack([lax.axis_index("row"), lax.axis_index("col")]).astype(jnp.int32)
    sums = pl.pallas_call(
        functools.partial(pair_kernel, nrows, ncols, tiles),
        out_shape=[block] * (nrows + ncols),
        in_specs=[smem] * 3 + [hbm] + [vmem] * (nrows + ncols - 2),
        out_specs=[vmem] * (nrows + ncols),
        scratch_shapes=[
            pltpu.VMEM((row_tiles * ROWS, TILE), jnp.float32),
            pltpu.VMEM((col_tiles * ROWS, TILE), jnp.float32),
            pltpu.VMEM((row_tiles * TILE, TILE), jnp.bfloat16),
            pltpu.VMEM((col_tiles * TILE, 4 * TILE), jnp.bfloat16),
            pltpu.VMEM((row_tiles * 32, TILE), jnp.bfloat16),
            pltpu.VMEM((col_tiles * 32, TILE), jnp.bfloat16),
            pltpu.VMEM((row_tiles * ROWS, 2 * TILE), jnp.float32),
            pltpu.VMEM((col_tiles * ROWS, 2 * TILE), jnp.float32),
            pltpu.VMEM((TILE, 4 * TILE), jnp.float32),
            pltpu.VMEM((TILE, 4 * TILE), jnp.float32),
            pltpu.VMEM((TILE, 6 * TILE), jnp.bfloat16),
            pltpu.VMEM((TILE, 6 * TILE), jnp.bfloat16),
            pltpu.SemaphoreType.DMA(()),
        ],
        compiler_params=pltpu.CompilerParams(vmem_limit_bytes=VMEM_BYTES),
        name="pairs",
    )(where, pair_slots, pair_count, packed, *from_row, *from_col)
    parts = [sums[0], sums[ncols]]
    parts += [swap(sums[k], "col", ncols, k) for k in range(1, ncols)]
    parts += [swap(sums[ncols + k], "row", nrows, k) for k in range(1, nrows)]
    velocity, stretching = pl.pallas_call(
        total_kernel,
        out_shape=[jax.ShapeDtypeStruct((3, per_dev), jnp.float32)] * 2,
        in_specs=[vmem] * len(parts),
        out_specs=[vmem, vmem],
        compiler_params=pltpu.CompilerParams(vmem_limit_bytes=VMEM_BYTES),
        name="totals",
    )(*parts)
    return velocity, stretching


def solution(mesh):
    whole = ("groups", "row", "col")
    in_specs = (P(None, whole), P(None, whole), P(whole), P(whole), P(whole), P(None, whole), P(whole))
    out_specs = (P(None, whole), P(None, whole))
    return jax.shard_map(shards, mesh=mesh, in_specs=in_specs, out_specs=out_specs, check_vma=False)
```

```python
import functools
import math

import jax
import jax.numpy as jnp
from jax import lax
from jax.experimental import pallas as pl
from jax.experimental.pallas import tpu as pltpu
from jax.sharding import PartitionSpec as P

TILE = 128
ROWS = 8
STEPS = 4
FEAT = 32
VMEM_BYTES = 48 * 1024 * 1024
PACK_BYTES = 60 * 1024 * 1024

biot_factor = -1.0 / (4.0 * math.pi)


def row_ids(count=ROWS):
    return lax.broadcasted_iota(jnp.int32, (count, TILE), 0)


def roll_rows(value, shift):
    return pltpu.roll(value, shift % ROWS, 0)


def pack_kernel(counts_ref, pos_hbm, str_hbm, core_hbm, order_hbm, out_ref, stored, order_ref, arrived):
    tiles = order_ref.shape[1] // TILE
    pairs = (
        (pos_hbm, stored.at[0:3, :]),
        (str_hbm, stored.at[3:6, :]),
        (core_hbm, stored.at[6:7, :]),
        (order_hbm, order_ref),
    )
    copies = [pltpu.make_async_copy(src, dst, arrived.at[k]) for k, (src, dst) in enumerate(pairs)]
    for copy in copies:
        copy.start()
    stored[7:8, :] = jnp.zeros((1, stored.shape[1]), jnp.float32)
    for copy in copies:
        copy.wait()
    lane = lax.broadcasted_iota(jnp.int32, (ROWS, TILE), 1)
    rows = row_ids()
    is_strength = (rows >= 3) & (rows < 6)
    for tile in range(tiles):
        where_from = jnp.broadcast_to(order_ref[:, tile * TILE : (tile + 1) * TILE], (ROWS, TILE))
        inside = where_from & (TILE - 1)
        block = where_from >> 7
        value = jnp.zeros((ROWS, TILE), jnp.float32)
        for source in range(tiles):
            part = jnp.take_along_axis(stored[:, source * TILE : (source + 1) * TILE], inside, axis=1)
            value = jnp.where(block == source, part, value)
        live = lane < counts_ref[tile]
        value = jnp.where(is_strength & ~live, 0.0, value)
        value = jnp.where(rows == 7, live.astype(jnp.float32), value)
        out_ref[tile * ROWS : (tile + 1) * ROWS, :] = value


def split_three(value):
    first = value.astype(jnp.bfloat16).astype(jnp.float32)
    rest = value - first
    second = rest.astype(jnp.bfloat16).astype(jnp.float32)
    return first, second, rest - second


def split_two(value):
    high = value.astype(jnp.bfloat16)
    return high, (value - high.astype(jnp.float32)).astype(jnp.bfloat16)


def features(tile, rows):
    down1, down2 = roll_rows(tile, 1), roll_rows(tile, 2)
    pos1 = jnp.where(rows == 5, roll_rows(tile, 5), down2)
    pos2 = jnp.where(rows == 3, down1, roll_rows(tile, 4))
    str1 = jnp.where(rows == 5, down2, roll_rows(tile, 7))
    str2 = jnp.where(rows == 3, roll_rows(tile, 6), down1)
    cross = pos1 * str2 - pos2 * str1
    value = jnp.where(rows < 3, roll_rows(tile, 5), jnp.where(rows < 6, cross, 0.0))
    return jnp.concatenate([*split_three(value), jnp.zeros_like(value)], axis=0)


def add_pieces(terms):
    return terms[0:ROWS, :] + (terms[ROWS : 2 * ROWS, :] + terms[2 * ROWS : 3 * ROWS, :])


def tile_scalars(tile, rows):
    position = jnp.where(rows < 3, tile, 0.0)
    strength = jnp.where(rows < 3, roll_rows(tile, 5), 0.0)
    half = 0.5 * tile[6:7, :] * tile[6:7, :]
    coarse = position.astype(jnp.bfloat16).astype(jnp.float32)
    norm = jnp.sum(coarse * coarse, axis=0, keepdims=True)
    rest = jnp.sum((position - coarse) * (position + coarse), axis=0, keepdims=True) + half
    along = jnp.sum(position * strength, axis=0, keepdims=True)
    return position, strength, half, norm, rest, along


def target_side(tile, rows):
    position, strength, half, norm, rest, along = tile_scalars(tile, rows)
    upper = jnp.where(rows == 3, norm, position)
    upper = jnp.where(rows == 4, along, upper)
    upper = jnp.where(rows == 5, half, upper)
    upper = jnp.where(rows == 6, 1.0, upper)
    upper = jnp.where(rows == 7, rest, upper)
    lower = jnp.where(rows == 3, 1.0, strength)
    first, second, third = split_three(jnp.concatenate([upper, lower], axis=0))
    stacked = jnp.concatenate([first, first, first, second, second, second, third, third], axis=0)
    return stacked.astype(jnp.bfloat16).T


def source_side(tile, rows):
    position, strength, half, norm, rest, along = tile_scalars(tile, rows)
    zero = jnp.zeros_like(position)
    one = jnp.ones_like(position)
    dist = jnp.where(rows == 6, norm, jnp.where((rows == 3) | (rows == 7), one, -2.0 * position))
    fine = jnp.where(rows == 3, rest, zero)
    back = jnp.where(rows == 6, along, -strength)
    core = jnp.where(rows == 6, half, jnp.where(rows == 5, one, zero))
    unit = jnp.where(rows == 4, one, zero)
    shift = split_three(-position)
    halves = (
        [jnp.concatenate([p, f], axis=0) for p, f in zip(split_three(dist), split_three(fine))],
        [jnp.concatenate([u, p], axis=0) for u, p in zip((unit, zero, zero), shift)],
        [jnp.concatenate([p, zero], axis=0) for p in split_three(back)],
        [jnp.concatenate([p, zero], axis=0) for p in split_three(core)],
    )
    blocks = []
    for pieces in halves:
        first, second, third = [p.astype(jnp.bfloat16) for p in pieces]
        blocks.append(jnp.concatenate([first, second, third, first, second, third, first, second], axis=0))
    return jnp.concatenate(blocks, axis=1)


def cycle(value, start, rows):
    one = jnp.where(rows == 2, roll_rows(value, 2 - start), roll_rows(value, -1 - start))
    two = jnp.where(rows == 0, roll_rows(value, -2 - start), roll_rows(value, 1 - start))
    return one, two


def finish_tile(tile, smooth, grad, rows):
    pos1, pos2 = cycle(tile, 0, rows)
    str1, str2 = cycle(tile, 3, rows)
    smooth1, smooth2 = cycle(smooth, 0, rows)
    grad1, grad2 = cycle(grad, 0, rows)
    velocity = pos1 * smooth2 - pos2 * smooth1 - roll_rows(smooth, -3)
    turn = str1 * smooth2 - str2 * smooth1
    stretch = turn - 3.0 * (pos1 * grad2 - pos2 * grad1 - roll_rows(grad, -3))
    return biot_factor * jnp.where(rows < 3, velocity, roll_rows(stretch, 3)) * tile[7:8, :]


def evaluate(products, pieces):
    for start in range(0, TILE, 16):
        at = slice(start, start + 16)
        dist, front, back, core = (products[at, k * TILE : (k + 1) * TILE] for k in range(4))
        inv = lax.rsqrt(dist)
        inv2 = inv * inv
        inv3 = inv2 * inv
        tail = core * (inv3 * inv2)
        smooth = inv3 + 1.5 * tail
        grad = inv2 * (smooth + tail)
        for k, value in enumerate((smooth, grad * front, grad * back)):
            high, low = split_two(value)
            pieces[at, 2 * k * TILE : (2 * k + 1) * TILE] = high
            pieces[at, (2 * k + 1) * TILE : (2 * k + 2) * TILE] = low


def tile_at(tile):
    return pl.ds(pl.multiple_of(tile * ROWS, ROWS), ROWS)


def wide_at(tile):
    return pl.ds(pl.multiple_of(tile * TILE, TILE), TILE)


def feat_at(tile):
    return pl.ds(pl.multiple_of(tile * FEAT, FEAT), FEAT)


def target_terms(feat, values):
    smooth, front = values[:, : 2 * TILE], values[:, 2 * TILE : 4 * TILE]
    terms = lax.dot_general(
        jnp.concatenate([feat, feat], axis=1),
        jnp.concatenate([smooth, front], axis=0),
        (((1,), (1,)), ((), ())),
        preferred_element_type=jnp.float32,
    )
    return add_pieces(terms)


def source_terms(feat, values):
    high = jnp.concatenate([values[:, :TILE], values[:, 4 * TILE : 5 * TILE]], axis=1)
    low = jnp.concatenate([values[:, TILE : 2 * TILE], values[:, 5 * TILE :]], axis=1)
    both = jnp.concatenate([high, low], axis=0)
    terms = jnp.dot(jnp.concatenate([feat, feat], axis=1), both, preferred_element_type=jnp.float32)
    return add_pieces(terms)


def own_kernel(packed_ref, block, left, right, feat, sums, origin_ref, *scratch):
    products, pieces, arrived = scratch[0:2], scratch[2:4], scratch[4]
    tiles = block.shape[0] // ROWS
    rows = row_ids()
    copy = pltpu.make_async_copy(packed_ref, block, arrived)
    copy.start()
    copy.wait()
    total = block[0:ROWS, :]
    for tile in range(1, tiles):
        total = total + block[tile * ROWS : (tile + 1) * ROWS, :]
    origin = jnp.sum(total, axis=1, keepdims=True) * (1.0 / (tiles * TILE))
    origin = jnp.where(rows < 3, jnp.broadcast_to(origin, (ROWS, TILE)), 0.0)
    origin_ref[...] = origin
    for tile in range(tiles):
        here = block[tile * ROWS : (tile + 1) * ROWS, :] - origin
        wide = slice(tile * TILE, (tile + 1) * TILE)
        left[wide, :] = target_side(here, rows)
        right[wide, :] = source_side(here, rows)
        feat[tile * FEAT : (tile + 1) * FEAT, :] = features(here, rows).astype(jnp.bfloat16)
    for step in range(tiles + 2):
        if step < tiles:
            wide = slice(step * TILE, (step + 1) * TILE)
            products[step % 2][...] = jnp.dot(left[wide, :], right[wide, :], preferred_element_type=jnp.float32)
        if 1 <= step <= tiles:
            evaluate(products[(step - 1) % 2], pieces[(step - 1) % 2])
        if step >= 2:
            tile = step - 2
            terms = target_terms(feat[tile * FEAT : (tile + 1) * FEAT, :], pieces[tile % 2])
            sums[tile * ROWS : (tile + 1) * ROWS, :] = terms


def join_kernel(*refs):
    outs = refs[len(refs) * 2 // 3 :]
    for k, out in enumerate(outs):
        half = out.shape[0] // 2
        out[:half, :] = refs[2 * k][...]
        out[half:, :] = refs[2 * k + 1][...]


def pair_kernel(row_stages, col_stages, tiles, where_ref, slots_ref, count_ref, *refs):
    own_block, own_left, own_right, own_feat, own_sums, origin_ref = refs[:6]
    refs = refs[6:]
    row_ins, col_ins, refs = refs[:col_stages], refs[col_stages : col_stages + row_stages], refs[col_stages + row_stages :]
    row_outs, col_outs, scratch = refs[:2], refs[2:4], refs[4:]
    row_blk, col_blk, left, right, row_feat, col_feat, row_sum, col_sum = scratch[:8]
    products, pieces = scratch[8:10], scratch[10:12]
    per = tiles * ROWS
    rows = row_ids()
    my_row, my_col = where_ref[0], where_ref[1]
    count = count_ref[0]
    origin = origin_ref[...]

    row_sum[...] = jnp.zeros_like(row_sum)
    col_sum[...] = jnp.zeros_like(col_sum)
    pieces[1][...] = jnp.zeros_like(pieces[1])
    for block, feat, me in ((row_blk, row_feat, my_col), (col_blk, col_feat, my_row)):
        block[pl.ds(pl.multiple_of(me * per, per), per), :] = own_block[...]
        feat[pl.ds(pl.multiple_of(me * tiles * FEAT, tiles * FEAT), tiles * FEAT), :] = own_feat[...]
    row_sum[pl.ds(pl.multiple_of(my_col * per, per), per), :] = own_sums[...]
    left[pl.ds(pl.multiple_of(my_col * tiles * TILE, tiles * TILE), tiles * TILE), :] = own_left[...]
    right[pl.ds(pl.multiple_of(my_row * tiles * TILE, tiles * TILE), tiles * TILE), :] = own_right[...]

    def prepare_row(tile, here):
        left[wide_at(tile), :] = target_side(here, rows)
        row_feat[feat_at(tile), :] = features(here, rows).astype(jnp.bfloat16)

    def prepare_col(tile, here):
        right[wide_at(tile), :] = source_side(here, rows)
        col_feat[feat_at(tile), :] = features(here, rows).astype(jnp.bfloat16)

    for block, me, ins, prepare in ((row_blk, my_col, row_ins, prepare_row), (col_blk, my_row, col_ins, prepare_col)):
        for stage, source in enumerate(ins):

            def visit_tile(step, carry, stage=stage, source=source, block=block, me=me, prepare=prepare):
                tile = (me ^ (2**stage + step // tiles)) * tiles + step % tiles
                value = source[tile_at(step), :]
                block[tile_at(tile), :] = value
                prepare(tile, value - origin)
                return carry

            lax.fori_loop(0, 2**stage * tiles, visit_tile, 0, unroll=4)

    last = slots_ref.shape[1] - 1

    def multiply(slot, out):
        slot = jnp.minimum(slot, last)
        tgt, src = slots_ref[0, slot], slots_ref[1, slot]
        out[...] = jnp.dot(left[wide_at(tgt), :], right[wide_at(src), :], preferred_element_type=jnp.float32)

    def add_up(slot, values):
        kept = jnp.clip(slot, 0, last)
        tgt, src = slots_ref[0, kept], slots_ref[1, kept]
        own = (tgt // tiles == my_col) & (src // tiles == my_row) & (tgt % tiles == src % tiles)
        alive = jnp.where((slot >= tiles) & (slot < count), 1.0, 0.0)
        react = jnp.where(own, 0.0, alive)
        row_sum[tile_at(tgt), :] += alive * target_terms(col_feat[feat_at(src), :], values)
        col_sum[tile_at(src), :] += react * source_terms(row_feat[feat_at(tgt), :], values)

    multiply(tiles, products[0])

    def visit(step, carry):
        for k in range(STEPS):
            slot = tiles + step * STEPS + k
            multiply(slot + 1, products[(k + 1) % 2])
            evaluate(products[k % 2], pieces[k % 2])
            add_up(slot - 1, pieces[(k + 1) % 2])
        return carry

    lax.fori_loop(0, (count - tiles + STEPS) // STEPS, visit, 0)

    for block, sums, me, results in ((row_blk, row_sum, my_col, row_outs), (col_blk, col_sum, my_row, col_outs)):
        for part, result in enumerate(results):
            half = result.shape[0] // per

            def close(step, carry, first=part * half, block=block, sums=sums, me=me, result=result):
                tile = (me ^ (first + step // tiles)) * tiles + step % tiles
                terms = sums[tile_at(tile), :]
                done = finish_tile(block[tile_at(tile), :] - origin, terms[:, :TILE], terms[:, TILE:], rows)
                result[tile_at(step), :] = done
                return carry

            lax.fori_loop(0, half * tiles, close, 0, unroll=8)


def halve_kernel(*refs):
    axes = len(refs) // 4
    for k in range(axes):
        kept, came = refs[2 * k], refs[2 * k + 1]
        keep, send = refs[2 * axes + 2 * k], refs[2 * axes + 2 * k + 1]
        half = keep.shape[0]
        keep[...] = kept[:half, :] + came[:half, :]
        send[...] = kept[half:, :] + came[half:, :]


def total_kernel(*refs):
    vel_ref, str_ref = refs[-2:]
    tiles = vel_ref.shape[1] // TILE
    for tile in range(tiles):
        at = slice(tile * ROWS, (tile + 1) * ROWS)
        total = refs[0][at, :]
        for ref in refs[1:-2]:
            total = total + ref[at, :]
        vel_ref[:, tile * TILE : (tile + 1) * TILE] = total[0:3, :]
        str_ref[:, tile * TILE : (tile + 1) * TILE] = total[3:6, :]


def stages_of(size):
    stages = size.bit_length() - 1
    assert size == 2**stages and stages >= 1, size
    return stages


def shards(positions, strengths, cores, order, tile_counts, pair_slots, pair_count):
    tiles = tile_counts.shape[0]
    per_dev = tiles * TILE
    nrows = lax.axis_size("row")
    ncols = lax.axis_size("col")
    sizes = {"col": ncols, "row": nrows}
    stages = {axis: stages_of(size) for axis, size in sizes.items()}
    row_tiles, col_tiles = ncols * tiles, nrows * tiles
    smem = pl.BlockSpec(memory_space=pltpu.SMEM)
    vmem = pl.BlockSpec(memory_space=pltpu.VMEM)
    hbm = pl.BlockSpec(memory_space=pltpu.HBM)
    params = pltpu.CompilerParams(vmem_limit_bytes=VMEM_BYTES)

    def blocks(count):
        return jax.ShapeDtypeStruct((count * tiles * ROWS, TILE), jnp.float32)

    packed = pl.pallas_call(
        pack_kernel,
        out_shape=blocks(1),
        in_specs=[smem] + [hbm] * 4,
        out_specs=vmem,
        scratch_shapes=[
            pltpu.VMEM((ROWS, per_dev), jnp.float32),
            pltpu.VMEM((1, per_dev), jnp.int32),
            pltpu.SemaphoreType.DMA((4,)),
        ],
        compiler_params=pltpu.CompilerParams(vmem_limit_bytes=PACK_BYTES),
        name="pack",
    )(tile_counts, positions, strengths, cores.reshape(1, per_dev), order.reshape(1, per_dev))

    def swap(value, axis, stage):
        return lax.ppermute(value, axis, [(d, d ^ 2**stage) for d in range(sizes[axis])])

    phases = [
        pltpu.VMEM((TILE, 4 * TILE), jnp.float32),
        pltpu.VMEM((TILE, 4 * TILE), jnp.float32),
        pltpu.VMEM((TILE, 6 * TILE), jnp.bfloat16),
        pltpu.VMEM((TILE, 6 * TILE), jnp.bfloat16),
    ]
    own = pl.pallas_call(
        own_kernel,
        out_shape=[
            blocks(1),
            jax.ShapeDtypeStruct((per_dev, TILE), jnp.bfloat16),
            jax.ShapeDtypeStruct((per_dev, 4 * TILE), jnp.bfloat16),
            jax.ShapeDtypeStruct((tiles * FEAT, TILE), jnp.bfloat16),
            jax.ShapeDtypeStruct((tiles * ROWS, 2 * TILE), jnp.float32),
            jax.ShapeDtypeStruct((ROWS, TILE), jnp.float32),
        ],
        in_specs=[hbm],
        out_specs=[vmem] * 6,
        scratch_shapes=[*phases, pltpu.SemaphoreType.DMA(())],
        compiler_params=params,
        cost_estimate=pl.CostEstimate(flops=tiles * 300 * TILE * TILE, bytes_accessed=2**21, transcendentals=0),
        name="own",
    )(packed)

    held = {axis: packed for axis in sizes}
    came = {axis: [] for axis in sizes}
    for stage in range(max(stages.values())):
        active = [axis for axis in sizes if stage < stages[axis]]
        for axis in active:
            came[axis].append(swap(held[axis], axis, stage))
        onward = [axis for axis in active if stage + 1 < stages[axis]]
        if onward:
            joined = pl.pallas_call(
                join_kernel,
                out_shape=[blocks(2 ** (stage + 1))] * len(onward),
                in_specs=[vmem] * (2 * len(onward)),
                out_specs=[vmem] * len(onward),
                compiler_params=params,
                name="join",
            )(*[part for axis in onward for part in (held[axis] if stage else own[0], came[axis][-1])])
            held.update(zip(onward, joined))

    where = jnp.stack([lax.axis_index("row"), lax.axis_index("col")]).astype(jnp.int32)
    sums = pl.pallas_call(
        functools.partial(pair_kernel, stages["row"], stages["col"], tiles),
        out_shape=[blocks(ncols // 2)] * 2 + [blocks(nrows // 2)] * 2,
        in_specs=[smem] * 3 + [vmem] * (6 + stages["row"] + stages["col"]),
        out_specs=[vmem] * 4,
        scratch_shapes=[
            pltpu.VMEM((row_tiles * ROWS, TILE), jnp.float32),
            pltpu.VMEM((col_tiles * ROWS, TILE), jnp.float32),
            pltpu.VMEM((row_tiles * TILE, TILE), jnp.bfloat16),
            pltpu.VMEM((col_tiles * TILE, 4 * TILE), jnp.bfloat16),
            pltpu.VMEM((row_tiles * FEAT, TILE), jnp.bfloat16),
            pltpu.VMEM((col_tiles * FEAT, TILE), jnp.bfloat16),
            pltpu.VMEM((row_tiles * ROWS, 2 * TILE), jnp.float32),
            pltpu.VMEM((col_tiles * ROWS, 2 * TILE), jnp.float32),
            *phases,
        ],
        compiler_params=params,
        name="pairs",
    )(where, pair_slots, pair_count, *own, *came["col"], *came["row"])

    keep = {"col": sums[0], "row": sums[2]}
    send = {"col": sums[1], "row": sums[3]}
    for stage in reversed(range(1, max(stages.values()))):
        active = [axis for axis in sizes if stage < stages[axis]]
        back = [swap(send[axis], axis, stage) for axis in active]
        split = pl.pallas_call(
            halve_kernel,
            out_shape=[blocks(2 ** (stage - 1))] * (2 * len(active)),
            in_specs=[vmem] * (2 * len(active)),
            out_specs=[vmem] * (2 * len(active)),
            compiler_params=params,
            name="halve",
        )(*[part for axis, value in zip(active, back) for part in (keep[axis], value)])
        for k, axis in enumerate(active):
            keep[axis], send[axis] = split[2 * k], split[2 * k + 1]
    parts = [keep["col"], keep["row"], swap(send["col"], "col", 0), swap(send["row"], "row", 0)]
    velocity, stretching = pl.pallas_call(
        total_kernel,
        out_shape=[jax.ShapeDtypeStruct((3, per_dev), jnp.float32)] * 2,
        in_specs=[vmem] * len(parts),
        out_specs=[vmem, vmem],
        compiler_params=params,
        name="totals",
    )(*parts)
    return velocity, stretching


def solution(mesh):
    whole = ("groups", "row", "col")
    in_specs = (P(None, whole), P(None, whole), P(whole), P(whole), P(whole), P(None, whole), P(whole))
    out_specs = (P(None, whole), P(None, whole))
    return jax.shard_map(shards, mesh=mesh, in_specs=in_specs, out_specs=out_specs, check_vma=False)
```

```python
import functools
import math

import jax
import jax.numpy as jnp
from jax import lax
from jax.experimental import pallas as pl
from jax.experimental.pallas import tpu as pltpu
from jax.sharding import PartitionSpec as P

TILE = 128
ROWS = 8
STEPS = 4
FEAT = 32
VMEM_BYTES = 48 * 1024 * 1024
PACK_BYTES = 60 * 1024 * 1024

biot_factor = -1.0 / (4.0 * math.pi)


def row_ids(count=ROWS):
    return lax.broadcasted_iota(jnp.int32, (count, TILE), 0)


def roll_rows(value, shift):
    return pltpu.roll(value, shift % ROWS, 0)


def pack_kernel(counts_ref, pos_hbm, str_hbm, core_hbm, order_hbm, out_ref, stored, order_ref, arrived):
    tiles = order_ref.shape[1] // TILE
    pairs = (
        (pos_hbm, stored.at[0:3, :]),
        (str_hbm, stored.at[3:6, :]),
        (core_hbm, stored.at[6:7, :]),
        (order_hbm, order_ref),
    )
    copies = [pltpu.make_async_copy(src, dst, arrived.at[k]) for k, (src, dst) in enumerate(pairs)]
    for copy in copies:
        copy.start()
    stored[7:8, :] = jnp.zeros((1, stored.shape[1]), jnp.float32)
    for copy in copies:
        copy.wait()
    lane = lax.broadcasted_iota(jnp.int32, (ROWS, TILE), 1)
    rows = row_ids()
    is_strength = (rows >= 3) & (rows < 6)
    for tile in range(tiles):
        where_from = jnp.broadcast_to(order_ref[:, tile * TILE : (tile + 1) * TILE], (ROWS, TILE))
        inside = where_from & (TILE - 1)
        block = where_from >> 7
        value = jnp.zeros((ROWS, TILE), jnp.float32)
        for source in range(tiles):
            part = jnp.take_along_axis(stored[:, source * TILE : (source + 1) * TILE], inside, axis=1)
            value = jnp.where(block == source, part, value)
        live = lane < counts_ref[tile]
        value = jnp.where(is_strength & ~live, 0.0, value)
        value = jnp.where(rows == 7, live.astype(jnp.float32), value)
        out_ref[tile * ROWS : (tile + 1) * ROWS, :] = value


def split_three(value):
    first = value.astype(jnp.bfloat16).astype(jnp.float32)
    rest = value - first
    second = rest.astype(jnp.bfloat16).astype(jnp.float32)
    return first, second, rest - second


def split_two(value):
    high = value.astype(jnp.bfloat16)
    return high, (value - high.astype(jnp.float32)).astype(jnp.bfloat16)


def features(tile, rows):
    down1, down2 = roll_rows(tile, 1), roll_rows(tile, 2)
    pos1 = jnp.where(rows == 5, roll_rows(tile, 5), down2)
    pos2 = jnp.where(rows == 3, down1, roll_rows(tile, 4))
    str1 = jnp.where(rows == 5, down2, roll_rows(tile, 7))
    str2 = jnp.where(rows == 3, roll_rows(tile, 6), down1)
    cross = pos1 * str2 - pos2 * str1
    value = jnp.where(rows < 3, roll_rows(tile, 5), jnp.where(rows < 6, cross, 0.0))
    return jnp.concatenate([*split_three(value), jnp.zeros_like(value)], axis=0)


def add_pieces(terms):
    return terms[0:ROWS, :] + (terms[ROWS : 2 * ROWS, :] + terms[2 * ROWS : 3 * ROWS, :])


def tile_scalars(tile, rows):
    position = jnp.where(rows < 3, tile, 0.0)
    strength = jnp.where(rows < 3, roll_rows(tile, 5), 0.0)
    half = 0.5 * tile[6:7, :] * tile[6:7, :]
    coarse = position.astype(jnp.bfloat16).astype(jnp.float32)
    norm = jnp.sum(coarse * coarse, axis=0, keepdims=True)
    rest = jnp.sum((position - coarse) * (position + coarse), axis=0, keepdims=True) + half
    along = jnp.sum(position * strength, axis=0, keepdims=True)
    return position, strength, half, norm, rest, along


def target_side(tile, rows):
    position, strength, half, norm, rest, along = tile_scalars(tile, rows)
    upper = jnp.where(rows == 3, norm, position)
    upper = jnp.where(rows == 4, along, upper)
    upper = jnp.where(rows == 5, half, upper)
    upper = jnp.where(rows == 6, 1.0, upper)
    upper = jnp.where(rows == 7, rest, upper)
    lower = jnp.where(rows == 3, 1.0, strength)
    first, second, third = split_three(jnp.concatenate([upper, lower], axis=0))
    stacked = jnp.concatenate([first, first, first, second, second, second, third, third], axis=0)
    return stacked.astype(jnp.bfloat16).T


def source_side(tile, rows):
    position, strength, half, norm, rest, along = tile_scalars(tile, rows)
    zero = jnp.zeros_like(position)
    one = jnp.ones_like(position)
    dist = jnp.where(rows == 6, norm, jnp.where((rows == 3) | (rows == 7), one, -2.0 * position))
    fine = jnp.where(rows == 3, rest, zero)
    back = jnp.where(rows == 6, along, -strength)
    core = jnp.where(rows == 6, half, jnp.where(rows == 5, one, zero))
    unit = jnp.where(rows == 4, one, zero)
    shift = split_three(-position)
    halves = (
        [jnp.concatenate([p, f], axis=0) for p, f in zip(split_three(dist), split_three(fine))],
        [jnp.concatenate([u, p], axis=0) for u, p in zip((unit, zero, zero), shift)],
        [jnp.concatenate([p, zero], axis=0) for p in split_three(back)],
        [jnp.concatenate([p, zero], axis=0) for p in split_three(core)],
    )
    blocks = []
    for pieces in halves:
        first, second, third = [p.astype(jnp.bfloat16) for p in pieces]
        blocks.append(jnp.concatenate([first, second, third, first, second, third, first, second], axis=0))
    return jnp.concatenate(blocks, axis=1)


def cycle(value, start, rows):
    one = jnp.where(rows == 2, roll_rows(value, 2 - start), roll_rows(value, -1 - start))
    two = jnp.where(rows == 0, roll_rows(value, -2 - start), roll_rows(value, 1 - start))
    return one, two


def finish_tile(tile, smooth, grad, rows):
    pos1, pos2 = cycle(tile, 0, rows)
    str1, str2 = cycle(tile, 3, rows)
    smooth1, smooth2 = cycle(smooth, 0, rows)
    grad1, grad2 = cycle(grad, 0, rows)
    velocity = pos1 * smooth2 - pos2 * smooth1 - roll_rows(smooth, -3)
    turn = str1 * smooth2 - str2 * smooth1
    stretch = turn - 3.0 * (pos1 * grad2 - pos2 * grad1 - roll_rows(grad, -3))
    return biot_factor * jnp.where(rows < 3, velocity, roll_rows(stretch, 3)) * tile[7:8, :]


def evaluate(products, pieces):
    for start in range(0, TILE, 16):
        at = slice(start, start + 16)
        dist, front, back, core = (products[at, k * TILE : (k + 1) * TILE] for k in range(4))
        inv = lax.rsqrt(dist)
        inv2 = inv * inv
        inv3 = inv2 * inv
        tail = core * (inv3 * inv2)
        smooth = inv3 + 1.5 * tail
        grad = inv2 * (smooth + tail)
        for k, value in enumerate((smooth, grad * front, grad * back)):
            high, low = split_two(value)
            pieces[at, 2 * k * TILE : (2 * k + 1) * TILE] = high
            pieces[at, (2 * k + 1) * TILE : (2 * k + 2) * TILE] = low


def tile_at(tile):
    return pl.ds(pl.multiple_of(tile * ROWS, ROWS), ROWS)


def wide_at(tile):
    return pl.ds(pl.multiple_of(tile * TILE, TILE), TILE)


def feat_at(tile):
    return pl.ds(pl.multiple_of(tile * FEAT, FEAT), FEAT)


def target_terms(feat, values):
    smooth, front = values[:, : 2 * TILE], values[:, 2 * TILE : 4 * TILE]
    terms = lax.dot_general(
        jnp.concatenate([feat, feat], axis=1),
        jnp.concatenate([smooth, front], axis=0),
        (((1,), (1,)), ((), ())),
        preferred_element_type=jnp.float32,
    )
    return add_pieces(terms)


def source_terms(feat, values):
    high = jnp.concatenate([values[:, :TILE], values[:, 4 * TILE : 5 * TILE]], axis=1)
    low = jnp.concatenate([values[:, TILE : 2 * TILE], values[:, 5 * TILE :]], axis=1)
    both = jnp.concatenate([high, low], axis=0)
    terms = jnp.dot(jnp.concatenate([feat, feat], axis=1), both, preferred_element_type=jnp.float32)
    return add_pieces(terms)


def own_kernel(slots_ref, packed_ref, block, left, right, feat, sums, origin_ref, *scratch):
    del slots_ref
    products, pieces, arrived = scratch[0:2], scratch[2:4], scratch[4]
    tiles = block.shape[0] // ROWS
    rows = row_ids()
    copy = pltpu.make_async_copy(packed_ref, block, arrived)
    copy.start()
    copy.wait()
    total = block[0:ROWS, :]
    for tile in range(1, tiles):
        total = total + block[tile * ROWS : (tile + 1) * ROWS, :]
    origin = jnp.sum(total, axis=1, keepdims=True) * (1.0 / (tiles * TILE))
    origin = jnp.where(rows < 3, jnp.broadcast_to(origin, (ROWS, TILE)), 0.0)
    origin_ref[...] = origin
    for tile in range(tiles):
        here = block[tile * ROWS : (tile + 1) * ROWS, :] - origin
        wide = slice(tile * TILE, (tile + 1) * TILE)
        left[wide, :] = target_side(here, rows)
        right[wide, :] = source_side(here, rows)
        feat[tile * FEAT : (tile + 1) * FEAT, :] = features(here, rows).astype(jnp.bfloat16)
    for step in range(tiles + 2):
        if step < tiles:
            wide = slice(step * TILE, (step + 1) * TILE)
            products[step % 2][...] = jnp.dot(left[wide, :], right[wide, :], preferred_element_type=jnp.float32)
        if 1 <= step <= tiles:
            evaluate(products[(step - 1) % 2], pieces[(step - 1) % 2])
        if step >= 2:
            tile = step - 2
            terms = target_terms(feat[tile * FEAT : (tile + 1) * FEAT, :], pieces[tile % 2])
            sums[tile * ROWS : (tile + 1) * ROWS, :] = terms


def join_kernel(*refs):
    out, start = refs[-1], 0
    for ref in refs[:-1]:
        out[start : start + ref.shape[0], :] = ref[...]
        start += ref.shape[0]


def pair_kernel(nrows, ncols, tiles, where_ref, slots_ref, count_ref, *refs):
    own_block, own_left, own_right, own_feat, own_sums, origin_ref = refs[:6]
    refs = refs[6:]
    halves = nrows // 2
    row_ins, far_ins, near_in, refs = refs[: ncols - 1], refs[ncols - 1 : ncols + halves - 2], refs[ncols + halves - 2], refs[ncols + halves - 1 :]
    row_outs, col_outs, scratch = refs[:ncols], refs[ncols : ncols + halves], refs[ncols + halves :]
    row_blk, col_blk, left, right, row_feat, col_feat, row_sum, col_sum = scratch[:8]
    products, pieces = scratch[8:10], scratch[10:12]
    per = tiles * ROWS
    rows = row_ids()
    my_row, my_col = where_ref[0], where_ref[1]
    count = count_ref[0]
    row_sources = [(k, row_ins[k - 1], 0) for k in range(1, ncols)]
    col_sources = [(2 * m, far_ins[m - 1], 0) for m in range(1, halves)]
    col_sources += [(2 * m + 1, near_in, m * per) for m in range(halves)]
    origin = origin_ref[...]

    row_sum[...] = jnp.zeros_like(row_sum)
    col_sum[...] = jnp.zeros_like(col_sum)
    pieces[1][...] = jnp.zeros_like(pieces[1])
    for block, feat, me in ((row_blk, row_feat, my_col), (col_blk, col_feat, my_row)):
        block[pl.ds(pl.multiple_of(me * per, per), per), :] = own_block[...]
        feat[pl.ds(pl.multiple_of(me * tiles * FEAT, tiles * FEAT), tiles * FEAT), :] = own_feat[...]
    row_sum[pl.ds(pl.multiple_of(my_col * per, per), per), :] = own_sums[...]
    left[pl.ds(pl.multiple_of(my_col * tiles * TILE, tiles * TILE), tiles * TILE), :] = own_left[...]
    right[pl.ds(pl.multiple_of(my_row * tiles * TILE, tiles * TILE), tiles * TILE), :] = own_right[...]

    def prepare_row(tile, here):
        left[wide_at(tile), :] = target_side(here, rows)
        row_feat[feat_at(tile), :] = features(here, rows).astype(jnp.bfloat16)

    def prepare_col(tile, here):
        right[wide_at(tile), :] = source_side(here, rows)
        col_feat[feat_at(tile), :] = features(here, rows).astype(jnp.bfloat16)

    def prepare(step, carry):
        for sources, block, me, operands in (
            (row_sources, row_blk, my_col, prepare_row),
            (col_sources, col_blk, my_row, prepare_col),
        ):
            for k, source, start in sources:
                tile = (me ^ k) * tiles + step
                value = source[pl.ds(pl.multiple_of(start + step * ROWS, ROWS), ROWS), :]
                block[tile_at(tile), :] = value
                operands(tile, value - origin)
        return carry

    lax.fori_loop(0, tiles, prepare, 0, unroll=2)

    last = slots_ref.shape[1] - 1

    def multiply(slot, out):
        slot = jnp.minimum(slot, last)
        tgt, src = slots_ref[0, slot], slots_ref[1, slot]
        out[...] = jnp.dot(left[wide_at(tgt), :], right[wide_at(src), :], preferred_element_type=jnp.float32)

    def add_up(slot, values):
        kept = jnp.clip(slot, 0, last)
        tgt, src = slots_ref[0, kept], slots_ref[1, kept]
        own = (tgt // tiles == my_col) & (src // tiles == my_row) & (tgt % tiles == src % tiles)
        alive = jnp.where((slot >= tiles) & (slot < count), 1.0, 0.0)
        react = jnp.where(own, 0.0, alive)
        row_sum[tile_at(tgt), :] += alive * target_terms(col_feat[feat_at(src), :], values)
        col_sum[tile_at(src), :] += react * source_terms(row_feat[feat_at(tgt), :], values)

    multiply(tiles, products[0])

    def visit(step, carry):
        for k in range(STEPS):
            slot = tiles + step * STEPS + k
            multiply(slot + 1, products[(k + 1) % 2])
            evaluate(products[k % 2], pieces[k % 2])
            add_up(slot - 1, pieces[(k + 1) % 2])
        return carry

    lax.fori_loop(0, (count - tiles + STEPS) // STEPS, visit, 0)

    row_results = [(k, row_outs[k], 0) for k in range(ncols)]
    col_results = [(k, col_outs[k // 2], k % 2 * per) for k in range(nrows)]

    def close(step, carry):
        for results, block, sums, me in (
            (row_results, row_blk, row_sum, my_col),
            (col_results, col_blk, col_sum, my_row),
        ):
            for k, result, start in results:
                at = tile_at((me ^ k) * tiles + step)
                terms = sums[at, :]
                done = finish_tile(block[at, :] - origin, terms[:, :TILE], terms[:, TILE:], rows)
                result[pl.ds(pl.multiple_of(start + step * ROWS, ROWS), ROWS), :] = done
        return carry

    lax.fori_loop(0, tiles, close, 0, unroll=2)


def halve_kernel(*refs):
    keep, send = refs[-2:]
    half = keep.shape[0]
    total = refs[0][...]
    for ref in refs[1:-2]:
        total = total + ref[...]
    keep[...] = total[:half, :]
    send[...] = total[half:, :]


def total_kernel(*refs):
    vel_ref, str_ref = refs[-2:]
    tiles = vel_ref.shape[1] // TILE
    for tile in range(tiles):
        at = slice(tile * ROWS, (tile + 1) * ROWS)
        total = refs[0][at, :]
        for ref in refs[1:-2]:
            total = total + ref[at, :]
        vel_ref[:, tile * TILE : (tile + 1) * TILE] = total[0:3, :]
        str_ref[:, tile * TILE : (tile + 1) * TILE] = total[3:6, :]


def shards(positions, strengths, cores, order, tile_counts, pair_slots, pair_count):
    tiles = tile_counts.shape[0]
    per_dev = tiles * TILE
    nrows = lax.axis_size("row")
    ncols = lax.axis_size("col")
    halves = nrows // 2
    assert nrows == 2 * halves and nrows & (nrows - 1) == 0 and ncols & (ncols - 1) == 0
    row_tiles, col_tiles = ncols * tiles, nrows * tiles
    smem = pl.BlockSpec(memory_space=pltpu.SMEM)
    vmem = pl.BlockSpec(memory_space=pltpu.VMEM)
    hbm = pl.BlockSpec(memory_space=pltpu.HBM)
    params = pltpu.CompilerParams(vmem_limit_bytes=VMEM_BYTES)

    def blocks(count):
        return jax.ShapeDtypeStruct((count * tiles * ROWS, TILE), jnp.float32)

    packed = pl.pallas_call(
        pack_kernel,
        out_shape=blocks(1),
        in_specs=[smem] + [hbm] * 4,
        out_specs=vmem,
        scratch_shapes=[
            pltpu.VMEM((ROWS, per_dev), jnp.float32),
            pltpu.VMEM((1, per_dev), jnp.int32),
            pltpu.SemaphoreType.DMA((4,)),
        ],
        compiler_params=pltpu.CompilerParams(vmem_limit_bytes=PACK_BYTES),
        name="pack",
    )(tile_counts, positions, strengths, cores.reshape(1, per_dev), order.reshape(1, per_dev))

    def swap(value, axis, size, k):
        return lax.ppermute(value, axis, [(d, d ^ k) for d in range(size)])

    phases = [
        pltpu.VMEM((TILE, 4 * TILE), jnp.float32),
        pltpu.VMEM((TILE, 4 * TILE), jnp.float32),
        pltpu.VMEM((TILE, 6 * TILE), jnp.bfloat16),
        pltpu.VMEM((TILE, 6 * TILE), jnp.bfloat16),
    ]
    own = pl.pallas_call(
        own_kernel,
        out_shape=[
            blocks(1),
            jax.ShapeDtypeStruct((per_dev, TILE), jnp.bfloat16),
            jax.ShapeDtypeStruct((per_dev, 4 * TILE), jnp.bfloat16),
            jax.ShapeDtypeStruct((tiles * FEAT, TILE), jnp.bfloat16),
            jax.ShapeDtypeStruct((tiles * ROWS, 2 * TILE), jnp.float32),
            jax.ShapeDtypeStruct((ROWS, TILE), jnp.float32),
        ],
        in_specs=[smem, hbm],
        out_specs=[vmem] * 6,
        scratch_shapes=[*phases, pltpu.SemaphoreType.DMA(())],
        compiler_params=params,
        cost_estimate=pl.CostEstimate(flops=tiles * 300 * TILE * TILE, bytes_accessed=2**21, transcendentals=0),
        name="own",
    )(pair_slots, packed)

    far = [swap(packed, "row", nrows, 2 * m) for m in range(1, halves)]
    from_row = [swap(packed, "col", ncols, k) for k in range(1, ncols)]
    joined = pl.pallas_call(
        join_kernel,
        out_shape=blocks(halves),
        in_specs=[vmem] * halves,
        out_specs=vmem,
        compiler_params=params,
        name="join",
    )(own[0], *far)
    near = swap(joined, "row", nrows, 1)

    where = jnp.stack([lax.axis_index("row"), lax.axis_index("col")]).astype(jnp.int32)
    sums = pl.pallas_call(
        functools.partial(pair_kernel, nrows, ncols, tiles),
        out_shape=[blocks(1)] * ncols + [blocks(2)] * halves,
        in_specs=[smem] * 3 + [vmem] * (5 + ncols + halves),
        out_specs=[vmem] * (ncols + halves),
        scratch_shapes=[
            pltpu.VMEM((row_tiles * ROWS, TILE), jnp.float32),
            pltpu.VMEM((col_tiles * ROWS, TILE), jnp.float32),
            pltpu.VMEM((row_tiles * TILE, TILE), jnp.bfloat16),
            pltpu.VMEM((col_tiles * TILE, 4 * TILE), jnp.bfloat16),
            pltpu.VMEM((row_tiles * FEAT, TILE), jnp.bfloat16),
            pltpu.VMEM((col_tiles * FEAT, TILE), jnp.bfloat16),
            pltpu.VMEM((row_tiles * ROWS, 2 * TILE), jnp.float32),
            pltpu.VMEM((col_tiles * ROWS, 2 * TILE), jnp.float32),
            *phases,
        ],
        compiler_params=params,
        name="pairs",
    )(where, pair_slots, pair_count, *own, *from_row, *far, near)

    far_back = [swap(sums[ncols + m], "row", nrows, 2 * m) for m in range(1, halves)]
    row_back = [swap(sums[k], "col", ncols, k) for k in range(1, ncols)]
    keep, send = pl.pallas_call(
        halve_kernel,
        out_shape=[blocks(1)] * 2,
        in_specs=[vmem] * halves,
        out_specs=[vmem] * 2,
        compiler_params=params,
        name="halve",
    )(sums[ncols], *far_back)
    parts = [sums[0], keep, *row_back, swap(send, "row", nrows, 1)]
    velocity, stretching = pl.pallas_call(
        total_kernel,
        out_shape=[jax.ShapeDtypeStruct((3, per_dev), jnp.float32)] * 2,
        in_specs=[vmem] * len(parts),
        out_specs=[vmem, vmem],
        compiler_params=params,
        name="totals",
    )(*parts)
    return velocity, stretching


def solution(mesh):
    whole = ("groups", "row", "col")
    in_specs = (P(None, whole), P(None, whole), P(whole), P(whole), P(whole), P(None, whole), P(whole))
    out_specs = (P(None, whole), P(None, whole))
    return jax.shard_map(shards, mesh=mesh, in_specs=in_specs, out_specs=out_specs, check_vma=False)
```

```python
import functools
import math

import jax
import jax.numpy as jnp
from jax import lax
from jax.experimental import pallas as pl
from jax.experimental.pallas import tpu as pltpu
from jax.sharding import PartitionSpec as P

TILE = 128
ROWS = 8
STEPS = 4
FEAT = 32
VMEM_BYTES = 48 * 1024 * 1024

biot_factor = -1.0 / (4.0 * math.pi)


def row_ids(count=ROWS):
    return lax.broadcasted_iota(jnp.int32, (count, TILE), 0)


def roll_rows(value, shift):
    return pltpu.roll(value, shift % ROWS, 0)


def pack_kernel(
    counts_hbm, pos_hbm, str_hbm, core_hbm, order_hbm, slots_hbm,
    out_ref, slots_ref, stored, order_ref, counts_ref, arrived,
):
    tiles = order_ref.shape[1] // TILE
    pairs = (
        (pos_hbm, stored.at[0:3, :]),
        (str_hbm, stored.at[3:6, :]),
        (core_hbm, stored.at[6:7, :]),
        (order_hbm, order_ref),
        (counts_hbm, counts_ref),
        (slots_hbm, slots_ref),
    )
    copies = [pltpu.make_async_copy(src, dst, arrived.at[k]) for k, (src, dst) in enumerate(pairs)]
    for copy in copies:
        copy.start()
    stored[7:8, :] = jnp.zeros((1, stored.shape[1]), jnp.float32)
    for copy in copies:
        copy.wait()
    lane = lax.broadcasted_iota(jnp.int32, (ROWS, TILE), 1)
    rows = row_ids()
    is_strength = (rows >= 3) & (rows < 6)
    for tile in range(tiles):
        where_from = jnp.broadcast_to(order_ref[:, tile * TILE : (tile + 1) * TILE], (ROWS, TILE))
        inside = where_from & (TILE - 1)
        block = where_from >> 7
        value = jnp.zeros((ROWS, TILE), jnp.float32)
        for source in range(tiles):
            part = jnp.take_along_axis(stored[:, source * TILE : (source + 1) * TILE], inside, axis=1)
            value = jnp.where(block == source, part, value)
        live = lane < counts_ref[tile]
        value = jnp.where(is_strength & ~live, 0.0, value)
        value = jnp.where(rows == 7, live.astype(jnp.float32), value)
        out_ref[tile * ROWS : (tile + 1) * ROWS, :] = value


def split_three(value):
    first = value.astype(jnp.bfloat16).astype(jnp.float32)
    rest = value - first
    second = rest.astype(jnp.bfloat16).astype(jnp.float32)
    return first, second, rest - second


def split_two(value):
    high = value.astype(jnp.bfloat16)
    return high, (value - high.astype(jnp.float32)).astype(jnp.bfloat16)


def features(tile, rows):
    down1, down2 = roll_rows(tile, 1), roll_rows(tile, 2)
    pos1 = jnp.where(rows == 5, roll_rows(tile, 5), down2)
    pos2 = jnp.where(rows == 3, down1, roll_rows(tile, 4))
    str1 = jnp.where(rows == 5, down2, roll_rows(tile, 7))
    str2 = jnp.where(rows == 3, roll_rows(tile, 6), down1)
    cross = pos1 * str2 - pos2 * str1
    value = jnp.where(rows < 3, roll_rows(tile, 5), jnp.where(rows < 6, cross, 0.0))
    return jnp.concatenate([*split_three(value), jnp.zeros_like(value)], axis=0)


def add_pieces(terms):
    return terms[0:ROWS, :] + (terms[ROWS : 2 * ROWS, :] + terms[2 * ROWS : 3 * ROWS, :])


def tile_scalars(tile, rows):
    position = jnp.where(rows < 3, tile, 0.0)
    strength = jnp.where(rows < 3, roll_rows(tile, 5), 0.0)
    half = 0.5 * tile[6:7, :] * tile[6:7, :]
    coarse = position.astype(jnp.bfloat16).astype(jnp.float32)
    norm = jnp.sum(coarse * coarse, axis=0, keepdims=True)
    rest = jnp.sum((position - coarse) * (position + coarse), axis=0, keepdims=True) + half
    along = jnp.sum(position * strength, axis=0, keepdims=True)
    return position, strength, half, norm, rest, along


def target_side(tile, rows):
    position, strength, half, norm, rest, along = tile_scalars(tile, rows)
    upper = jnp.where(rows == 3, norm, position)
    upper = jnp.where(rows == 4, along, upper)
    upper = jnp.where(rows == 5, half, upper)
    upper = jnp.where(rows == 6, 1.0, upper)
    upper = jnp.where(rows == 7, rest, upper)
    lower = jnp.where(rows == 3, 1.0, strength)
    first, second, third = split_three(jnp.concatenate([upper, lower], axis=0))
    stacked = jnp.concatenate([first, first, first, second, second, second, third, third], axis=0)
    return stacked.astype(jnp.bfloat16).T


def source_side(tile, rows):
    position, strength, half, norm, rest, along = tile_scalars(tile, rows)
    zero = jnp.zeros_like(position)
    one = jnp.ones_like(position)
    dist = jnp.where(rows == 6, norm, jnp.where((rows == 3) | (rows == 7), one, -2.0 * position))
    fine = jnp.where(rows == 3, rest, zero)
    back = jnp.where(rows == 6, along, -strength)
    core = jnp.where(rows == 6, half, jnp.where(rows == 5, one, zero))
    unit = jnp.where(rows == 4, one, zero)
    shift = split_three(-position)
    halves = (
        [jnp.concatenate([p, f], axis=0) for p, f in zip(split_three(dist), split_three(fine))],
        [jnp.concatenate([u, p], axis=0) for u, p in zip((unit, zero, zero), shift)],
        [jnp.concatenate([p, zero], axis=0) for p in split_three(back)],
        [jnp.concatenate([p, zero], axis=0) for p in split_three(core)],
    )
    blocks = []
    for pieces in halves:
        first, second, third = [p.astype(jnp.bfloat16) for p in pieces]
        blocks.append(jnp.concatenate([first, second, third, first, second, third, first, second], axis=0))
    return jnp.concatenate(blocks, axis=1)


def cycle(value, start, rows):
    one = jnp.where(rows == 2, roll_rows(value, 2 - start), roll_rows(value, -1 - start))
    two = jnp.where(rows == 0, roll_rows(value, -2 - start), roll_rows(value, 1 - start))
    return one, two


def finish_tile(tile, smooth, grad, rows):
    pos1, pos2 = cycle(tile, 0, rows)
    str1, str2 = cycle(tile, 3, rows)
    smooth1, smooth2 = cycle(smooth, 0, rows)
    grad1, grad2 = cycle(grad, 0, rows)
    velocity = pos1 * smooth2 - pos2 * smooth1 - roll_rows(smooth, -3)
    turn = str1 * smooth2 - str2 * smooth1
    stretch = turn - 3.0 * (pos1 * grad2 - pos2 * grad1 - roll_rows(grad, -3))
    return biot_factor * jnp.where(rows < 3, velocity, roll_rows(stretch, 3)) * tile[7:8, :]


def evaluate(products, pieces):
    for start in range(0, TILE, 16):
        at = slice(start, start + 16)
        dist, front, back, core = (products[at, k * TILE : (k + 1) * TILE] for k in range(4))
        inv = lax.rsqrt(dist)
        inv2 = inv * inv
        inv3 = inv2 * inv
        tail = core * (inv3 * inv2)
        smooth = inv3 + 1.5 * tail
        grad = inv2 * (smooth + tail)
        for k, value in enumerate((smooth, grad * front, grad * back)):
            high, low = split_two(value)
            pieces[at, 2 * k * TILE : (2 * k + 1) * TILE] = high
            pieces[at, (2 * k + 1) * TILE : (2 * k + 2) * TILE] = low


def tile_at(tile):
    return pl.ds(pl.multiple_of(tile * ROWS, ROWS), ROWS)


def wide_at(tile):
    return pl.ds(pl.multiple_of(tile * TILE, TILE), TILE)


def feat_at(tile):
    return pl.ds(pl.multiple_of(tile * FEAT, FEAT), FEAT)


def target_terms(feat, values):
    smooth, front = values[:, : 2 * TILE], values[:, 2 * TILE : 4 * TILE]
    terms = lax.dot_general(
        jnp.concatenate([feat, feat], axis=1),
        jnp.concatenate([smooth, front], axis=0),
        (((1,), (1,)), ((), ())),
        preferred_element_type=jnp.float32,
    )
    return add_pieces(terms)


def source_terms(feat, values):
    high = jnp.concatenate([values[:, :TILE], values[:, 4 * TILE : 5 * TILE]], axis=1)
    low = jnp.concatenate([values[:, TILE : 2 * TILE], values[:, 5 * TILE :]], axis=1)
    both = jnp.concatenate([high, low], axis=0)
    terms = jnp.dot(jnp.concatenate([feat, feat], axis=1), both, preferred_element_type=jnp.float32)
    return add_pieces(terms)


def own_kernel(block, left, right, feat, sums, origin_ref, *scratch):
    products, pieces = scratch[0:2], scratch[2:4]
    tiles = block.shape[0] // ROWS
    rows = row_ids()
    total = block[0:ROWS, :]
    for tile in range(1, tiles):
        total = total + block[tile * ROWS : (tile + 1) * ROWS, :]
    origin = jnp.sum(total, axis=1, keepdims=True) * (1.0 / (tiles * TILE))
    origin = jnp.where(rows < 3, jnp.broadcast_to(origin, (ROWS, TILE)), 0.0)
    origin_ref[...] = origin
    for tile in range(tiles):
        here = block[tile * ROWS : (tile + 1) * ROWS, :] - origin
        wide = slice(tile * TILE, (tile + 1) * TILE)
        left[wide, :] = target_side(here, rows)
        right[wide, :] = source_side(here, rows)
        feat[tile * FEAT : (tile + 1) * FEAT, :] = features(here, rows).astype(jnp.bfloat16)
    for step in range(tiles + 2):
        if step < tiles:
            wide = slice(step * TILE, (step + 1) * TILE)
            products[step % 2][...] = jnp.dot(left[wide, :], right[wide, :], preferred_element_type=jnp.float32)
        if 1 <= step <= tiles:
            evaluate(products[(step - 1) % 2], pieces[(step - 1) % 2])
        if step >= 2:
            tile = step - 2
            terms = target_terms(feat[tile * FEAT : (tile + 1) * FEAT, :], pieces[tile % 2])
            sums[tile * ROWS : (tile + 1) * ROWS, :] = terms


def join_kernel(*refs):
    out, start = refs[-1], 0
    for ref in refs[:-1]:
        out[start : start + ref.shape[0], :] = ref[...]
        start += ref.shape[0]


def pair_kernel(nrows, ncols, tiles, where_ref, slots_ref, count_ref, *refs):
    own_block, own_left, own_right, own_feat, own_sums, origin_ref = refs[:6]
    refs = refs[6:]
    halves = nrows // 2
    row_ins, far_ins, near_in, refs = refs[: ncols - 1], refs[ncols - 1 : ncols + halves - 2], refs[ncols + halves - 2], refs[ncols + halves - 1 :]
    row_outs, col_outs, scratch = refs[:ncols], refs[ncols : ncols + halves], refs[ncols + halves :]
    row_blk, col_blk, left, right, row_feat, col_feat, row_sum, col_sum = scratch[:8]
    products, pieces = scratch[8:10], scratch[10:12]
    per = tiles * ROWS
    rows = row_ids()
    my_row, my_col = where_ref[0], where_ref[1]
    count = count_ref[0]
    row_sources = [(k, row_ins[k - 1], 0) for k in range(1, ncols)]
    col_sources = [(2 * m, far_ins[m - 1], 0) for m in range(1, halves)]
    col_sources += [(2 * m + 1, near_in, m * per) for m in range(halves)]
    origin = origin_ref[...]

    row_sum[...] = jnp.zeros_like(row_sum)
    col_sum[...] = jnp.zeros_like(col_sum)
    pieces[1][...] = jnp.zeros_like(pieces[1])
    for block, feat, me in ((row_blk, row_feat, my_col), (col_blk, col_feat, my_row)):
        block[pl.ds(pl.multiple_of(me * per, per), per), :] = own_block[...]
        feat[pl.ds(pl.multiple_of(me * tiles * FEAT, tiles * FEAT), tiles * FEAT), :] = own_feat[...]
    row_sum[pl.ds(pl.multiple_of(my_col * per, per), per), :] = own_sums[...]
    left[pl.ds(pl.multiple_of(my_col * tiles * TILE, tiles * TILE), tiles * TILE), :] = own_left[...]
    right[pl.ds(pl.multiple_of(my_row * tiles * TILE, tiles * TILE), tiles * TILE), :] = own_right[...]

    def prepare_row(tile, here):
        left[wide_at(tile), :] = target_side(here, rows)
        row_feat[feat_at(tile), :] = features(here, rows).astype(jnp.bfloat16)

    def prepare_col(tile, here):
        right[wide_at(tile), :] = source_side(here, rows)
        col_feat[feat_at(tile), :] = features(here, rows).astype(jnp.bfloat16)

    def prepare(step, carry):
        for sources, block, me, operands in (
            (row_sources, row_blk, my_col, prepare_row),
            (col_sources, col_blk, my_row, prepare_col),
        ):
            for k, source, start in sources:
                tile = (me ^ k) * tiles + step
                value = source[pl.ds(pl.multiple_of(start + step * ROWS, ROWS), ROWS), :]
                block[tile_at(tile), :] = value
                operands(tile, value - origin)
        return carry

    lax.fori_loop(0, tiles, prepare, 0, unroll=2)

    last = slots_ref.shape[1] - 1

    def multiply(slot, out):
        slot = jnp.minimum(slot, last)
        tgt, src = slots_ref[0, slot], slots_ref[1, slot]
        out[...] = jnp.dot(left[wide_at(tgt), :], right[wide_at(src), :], preferred_element_type=jnp.float32)

    def add_up(slot, values):
        kept = jnp.clip(slot, 0, last)
        tgt, src = slots_ref[0, kept], slots_ref[1, kept]
        own = (tgt // tiles == my_col) & (src // tiles == my_row) & (tgt % tiles == src % tiles)
        alive = jnp.where((slot >= tiles) & (slot < count), 1.0, 0.0)
        react = jnp.where(own, 0.0, alive)
        row_sum[tile_at(tgt), :] += alive * target_terms(col_feat[feat_at(src), :], values)
        col_sum[tile_at(src), :] += react * source_terms(row_feat[feat_at(tgt), :], values)

    multiply(tiles, products[0])

    def visit(step, carry):
        for k in range(STEPS):
            slot = tiles + step * STEPS + k
            multiply(slot + 1, products[(k + 1) % 2])
            evaluate(products[k % 2], pieces[k % 2])
            add_up(slot - 1, pieces[(k + 1) % 2])
        return carry

    lax.fori_loop(0, (count - tiles + STEPS) // STEPS, visit, 0)

    row_results = [(k, row_outs[k], 0) for k in range(ncols)]
    col_results = [(k, col_outs[k // 2], k % 2 * per) for k in range(nrows)]

    def close(step, carry):
        for results, block, sums, me in (
            (row_results, row_blk, row_sum, my_col),
            (col_results, col_blk, col_sum, my_row),
        ):
            for k, result, start in results:
                at = tile_at((me ^ k) * tiles + step)
                terms = sums[at, :]
                done = finish_tile(block[at, :] - origin, terms[:, :TILE], terms[:, TILE:], rows)
                result[pl.ds(pl.multiple_of(start + step * ROWS, ROWS), ROWS), :] = done
        return carry

    lax.fori_loop(0, tiles, close, 0, unroll=2)


def halve_kernel(*refs):
    keep, send = refs[-2:]
    half = keep.shape[0]
    total = refs[0][...]
    for ref in refs[1:-2]:
        total = total + ref[...]
    keep[...] = total[:half, :]
    send[...] = total[half:, :]


def total_kernel(*refs):
    vel_ref, str_ref = refs[-2:]
    tiles = vel_ref.shape[1] // TILE
    for tile in range(tiles):
        at = slice(tile * ROWS, (tile + 1) * ROWS)
        total = refs[0][at, :]
        for ref in refs[1:-2]:
            total = total + ref[at, :]
        vel_ref[:, tile * TILE : (tile + 1) * TILE] = total[0:3, :]
        str_ref[:, tile * TILE : (tile + 1) * TILE] = total[3:6, :]


def shards(positions, strengths, cores, order, tile_counts, pair_slots, pair_count):
    tiles = tile_counts.shape[0]
    per_dev = tiles * TILE
    nrows = lax.axis_size("row")
    ncols = lax.axis_size("col")
    halves = nrows // 2
    assert nrows == 2 * halves and nrows & (nrows - 1) == 0 and ncols & (ncols - 1) == 0
    row_tiles, col_tiles = ncols * tiles, nrows * tiles
    smem = pl.BlockSpec(memory_space=pltpu.SMEM)
    vmem = pl.BlockSpec(memory_space=pltpu.VMEM)
    hbm = pl.BlockSpec(memory_space=pltpu.HBM)
    params = pltpu.CompilerParams(vmem_limit_bytes=VMEM_BYTES)

    def blocks(count):
        return jax.ShapeDtypeStruct((count * tiles * ROWS, TILE), jnp.float32)

    def in_hbm(value):
        return pltpu.with_memory_space_constraint(value, pltpu.HBM)

    inputs = (tile_counts, positions, strengths, cores.reshape(1, per_dev), order.reshape(1, per_dev), pair_slots)
    packed, slots = pl.pallas_call(
        pack_kernel,
        out_shape=[blocks(1), jax.ShapeDtypeStruct(pair_slots.shape, jnp.int32)],
        in_specs=[hbm] * len(inputs),
        out_specs=[vmem, smem],
        scratch_shapes=[
            pltpu.VMEM((ROWS, per_dev), jnp.float32),
            pltpu.VMEM((1, per_dev), jnp.int32),
            pltpu.SMEM(tile_counts.shape, jnp.int32),
            pltpu.SemaphoreType.DMA((len(inputs),)),
        ],
        compiler_params=params,
        name="pack",
    )(*map(in_hbm, inputs))

    def swap(value, axis, size, k):
        return lax.ppermute(value, axis, [(d, d ^ k) for d in range(size)])

    phases = [
        pltpu.VMEM((TILE, 4 * TILE), jnp.float32),
        pltpu.VMEM((TILE, 4 * TILE), jnp.float32),
        pltpu.VMEM((TILE, 6 * TILE), jnp.bfloat16),
        pltpu.VMEM((TILE, 6 * TILE), jnp.bfloat16),
    ]
    own = pl.pallas_call(
        own_kernel,
        out_shape=[
            jax.ShapeDtypeStruct((per_dev, TILE), jnp.bfloat16),
            jax.ShapeDtypeStruct((per_dev, 4 * TILE), jnp.bfloat16),
            jax.ShapeDtypeStruct((tiles * FEAT, TILE), jnp.bfloat16),
            jax.ShapeDtypeStruct((tiles * ROWS, 2 * TILE), jnp.float32),
            jax.ShapeDtypeStruct((ROWS, TILE), jnp.float32),
        ],
        in_specs=[vmem],
        out_specs=[vmem] * 5,
        scratch_shapes=phases,
        compiler_params=params,
        cost_estimate=pl.CostEstimate(flops=tiles * 300 * TILE * TILE, bytes_accessed=2**21, transcendentals=0),
        name="own",
    )(packed)

    far = [swap(packed, "row", nrows, 2 * m) for m in range(1, halves)]
    from_row = [swap(packed, "col", ncols, k) for k in range(1, ncols)]
    joined = pl.pallas_call(
        join_kernel,
        out_shape=blocks(halves),
        in_specs=[vmem] * halves,
        out_specs=vmem,
        compiler_params=params,
        name="join",
    )(packed, *far)
    near = swap(joined, "row", nrows, 1)

    where = jnp.stack([lax.axis_index("row"), lax.axis_index("col")]).astype(jnp.int32)
    sums = pl.pallas_call(
        functools.partial(pair_kernel, nrows, ncols, tiles),
        out_shape=[blocks(1)] * ncols + [blocks(2)] * halves,
        in_specs=[smem] * 3 + [vmem] * (5 + ncols + halves),
        out_specs=[vmem] * (ncols + halves),
        scratch_shapes=[
            pltpu.VMEM((row_tiles * ROWS, TILE), jnp.float32),
            pltpu.VMEM((col_tiles * ROWS, TILE), jnp.float32),
            pltpu.VMEM((row_tiles * TILE, TILE), jnp.bfloat16),
            pltpu.VMEM((col_tiles * TILE, 4 * TILE), jnp.bfloat16),
            pltpu.VMEM((row_tiles * FEAT, TILE), jnp.bfloat16),
            pltpu.VMEM((col_tiles * FEAT, TILE), jnp.bfloat16),
            pltpu.VMEM((row_tiles * ROWS, 2 * TILE), jnp.float32),
            pltpu.VMEM((col_tiles * ROWS, 2 * TILE), jnp.float32),
            *phases,
        ],
        compiler_params=params,
        name="pairs",
    )(where, slots, pair_count, packed, *own, *from_row, *far, near)

    far_back = [swap(sums[ncols + m], "row", nrows, 2 * m) for m in range(1, halves)]
    row_back = [swap(sums[k], "col", ncols, k) for k in range(1, ncols)]
    keep, send = pl.pallas_call(
        halve_kernel,
        out_shape=[blocks(1)] * 2,
        in_specs=[vmem] * halves,
        out_specs=[vmem] * 2,
        compiler_params=params,
        name="halve",
    )(sums[ncols], *far_back)
    parts = [sums[0], keep, *row_back, swap(send, "row", nrows, 1)]
    velocity, stretching = pl.pallas_call(
        total_kernel,
        out_shape=[jax.ShapeDtypeStruct((3, per_dev), jnp.float32)] * 2,
        in_specs=[vmem] * len(parts),
        out_specs=[vmem, vmem],
        compiler_params=params,
        name="totals",
    )(*parts)
    return velocity, stretching


def solution(mesh):
    whole = ("groups", "row", "col")
    in_specs = (P(None, whole), P(None, whole), P(whole), P(whole), P(whole), P(None, whole), P(whole))
    out_specs = (P(None, whole), P(None, whole))
    return jax.shard_map(shards, mesh=mesh, in_specs=in_specs, out_specs=out_specs, check_vma=False)
```

```python
import functools
import math

import jax
import jax.numpy as jnp
from jax import lax
from jax.experimental import pallas as pl
from jax.experimental.pallas import tpu as pltpu
from jax.sharding import PartitionSpec as P

TILE = 128
ROWS = 8
STEPS = 4
LEAD = 2
FEAT = 32
VMEM_BYTES = 48 * 1024 * 1024

biot_factor = -1.0 / (4.0 * math.pi)


def row_ids(count=ROWS):
    return lax.broadcasted_iota(jnp.int32, (count, TILE), 0)


def roll_rows(value, shift):
    return pltpu.roll(value, shift % ROWS, 0)


def pack_kernel(
    counts_hbm, pos_hbm, str_hbm, core_hbm, order_hbm, slots_hbm,
    out_ref, slots_ref, stored, order_ref, counts_ref, arrived,
):
    tiles = order_ref.shape[1] // TILE
    pairs = (
        (pos_hbm, stored.at[0:3, :]),
        (str_hbm, stored.at[3:6, :]),
        (core_hbm, stored.at[6:7, :]),
        (order_hbm, order_ref),
        (counts_hbm, counts_ref),
        (slots_hbm, slots_ref),
    )
    copies = [pltpu.make_async_copy(src, dst, arrived.at[k]) for k, (src, dst) in enumerate(pairs)]
    for copy in copies:
        copy.start()
    stored[7:8, :] = jnp.zeros((1, stored.shape[1]), jnp.float32)
    for copy in copies:
        copy.wait()
    lane = lax.broadcasted_iota(jnp.int32, (ROWS, TILE), 1)
    rows = row_ids()
    is_strength = (rows >= 3) & (rows < 6)
    for tile in range(tiles):
        where_from = jnp.broadcast_to(order_ref[:, tile * TILE : (tile + 1) * TILE], (ROWS, TILE))
        inside = where_from & (TILE - 1)
        block = where_from >> 7
        value = jnp.zeros((ROWS, TILE), jnp.float32)
        for source in range(tiles):
            part = jnp.take_along_axis(stored[:, source * TILE : (source + 1) * TILE], inside, axis=1)
            value = jnp.where(block == source, part, value)
        live = lane < counts_ref[tile]
        value = jnp.where(is_strength & ~live, 0.0, value)
        value = jnp.where(rows == 7, live.astype(jnp.float32), value)
        out_ref[tile * ROWS : (tile + 1) * ROWS, :] = value


def split_three(value):
    first = value.astype(jnp.bfloat16).astype(jnp.float32)
    rest = value - first
    second = rest.astype(jnp.bfloat16).astype(jnp.float32)
    return first, second, rest - second


def split_two(value):
    high = value.astype(jnp.bfloat16)
    return high, (value - high.astype(jnp.float32)).astype(jnp.bfloat16)


def features(tile, rows):
    down1, down2 = roll_rows(tile, 1), roll_rows(tile, 2)
    pos1 = jnp.where(rows == 5, roll_rows(tile, 5), down2)
    pos2 = jnp.where(rows == 3, down1, roll_rows(tile, 4))
    str1 = jnp.where(rows == 5, down2, roll_rows(tile, 7))
    str2 = jnp.where(rows == 3, roll_rows(tile, 6), down1)
    cross = pos1 * str2 - pos2 * str1
    value = jnp.where(rows < 3, roll_rows(tile, 5), jnp.where(rows < 6, cross, 0.0))
    return jnp.concatenate([*split_three(value), jnp.zeros_like(value)], axis=0)


def add_pieces(terms):
    return terms[0:ROWS, :] + (terms[ROWS : 2 * ROWS, :] + terms[2 * ROWS : 3 * ROWS, :])


def tile_scalars(tile, rows):
    position = jnp.where(rows < 3, tile, 0.0)
    strength = jnp.where(rows < 3, roll_rows(tile, 5), 0.0)
    half = 0.5 * tile[6:7, :] * tile[6:7, :]
    coarse = position.astype(jnp.bfloat16).astype(jnp.float32)
    norm = jnp.sum(coarse * coarse, axis=0, keepdims=True)
    rest = jnp.sum((position - coarse) * (position + coarse), axis=0, keepdims=True) + half
    along = jnp.sum(position * strength, axis=0, keepdims=True)
    return position, strength, half, norm, rest, along


def target_side(tile, rows):
    position, strength, half, norm, rest, along = tile_scalars(tile, rows)
    upper = jnp.where(rows == 3, norm, position)
    upper = jnp.where(rows == 4, along, upper)
    upper = jnp.where(rows == 5, half, upper)
    upper = jnp.where(rows == 6, 1.0, upper)
    upper = jnp.where(rows == 7, rest, upper)
    lower = jnp.where(rows == 3, 1.0, strength)
    first, second, third = split_three(jnp.concatenate([upper, lower], axis=0))
    stacked = jnp.concatenate([first, first, first, second, second, second, third, third], axis=0)
    return stacked.astype(jnp.bfloat16).T


def source_side(tile, rows):
    position, strength, half, norm, rest, along = tile_scalars(tile, rows)
    zero = jnp.zeros_like(position)
    one = jnp.ones_like(position)
    dist = jnp.where(rows == 6, norm, jnp.where((rows == 3) | (rows == 7), one, -2.0 * position))
    fine = jnp.where(rows == 3, rest, zero)
    back = jnp.where(rows == 6, along, -strength)
    core = jnp.where(rows == 6, half, jnp.where(rows == 5, one, zero))
    unit = jnp.where(rows == 4, one, zero)
    shift = split_three(-position)
    halves = (
        [jnp.concatenate([p, f], axis=0) for p, f in zip(split_three(dist), split_three(fine))],
        [jnp.concatenate([u, p], axis=0) for u, p in zip((unit, zero, zero), shift)],
        [jnp.concatenate([p, zero], axis=0) for p in split_three(back)],
        [jnp.concatenate([p, zero], axis=0) for p in split_three(core)],
    )
    blocks = []
    for pieces in halves:
        first, second, third = [p.astype(jnp.bfloat16) for p in pieces]
        blocks.append(jnp.concatenate([first, second, third, first, second, third, first, second], axis=0))
    return jnp.concatenate(blocks, axis=1)


def cycle(value, start, rows):
    one = jnp.where(rows == 2, roll_rows(value, 2 - start), roll_rows(value, -1 - start))
    two = jnp.where(rows == 0, roll_rows(value, -2 - start), roll_rows(value, 1 - start))
    return one, two


def finish_tile(tile, smooth, grad, rows):
    pos1, pos2 = cycle(tile, 0, rows)
    str1, str2 = cycle(tile, 3, rows)
    smooth1, smooth2 = cycle(smooth, 0, rows)
    grad1, grad2 = cycle(grad, 0, rows)
    velocity = pos1 * smooth2 - pos2 * smooth1 - roll_rows(smooth, -3)
    turn = str1 * smooth2 - str2 * smooth1
    stretch = turn - 3.0 * (pos1 * grad2 - pos2 * grad1 - roll_rows(grad, -3))
    return biot_factor * jnp.where(rows < 3, velocity, roll_rows(stretch, 3)) * tile[7:8, :]


def evaluate(products, pieces):
    for start in range(0, TILE, 16):
        at = slice(start, start + 16)
        dist, front, back, core = (products[at, k * TILE : (k + 1) * TILE] for k in range(4))
        inv = lax.rsqrt(dist)
        inv2 = inv * inv
        inv3 = inv2 * inv
        tail = core * (inv3 * inv2)
        smooth = inv3 + 1.5 * tail
        grad = inv2 * (smooth + tail)
        for k, value in enumerate((smooth, grad * front, grad * back)):
            high, low = split_two(value)
            pieces[at, 2 * k * TILE : (2 * k + 1) * TILE] = high
            pieces[at, (2 * k + 1) * TILE : (2 * k + 2) * TILE] = low


def tile_at(tile):
    return pl.ds(pl.multiple_of(tile * ROWS, ROWS), ROWS)


def wide_at(tile):
    return pl.ds(pl.multiple_of(tile * TILE, TILE), TILE)


def feat_at(tile):
    return pl.ds(pl.multiple_of(tile * FEAT, FEAT), FEAT)


def target_terms(feat, values):
    smooth, front = values[:, : 2 * TILE], values[:, 2 * TILE : 4 * TILE]
    terms = lax.dot_general(
        jnp.concatenate([feat, feat], axis=1),
        jnp.concatenate([smooth, front], axis=0),
        (((1,), (1,)), ((), ())),
        preferred_element_type=jnp.float32,
    )
    return add_pieces(terms)


def source_terms(feat, values):
    high = jnp.concatenate([values[:, :TILE], values[:, 4 * TILE : 5 * TILE]], axis=1)
    low = jnp.concatenate([values[:, TILE : 2 * TILE], values[:, 5 * TILE :]], axis=1)
    both = jnp.concatenate([high, low], axis=0)
    terms = jnp.dot(jnp.concatenate([feat, feat], axis=1), both, preferred_element_type=jnp.float32)
    return add_pieces(terms)


def own_kernel(block, left, right, feat, sums, origin_ref, *scratch):
    products, pieces = scratch[:STEPS], scratch[STEPS:]
    tiles = block.shape[0] // ROWS
    rows = row_ids()
    total = block[0:ROWS, :]
    for tile in range(1, tiles):
        total = total + block[tile * ROWS : (tile + 1) * ROWS, :]
    origin = jnp.sum(total, axis=1, keepdims=True) * (1.0 / (tiles * TILE))
    origin = jnp.where(rows < 3, jnp.broadcast_to(origin, (ROWS, TILE)), 0.0)
    origin_ref[...] = origin
    for tile in range(tiles):
        here = block[tile * ROWS : (tile + 1) * ROWS, :] - origin
        wide = slice(tile * TILE, (tile + 1) * TILE)
        left[wide, :] = target_side(here, rows)
        right[wide, :] = source_side(here, rows)
        feat[tile * FEAT : (tile + 1) * FEAT, :] = features(here, rows).astype(jnp.bfloat16)
    for step in range(tiles + 2 * LEAD):
        if step < tiles:
            wide = slice(step * TILE, (step + 1) * TILE)
            products[step % STEPS][...] = jnp.dot(left[wide, :], right[wide, :], preferred_element_type=jnp.float32)
        if LEAD <= step < tiles + LEAD:
            evaluate(products[(step - LEAD) % STEPS], pieces[(step - LEAD) % STEPS])
        if step >= 2 * LEAD:
            tile = step - 2 * LEAD
            terms = target_terms(feat[tile * FEAT : (tile + 1) * FEAT, :], pieces[tile % STEPS])
            sums[tile * ROWS : (tile + 1) * ROWS, :] = terms


def join_kernel(*refs):
    out, start = refs[-1], 0
    for ref in refs[:-1]:
        out[start : start + ref.shape[0], :] = ref[...]
        start += ref.shape[0]


def pair_kernel(nrows, ncols, tiles, where_ref, slots_ref, *refs):
    own_block, own_left, own_right, own_feat, own_sums, origin_ref = refs[:6]
    refs = refs[6:]
    halves = nrows // 2
    row_ins, far_ins, near_in, refs = refs[: ncols - 1], refs[ncols - 1 : ncols + halves - 2], refs[ncols + halves - 2], refs[ncols + halves - 1 :]
    row_outs, col_outs, scratch = refs[:ncols], refs[ncols : ncols + halves], refs[ncols + halves :]
    row_blk, col_blk, left, right, row_feat, col_feat, row_sum, col_sum = scratch[:8]
    products, pieces = scratch[8 : 8 + STEPS], scratch[8 + STEPS :]
    per = tiles * ROWS
    rows = row_ids()
    my_row, my_col = where_ref[0], where_ref[1]
    count = where_ref[2]
    row_sources = [(k, row_ins[k - 1], 0) for k in range(1, ncols)]
    col_sources = [(2 * m, far_ins[m - 1], 0) for m in range(1, halves)]
    col_sources += [(2 * m + 1, near_in, m * per) for m in range(halves)]
    origin = origin_ref[...]

    row_sum[...] = jnp.zeros_like(row_sum)
    col_sum[...] = jnp.zeros_like(col_sum)
    for k in range(STEPS - LEAD, STEPS):
        pieces[k][...] = jnp.zeros_like(pieces[k])
    for block, feat, me in ((row_blk, row_feat, my_col), (col_blk, col_feat, my_row)):
        block[pl.ds(pl.multiple_of(me * per, per), per), :] = own_block[...]
        feat[pl.ds(pl.multiple_of(me * tiles * FEAT, tiles * FEAT), tiles * FEAT), :] = own_feat[...]
    row_sum[pl.ds(pl.multiple_of(my_col * per, per), per), :] = own_sums[...]
    left[pl.ds(pl.multiple_of(my_col * tiles * TILE, tiles * TILE), tiles * TILE), :] = own_left[...]
    right[pl.ds(pl.multiple_of(my_row * tiles * TILE, tiles * TILE), tiles * TILE), :] = own_right[...]

    def prepare_row(tile, here):
        left[wide_at(tile), :] = target_side(here, rows)
        row_feat[feat_at(tile), :] = features(here, rows).astype(jnp.bfloat16)

    def prepare_col(tile, here):
        right[wide_at(tile), :] = source_side(here, rows)
        col_feat[feat_at(tile), :] = features(here, rows).astype(jnp.bfloat16)

    def prepare(step, carry):
        for sources, block, me, operands in (
            (row_sources, row_blk, my_col, prepare_row),
            (col_sources, col_blk, my_row, prepare_col),
        ):
            for k, source, start in sources:
                tile = (me ^ k) * tiles + step
                value = source[pl.ds(pl.multiple_of(start + step * ROWS, ROWS), ROWS), :]
                block[tile_at(tile), :] = value
                operands(tile, value - origin)
        return carry

    lax.fori_loop(0, tiles, prepare, 0, unroll=2)

    last = slots_ref.shape[1] - 1

    def multiply(slot, out):
        slot = jnp.minimum(slot, last)
        tgt, src = slots_ref[0, slot], slots_ref[1, slot]
        out[...] = jnp.dot(left[wide_at(tgt), :], right[wide_at(src), :], preferred_element_type=jnp.float32)

    def add_up(slot, values):
        kept = jnp.clip(slot, 0, last)
        tgt, src = slots_ref[0, kept], slots_ref[1, kept]
        own = (tgt // tiles == my_col) & (src // tiles == my_row) & (tgt % tiles == src % tiles)
        alive = jnp.where((slot >= tiles) & (slot < count), 1.0, 0.0)
        react = jnp.where(own, 0.0, alive)
        row_sum[tile_at(tgt), :] += alive * target_terms(col_feat[feat_at(src), :], values)
        col_sum[tile_at(src), :] += react * source_terms(row_feat[feat_at(tgt), :], values)

    for k in range(LEAD):
        multiply(tiles + k, products[k])
    loops = (count - tiles + STEPS - 1) // STEPS

    def visit(step, carry):
        for k in range(STEPS):
            slot = tiles + step * STEPS + k
            multiply(slot + LEAD, products[(k + LEAD) % STEPS])
            evaluate(products[k], pieces[k])
            add_up(slot - LEAD, pieces[(k - LEAD) % STEPS])
        return carry

    lax.fori_loop(0, loops, visit, 0)
    for k in range(LEAD):
        add_up(tiles + loops * STEPS - LEAD + k, pieces[STEPS - LEAD + k])

    row_results = [(k, row_outs[k], 0) for k in range(ncols)]
    col_results = [(k, col_outs[k // 2], k % 2 * per) for k in range(nrows)]

    def close(step, carry):
        for results, block, sums, me in (
            (row_results, row_blk, row_sum, my_col),
            (col_results, col_blk, col_sum, my_row),
        ):
            for k, result, start in results:
                at = tile_at((me ^ k) * tiles + step)
                terms = sums[at, :]
                done = finish_tile(block[at, :] - origin, terms[:, :TILE], terms[:, TILE:], rows)
                result[pl.ds(pl.multiple_of(start + step * ROWS, ROWS), ROWS), :] = done
        return carry

    lax.fori_loop(0, tiles, close, 0, unroll=2)


def halve_kernel(*refs):
    keep, send = refs[-2:]
    half = keep.shape[0]
    total = refs[0][...]
    for ref in refs[1:-2]:
        total = total + ref[...]
    keep[...] = total[:half, :]
    send[...] = total[half:, :]


def total_kernel(*refs):
    vel_ref, str_ref = refs[-2:]
    tiles = vel_ref.shape[1] // TILE
    for tile in range(tiles):
        at = slice(tile * ROWS, (tile + 1) * ROWS)
        total = refs[0][at, :]
        for ref in refs[1:-2]:
            total = total + ref[at, :]
        vel_ref[:, tile * TILE : (tile + 1) * TILE] = total[0:3, :]
        str_ref[:, tile * TILE : (tile + 1) * TILE] = total[3:6, :]


def shards(positions, strengths, cores, order, tile_counts, pair_slots, pair_count):
    tiles = tile_counts.shape[0]
    per_dev = tiles * TILE
    nrows = lax.axis_size("row")
    ncols = lax.axis_size("col")
    halves = nrows // 2
    assert nrows == 2 * halves and nrows & (nrows - 1) == 0 and ncols & (ncols - 1) == 0
    row_tiles, col_tiles = ncols * tiles, nrows * tiles
    smem = pl.BlockSpec(memory_space=pltpu.SMEM)
    vmem = pl.BlockSpec(memory_space=pltpu.VMEM)
    hbm = pl.BlockSpec(memory_space=pltpu.HBM)
    params = pltpu.CompilerParams(vmem_limit_bytes=VMEM_BYTES)

    def blocks(count):
        return jax.ShapeDtypeStruct((count * tiles * ROWS, TILE), jnp.float32)

    def in_hbm(value):
        return pltpu.with_memory_space_constraint(value, pltpu.HBM)

    inputs = (tile_counts, positions, strengths, cores.reshape(1, per_dev), order.reshape(1, per_dev), pair_slots)
    packed, slots = pl.pallas_call(
        pack_kernel,
        out_shape=[blocks(1), jax.ShapeDtypeStruct(pair_slots.shape, jnp.int32)],
        in_specs=[hbm] * len(inputs),
        out_specs=[vmem, smem],
        scratch_shapes=[
            pltpu.VMEM((ROWS, per_dev), jnp.float32),
            pltpu.VMEM((1, per_dev), jnp.int32),
            pltpu.SMEM(tile_counts.shape, jnp.int32),
            pltpu.SemaphoreType.DMA((len(inputs),)),
        ],
        compiler_params=params,
        name="pack",
    )(*map(in_hbm, inputs))

    def swap(value, axis, size, k):
        return lax.ppermute(value, axis, [(d, d ^ k) for d in range(size)])

    phases = [pltpu.VMEM((TILE, 4 * TILE), jnp.float32)] * STEPS + [pltpu.VMEM((TILE, 6 * TILE), jnp.bfloat16)] * STEPS
    own = pl.pallas_call(
        own_kernel,
        out_shape=[
            jax.ShapeDtypeStruct((per_dev, TILE), jnp.bfloat16),
            jax.ShapeDtypeStruct((per_dev, 4 * TILE), jnp.bfloat16),
            jax.ShapeDtypeStruct((tiles * FEAT, TILE), jnp.bfloat16),
            jax.ShapeDtypeStruct((tiles * ROWS, 2 * TILE), jnp.float32),
            jax.ShapeDtypeStruct((ROWS, TILE), jnp.float32),
        ],
        in_specs=[vmem],
        out_specs=[vmem] * 5,
        scratch_shapes=phases,
        compiler_params=params,
        cost_estimate=pl.CostEstimate(flops=tiles * 300 * TILE * TILE, bytes_accessed=2**21, transcendentals=0),
        name="own",
    )(packed)

    far = [swap(packed, "row", nrows, 2 * m) for m in range(1, halves)]
    from_row = [swap(packed, "col", ncols, k) for k in range(1, ncols)]
    joined = pl.pallas_call(
        join_kernel,
        out_shape=blocks(halves),
        in_specs=[vmem] * halves,
        out_specs=vmem,
        compiler_params=params,
        name="join",
    )(packed, *far)
    near = swap(joined, "row", nrows, 1)

    where = jnp.stack([lax.axis_index("row"), lax.axis_index("col"), pair_count[0]]).astype(jnp.int32)
    sums = pl.pallas_call(
        functools.partial(pair_kernel, nrows, ncols, tiles),
        out_shape=[blocks(1)] * ncols + [blocks(2)] * halves,
        in_specs=[smem] * 2 + [vmem] * (5 + ncols + halves),
        out_specs=[vmem] * (ncols + halves),
        scratch_shapes=[
            pltpu.VMEM((row_tiles * ROWS, TILE), jnp.float32),
            pltpu.VMEM((col_tiles * ROWS, TILE), jnp.float32),
            pltpu.VMEM((row_tiles * TILE, TILE), jnp.bfloat16),
            pltpu.VMEM((col_tiles * TILE, 4 * TILE), jnp.bfloat16),
            pltpu.VMEM((row_tiles * FEAT, TILE), jnp.bfloat16),
            pltpu.VMEM((col_tiles * FEAT, TILE), jnp.bfloat16),
            pltpu.VMEM((row_tiles * ROWS, 2 * TILE), jnp.float32),
            pltpu.VMEM((col_tiles * ROWS, 2 * TILE), jnp.float32),
            *phases,
        ],
        compiler_params=params,
        name="pairs",
    )(where, slots, packed, *own, *from_row, *far, near)

    far_back = [swap(sums[ncols + m], "row", nrows, 2 * m) for m in range(1, halves)]
    row_back = [swap(sums[k], "col", ncols, k) for k in range(1, ncols)]
    keep, send = pl.pallas_call(
        halve_kernel,
        out_shape=[blocks(1)] * 2,
        in_specs=[vmem] * halves,
        out_specs=[vmem] * 2,
        compiler_params=params,
        name="halve",
    )(sums[ncols], *far_back)
    parts = [sums[0], keep, *row_back, swap(send, "row", nrows, 1)]
    velocity, stretching = pl.pallas_call(
        total_kernel,
        out_shape=[jax.ShapeDtypeStruct((3, per_dev), jnp.float32)] * 2,
        in_specs=[vmem] * len(parts),
        out_specs=[vmem, vmem],
        compiler_params=params,
        name="totals",
    )(*parts)
    return velocity, stretching


def solution(mesh):
    whole = ("groups", "row", "col")
    in_specs = (P(None, whole), P(None, whole), P(whole), P(whole), P(whole), P(None, whole), P(whole))
    out_specs = (P(None, whole), P(None, whole))
    return jax.shard_map(shards, mesh=mesh, in_specs=in_specs, out_specs=out_specs, check_vma=False)
```

```python
import functools
import math

import jax
import jax.numpy as jnp
from jax import lax
from jax.experimental import pallas as pl
from jax.experimental.pallas import tpu as pltpu
from jax.sharding import PartitionSpec as P

TILE = 128
ROWS = 8
STEPS = 4
LEAD = 2
FEAT = 32
TERMS = 64
VMEM_BYTES = 48 * 1024 * 1024

biot_factor = -1.0 / (4.0 * math.pi)


def row_ids(count=ROWS):
    return lax.broadcasted_iota(jnp.int32, (count, TILE), 0)


def roll_rows(value, shift):
    return pltpu.roll(value, shift % ROWS, 0)


def pack_kernel(
    counts_hbm, pos_hbm, str_hbm, core_hbm, order_hbm, slots_hbm,
    out_ref, slots_ref, stored, order_ref, counts_ref, arrived,
):
    tiles = order_ref.shape[1] // TILE
    pairs = (
        (pos_hbm, stored.at[0:3, :]),
        (str_hbm, stored.at[3:6, :]),
        (core_hbm, stored.at[6:7, :]),
        (order_hbm, order_ref),
        (counts_hbm, counts_ref),
        (slots_hbm, slots_ref),
    )
    copies = [pltpu.make_async_copy(src, dst, arrived.at[k]) for k, (src, dst) in enumerate(pairs)]
    for copy in copies:
        copy.start()
    stored[7:8, :] = jnp.zeros((1, stored.shape[1]), jnp.float32)
    for copy in copies:
        copy.wait()
    lane = lax.broadcasted_iota(jnp.int32, (ROWS, TILE), 1)
    rows = row_ids()
    is_strength = (rows >= 3) & (rows < 6)
    for tile in range(tiles):
        where_from = jnp.broadcast_to(order_ref[:, tile * TILE : (tile + 1) * TILE], (ROWS, TILE))
        inside = where_from & (TILE - 1)
        block = where_from >> 7
        value = jnp.zeros((ROWS, TILE), jnp.float32)
        for source in range(tiles):
            part = jnp.take_along_axis(stored[:, source * TILE : (source + 1) * TILE], inside, axis=1)
            value = jnp.where(block == source, part, value)
        live = lane < counts_ref[tile]
        value = jnp.where(is_strength & ~live, 0.0, value)
        value = jnp.where(rows == 7, live.astype(jnp.float32), value)
        out_ref[tile * ROWS : (tile + 1) * ROWS, :] = value


def split_three(value):
    first = value.astype(jnp.bfloat16).astype(jnp.float32)
    rest = value - first
    second = rest.astype(jnp.bfloat16).astype(jnp.float32)
    return first, second, rest - second


def split_two(value):
    high = value.astype(jnp.bfloat16)
    return high, (value - high.astype(jnp.float32)).astype(jnp.bfloat16)


def features(tile, rows):
    down1, down2 = roll_rows(tile, 1), roll_rows(tile, 2)
    pos1 = jnp.where(rows == 5, roll_rows(tile, 5), down2)
    pos2 = jnp.where(rows == 3, down1, roll_rows(tile, 4))
    str1 = jnp.where(rows == 5, down2, roll_rows(tile, 7))
    str2 = jnp.where(rows == 3, roll_rows(tile, 6), down1)
    cross = pos1 * str2 - pos2 * str1
    value = jnp.where(rows < 3, roll_rows(tile, 5), jnp.where(rows < 6, cross, 0.0))
    return jnp.concatenate([*split_three(value), jnp.zeros_like(value)], axis=0)


def add_pieces(terms):
    return terms[0:ROWS, :] + (terms[ROWS : 2 * ROWS, :] + terms[2 * ROWS : 3 * ROWS, :])


def tile_scalars(tile, rows):
    position = jnp.where(rows < 3, tile, 0.0)
    strength = jnp.where(rows < 3, roll_rows(tile, 5), 0.0)
    half = 0.5 * tile[6:7, :] * tile[6:7, :]
    coarse = position.astype(jnp.bfloat16).astype(jnp.float32)
    norm = jnp.sum(coarse * coarse, axis=0, keepdims=True)
    rest = jnp.sum((position - coarse) * (position + coarse), axis=0, keepdims=True) + half
    along = jnp.sum(position * strength, axis=0, keepdims=True)
    return position, strength, half, norm, rest, along


def target_side(tile, rows):
    _, _, half, norm, rest, along = tile_scalars(tile, rows)
    shared = jnp.where(rows < 6, tile, 1.0)
    alone = jnp.where(rows == 0, norm, jnp.where(rows == 1, rest, jnp.where(rows == 2, along, 0.0)))
    alone = jnp.where(rows == 3, half, alone)
    first, second, third = split_three(shared)
    alone1, alone2, alone3 = split_three(alone)
    both = jnp.where(rows < 4, alone1, roll_rows(alone2, 4))
    stacked = jnp.concatenate([first, both, first, first, second, second, third, alone3], axis=0)
    return stacked.astype(jnp.bfloat16).T


def source_side(tile, rows):
    position, strength, half, norm, rest, along = tile_scalars(tile, rows)
    zero = jnp.zeros_like(position)
    one = jnp.ones_like(position)
    dist = jnp.where(rows == 6, norm, jnp.where(rows == 7, rest, -2.0 * position))
    front = -roll_rows(position, 3)
    back = jnp.where(rows == 6, along, -strength)
    core = jnp.where(rows == 6, half, zero)
    pick = rows & 3
    picks = (jnp.where(pick < 2, one, zero), jnp.where(pick == 2, one, zero), zero, jnp.where(pick == 3, one, zero))
    blocks = []
    for value, picked in zip((dist, front, back, core), picks):
        first, second, third = split_three(value)
        parts = [first, picked, second, third, first, second, first, picked]
        blocks.append(jnp.concatenate(parts, axis=0).astype(jnp.bfloat16))
    return jnp.concatenate(blocks, axis=1)


def cycle(value, start, rows):
    one = jnp.where(rows == 2, roll_rows(value, 2 - start), roll_rows(value, -1 - start))
    two = jnp.where(rows == 0, roll_rows(value, -2 - start), roll_rows(value, 1 - start))
    return one, two


def finish_tile(tile, smooth, grad, rows):
    pos1, pos2 = cycle(tile, 0, rows)
    str1, str2 = cycle(tile, 3, rows)
    smooth1, smooth2 = cycle(smooth, 0, rows)
    grad1, grad2 = cycle(grad, 0, rows)
    velocity = pos1 * smooth2 - pos2 * smooth1 - roll_rows(smooth, -3)
    turn = str1 * smooth2 - str2 * smooth1
    stretch = turn - 3.0 * (pos1 * grad2 - pos2 * grad1 - roll_rows(grad, -3))
    return biot_factor * jnp.where(rows < 3, velocity, roll_rows(stretch, 3)) * tile[7:8, :]


def evaluate(products, pieces):
    for start in range(0, TILE, 16):
        at = slice(start, start + 16)
        dist, front, back, core = (products[at, k * TILE : (k + 1) * TILE] for k in range(4))
        inv = lax.rsqrt(dist)
        inv2 = inv * inv
        inv3 = inv2 * inv
        tail = core * (inv3 * inv2)
        smooth = inv3 + 1.5 * tail
        grad = inv2 * (smooth + tail)
        for k, value in enumerate((smooth, grad * front, grad * back)):
            high, low = split_two(value)
            pieces[at, 2 * k * TILE : (2 * k + 1) * TILE] = high
            pieces[at, (2 * k + 1) * TILE : (2 * k + 2) * TILE] = low


def tile_at(tile):
    return pl.ds(pl.multiple_of(tile * ROWS, ROWS), ROWS)


def term_at(tile):
    return pl.ds(pl.multiple_of(tile * TERMS, TERMS), TERMS)


def wide_at(tile):
    return pl.ds(pl.multiple_of(tile * TILE, TILE), TILE)


def feat_at(tile):
    return pl.ds(pl.multiple_of(tile * FEAT, FEAT), FEAT)


def target_terms(feat, values):
    smooth, front = values[:, : 2 * TILE], values[:, 2 * TILE : 4 * TILE]
    terms = lax.dot_general(
        jnp.concatenate([feat, feat], axis=1),
        jnp.concatenate([smooth, front], axis=0),
        (((1,), (1,)), ((), ())),
        preferred_element_type=jnp.float32,
    )
    return add_pieces(terms)


def source_terms(feat, values):
    high = jnp.concatenate([values[:, :TILE], values[:, 4 * TILE : 5 * TILE]], axis=1)
    low = jnp.concatenate([values[:, TILE : 2 * TILE], values[:, 5 * TILE :]], axis=1)
    both = jnp.concatenate([high, low], axis=0)
    terms = jnp.dot(jnp.concatenate([feat, feat], axis=1), both, preferred_element_type=jnp.float32)
    return add_pieces(terms)


def own_kernel(block, left, right, feat, sums, origin_ref, *scratch):
    products, pieces = scratch[:STEPS], scratch[STEPS:]
    tiles = block.shape[0] // ROWS
    rows = row_ids()
    total = block[0:ROWS, :]
    for tile in range(1, tiles):
        total = total + block[tile * ROWS : (tile + 1) * ROWS, :]
    origin = jnp.sum(total, axis=1, keepdims=True) * (1.0 / (tiles * TILE))
    origin = jnp.where(rows < 3, jnp.broadcast_to(origin, (ROWS, TILE)), 0.0)
    origin_ref[...] = origin
    for tile in range(tiles):
        here = block[tile * ROWS : (tile + 1) * ROWS, :] - origin
        wide = slice(tile * TILE, (tile + 1) * TILE)
        left[wide, :] = target_side(here, rows)
        right[tile * TERMS : (tile + 1) * TERMS, :] = source_side(here, rows)
        feat[tile * FEAT : (tile + 1) * FEAT, :] = features(here, rows).astype(jnp.bfloat16)
    for step in range(tiles + 2 * LEAD):
        if step < tiles:
            target, source = left[step * TILE : (step + 1) * TILE, :], right[step * TERMS : (step + 1) * TERMS, :]
            products[step % STEPS][...] = jnp.dot(target, source, preferred_element_type=jnp.float32)
        if LEAD <= step < tiles + LEAD:
            evaluate(products[(step - LEAD) % STEPS], pieces[(step - LEAD) % STEPS])
        if step >= 2 * LEAD:
            tile = step - 2 * LEAD
            terms = target_terms(feat[tile * FEAT : (tile + 1) * FEAT, :], pieces[tile % STEPS])
            sums[tile * ROWS : (tile + 1) * ROWS, :] = terms


def join_kernel(*refs):
    out, start = refs[-1], 0
    for ref in refs[:-1]:
        out[start : start + ref.shape[0], :] = ref[...]
        start += ref.shape[0]


def pair_kernel(nrows, ncols, tiles, where_ref, slots_ref, *refs):
    own_block, own_left, own_right, own_feat, own_sums, origin_ref = refs[:6]
    refs = refs[6:]
    halves = nrows // 2
    row_ins, far_ins, near_in, refs = refs[: ncols - 1], refs[ncols - 1 : ncols + halves - 2], refs[ncols + halves - 2], refs[ncols + halves - 1 :]
    row_outs, col_outs, scratch = refs[:ncols], refs[ncols : ncols + halves], refs[ncols + halves :]
    row_blk, col_blk, left, right, row_feat, col_feat, row_sum, col_sum = scratch[:8]
    products, pieces = scratch[8 : 8 + STEPS], scratch[8 + STEPS :]
    per = tiles * ROWS
    rows = row_ids()
    my_row, my_col = where_ref[0], where_ref[1]
    count = where_ref[2]
    row_sources = [(k, row_ins[k - 1], 0) for k in range(1, ncols)]
    col_sources = [(2 * m, far_ins[m - 1], 0) for m in range(1, halves)]
    col_sources += [(2 * m + 1, near_in, m * per) for m in range(halves)]
    origin = origin_ref[...]

    row_sum[...] = jnp.zeros_like(row_sum)
    col_sum[...] = jnp.zeros_like(col_sum)
    for k in range(STEPS - LEAD, STEPS):
        pieces[k][...] = jnp.zeros_like(pieces[k])
    for block, feat, me in ((row_blk, row_feat, my_col), (col_blk, col_feat, my_row)):
        block[pl.ds(pl.multiple_of(me * per, per), per), :] = own_block[...]
        feat[pl.ds(pl.multiple_of(me * tiles * FEAT, tiles * FEAT), tiles * FEAT), :] = own_feat[...]
    row_sum[pl.ds(pl.multiple_of(my_col * per, per), per), :] = own_sums[...]
    left[pl.ds(pl.multiple_of(my_col * tiles * TILE, tiles * TILE), tiles * TILE), :] = own_left[...]
    right[pl.ds(pl.multiple_of(my_row * tiles * TERMS, tiles * TERMS), tiles * TERMS), :] = own_right[...]

    def prepare_row(tile, here):
        left[wide_at(tile), :] = target_side(here, rows)
        row_feat[feat_at(tile), :] = features(here, rows).astype(jnp.bfloat16)

    def prepare_col(tile, here):
        right[term_at(tile), :] = source_side(here, rows)
        col_feat[feat_at(tile), :] = features(here, rows).astype(jnp.bfloat16)

    def prepare(step, carry):
        for sources, block, me, operands in (
            (row_sources, row_blk, my_col, prepare_row),
            (col_sources, col_blk, my_row, prepare_col),
        ):
            for k, source, start in sources:
                tile = (me ^ k) * tiles + step
                value = source[pl.ds(pl.multiple_of(start + step * ROWS, ROWS), ROWS), :]
                block[tile_at(tile), :] = value
                operands(tile, value - origin)
        return carry

    lax.fori_loop(0, tiles, prepare, 0, unroll=2)

    last = slots_ref.shape[1] - 1

    def multiply(slot, out):
        slot = jnp.minimum(slot, last)
        tgt, src = slots_ref[0, slot], slots_ref[1, slot]
        out[...] = jnp.dot(left[wide_at(tgt), :], right[term_at(src), :], preferred_element_type=jnp.float32)

    def add_up(slot, values):
        kept = jnp.clip(slot, 0, last)
        tgt, src = slots_ref[0, kept], slots_ref[1, kept]
        own = (tgt // tiles == my_col) & (src // tiles == my_row) & (tgt % tiles == src % tiles)
        alive = jnp.where((slot >= tiles) & (slot < count), 1.0, 0.0)
        react = jnp.where(own, 0.0, alive)
        row_sum[tile_at(tgt), :] += alive * target_terms(col_feat[feat_at(src), :], values)
        col_sum[tile_at(src), :] += react * source_terms(row_feat[feat_at(tgt), :], values)

    for k in range(LEAD):
        multiply(tiles + k, products[k])
    loops = (count - tiles + STEPS - 1) // STEPS

    def visit(step, carry):
        for k in range(STEPS):
            slot = tiles + step * STEPS + k
            multiply(slot + LEAD, products[(k + LEAD) % STEPS])
            evaluate(products[k], pieces[k])
            add_up(slot - LEAD, pieces[(k - LEAD) % STEPS])
        return carry

    lax.fori_loop(0, loops, visit, 0)
    for k in range(LEAD):
        add_up(tiles + loops * STEPS - LEAD + k, pieces[STEPS - LEAD + k])

    row_results = [(k, row_outs[k], 0) for k in range(ncols)]
    col_results = [(k, col_outs[k // 2], k % 2 * per) for k in range(nrows)]

    def close(step, carry):
        for results, block, sums, me in (
            (row_results, row_blk, row_sum, my_col),
            (col_results, col_blk, col_sum, my_row),
        ):
            for k, result, start in results:
                at = tile_at((me ^ k) * tiles + step)
                terms = sums[at, :]
                done = finish_tile(block[at, :] - origin, terms[:, :TILE], terms[:, TILE:], rows)
                result[pl.ds(pl.multiple_of(start + step * ROWS, ROWS), ROWS), :] = done
        return carry

    lax.fori_loop(0, tiles, close, 0, unroll=2)


def halve_kernel(*refs):
    keep, send = refs[-2:]
    half = keep.shape[0]
    total = refs[0][...]
    for ref in refs[1:-2]:
        total = total + ref[...]
    keep[...] = total[:half, :]
    send[...] = total[half:, :]


def total_kernel(*refs):
    vel_ref, str_ref = refs[-2:]
    tiles = vel_ref.shape[1] // TILE
    for tile in range(tiles):
        at = slice(tile * ROWS, (tile + 1) * ROWS)
        total = refs[0][at, :]
        for ref in refs[1:-2]:
            total = total + ref[at, :]
        vel_ref[:, tile * TILE : (tile + 1) * TILE] = total[0:3, :]
        str_ref[:, tile * TILE : (tile + 1) * TILE] = total[3:6, :]


def shards(positions, strengths, cores, order, tile_counts, pair_slots, pair_count):
    tiles = tile_counts.shape[0]
    per_dev = tiles * TILE
    nrows = lax.axis_size("row")
    ncols = lax.axis_size("col")
    halves = nrows // 2
    assert nrows == 2 * halves and nrows & (nrows - 1) == 0 and ncols & (ncols - 1) == 0
    row_tiles, col_tiles = ncols * tiles, nrows * tiles
    smem = pl.BlockSpec(memory_space=pltpu.SMEM)
    vmem = pl.BlockSpec(memory_space=pltpu.VMEM)
    hbm = pl.BlockSpec(memory_space=pltpu.HBM)
    params = pltpu.CompilerParams(vmem_limit_bytes=VMEM_BYTES)

    def blocks(count):
        return jax.ShapeDtypeStruct((count * tiles * ROWS, TILE), jnp.float32)

    def in_hbm(value):
        return pltpu.with_memory_space_constraint(value, pltpu.HBM)

    inputs = (tile_counts, positions, strengths, cores.reshape(1, per_dev), order.reshape(1, per_dev), pair_slots)
    packed, slots = pl.pallas_call(
        pack_kernel,
        out_shape=[blocks(1), jax.ShapeDtypeStruct(pair_slots.shape, jnp.int32)],
        in_specs=[hbm] * len(inputs),
        out_specs=[vmem, smem],
        scratch_shapes=[
            pltpu.VMEM((ROWS, per_dev), jnp.float32),
            pltpu.VMEM((1, per_dev), jnp.int32),
            pltpu.SMEM(tile_counts.shape, jnp.int32),
            pltpu.SemaphoreType.DMA((len(inputs),)),
        ],
        compiler_params=params,
        name="pack",
    )(*map(in_hbm, inputs))

    def swap(value, axis, size, k):
        return lax.ppermute(value, axis, [(d, d ^ k) for d in range(size)])

    phases = [pltpu.VMEM((TILE, 4 * TILE), jnp.float32)] * STEPS + [pltpu.VMEM((TILE, 6 * TILE), jnp.bfloat16)] * STEPS
    own = pl.pallas_call(
        own_kernel,
        out_shape=[
            jax.ShapeDtypeStruct((per_dev, TERMS), jnp.bfloat16),
            jax.ShapeDtypeStruct((tiles * TERMS, 4 * TILE), jnp.bfloat16),
            jax.ShapeDtypeStruct((tiles * FEAT, TILE), jnp.bfloat16),
            jax.ShapeDtypeStruct((tiles * ROWS, 2 * TILE), jnp.float32),
            jax.ShapeDtypeStruct((ROWS, TILE), jnp.float32),
        ],
        in_specs=[vmem],
        out_specs=[vmem] * 5,
        scratch_shapes=phases,
        compiler_params=params,
        cost_estimate=pl.CostEstimate(flops=tiles * 300 * TILE * TILE, bytes_accessed=2**21, transcendentals=0),
        name="own",
    )(packed)

    far = [swap(packed, "row", nrows, 2 * m) for m in range(1, halves)]
    from_row = [swap(packed, "col", ncols, k) for k in range(1, ncols)]
    joined = pl.pallas_call(
        join_kernel,
        out_shape=blocks(halves),
        in_specs=[vmem] * halves,
        out_specs=vmem,
        compiler_params=params,
        name="join",
    )(packed, *far)
    near = swap(joined, "row", nrows, 1)

    where = jnp.stack([lax.axis_index("row"), lax.axis_index("col"), pair_count[0]]).astype(jnp.int32)
    sums = pl.pallas_call(
        functools.partial(pair_kernel, nrows, ncols, tiles),
        out_shape=[blocks(1)] * ncols + [blocks(2)] * halves,
        in_specs=[smem] * 2 + [vmem] * (5 + ncols + halves),
        out_specs=[vmem] * (ncols + halves),
        scratch_shapes=[
            pltpu.VMEM((row_tiles * ROWS, TILE), jnp.float32),
            pltpu.VMEM((col_tiles * ROWS, TILE), jnp.float32),
            pltpu.VMEM((row_tiles * TILE, TERMS), jnp.bfloat16),
            pltpu.VMEM((col_tiles * TERMS, 4 * TILE), jnp.bfloat16),
            pltpu.VMEM((row_tiles * FEAT, TILE), jnp.bfloat16),
            pltpu.VMEM((col_tiles * FEAT, TILE), jnp.bfloat16),
            pltpu.VMEM((row_tiles * ROWS, 2 * TILE), jnp.float32),
            pltpu.VMEM((col_tiles * ROWS, 2 * TILE), jnp.float32),
            *phases,
        ],
        compiler_params=params,
        name="pairs",
    )(where, slots, packed, *own, *from_row, *far, near)

    far_back = [swap(sums[ncols + m], "row", nrows, 2 * m) for m in range(1, halves)]
    row_back = [swap(sums[k], "col", ncols, k) for k in range(1, ncols)]
    keep, send = pl.pallas_call(
        halve_kernel,
        out_shape=[blocks(1)] * 2,
        in_specs=[vmem] * halves,
        out_specs=[vmem] * 2,
        compiler_params=params,
        name="halve",
    )(sums[ncols], *far_back)
    parts = [sums[0], keep, *row_back, swap(send, "row", nrows, 1)]
    velocity, stretching = pl.pallas_call(
        total_kernel,
        out_shape=[jax.ShapeDtypeStruct((3, per_dev), jnp.float32)] * 2,
        in_specs=[vmem] * len(parts),
        out_specs=[vmem, vmem],
        compiler_params=params,
        name="totals",
    )(*parts)
    return velocity, stretching


def solution(mesh):
    whole = ("groups", "row", "col")
    in_specs = (P(None, whole), P(None, whole), P(whole), P(whole), P(whole), P(None, whole), P(whole))
    out_specs = (P(None, whole), P(None, whole))
    return jax.shard_map(shards, mesh=mesh, in_specs=in_specs, out_specs=out_specs, check_vma=False)
```

```python
import functools
import math

import jax
import jax.numpy as jnp
from jax import lax
from jax.experimental import pallas as pl
from jax.experimental.pallas import tpu as pltpu
from jax.sharding import PartitionSpec as P

TILE = 128
ROWS = 8
STEPS = 4
LEAD = 2
FEAT = 32
TERMS = 64
VMEM_BYTES = 48 * 1024 * 1024

biot_factor = -1.0 / (4.0 * math.pi)


def row_ids(count=ROWS):
    return lax.broadcasted_iota(jnp.int32, (count, TILE), 0)


def roll_rows(value, shift):
    return pltpu.roll(value, shift % ROWS, 0)


def pack_kernel(
    counts_hbm, pos_hbm, str_hbm, core_hbm, order_hbm, slots_hbm,
    out_ref, slots_ref, stored, order_ref, counts_ref, arrived,
):
    tiles = order_ref.shape[1] // TILE
    pairs = (
        (pos_hbm, stored.at[0:3, :]),
        (str_hbm, stored.at[3:6, :]),
        (core_hbm, stored.at[6:7, :]),
        (order_hbm, order_ref),
        (counts_hbm, counts_ref),
        (slots_hbm, slots_ref),
    )
    copies = [pltpu.make_async_copy(src, dst, arrived.at[k]) for k, (src, dst) in enumerate(pairs)]
    for copy in copies:
        copy.start()
    stored[7:8, :] = jnp.zeros((1, stored.shape[1]), jnp.float32)
    for copy in copies:
        copy.wait()
    lane = lax.broadcasted_iota(jnp.int32, (ROWS, TILE), 1)
    rows = row_ids()
    is_strength = (rows >= 3) & (rows < 6)
    for tile in range(tiles):
        where_from = jnp.broadcast_to(order_ref[:, tile * TILE : (tile + 1) * TILE], (ROWS, TILE))
        inside = where_from & (TILE - 1)
        block = where_from >> 7
        value = jnp.zeros((ROWS, TILE), jnp.float32)
        for source in range(tiles):
            part = jnp.take_along_axis(stored[:, source * TILE : (source + 1) * TILE], inside, axis=1)
            value = jnp.where(block == source, part, value)
        live = lane < counts_ref[tile]
        value = jnp.where(is_strength & ~live, 0.0, value)
        value = jnp.where(rows == 7, live.astype(jnp.float32), value)
        out_ref[tile * ROWS : (tile + 1) * ROWS, :] = value


def split_three(value):
    first = value.astype(jnp.bfloat16).astype(jnp.float32)
    rest = value - first
    second = rest.astype(jnp.bfloat16).astype(jnp.float32)
    return first, second, rest - second


def split_two(value):
    high = value.astype(jnp.bfloat16)
    return high, (value - high.astype(jnp.float32)).astype(jnp.bfloat16)


def features(tile, rows):
    down1, down2 = roll_rows(tile, 1), roll_rows(tile, 2)
    pos1 = jnp.where(rows == 5, roll_rows(tile, 5), down2)
    pos2 = jnp.where(rows == 3, down1, roll_rows(tile, 4))
    str1 = jnp.where(rows == 5, down2, roll_rows(tile, 7))
    str2 = jnp.where(rows == 3, roll_rows(tile, 6), down1)
    cross = pos1 * str2 - pos2 * str1
    value = jnp.where(rows < 3, roll_rows(tile, 5), jnp.where(rows < 6, cross, 0.0))
    return jnp.concatenate([*split_three(value), jnp.zeros_like(value)], axis=0)


def add_pieces(terms):
    return terms[0:ROWS, :] + (terms[ROWS : 2 * ROWS, :] + terms[2 * ROWS : 3 * ROWS, :])


def tile_scalars(tile, rows):
    position = jnp.where(rows < 3, tile, 0.0)
    strength = jnp.where(rows < 3, roll_rows(tile, 5), 0.0)
    half = 0.5 * tile[6:7, :] * tile[6:7, :]
    coarse = position.astype(jnp.bfloat16).astype(jnp.float32)
    norm = jnp.sum(coarse * coarse, axis=0, keepdims=True)
    rest = jnp.sum((position - coarse) * (position + coarse), axis=0, keepdims=True) + half
    along = jnp.sum(position * strength, axis=0, keepdims=True)
    return position, strength, half, norm, rest, along


def target_side(tile, rows):
    _, _, half, norm, rest, along = tile_scalars(tile, rows)
    shared = jnp.where(rows < 6, tile, 1.0)
    alone = jnp.where(rows == 0, norm, jnp.where(rows == 1, rest, jnp.where(rows == 2, along, 0.0)))
    alone = jnp.where(rows == 3, half, alone)
    first, second, third = split_three(shared)
    alone1, alone2, alone3 = split_three(alone)
    both = jnp.where(rows < 4, alone1, roll_rows(alone2, 4))
    stacked = jnp.concatenate([first, both, first, first, second, second, third, alone3], axis=0)
    return stacked.astype(jnp.bfloat16).T


def source_side(tile, rows):
    position, strength, half, norm, rest, along = tile_scalars(tile, rows)
    zero = jnp.zeros_like(position)
    one = jnp.ones_like(position)
    dist = jnp.where(rows == 6, norm, jnp.where(rows == 7, rest, -2.0 * position))
    front = -roll_rows(position, 3)
    back = jnp.where(rows == 6, along, -strength)
    core = jnp.where(rows == 6, half, zero)
    pick = rows & 3
    picks = (jnp.where(pick < 2, one, zero), jnp.where(pick == 2, one, zero), zero, jnp.where(pick == 3, one, zero))
    blocks = []
    for value, picked in zip((dist, front, back, core), picks):
        first, second, third = split_three(value)
        parts = [first, picked, second, third, first, second, first, picked]
        blocks.append(jnp.concatenate(parts, axis=0).astype(jnp.bfloat16))
    return jnp.concatenate(blocks, axis=1)


def cross(left, right):
    return [left[1] * right[2] - left[2] * right[1], left[2] * right[0] - left[0] * right[2], left[0] * right[1] - left[1] * right[0]]


def finish_block(tile_row, smooth_row, grad_row, origin):
    position = [tile_row(k) - origin[k : k + 1, :] for k in range(3)]
    strength = [tile_row(3 + k) for k in range(3)]
    scale = biot_factor * tile_row(7)
    smooth = [smooth_row(k) for k in range(6)]
    grad = [grad_row(k) for k in range(6)]
    velocity = [turn - part for turn, part in zip(cross(position, smooth[:3]), smooth[3:])]
    lever = [turn - part for turn, part in zip(cross(position, grad[:3]), grad[3:])]
    stretch = [turn - 3.0 * part for turn, part in zip(cross(strength, smooth[:3]), lever)]
    return [scale * value for value in velocity + stretch]


def evaluate(products, pieces):
    for start in range(0, TILE, 16):
        at = slice(start, start + 16)
        dist, front, back, core = (products[at, k * TILE : (k + 1) * TILE] for k in range(4))
        inv = lax.rsqrt(dist)
        inv2 = inv * inv
        inv3 = inv2 * inv
        tail = core * (inv3 * inv2)
        smooth = inv3 + 1.5 * tail
        grad = inv2 * (smooth + tail)
        for k, value in enumerate((smooth, grad * front, grad * back)):
            high, low = split_two(value)
            pieces[at, 2 * k * TILE : (2 * k + 1) * TILE] = high
            pieces[at, (2 * k + 1) * TILE : (2 * k + 2) * TILE] = low


def tile_at(tile):
    return pl.ds(pl.multiple_of(tile * ROWS, ROWS), ROWS)


def term_at(tile):
    return pl.ds(pl.multiple_of(tile * TERMS, TERMS), TERMS)


def wide_at(tile):
    return pl.ds(pl.multiple_of(tile * TILE, TILE), TILE)


def feat_at(tile):
    return pl.ds(pl.multiple_of(tile * FEAT, FEAT), FEAT)


def target_terms(feat, values):
    smooth, front = values[:, : 2 * TILE], values[:, 2 * TILE : 4 * TILE]
    terms = lax.dot_general(
        jnp.concatenate([feat, feat], axis=1),
        jnp.concatenate([smooth, front], axis=0),
        (((1,), (1,)), ((), ())),
        preferred_element_type=jnp.float32,
    )
    return add_pieces(terms)


def source_terms(feat, values):
    high = jnp.concatenate([values[:, :TILE], values[:, 4 * TILE : 5 * TILE]], axis=1)
    low = jnp.concatenate([values[:, TILE : 2 * TILE], values[:, 5 * TILE :]], axis=1)
    both = jnp.concatenate([high, low], axis=0)
    terms = jnp.dot(jnp.concatenate([feat, feat], axis=1), both, preferred_element_type=jnp.float32)
    return add_pieces(terms)


def own_kernel(block, left, right, feat, sums, origin_ref, *scratch):
    products, pieces = scratch[:STEPS], scratch[STEPS:]
    tiles = block.shape[0] // ROWS
    rows = row_ids()
    total = block[0:ROWS, :]
    for tile in range(1, tiles):
        total = total + block[tile * ROWS : (tile + 1) * ROWS, :]
    origin = jnp.sum(total, axis=1, keepdims=True) * (1.0 / (tiles * TILE))
    origin = jnp.where(rows < 3, jnp.broadcast_to(origin, (ROWS, TILE)), 0.0)
    origin_ref[...] = origin
    for tile in range(tiles):
        here = block[tile * ROWS : (tile + 1) * ROWS, :] - origin
        wide = slice(tile * TILE, (tile + 1) * TILE)
        left[wide, :] = target_side(here, rows)
        right[tile * TERMS : (tile + 1) * TERMS, :] = source_side(here, rows)
        feat[tile * FEAT : (tile + 1) * FEAT, :] = features(here, rows).astype(jnp.bfloat16)
    for step in range(tiles + 2 * LEAD):
        if step < tiles:
            target, source = left[step * TILE : (step + 1) * TILE, :], right[step * TERMS : (step + 1) * TERMS, :]
            products[step % STEPS][...] = jnp.dot(target, source, preferred_element_type=jnp.float32)
        if LEAD <= step < tiles + LEAD:
            evaluate(products[(step - LEAD) % STEPS], pieces[(step - LEAD) % STEPS])
        if step >= 2 * LEAD:
            tile = step - 2 * LEAD
            terms = target_terms(feat[tile * FEAT : (tile + 1) * FEAT, :], pieces[tile % STEPS])
            sums[tile * ROWS : (tile + 1) * ROWS, :] = terms


def join_kernel(*refs):
    out, start = refs[-1], 0
    for ref in refs[:-1]:
        out[start : start + ref.shape[0], :] = ref[...]
        start += ref.shape[0]


def pair_kernel(nrows, ncols, tiles, where_ref, slots_ref, *refs):
    own_block, own_left, own_right, own_feat, own_sums, origin_ref = refs[:6]
    refs = refs[6:]
    halves = nrows // 2
    row_ins, far_ins, near_in, refs = refs[: ncols - 1], refs[ncols - 1 : ncols + halves - 2], refs[ncols + halves - 2], refs[ncols + halves - 1 :]
    row_outs, col_outs, scratch = refs[:ncols], refs[ncols : ncols + halves], refs[ncols + halves :]
    row_blk, col_blk, left, right, row_feat, col_feat = scratch[:6]
    row_sum, col_sum = scratch[6:8], scratch[8:10]
    products, pieces = scratch[10 : 10 + STEPS], scratch[10 + STEPS :]
    per = tiles * ROWS
    rows = row_ids()
    my_row, my_col = where_ref[0], where_ref[1]
    count = where_ref[2]
    row_sources = [(k, row_ins[k - 1], 0) for k in range(1, ncols)]
    col_sources = [(2 * m, far_ins[m - 1], 0) for m in range(1, halves)]
    col_sources += [(2 * m + 1, near_in, m * per) for m in range(halves)]
    origin = origin_ref[...]

    for ref in (*row_sum, *col_sum):
        ref[...] = jnp.zeros_like(ref)
    for k in range(STEPS - LEAD, STEPS):
        pieces[k][...] = jnp.zeros_like(pieces[k])
    for block, feat, me in ((row_blk, row_feat, my_col), (col_blk, col_feat, my_row)):
        block[pl.ds(pl.multiple_of(me * per, per), per), :] = own_block[...]
        feat[pl.ds(pl.multiple_of(me * tiles * FEAT, tiles * FEAT), tiles * FEAT), :] = own_feat[...]
    for k, ref in enumerate(row_sum):
        ref[pl.ds(pl.multiple_of(my_col * per, per), per), :] = own_sums[:, k * TILE : (k + 1) * TILE]
    left[pl.ds(pl.multiple_of(my_col * tiles * TILE, tiles * TILE), tiles * TILE), :] = own_left[...]
    right[pl.ds(pl.multiple_of(my_row * tiles * TERMS, tiles * TERMS), tiles * TERMS), :] = own_right[...]

    def prepare_row(tile, here):
        left[wide_at(tile), :] = target_side(here, rows)
        row_feat[feat_at(tile), :] = features(here, rows).astype(jnp.bfloat16)

    def prepare_col(tile, here):
        right[term_at(tile), :] = source_side(here, rows)
        col_feat[feat_at(tile), :] = features(here, rows).astype(jnp.bfloat16)

    def prepare(step, carry):
        for sources, block, me, operands in (
            (row_sources, row_blk, my_col, prepare_row),
            (col_sources, col_blk, my_row, prepare_col),
        ):
            for k, source, start in sources:
                tile = (me ^ k) * tiles + step
                value = source[pl.ds(pl.multiple_of(start + step * ROWS, ROWS), ROWS), :]
                block[tile_at(tile), :] = value
                operands(tile, value - origin)
        return carry

    lax.fori_loop(0, tiles, prepare, 0, unroll=2)

    last = slots_ref.shape[1] - 1

    def multiply(slot, out):
        slot = jnp.minimum(slot, last)
        tgt, src = slots_ref[0, slot], slots_ref[1, slot]
        out[...] = jnp.dot(left[wide_at(tgt), :], right[term_at(src), :], preferred_element_type=jnp.float32)

    def add_up(slot, values):
        kept = jnp.clip(slot, 0, last)
        tgt, src = slots_ref[0, kept], slots_ref[1, kept]
        own = (tgt // tiles == my_col) & (src // tiles == my_row) & (tgt % tiles == src % tiles)
        alive = jnp.where((slot >= tiles) & (slot < count), 1.0, 0.0)
        react = jnp.where(own, 0.0, alive)
        to_target = alive * target_terms(col_feat[feat_at(src), :], values)
        to_source = react * source_terms(row_feat[feat_at(tgt), :], values)
        for k in range(2):
            row_sum[k][tile_at(tgt), :] += to_target[:, k * TILE : (k + 1) * TILE]
            col_sum[k][tile_at(src), :] += to_source[:, k * TILE : (k + 1) * TILE]

    for k in range(LEAD):
        multiply(tiles + k, products[k])
    loops = (count - tiles + STEPS - 1) // STEPS

    def visit(step, carry):
        for k in range(STEPS):
            slot = tiles + step * STEPS + k
            multiply(slot + LEAD, products[(k + LEAD) % STEPS])
            evaluate(products[k], pieces[k])
            add_up(slot - LEAD, pieces[(k - LEAD) % STEPS])
        return carry

    lax.fori_loop(0, loops, visit, 0)
    for k in range(LEAD):
        add_up(tiles + loops * STEPS - LEAD + k, pieces[STEPS - LEAD + k])

    row_results = [(k, row_outs[k], 0) for k in range(ncols)]
    col_results = [(k, col_outs[k // 2], k % 2 * per) for k in range(nrows)]

    for results, block, sums, me in (
        (row_results, row_blk, row_sum, my_col),
        (col_results, col_blk, col_sum, my_row),
    ):
        for k, result, start in results:
            base = pl.multiple_of((me ^ k) * per, per)

            def rows_of(ref, base=base):
                return lambda row: ref[pl.ds(base + row, tiles, stride=ROWS), :]

            done = finish_block(rows_of(block), *map(rows_of, sums), origin)
            for row, value in enumerate(done):
                result[pl.ds(start + row, tiles, stride=ROWS), :] = value


def halve_kernel(*refs):
    keep, send = refs[-2:]
    half = keep.shape[0]
    total = refs[0][...]
    for ref in refs[1:-2]:
        total = total + ref[...]
    keep[...] = total[:half, :]
    send[...] = total[half:, :]


def total_kernel(*refs):
    vel_ref, str_ref = refs[-2:]
    tiles = vel_ref.shape[1] // TILE
    for tile in range(tiles):
        at = slice(tile * ROWS, (tile + 1) * ROWS)
        total = refs[0][at, :]
        for ref in refs[1:-2]:
            total = total + ref[at, :]
        vel_ref[:, tile * TILE : (tile + 1) * TILE] = total[0:3, :]
        str_ref[:, tile * TILE : (tile + 1) * TILE] = total[3:6, :]


def shards(positions, strengths, cores, order, tile_counts, pair_slots, pair_count):
    tiles = tile_counts.shape[0]
    per_dev = tiles * TILE
    nrows = lax.axis_size("row")
    ncols = lax.axis_size("col")
    halves = nrows // 2
    assert nrows == 2 * halves and nrows & (nrows - 1) == 0 and ncols & (ncols - 1) == 0
    row_tiles, col_tiles = ncols * tiles, nrows * tiles
    smem = pl.BlockSpec(memory_space=pltpu.SMEM)
    vmem = pl.BlockSpec(memory_space=pltpu.VMEM)
    hbm = pl.BlockSpec(memory_space=pltpu.HBM)
    params = pltpu.CompilerParams(vmem_limit_bytes=VMEM_BYTES)

    def blocks(count):
        return jax.ShapeDtypeStruct((count * tiles * ROWS, TILE), jnp.float32)

    def in_hbm(value):
        return pltpu.with_memory_space_constraint(value, pltpu.HBM)

    inputs = (tile_counts, positions, strengths, cores.reshape(1, per_dev), order.reshape(1, per_dev), pair_slots)
    packed, slots = pl.pallas_call(
        pack_kernel,
        out_shape=[blocks(1), jax.ShapeDtypeStruct(pair_slots.shape, jnp.int32)],
        in_specs=[hbm] * len(inputs),
        out_specs=[vmem, smem],
        scratch_shapes=[
            pltpu.VMEM((ROWS, per_dev), jnp.float32),
            pltpu.VMEM((1, per_dev), jnp.int32),
            pltpu.SMEM(tile_counts.shape, jnp.int32),
            pltpu.SemaphoreType.DMA((len(inputs),)),
        ],
        compiler_params=params,
        name="pack",
    )(*map(in_hbm, inputs))

    def swap(value, axis, size, k):
        return lax.ppermute(value, axis, [(d, d ^ k) for d in range(size)])

    phases = [pltpu.VMEM((TILE, 4 * TILE), jnp.float32)] * STEPS + [pltpu.VMEM((TILE, 6 * TILE), jnp.bfloat16)] * STEPS
    own = pl.pallas_call(
        own_kernel,
        out_shape=[
            jax.ShapeDtypeStruct((per_dev, TERMS), jnp.bfloat16),
            jax.ShapeDtypeStruct((tiles * TERMS, 4 * TILE), jnp.bfloat16),
            jax.ShapeDtypeStruct((tiles * FEAT, TILE), jnp.bfloat16),
            jax.ShapeDtypeStruct((tiles * ROWS, 2 * TILE), jnp.float32),
            jax.ShapeDtypeStruct((ROWS, TILE), jnp.float32),
        ],
        in_specs=[vmem],
        out_specs=[vmem] * 5,
        scratch_shapes=phases,
        compiler_params=params,
        cost_estimate=pl.CostEstimate(flops=tiles * 300 * TILE * TILE, bytes_accessed=2**21, transcendentals=0),
        name="own",
    )(packed)

    far = [swap(packed, "row", nrows, 2 * m) for m in range(1, halves)]
    from_row = [swap(packed, "col", ncols, k) for k in range(1, ncols)]
    joined = pl.pallas_call(
        join_kernel,
        out_shape=blocks(halves),
        in_specs=[vmem] * halves,
        out_specs=vmem,
        compiler_params=params,
        name="join",
    )(packed, *far)
    near = swap(joined, "row", nrows, 1)

    where = jnp.stack([lax.axis_index("row"), lax.axis_index("col"), pair_count[0]]).astype(jnp.int32)
    sums = pl.pallas_call(
        functools.partial(pair_kernel, nrows, ncols, tiles),
        out_shape=[blocks(1)] * ncols + [blocks(2)] * halves,
        in_specs=[smem] * 2 + [vmem] * (5 + ncols + halves),
        out_specs=[vmem] * (ncols + halves),
        scratch_shapes=[
            pltpu.VMEM((row_tiles * ROWS, TILE), jnp.float32),
            pltpu.VMEM((col_tiles * ROWS, TILE), jnp.float32),
            pltpu.VMEM((row_tiles * TILE, TERMS), jnp.bfloat16),
            pltpu.VMEM((col_tiles * TERMS, 4 * TILE), jnp.bfloat16),
            pltpu.VMEM((row_tiles * FEAT, TILE), jnp.bfloat16),
            pltpu.VMEM((col_tiles * FEAT, TILE), jnp.bfloat16),
            *[pltpu.VMEM((row_tiles * ROWS, TILE), jnp.float32)] * 2,
            *[pltpu.VMEM((col_tiles * ROWS, TILE), jnp.float32)] * 2,
            *phases,
        ],
        compiler_params=params,
        name="pairs",
    )(where, slots, packed, *own, *from_row, *far, near)

    far_back = [swap(sums[ncols + m], "row", nrows, 2 * m) for m in range(1, halves)]
    row_back = [swap(sums[k], "col", ncols, k) for k in range(1, ncols)]
    keep, send = pl.pallas_call(
        halve_kernel,
        out_shape=[blocks(1)] * 2,
        in_specs=[vmem] * halves,
        out_specs=[vmem] * 2,
        compiler_params=params,
        name="halve",
    )(sums[ncols], *far_back)
    parts = [sums[0], keep, *row_back, swap(send, "row", nrows, 1)]
    velocity, stretching = pl.pallas_call(
        total_kernel,
        out_shape=[jax.ShapeDtypeStruct((3, per_dev), jnp.float32)] * 2,
        in_specs=[vmem] * len(parts),
        out_specs=[vmem, vmem],
        compiler_params=params,
        name="totals",
    )(*parts)
    return velocity, stretching


def solution(mesh):
    whole = ("groups", "row", "col")
    in_specs = (P(None, whole), P(None, whole), P(whole), P(whole), P(whole), P(None, whole), P(whole))
    out_specs = (P(None, whole), P(None, whole))
    return jax.shard_map(shards, mesh=mesh, in_specs=in_specs, out_specs=out_specs, check_vma=False)
```

```python
import functools
import math

import jax
import jax.numpy as jnp
from jax import lax
from jax.experimental import pallas as pl
from jax.experimental.pallas import tpu as pltpu
from jax.sharding import PartitionSpec as P

TILE = 128
ROWS = 8
STEPS = 4
LEAD = 2
FEAT = 32
TERMS = 64
VMEM_BYTES = 48 * 1024 * 1024

biot_factor = -1.0 / (4.0 * math.pi)


def row_ids(count=ROWS):
    return lax.broadcasted_iota(jnp.int32, (count, TILE), 0)


def roll_rows(value, shift):
    return pltpu.roll(value, shift % ROWS, 0)


def pack_kernel(
    counts_hbm, pos_hbm, str_hbm, core_hbm, order_hbm, slots_hbm,
    out_ref, slots_ref, stored, order_ref, counts_ref, arrived,
):
    tiles = order_ref.shape[1] // TILE
    pairs = (
        (pos_hbm, stored.at[0:3, :]),
        (str_hbm, stored.at[3:6, :]),
        (core_hbm, stored.at[6:7, :]),
        (order_hbm, order_ref),
        (counts_hbm, counts_ref),
        (slots_hbm, slots_ref),
    )
    copies = [pltpu.make_async_copy(src, dst, arrived.at[k]) for k, (src, dst) in enumerate(pairs)]
    for copy in copies:
        copy.start()
    stored[7:8, :] = jnp.zeros((1, stored.shape[1]), jnp.float32)
    for copy in copies:
        copy.wait()
    lane = lax.broadcasted_iota(jnp.int32, (ROWS, TILE), 1)
    rows = row_ids()
    is_strength = (rows >= 3) & (rows < 6)
    for tile in range(tiles):
        where_from = jnp.broadcast_to(order_ref[:, tile * TILE : (tile + 1) * TILE], (ROWS, TILE))
        inside = where_from & (TILE - 1)
        block = where_from >> 7
        value = jnp.zeros((ROWS, TILE), jnp.float32)
        for source in range(tiles):
            part = jnp.take_along_axis(stored[:, source * TILE : (source + 1) * TILE], inside, axis=1)
            value = jnp.where(block == source, part, value)
        live = lane < counts_ref[tile]
        value = jnp.where(is_strength & ~live, 0.0, value)
        value = jnp.where(rows == 7, live.astype(jnp.float32), value)
        out_ref[tile * ROWS : (tile + 1) * ROWS, :] = value


def split_three(value):
    first = value.astype(jnp.bfloat16).astype(jnp.float32)
    rest = value - first
    second = rest.astype(jnp.bfloat16).astype(jnp.float32)
    return first, second, rest - second


def split_two(value):
    high = value.astype(jnp.bfloat16)
    return high, (value - high.astype(jnp.float32)).astype(jnp.bfloat16)


def features(tile, rows):
    down1, down2 = roll_rows(tile, 1), roll_rows(tile, 2)
    pos1 = jnp.where(rows == 5, roll_rows(tile, 5), down2)
    pos2 = jnp.where(rows == 3, down1, roll_rows(tile, 4))
    str1 = jnp.where(rows == 5, down2, roll_rows(tile, 7))
    str2 = jnp.where(rows == 3, roll_rows(tile, 6), down1)
    cross = pos1 * str2 - pos2 * str1
    value = jnp.where(rows < 3, roll_rows(tile, 5), jnp.where(rows < 6, cross, 0.0))
    return jnp.concatenate([*split_three(value), jnp.zeros_like(value)], axis=0)


def add_pieces(terms):
    return terms[0:ROWS, :] + (terms[ROWS : 2 * ROWS, :] + terms[2 * ROWS : 3 * ROWS, :])


def tile_scalars(tile, rows):
    position = jnp.where(rows < 3, tile, 0.0)
    strength = jnp.where(rows < 3, roll_rows(tile, 5), 0.0)
    half = 0.5 * tile[6:7, :] * tile[6:7, :]
    coarse = position.astype(jnp.bfloat16).astype(jnp.float32)
    norm = jnp.sum(coarse * coarse, axis=0, keepdims=True)
    rest = jnp.sum((position - coarse) * (position + coarse), axis=0, keepdims=True) + half
    along = jnp.sum(position * strength, axis=0, keepdims=True)
    return position, strength, half, norm, rest, along


def target_side(tile, rows):
    _, _, half, norm, rest, along = tile_scalars(tile, rows)
    shared = jnp.where(rows < 6, tile, 1.0)
    alone = jnp.where(rows == 0, norm, jnp.where(rows == 1, rest, jnp.where(rows == 2, along, 0.0)))
    alone = jnp.where(rows == 3, half, alone)
    first, second, third = split_three(shared)
    alone1, alone2, alone3 = split_three(alone)
    both = jnp.where(rows < 4, alone1, roll_rows(alone2, 4))
    stacked = jnp.concatenate([first, both, first, first, second, second, third, alone3], axis=0)
    return stacked.astype(jnp.bfloat16).T


def source_side(tile, rows):
    position, strength, half, norm, rest, along = tile_scalars(tile, rows)
    zero = jnp.zeros_like(position)
    one = jnp.ones_like(position)
    dist = jnp.where(rows == 6, norm, jnp.where(rows == 7, rest, -2.0 * position))
    front = -roll_rows(position, 3)
    back = jnp.where(rows == 6, along, -strength)
    core = jnp.where(rows == 6, half, zero)
    pick = rows & 3
    picks = (jnp.where(pick < 2, one, zero), jnp.where(pick == 2, one, zero), zero, jnp.where(pick == 3, one, zero))
    blocks = []
    for value, picked in zip((dist, front, back, core), picks):
        first, second, third = split_three(value)
        parts = [first, picked, second, third, first, second, first, picked]
        blocks.append(jnp.concatenate(parts, axis=0).astype(jnp.bfloat16))
    return jnp.concatenate(blocks, axis=1)


def cross(left, right):
    return [left[1] * right[2] - left[2] * right[1], left[2] * right[0] - left[0] * right[2], left[0] * right[1] - left[1] * right[0]]


def finish_block(tile_row, smooth_row, grad_row, origin):
    position = [tile_row(k) - origin[k : k + 1, :] for k in range(3)]
    strength = [tile_row(3 + k) for k in range(3)]
    scale = biot_factor * tile_row(7)
    smooth = [smooth_row(k) for k in range(6)]
    grad = [grad_row(k) for k in range(6)]
    velocity = [turn - part for turn, part in zip(cross(position, smooth[:3]), smooth[3:])]
    lever = [turn - part for turn, part in zip(cross(position, grad[:3]), grad[3:])]
    stretch = [turn - 3.0 * part for turn, part in zip(cross(strength, smooth[:3]), lever)]
    return [scale * value for value in velocity + stretch]


def evaluate(products, pieces):
    for start in range(0, TILE, 16):
        at = slice(start, start + 16)
        dist, front, back, core = (products[at, k * TILE : (k + 1) * TILE] for k in range(4))
        inv = lax.rsqrt(dist)
        inv2 = inv * inv
        inv3 = inv2 * inv
        tail = core * (inv3 * inv2)
        smooth = inv3 + 1.5 * tail
        grad = inv2 * (smooth + tail)
        for k, value in enumerate((smooth, grad * front, grad * back)):
            high, low = split_two(value)
            pieces[at, 2 * k * TILE : (2 * k + 1) * TILE] = high
            pieces[at, (2 * k + 1) * TILE : (2 * k + 2) * TILE] = low


def tile_at(tile):
    return pl.ds(pl.multiple_of(tile * ROWS, ROWS), ROWS)


def term_at(tile):
    return pl.ds(pl.multiple_of(tile * TERMS, TERMS), TERMS)


def wide_at(tile):
    return pl.ds(pl.multiple_of(tile * TILE, TILE), TILE)


def feat_at(tile):
    return pl.ds(pl.multiple_of(tile * FEAT, FEAT), FEAT)


def target_terms(feat, values):
    smooth, front = values[:, : 2 * TILE], values[:, 2 * TILE : 4 * TILE]
    terms = lax.dot_general(
        jnp.concatenate([feat, feat], axis=1),
        jnp.concatenate([smooth, front], axis=0),
        (((1,), (1,)), ((), ())),
        preferred_element_type=jnp.float32,
    )
    return add_pieces(terms)


def source_terms(feat, values):
    high = jnp.concatenate([values[:, :TILE], values[:, 4 * TILE : 5 * TILE]], axis=1)
    low = jnp.concatenate([values[:, TILE : 2 * TILE], values[:, 5 * TILE :]], axis=1)
    both = jnp.concatenate([high, low], axis=0)
    terms = jnp.dot(jnp.concatenate([feat, feat], axis=1), both, preferred_element_type=jnp.float32)
    return add_pieces(terms)


def own_kernel(block, left, right, feat, sums, origin_ref, *pieces):
    tiles = block.shape[0] // ROWS
    rows = row_ids()
    total = block[0:ROWS, :]
    for tile in range(1, tiles):
        total = total + block[tile * ROWS : (tile + 1) * ROWS, :]
    origin = jnp.sum(total, axis=1, keepdims=True) * (1.0 / (tiles * TILE))
    origin = jnp.where(rows < 3, jnp.broadcast_to(origin, (ROWS, TILE)), 0.0)
    origin_ref[...] = origin
    for tile in range(tiles):
        here = block[tile * ROWS : (tile + 1) * ROWS, :] - origin
        wide = slice(tile * TILE, (tile + 1) * TILE)
        left[wide, :] = target_side(here, rows)
        right[tile * TERMS : (tile + 1) * TERMS, :] = source_side(here, rows)
        feat[tile * FEAT : (tile + 1) * FEAT, :] = features(here, rows).astype(jnp.bfloat16)
    for step in range(tiles + LEAD):
        if step < tiles:
            target, source = left[step * TILE : (step + 1) * TILE, :], right[step * TERMS : (step + 1) * TERMS, :]
            evaluate(jnp.dot(target, source, preferred_element_type=jnp.float32), pieces[step % STEPS])
        if step >= LEAD:
            tile = step - LEAD
            terms = target_terms(feat[tile * FEAT : (tile + 1) * FEAT, :], pieces[tile % STEPS])
            sums[tile * ROWS : (tile + 1) * ROWS, :] = terms


def join_kernel(*refs):
    out, start = refs[-1], 0
    for ref in refs[:-1]:
        out[start : start + ref.shape[0], :] = ref[...]
        start += ref.shape[0]


def pair_kernel(nrows, ncols, tiles, where_ref, slots_ref, *refs):
    own_block, own_left, own_right, own_feat, own_sums, origin_ref = refs[:6]
    refs = refs[6:]
    halves = nrows // 2
    row_ins, far_ins, near_in, refs = refs[: ncols - 1], refs[ncols - 1 : ncols + halves - 2], refs[ncols + halves - 2], refs[ncols + halves - 1 :]
    row_outs, col_outs, scratch = refs[:ncols], refs[ncols : ncols + halves], refs[ncols + halves :]
    row_blk, col_blk, left, right, row_feat, col_feat = scratch[:6]
    row_sum, col_sum = scratch[6:8], scratch[8:10]
    pieces = scratch[10:]
    per = tiles * ROWS
    rows = row_ids()
    my_row, my_col = where_ref[0], where_ref[1]
    count = where_ref[2]
    row_sources = [(k, row_ins[k - 1], 0) for k in range(1, ncols)]
    col_sources = [(2 * m, far_ins[m - 1], 0) for m in range(1, halves)]
    col_sources += [(2 * m + 1, near_in, m * per) for m in range(halves)]
    origin = origin_ref[...]

    for ref in (*row_sum, *col_sum):
        ref[...] = jnp.zeros_like(ref)
    for k in range(STEPS - LEAD, STEPS):
        pieces[k][...] = jnp.zeros_like(pieces[k])
    for block, feat, me in ((row_blk, row_feat, my_col), (col_blk, col_feat, my_row)):
        block[pl.ds(pl.multiple_of(me * per, per), per), :] = own_block[...]
        feat[pl.ds(pl.multiple_of(me * tiles * FEAT, tiles * FEAT), tiles * FEAT), :] = own_feat[...]
    for k, ref in enumerate(row_sum):
        ref[pl.ds(pl.multiple_of(my_col * per, per), per), :] = own_sums[:, k * TILE : (k + 1) * TILE]
    left[pl.ds(pl.multiple_of(my_col * tiles * TILE, tiles * TILE), tiles * TILE), :] = own_left[...]
    right[pl.ds(pl.multiple_of(my_row * tiles * TERMS, tiles * TERMS), tiles * TERMS), :] = own_right[...]

    def prepare_row(tile, here):
        left[wide_at(tile), :] = target_side(here, rows)
        row_feat[feat_at(tile), :] = features(here, rows).astype(jnp.bfloat16)

    def prepare_col(tile, here):
        right[term_at(tile), :] = source_side(here, rows)
        col_feat[feat_at(tile), :] = features(here, rows).astype(jnp.bfloat16)

    def prepare(step, carry):
        for sources, block, me, operands in (
            (row_sources, row_blk, my_col, prepare_row),
            (col_sources, col_blk, my_row, prepare_col),
        ):
            for k, source, start in sources:
                tile = (me ^ k) * tiles + step
                value = source[pl.ds(pl.multiple_of(start + step * ROWS, ROWS), ROWS), :]
                block[tile_at(tile), :] = value
                operands(tile, value - origin)
        return carry

    lax.fori_loop(0, tiles, prepare, 0, unroll=2)

    last = slots_ref.shape[1] - 1

    def multiply(slot):
        slot = jnp.minimum(slot, last)
        tgt, src = slots_ref[0, slot], slots_ref[1, slot]
        return jnp.dot(left[wide_at(tgt), :], right[term_at(src), :], preferred_element_type=jnp.float32)

    def add_up(slot, values):
        kept = jnp.clip(slot, 0, last)
        tgt, src = slots_ref[0, kept], slots_ref[1, kept]
        own = (tgt // tiles == my_col) & (src // tiles == my_row) & (tgt % tiles == src % tiles)
        alive = jnp.where((slot >= tiles) & (slot < count), 1.0, 0.0)
        react = jnp.where(own, 0.0, alive)
        to_target = alive * target_terms(col_feat[feat_at(src), :], values)
        to_source = react * source_terms(row_feat[feat_at(tgt), :], values)
        for k in range(2):
            row_sum[k][tile_at(tgt), :] += to_target[:, k * TILE : (k + 1) * TILE]
            col_sum[k][tile_at(src), :] += to_source[:, k * TILE : (k + 1) * TILE]

    loops = (count - tiles + STEPS - 1) // STEPS

    def visit(step, carry):
        for k in range(STEPS):
            slot = tiles + step * STEPS + k
            evaluate(multiply(slot), pieces[k])
            add_up(slot - LEAD, pieces[(k - LEAD) % STEPS])
        return carry

    lax.fori_loop(0, loops, visit, 0)
    for k in range(LEAD):
        add_up(tiles + loops * STEPS - LEAD + k, pieces[STEPS - LEAD + k])

    row_results = [(k, row_outs[k], 0) for k in range(ncols)]
    col_results = [(k, col_outs[k // 2], k % 2 * per) for k in range(nrows)]

    for results, block, sums, me in (
        (row_results, row_blk, row_sum, my_col),
        (col_results, col_blk, col_sum, my_row),
    ):
        for k, result, start in results:
            base = pl.multiple_of((me ^ k) * per, per)

            def rows_of(ref, base=base):
                return lambda row: ref[pl.ds(base + row, tiles, stride=ROWS), :]

            done = finish_block(rows_of(block), *map(rows_of, sums), origin)
            for row, value in enumerate(done):
                result[pl.ds(start + row, tiles, stride=ROWS), :] = value


def halve_kernel(*refs):
    keep, send = refs[-2:]
    half = keep.shape[0]
    total = refs[0][...]
    for ref in refs[1:-2]:
        total = total + ref[...]
    keep[...] = total[:half, :]
    send[...] = total[half:, :]


def total_kernel(*refs):
    vel_ref, str_ref = refs[-2:]
    tiles = vel_ref.shape[1] // TILE
    for tile in range(tiles):
        at = slice(tile * ROWS, (tile + 1) * ROWS)
        total = refs[0][at, :]
        for ref in refs[1:-2]:
            total = total + ref[at, :]
        vel_ref[:, tile * TILE : (tile + 1) * TILE] = total[0:3, :]
        str_ref[:, tile * TILE : (tile + 1) * TILE] = total[3:6, :]


def shards(positions, strengths, cores, order, tile_counts, pair_slots, pair_count):
    tiles = tile_counts.shape[0]
    per_dev = tiles * TILE
    nrows = lax.axis_size("row")
    ncols = lax.axis_size("col")
    halves = nrows // 2
    assert nrows == 2 * halves and nrows & (nrows - 1) == 0 and ncols & (ncols - 1) == 0
    row_tiles, col_tiles = ncols * tiles, nrows * tiles
    smem = pl.BlockSpec(memory_space=pltpu.SMEM)
    vmem = pl.BlockSpec(memory_space=pltpu.VMEM)
    hbm = pl.BlockSpec(memory_space=pltpu.HBM)
    params = pltpu.CompilerParams(vmem_limit_bytes=VMEM_BYTES)

    def blocks(count):
        return jax.ShapeDtypeStruct((count * tiles * ROWS, TILE), jnp.float32)

    def in_hbm(value):
        return pltpu.with_memory_space_constraint(value, pltpu.HBM)

    inputs = (tile_counts, positions, strengths, cores.reshape(1, per_dev), order.reshape(1, per_dev), pair_slots)
    packed, slots = pl.pallas_call(
        pack_kernel,
        out_shape=[blocks(1), jax.ShapeDtypeStruct(pair_slots.shape, jnp.int32)],
        in_specs=[hbm] * len(inputs),
        out_specs=[vmem, smem],
        scratch_shapes=[
            pltpu.VMEM((ROWS, per_dev), jnp.float32),
            pltpu.VMEM((1, per_dev), jnp.int32),
            pltpu.SMEM(tile_counts.shape, jnp.int32),
            pltpu.SemaphoreType.DMA((len(inputs),)),
        ],
        compiler_params=params,
        name="pack",
    )(*map(in_hbm, inputs))

    def swap(value, axis, size, k):
        return lax.ppermute(value, axis, [(d, d ^ k) for d in range(size)])

    phases = [pltpu.VMEM((TILE, 6 * TILE), jnp.bfloat16)] * STEPS
    own = pl.pallas_call(
        own_kernel,
        out_shape=[
            jax.ShapeDtypeStruct((per_dev, TERMS), jnp.bfloat16),
            jax.ShapeDtypeStruct((tiles * TERMS, 4 * TILE), jnp.bfloat16),
            jax.ShapeDtypeStruct((tiles * FEAT, TILE), jnp.bfloat16),
            jax.ShapeDtypeStruct((tiles * ROWS, 2 * TILE), jnp.float32),
            jax.ShapeDtypeStruct((ROWS, TILE), jnp.float32),
        ],
        in_specs=[vmem],
        out_specs=[vmem] * 5,
        scratch_shapes=phases,
        compiler_params=params,
        cost_estimate=pl.CostEstimate(flops=tiles * 300 * TILE * TILE, bytes_accessed=2**21, transcendentals=0),
        name="own",
    )(packed)

    far = [swap(packed, "row", nrows, 2 * m) for m in range(1, halves)]
    from_row = [swap(packed, "col", ncols, k) for k in range(1, ncols)]
    joined = pl.pallas_call(
        join_kernel,
        out_shape=blocks(halves),
        in_specs=[vmem] * halves,
        out_specs=vmem,
        compiler_params=params,
        name="join",
    )(packed, *far)
    near = swap(joined, "row", nrows, 1)

    where = jnp.stack([lax.axis_index("row"), lax.axis_index("col"), pair_count[0]]).astype(jnp.int32)
    sums = pl.pallas_call(
        functools.partial(pair_kernel, nrows, ncols, tiles),
        out_shape=[blocks(1)] * ncols + [blocks(2)] * halves,
        in_specs=[smem] * 2 + [vmem] * (5 + ncols + halves),
        out_specs=[vmem] * (ncols + halves),
        scratch_shapes=[
            pltpu.VMEM((row_tiles * ROWS, TILE), jnp.float32),
            pltpu.VMEM((col_tiles * ROWS, TILE), jnp.float32),
            pltpu.VMEM((row_tiles * TILE, TERMS), jnp.bfloat16),
            pltpu.VMEM((col_tiles * TERMS, 4 * TILE), jnp.bfloat16),
            pltpu.VMEM((row_tiles * FEAT, TILE), jnp.bfloat16),
            pltpu.VMEM((col_tiles * FEAT, TILE), jnp.bfloat16),
            *[pltpu.VMEM((row_tiles * ROWS, TILE), jnp.float32)] * 2,
            *[pltpu.VMEM((col_tiles * ROWS, TILE), jnp.float32)] * 2,
            *phases,
        ],
        compiler_params=params,
        name="pairs",
    )(where, slots, packed, *own, *from_row, *far, near)

    far_back = [swap(sums[ncols + m], "row", nrows, 2 * m) for m in range(1, halves)]
    row_back = [swap(sums[k], "col", ncols, k) for k in range(1, ncols)]
    keep, send = pl.pallas_call(
        halve_kernel,
        out_shape=[blocks(1)] * 2,
        in_specs=[vmem] * halves,
        out_specs=[vmem] * 2,
        compiler_params=params,
        name="halve",
    )(sums[ncols], *far_back)
    parts = [sums[0], keep, *row_back, swap(send, "row", nrows, 1)]
    velocity, stretching = pl.pallas_call(
        total_kernel,
        out_shape=[jax.ShapeDtypeStruct((3, per_dev), jnp.float32)] * 2,
        in_specs=[vmem] * len(parts),
        out_specs=[vmem, vmem],
        compiler_params=params,
        name="totals",
    )(*parts)
    return velocity, stretching


def solution(mesh):
    whole = ("groups", "row", "col")
    in_specs = (P(None, whole), P(None, whole), P(whole), P(whole), P(whole), P(None, whole), P(whole))
    out_specs = (P(None, whole), P(None, whole))
    return jax.shard_map(shards, mesh=mesh, in_specs=in_specs, out_specs=out_specs, check_vma=False)
```

```python
import functools
import math

import jax
import jax.numpy as jnp
from jax import lax
from jax.experimental import pallas as pl
from jax.experimental.pallas import tpu as pltpu
from jax.sharding import PartitionSpec as P

TILE = 128
ROWS = 8
STEPS = 4
LEAD = 2
FEAT = 32
TERMS = 64
VMEM_BYTES = 48 * 1024 * 1024

biot_factor = -1.0 / (4.0 * math.pi)


def row_ids(count=ROWS):
    return lax.broadcasted_iota(jnp.int32, (count, TILE), 0)


def roll_rows(value, shift):
    return pltpu.roll(value, shift % ROWS, 0)


def pack_kernel(
    counts_hbm, pos_hbm, str_hbm, core_hbm, order_hbm, slots_hbm,
    out_ref, slots_ref, stored, order_ref, counts_ref, arrived,
):
    tiles = order_ref.shape[1] // TILE
    pairs = (
        (pos_hbm, stored.at[0:3, :]),
        (str_hbm, stored.at[3:6, :]),
        (core_hbm, stored.at[6:7, :]),
        (order_hbm, order_ref),
        (counts_hbm, counts_ref),
        (slots_hbm, slots_ref),
    )
    copies = [pltpu.make_async_copy(src, dst, arrived.at[k]) for k, (src, dst) in enumerate(pairs)]
    for copy in copies:
        copy.start()
    stored[7:8, :] = jnp.zeros((1, stored.shape[1]), jnp.float32)
    for copy in copies:
        copy.wait()
    lane = lax.broadcasted_iota(jnp.int32, (ROWS, TILE), 1)
    rows = row_ids()
    is_strength = (rows >= 3) & (rows < 6)
    for tile in range(tiles):
        where_from = jnp.broadcast_to(order_ref[:, tile * TILE : (tile + 1) * TILE], (ROWS, TILE))
        inside = where_from & (TILE - 1)
        block = where_from >> 7
        value = jnp.zeros((ROWS, TILE), jnp.float32)
        for source in range(tiles):
            part = jnp.take_along_axis(stored[:, source * TILE : (source + 1) * TILE], inside, axis=1)
            value = jnp.where(block == source, part, value)
        live = lane < counts_ref[tile]
        value = jnp.where(is_strength & ~live, 0.0, value)
        value = jnp.where(rows == 7, live.astype(jnp.float32), value)
        out_ref[tile * ROWS : (tile + 1) * ROWS, :] = value


def split_three(value):
    first = value.astype(jnp.bfloat16).astype(jnp.float32)
    rest = value - first
    second = rest.astype(jnp.bfloat16).astype(jnp.float32)
    return first, second, rest - second


def split_two(value):
    high = value.astype(jnp.bfloat16)
    return high, (value - high.astype(jnp.float32)).astype(jnp.bfloat16)


def add_pieces(terms):
    return terms[0:ROWS, :] + (terms[ROWS : 2 * ROWS, :] + terms[2 * ROWS : 3 * ROWS, :])


def cross(left, right):
    return [left[1] * right[2] - left[2] * right[1], left[2] * right[0] - left[0] * right[2], left[0] * right[1] - left[1] * right[0]]


def describe(tile_row, origin):
    position = [tile_row(k) - origin[k : k + 1, :] for k in range(3)]
    strength = [tile_row(3 + k) for k in range(3)]
    core = tile_row(6)
    half = 0.5 * core * core
    coarse = [value.astype(jnp.bfloat16).astype(jnp.float32) for value in position]
    norm = coarse[0] * coarse[0] + coarse[1] * coarse[1] + coarse[2] * coarse[2]
    rest = [(value - near) * (value + near) for value, near in zip(position, coarse)]
    rest = rest[0] + rest[1] + rest[2] + half
    along = position[0] * strength[0] + position[1] * strength[1] + position[2] * strength[2]
    return position, strength, half, norm, rest, along


def put_rows(ref, start, tiles, values):
    for row, value in values.items():
        ref[pl.ds(start + row, tiles, stride=ROWS), :] = value


def negative(values):
    return [-value for value in values]


def numbered(first, values):
    return dict(enumerate(values, first))


def stage_features(ref, start, tiles, position, strength):
    put_rows(ref, start, tiles, numbered(0, strength + cross(position, strength)))


def stage_target(refs, start, tiles, description):
    position, strength, half, norm, rest, along = description
    put_rows(refs[0], start, tiles, numbered(0, position + strength))
    put_rows(refs[1], start, tiles, numbered(0, [norm, rest, along, half]))


def stage_source(refs, start, tiles, description):
    position, strength, half, norm, rest, along = description
    put_rows(refs[0], start, tiles, numbered(0, [-2.0 * value for value in position]) | {6: norm, 7: rest})
    put_rows(refs[1], start, tiles, numbered(3, negative(position)))
    put_rows(refs[2], start, tiles, numbered(0, negative(strength)) | {6: along})
    put_rows(refs[3], start, tiles, {6: half})


def features(tile, rows):
    value = jnp.where(rows < 6, tile, 0.0)
    return jnp.concatenate([*split_three(value), jnp.zeros_like(value)], axis=0).astype(jnp.bfloat16)


def target_side(shared, alone, rows):
    first, second, third = split_three(jnp.where(rows < 6, shared, 1.0))
    alone1, alone2, alone3 = split_three(jnp.where(rows < 4, alone, 0.0))
    both = jnp.where(rows < 4, alone1, roll_rows(alone2, 4))
    stacked = jnp.concatenate([first, both, first, first, second, second, third, alone3], axis=0)
    return stacked.astype(jnp.bfloat16).T


def source_side(dist, front, back, core, rows):
    zero = jnp.zeros_like(dist)
    one = jnp.ones_like(dist)
    values = (
        jnp.where((rows < 3) | (rows > 5), dist, 0.0),
        jnp.where((rows >= 3) & (rows < 6), front, 0.0),
        jnp.where((rows < 3) | (rows == 6), back, 0.0),
        jnp.where(rows == 6, core, 0.0),
    )
    pick = rows & 3
    picks = (jnp.where(pick < 2, one, zero), jnp.where(pick == 2, one, zero), zero, jnp.where(pick == 3, one, zero))
    blocks = []
    for value, picked in zip(values, picks):
        first, second, third = split_three(value)
        parts = [first, picked, second, third, first, second, first, picked]
        blocks.append(jnp.concatenate(parts, axis=0).astype(jnp.bfloat16))
    return jnp.concatenate(blocks, axis=1)


def finish_block(tile_row, smooth_row, grad_row, origin):
    position = [tile_row(k) - origin[k : k + 1, :] for k in range(3)]
    strength = [tile_row(3 + k) for k in range(3)]
    scale = biot_factor * tile_row(7)
    smooth = [smooth_row(k) for k in range(6)]
    grad = [grad_row(k) for k in range(6)]
    velocity = [turn - part for turn, part in zip(cross(position, smooth[:3]), smooth[3:])]
    lever = [turn - part for turn, part in zip(cross(position, grad[:3]), grad[3:])]
    stretch = [turn - 3.0 * part for turn, part in zip(cross(strength, smooth[:3]), lever)]
    return [scale * value for value in velocity + stretch]


def evaluate(products, pieces):
    for start in range(0, TILE, 16):
        at = slice(start, start + 16)
        dist, front, back, core = (products[at, k * TILE : (k + 1) * TILE] for k in range(4))
        inv = lax.rsqrt(dist)
        inv2 = inv * inv
        inv3 = inv2 * inv
        tail = core * (inv3 * inv2)
        smooth = inv3 + 1.5 * tail
        grad = inv2 * (smooth + tail)
        for k, value in enumerate((smooth, grad * front, grad * back)):
            high, low = split_two(value)
            pieces[at, 2 * k * TILE : (2 * k + 1) * TILE] = high
            pieces[at, (2 * k + 1) * TILE : (2 * k + 2) * TILE] = low


def tile_at(tile):
    return pl.ds(pl.multiple_of(tile * ROWS, ROWS), ROWS)


def term_at(tile):
    return pl.ds(pl.multiple_of(tile * TERMS, TERMS), TERMS)


def wide_at(tile):
    return pl.ds(pl.multiple_of(tile * TILE, TILE), TILE)


def feat_at(tile):
    return pl.ds(pl.multiple_of(tile * FEAT, FEAT), FEAT)


def target_terms(feat, values):
    smooth, front = values[:, : 2 * TILE], values[:, 2 * TILE : 4 * TILE]
    terms = lax.dot_general(
        jnp.concatenate([feat, feat], axis=1),
        jnp.concatenate([smooth, front], axis=0),
        (((1,), (1,)), ((), ())),
        preferred_element_type=jnp.float32,
    )
    return add_pieces(terms)


def source_terms(feat, values):
    high = jnp.concatenate([values[:, :TILE], values[:, 4 * TILE : 5 * TILE]], axis=1)
    low = jnp.concatenate([values[:, TILE : 2 * TILE], values[:, 5 * TILE :]], axis=1)
    both = jnp.concatenate([high, low], axis=0)
    terms = jnp.dot(jnp.concatenate([feat, feat], axis=1), both, preferred_element_type=jnp.float32)
    return add_pieces(terms)


def own_kernel(block, left, right, feat, sums, origin_ref, *scratch):
    products, pieces = scratch[:STEPS], scratch[STEPS : 2 * STEPS]
    stages, copied = scratch[2 * STEPS : -1], scratch[-1]
    copied[: block.shape[0], :] = block[...]
    tiles = block.shape[0] // ROWS
    rows = row_ids()
    total = block[0:ROWS, :]
    for tile in range(1, tiles):
        total = total + block[tile * ROWS : (tile + 1) * ROWS, :]
    origin = jnp.sum(total, axis=1, keepdims=True) * (1.0 / (tiles * TILE))
    origin = jnp.where(rows < 3, jnp.broadcast_to(origin, (ROWS, TILE)), 0.0)
    origin_ref[...] = origin
    description = describe(lambda row: copied[pl.ds(row, tiles, stride=ROWS), :], origin)
    stage_features(stages[0], 0, tiles, *description[:2])
    stage_target(stages[1:3], 0, tiles, description)
    stage_source(stages[3:], 0, tiles, description)
    for tile in range(tiles):
        staged = [ref[tile * ROWS : (tile + 1) * ROWS, :] for ref in stages]
        feat[tile * FEAT : (tile + 1) * FEAT, :] = features(staged[0], rows)
        left[tile * TILE : (tile + 1) * TILE, :] = target_side(*staged[1:3], rows)
        right[tile * TERMS : (tile + 1) * TERMS, :] = source_side(*staged[3:], rows)
    for step in range(tiles + 2 * LEAD):
        if step < tiles:
            target, source = left[step * TILE : (step + 1) * TILE, :], right[step * TERMS : (step + 1) * TERMS, :]
            products[step % STEPS][...] = jnp.dot(target, source, preferred_element_type=jnp.float32)
        if LEAD <= step < tiles + LEAD:
            evaluate(products[(step - LEAD) % STEPS], pieces[(step - LEAD) % STEPS])
        if step >= 2 * LEAD:
            tile = step - 2 * LEAD
            terms = target_terms(feat[tile * FEAT : (tile + 1) * FEAT, :], pieces[tile % STEPS])
            sums[tile * ROWS : (tile + 1) * ROWS, :] = terms


def join_kernel(*refs):
    out, start = refs[-1], 0
    for ref in refs[:-1]:
        out[start : start + ref.shape[0], :] = ref[...]
        start += ref.shape[0]


def pair_kernel(nrows, ncols, tiles, where_ref, slots_ref, *refs):
    own_block, own_left, own_right, own_feat, own_sums, origin_ref = refs[:6]
    refs = refs[6:]
    halves = nrows // 2
    row_ins, far_ins, near_in, refs = refs[: ncols - 1], refs[ncols - 1 : ncols + halves - 2], refs[ncols + halves - 2], refs[ncols + halves - 1 :]
    row_outs, col_outs, scratch = refs[:ncols], refs[ncols : ncols + halves], refs[ncols + halves :]
    left, right, row_feat, col_feat = scratch[:4]
    row_sum, col_sum = scratch[4:6], scratch[6:8]
    row_stage, col_stage = scratch[8:11], scratch[11:16]
    came, done = scratch[16:18]
    products, pieces = scratch[18 : 18 + STEPS], scratch[18 + STEPS :]
    per = tiles * ROWS
    rows = row_ids()
    my_row, my_col = where_ref[0], where_ref[1]
    count = where_ref[2]
    for number, ref in enumerate((own_block, *row_ins, *far_ins)):
        came[number * per : (number + 1) * per, :] = ref[...]
    near = ncols + halves - 1
    came[near * per : (near + halves) * per, :] = near_in[...]
    row_sources = [(k, k * per) for k in range(1, ncols)]
    col_sources = [(2 * m, (ncols - 1 + m) * per) for m in range(1, halves)]
    col_sources += [(2 * m + 1, (near + m) * per) for m in range(halves)]
    origin = origin_ref[...]

    for ref in (*row_sum, *col_sum):
        ref[...] = jnp.zeros_like(ref)
    for k in range(STEPS - LEAD, STEPS):
        pieces[k][...] = jnp.zeros_like(pieces[k])
    for feat, me in ((row_feat, my_col), (col_feat, my_row)):
        feat[pl.ds(pl.multiple_of(me * tiles * FEAT, tiles * FEAT), tiles * FEAT), :] = own_feat[...]
    for k, ref in enumerate(row_sum):
        ref[pl.ds(pl.multiple_of(my_col * per, per), per), :] = own_sums[:, k * TILE : (k + 1) * TILE]
    left[pl.ds(pl.multiple_of(my_col * tiles * TILE, tiles * TILE), tiles * TILE), :] = own_left[...]
    right[pl.ds(pl.multiple_of(my_row * tiles * TERMS, tiles * TERMS), tiles * TERMS), :] = own_right[...]

    def rows_of(ref, start):
        return lambda row: ref[pl.ds(start + row, tiles, stride=ROWS), :]

    for number, (_, start) in enumerate(row_sources):
        description = describe(rows_of(came, start), origin)
        stage_features(row_stage[0], number * per, tiles, *description[:2])
        stage_target(row_stage[1:], number * per, tiles, description)
    for number, (_, start) in enumerate(col_sources):
        description = describe(rows_of(came, start), origin)
        stage_features(col_stage[0], number * per, tiles, *description[:2])
        stage_source(col_stage[1:], number * per, tiles, description)

    def prepare(step, carry):
        for number, (k, _) in enumerate(row_sources):
            tile = (my_col ^ k) * tiles + step
            staged = [ref[pl.ds(pl.multiple_of(number * per + step * ROWS, ROWS), ROWS), :] for ref in row_stage]
            row_feat[feat_at(tile), :] = features(staged[0], rows)
            left[wide_at(tile), :] = target_side(*staged[1:], rows)
        for number, (k, _) in enumerate(col_sources):
            tile = (my_row ^ k) * tiles + step
            staged = [ref[pl.ds(pl.multiple_of(number * per + step * ROWS, ROWS), ROWS), :] for ref in col_stage]
            col_feat[feat_at(tile), :] = features(staged[0], rows)
            right[term_at(tile), :] = source_side(*staged[1:], rows)
        return carry

    lax.fori_loop(0, tiles, prepare, 0, unroll=2)

    last = slots_ref.shape[1] - 1

    def multiply(slot, out):
        slot = jnp.minimum(slot, last)
        tgt, src = slots_ref[0, slot], slots_ref[1, slot]
        out[...] = jnp.dot(left[wide_at(tgt), :], right[term_at(src), :], preferred_element_type=jnp.float32)

    def add_up(slot, values):
        kept = jnp.clip(slot, 0, last)
        tgt, src = slots_ref[0, kept], slots_ref[1, kept]
        own = (tgt // tiles == my_col) & (src // tiles == my_row) & (tgt % tiles == src % tiles)
        alive = jnp.where((slot >= tiles) & (slot < count), 1.0, 0.0)
        react = jnp.where(own, 0.0, alive)
        to_target = alive * target_terms(col_feat[feat_at(src), :], values)
        to_source = react * source_terms(row_feat[feat_at(tgt), :], values)
        for k in range(2):
            row_sum[k][tile_at(tgt), :] += to_target[:, k * TILE : (k + 1) * TILE]
            col_sum[k][tile_at(src), :] += to_source[:, k * TILE : (k + 1) * TILE]

    for k in range(LEAD):
        multiply(tiles + k, products[k])
    loops = (count - tiles + STEPS - 1) // STEPS

    def visit(step, carry):
        for k in range(STEPS):
            slot = tiles + step * STEPS + k
            multiply(slot + LEAD, products[(k + LEAD) % STEPS])
            evaluate(products[k], pieces[k])
            add_up(slot - LEAD, pieces[(k - LEAD) % STEPS])
        return carry

    lax.fori_loop(0, loops, visit, 0)
    for k in range(LEAD):
        add_up(tiles + loops * STEPS - LEAD + k, pieces[STEPS - LEAD + k])

    row_results = [(k, row_outs[k], 0) for k in range(ncols)]
    col_results = [(k, col_outs[k // 2], k % 2 * per) for k in range(nrows)]
    number = 0
    for results, sources, sums, me in (
        (row_results, row_sources, row_sum, my_col),
        (col_results, col_sources, col_sum, my_row),
    ):
        starts = dict(sources) | {0: 0}
        for k, result, start in results:
            base = pl.multiple_of((me ^ k) * per, per)
            values = finish_block(rows_of(came, starts[k]), *(rows_of(ref, base) for ref in sums), origin)
            put_rows(done, number * per, tiles, numbered(0, values))
            result[start : start + per, :] = done[number * per : (number + 1) * per, :]
            number += 1


def halve_kernel(*refs):
    keep, send = refs[-2:]
    half = keep.shape[0]
    total = refs[0][...]
    for ref in refs[1:-2]:
        total = total + ref[...]
    keep[...] = total[:half, :]
    send[...] = total[half:, :]


def total_kernel(*refs):
    vel_ref, str_ref = refs[-2:]
    tiles = vel_ref.shape[1] // TILE
    for tile in range(tiles):
        at = slice(tile * ROWS, (tile + 1) * ROWS)
        total = refs[0][at, :]
        for ref in refs[1:-2]:
            total = total + ref[at, :]
        vel_ref[:, tile * TILE : (tile + 1) * TILE] = total[0:3, :]
        str_ref[:, tile * TILE : (tile + 1) * TILE] = total[3:6, :]


def shards(positions, strengths, cores, order, tile_counts, pair_slots, pair_count):
    tiles = tile_counts.shape[0]
    per_dev = tiles * TILE
    nrows = lax.axis_size("row")
    ncols = lax.axis_size("col")
    halves = nrows // 2
    assert nrows == 2 * halves and nrows & (nrows - 1) == 0 and ncols & (ncols - 1) == 0
    row_tiles, col_tiles = ncols * tiles, nrows * tiles
    smem = pl.BlockSpec(memory_space=pltpu.SMEM)
    vmem = pl.BlockSpec(memory_space=pltpu.VMEM)
    hbm = pl.BlockSpec(memory_space=pltpu.HBM)
    params = pltpu.CompilerParams(vmem_limit_bytes=VMEM_BYTES)

    def blocks(count):
        return jax.ShapeDtypeStruct((count * tiles * ROWS, TILE), jnp.float32)

    def in_hbm(value):
        return pltpu.with_memory_space_constraint(value, pltpu.HBM)

    inputs = (tile_counts, positions, strengths, cores.reshape(1, per_dev), order.reshape(1, per_dev), pair_slots)
    packed, slots = pl.pallas_call(
        pack_kernel,
        out_shape=[blocks(1), jax.ShapeDtypeStruct(pair_slots.shape, jnp.int32)],
        in_specs=[hbm] * len(inputs),
        out_specs=[vmem, smem],
        scratch_shapes=[
            pltpu.VMEM((ROWS, per_dev), jnp.float32),
            pltpu.VMEM((1, per_dev), jnp.int32),
            pltpu.SMEM(tile_counts.shape, jnp.int32),
            pltpu.SemaphoreType.DMA((len(inputs),)),
        ],
        compiler_params=params,
        name="pack",
    )(*map(in_hbm, inputs))

    def swap(value, axis, size, k):
        return lax.ppermute(value, axis, [(d, d ^ k) for d in range(size)])

    def strided(count):
        return pltpu.VMEM(((count * tiles + 1) * ROWS, TILE), jnp.float32)

    phases = [pltpu.VMEM((TILE, 4 * TILE), jnp.float32)] * STEPS + [pltpu.VMEM((TILE, 6 * TILE), jnp.bfloat16)] * STEPS
    own = pl.pallas_call(
        own_kernel,
        out_shape=[
            jax.ShapeDtypeStruct((per_dev, TERMS), jnp.bfloat16),
            jax.ShapeDtypeStruct((tiles * TERMS, 4 * TILE), jnp.bfloat16),
            jax.ShapeDtypeStruct((tiles * FEAT, TILE), jnp.bfloat16),
            jax.ShapeDtypeStruct((tiles * ROWS, 2 * TILE), jnp.float32),
            jax.ShapeDtypeStruct((ROWS, TILE), jnp.float32),
        ],
        in_specs=[vmem],
        out_specs=[vmem] * 5,
        scratch_shapes=phases + [strided(1)] * 8,
        compiler_params=params,
        cost_estimate=pl.CostEstimate(flops=tiles * 300 * TILE * TILE, bytes_accessed=2**21, transcendentals=0),
        name="own",
    )(packed)

    far = [swap(packed, "row", nrows, 2 * m) for m in range(1, halves)]
    from_row = [swap(packed, "col", ncols, k) for k in range(1, ncols)]
    joined = pl.pallas_call(
        join_kernel,
        out_shape=blocks(halves),
        in_specs=[vmem] * halves,
        out_specs=vmem,
        compiler_params=params,
        name="join",
    )(packed, *far)
    near = swap(joined, "row", nrows, 1)

    where = jnp.stack([lax.axis_index("row"), lax.axis_index("col"), pair_count[0]]).astype(jnp.int32)
    sums = pl.pallas_call(
        functools.partial(pair_kernel, nrows, ncols, tiles),
        out_shape=[blocks(1)] * ncols + [blocks(2)] * halves,
        in_specs=[smem] * 2 + [vmem] * (5 + ncols + halves),
        out_specs=[vmem] * (ncols + halves),
        scratch_shapes=[
            pltpu.VMEM((row_tiles * TILE, TERMS), jnp.bfloat16),
            pltpu.VMEM((col_tiles * TERMS, 4 * TILE), jnp.bfloat16),
            pltpu.VMEM((row_tiles * FEAT, TILE), jnp.bfloat16),
            pltpu.VMEM((col_tiles * FEAT, TILE), jnp.bfloat16),
            *[strided(ncols)] * 2,
            *[strided(nrows)] * 2,
            *[strided(ncols - 1)] * 3,
            *[strided(nrows - 1)] * 5,
            strided(ncols + nrows - 1),
            strided(ncols + nrows),
            *phases,
        ],
        compiler_params=params,
        name="pairs",
    )(where, slots, packed, *own, *from_row, *far, near)

    far_back = [swap(sums[ncols + m], "row", nrows, 2 * m) for m in range(1, halves)]
    row_back = [swap(sums[k], "col", ncols, k) for k in range(1, ncols)]
    keep, send = pl.pallas_call(
        halve_kernel,
        out_shape=[blocks(1)] * 2,
        in_specs=[vmem] * halves,
        out_specs=[vmem] * 2,
        compiler_params=params,
        name="halve",
    )(sums[ncols], *far_back)
    parts = [sums[0], keep, *row_back, swap(send, "row", nrows, 1)]
    velocity, stretching = pl.pallas_call(
        total_kernel,
        out_shape=[jax.ShapeDtypeStruct((3, per_dev), jnp.float32)] * 2,
        in_specs=[vmem] * len(parts),
        out_specs=[vmem, vmem],
        compiler_params=params,
        name="totals",
    )(*parts)
    return velocity, stretching


def solution(mesh):
    whole = ("groups", "row", "col")
    in_specs = (P(None, whole), P(None, whole), P(whole), P(whole), P(whole), P(None, whole), P(whole))
    out_specs = (P(None, whole), P(None, whole))
    return jax.shard_map(shards, mesh=mesh, in_specs=in_specs, out_specs=out_specs, check_vma=False)
```

```python
import functools
import math

import jax
import jax.numpy as jnp
from jax import lax
from jax.experimental import pallas as pl
from jax.experimental.pallas import tpu as pltpu
from jax.sharding import PartitionSpec as P

TILE = 128
ROWS = 8
STEPS = 4
LEAD = 2
FEAT = 32
TERMS = 64
VMEM_BYTES = 48 * 1024 * 1024

biot_factor = -1.0 / (4.0 * math.pi)


def row_ids(count=ROWS):
    return lax.broadcasted_iota(jnp.int32, (count, TILE), 0)


def roll_rows(value, shift):
    return pltpu.roll(value, shift % ROWS, 0)


def pack_kernel(
    counts_hbm, pos_hbm, str_hbm, core_hbm, order_hbm, slots_hbm,
    out_ref, slots_ref, stored, order_ref, counts_ref, arrived,
):
    tiles = order_ref.shape[1] // TILE
    pairs = (
        (pos_hbm, stored.at[0:3, :]),
        (str_hbm, stored.at[3:6, :]),
        (core_hbm, stored.at[6:7, :]),
        (order_hbm, order_ref),
        (counts_hbm, counts_ref),
        (slots_hbm, slots_ref),
    )
    copies = [pltpu.make_async_copy(src, dst, arrived.at[k]) for k, (src, dst) in enumerate(pairs)]
    for copy in copies:
        copy.start()
    stored[7:8, :] = jnp.zeros((1, stored.shape[1]), jnp.float32)
    for copy in copies:
        copy.wait()
    lane = lax.broadcasted_iota(jnp.int32, (ROWS, TILE), 1)
    rows = row_ids()
    is_strength = (rows >= 3) & (rows < 6)
    for tile in range(tiles):
        where_from = jnp.broadcast_to(order_ref[:, tile * TILE : (tile + 1) * TILE], (ROWS, TILE))
        inside = where_from & (TILE - 1)
        block = where_from >> 7
        value = jnp.zeros((ROWS, TILE), jnp.float32)
        for source in range(tiles):
            part = jnp.take_along_axis(stored[:, source * TILE : (source + 1) * TILE], inside, axis=1)
            value = jnp.where(block == source, part, value)
        live = lane < counts_ref[tile]
        value = jnp.where(is_strength & ~live, 0.0, value)
        value = jnp.where(rows == 7, live.astype(jnp.float32), value)
        out_ref[tile * ROWS : (tile + 1) * ROWS, :] = value


def split_three(value):
    first = value.astype(jnp.bfloat16).astype(jnp.float32)
    rest = value - first
    second = rest.astype(jnp.bfloat16).astype(jnp.float32)
    return first, second, rest - second


def split_two(value):
    high = value.astype(jnp.bfloat16)
    return high, (value - high.astype(jnp.float32)).astype(jnp.bfloat16)


def add_pieces(terms):
    return terms[0:ROWS, :] + (terms[ROWS : 2 * ROWS, :] + terms[2 * ROWS : 3 * ROWS, :])


def cross(left, right):
    return [left[1] * right[2] - left[2] * right[1], left[2] * right[0] - left[0] * right[2], left[0] * right[1] - left[1] * right[0]]


def describe(tile_row, origin):
    position = [tile_row(k) - origin[k : k + 1, :] for k in range(3)]
    strength = [tile_row(3 + k) for k in range(3)]
    core = tile_row(6)
    half = 0.5 * core * core
    coarse = [value.astype(jnp.bfloat16).astype(jnp.float32) for value in position]
    norm = coarse[0] * coarse[0] + coarse[1] * coarse[1] + coarse[2] * coarse[2]
    rest = [(value - near) * (value + near) for value, near in zip(position, coarse)]
    rest = rest[0] + rest[1] + rest[2] + half
    along = position[0] * strength[0] + position[1] * strength[1] + position[2] * strength[2]
    return position, strength, half, norm, rest, along


def put_rows(ref, start, tiles, values):
    for row, value in values.items():
        ref[pl.ds(start + row, tiles, stride=ROWS), :] = value


def negative(values):
    return [-value for value in values]


def numbered(first, values):
    return dict(enumerate(values, first))


def stage_features(ref, start, tiles, position, strength):
    put_rows(ref, start, tiles, numbered(0, strength + cross(position, strength)))


def stage_target(refs, start, tiles, description):
    position, strength, half, norm, rest, along = description
    put_rows(refs[0], start, tiles, numbered(0, position + strength))
    put_rows(refs[1], start, tiles, numbered(0, [norm, rest, along, half]))


def stage_source(refs, start, tiles, description):
    position, strength, half, norm, rest, along = description
    put_rows(refs[0], start, tiles, numbered(0, [-2.0 * value for value in position]) | {6: norm, 7: rest})
    put_rows(refs[1], start, tiles, numbered(3, negative(position)))
    put_rows(refs[2], start, tiles, numbered(0, negative(strength)) | {6: along})
    put_rows(refs[3], start, tiles, {6: half})


def features(tile, rows):
    value = jnp.where(rows < 6, tile, 0.0)
    return jnp.concatenate([*split_three(value), jnp.zeros_like(value)], axis=0).astype(jnp.bfloat16)


def target_side(shared, alone, rows):
    first, second, third = split_three(jnp.where(rows < 6, shared, 1.0))
    alone1, alone2, alone3 = split_three(jnp.where(rows < 4, alone, 0.0))
    both = jnp.where(rows < 4, alone1, roll_rows(alone2, 4))
    stacked = jnp.concatenate([first, both, first, first, second, second, third, alone3], axis=0)
    return stacked.astype(jnp.bfloat16).T


def source_side(dist, front, back, core, rows):
    zero = jnp.zeros_like(dist)
    one = jnp.ones_like(dist)
    values = (
        jnp.where((rows < 3) | (rows > 5), dist, 0.0),
        jnp.where((rows >= 3) & (rows < 6), front, 0.0),
        jnp.where((rows < 3) | (rows == 6), back, 0.0),
        jnp.where(rows == 6, core, 0.0),
    )
    pick = rows & 3
    picks = (jnp.where(pick < 2, one, zero), jnp.where(pick == 2, one, zero), zero, jnp.where(pick == 3, one, zero))
    blocks = []
    for value, picked in zip(values, picks):
        first, second, third = split_three(value)
        parts = [first, picked, second, third, first, second, first, picked]
        blocks.append(jnp.concatenate(parts, axis=0).astype(jnp.bfloat16))
    return jnp.concatenate(blocks, axis=1)


def finish_block(tile_row, smooth_row, grad_row, origin):
    position = [tile_row(k) - origin[k : k + 1, :] for k in range(3)]
    strength = [tile_row(3 + k) for k in range(3)]
    scale = biot_factor * tile_row(7)
    smooth = [smooth_row(k) for k in range(6)]
    grad = [grad_row(k) for k in range(6)]
    velocity = [turn - part for turn, part in zip(cross(position, smooth[:3]), smooth[3:])]
    lever = [turn - part for turn, part in zip(cross(position, grad[:3]), grad[3:])]
    stretch = [turn - 3.0 * part for turn, part in zip(cross(strength, smooth[:3]), lever)]
    return [scale * value for value in velocity + stretch]


def evaluate(products, pieces):
    for start in range(0, TILE, 16):
        at = slice(start, start + 16)
        dist, front, back, core = (products[at, k * TILE : (k + 1) * TILE] for k in range(4))
        inv = lax.rsqrt(dist)
        inv2 = inv * inv
        inv3 = inv2 * inv
        tail = core * (inv3 * inv2)
        smooth = inv3 + 1.5 * tail
        grad = inv2 * (smooth + tail)
        for k, value in enumerate((smooth, grad * front, grad * back)):
            high, low = split_two(value)
            pieces[at, 2 * k * TILE : (2 * k + 1) * TILE] = high
            pieces[at, (2 * k + 1) * TILE : (2 * k + 2) * TILE] = low


def tile_at(tile):
    return pl.ds(pl.multiple_of(tile * ROWS, ROWS), ROWS)


def term_at(tile):
    return pl.ds(pl.multiple_of(tile * TERMS, TERMS), TERMS)


def wide_at(tile):
    return pl.ds(pl.multiple_of(tile * TILE, TILE), TILE)


def feat_at(tile):
    return pl.ds(pl.multiple_of(tile * FEAT, FEAT), FEAT)


def target_terms(feat, values):
    smooth, front = values[:, : 2 * TILE], values[:, 2 * TILE : 4 * TILE]
    terms = lax.dot_general(
        jnp.concatenate([feat, feat], axis=1),
        jnp.concatenate([smooth, front], axis=0),
        (((1,), (1,)), ((), ())),
        preferred_element_type=jnp.float32,
    )
    return add_pieces(terms)


def source_terms(feat, values):
    high = jnp.concatenate([values[:, :TILE], values[:, 4 * TILE : 5 * TILE]], axis=1)
    low = jnp.concatenate([values[:, TILE : 2 * TILE], values[:, 5 * TILE :]], axis=1)
    both = jnp.concatenate([high, low], axis=0)
    terms = jnp.dot(jnp.concatenate([feat, feat], axis=1), both, preferred_element_type=jnp.float32)
    return add_pieces(terms)


def own_kernel(block, left, right, feat, sums, origin_ref, *scratch):
    products, pieces = scratch[:STEPS], scratch[STEPS : 2 * STEPS]
    stages, copied = scratch[2 * STEPS : -1], scratch[-1]
    copied[: block.shape[0], :] = block[...]
    tiles = block.shape[0] // ROWS
    rows = row_ids()
    total = block[0:ROWS, :]
    for tile in range(1, tiles):
        total = total + block[tile * ROWS : (tile + 1) * ROWS, :]
    origin = jnp.sum(total, axis=1, keepdims=True) * (1.0 / (tiles * TILE))
    origin = jnp.where(rows < 3, jnp.broadcast_to(origin, (ROWS, TILE)), 0.0)
    origin_ref[...] = origin
    description = describe(lambda row: copied[pl.ds(row, tiles, stride=ROWS), :], origin)
    stage_features(stages[0], 0, tiles, *description[:2])
    stage_target(stages[1:3], 0, tiles, description)
    stage_source(stages[3:], 0, tiles, description)
    for tile in range(tiles):
        staged = [ref[tile * ROWS : (tile + 1) * ROWS, :] for ref in stages]
        feat[tile * FEAT : (tile + 1) * FEAT, :] = features(staged[0], rows)
        left[tile * TILE : (tile + 1) * TILE, :] = target_side(*staged[1:3], rows)
        right[tile * TERMS : (tile + 1) * TERMS, :] = source_side(*staged[3:], rows)
    for step in range(tiles + 2 * LEAD):
        if step < tiles:
            target, source = left[step * TILE : (step + 1) * TILE, :], right[step * TERMS : (step + 1) * TERMS, :]
            products[step % STEPS][...] = jnp.dot(target, source, preferred_element_type=jnp.float32)
        if LEAD <= step < tiles + LEAD:
            evaluate(products[(step - LEAD) % STEPS], pieces[(step - LEAD) % STEPS])
        if step >= 2 * LEAD:
            tile = step - 2 * LEAD
            terms = target_terms(feat[tile * FEAT : (tile + 1) * FEAT, :], pieces[tile % STEPS])
            sums[tile * ROWS : (tile + 1) * ROWS, :] = terms


def join_kernel(*refs):
    out, start = refs[-1], 0
    for ref in refs[:-1]:
        out[start : start + ref.shape[0], :] = ref[...]
        start += ref.shape[0]


def pair_kernel(nrows, ncols, tiles, where_ref, slots_ref, *refs):
    own_block, own_left, own_right, own_feat, own_sums, origin_ref = refs[:6]
    refs = refs[6:]
    halves = nrows // 2
    row_ins, far_ins, near_in, refs = refs[: ncols - 1], refs[ncols - 1 : ncols + halves - 2], refs[ncols + halves - 2], refs[ncols + halves - 1 :]
    row_outs, col_outs, scratch = refs[:ncols], refs[ncols : ncols + halves], refs[ncols + halves :]
    left, right, row_feat, col_feat = scratch[:4]
    row_sum, col_sum = scratch[4:6], scratch[6:8]
    row_stage, col_stage = scratch[8:11], scratch[11:16]
    came, done = scratch[16:18]
    products, pieces = scratch[18 : 18 + STEPS], scratch[18 + STEPS :]
    per = tiles * ROWS
    rows = row_ids()
    my_row, my_col = where_ref[0], where_ref[1]
    count = where_ref[2]
    for number, ref in enumerate((own_block, *row_ins, *far_ins)):
        came[number * per : (number + 1) * per, :] = ref[...]
    near = ncols + halves - 1
    came[near * per : (near + halves) * per, :] = near_in[...]
    row_sources = [(k, k * per) for k in range(1, ncols)]
    col_sources = [(2 * m, (ncols - 1 + m) * per) for m in range(1, halves)]
    col_sources += [(2 * m + 1, (near + m) * per) for m in range(halves)]
    origin = origin_ref[...]

    for ref in (*row_sum, *col_sum):
        ref[...] = jnp.zeros_like(ref)
    for k in range(STEPS - LEAD, STEPS):
        pieces[k][...] = jnp.zeros_like(pieces[k])
    for feat, me in ((row_feat, my_col), (col_feat, my_row)):
        feat[pl.ds(pl.multiple_of(me * tiles * FEAT, tiles * FEAT), tiles * FEAT), :] = own_feat[...]
    for k, ref in enumerate(row_sum):
        ref[pl.ds(pl.multiple_of(my_col * per, per), per), :] = own_sums[:, k * TILE : (k + 1) * TILE]
    left[pl.ds(pl.multiple_of(my_col * tiles * TILE, tiles * TILE), tiles * TILE), :] = own_left[...]
    right[pl.ds(pl.multiple_of(my_row * tiles * TERMS, tiles * TERMS), tiles * TERMS), :] = own_right[...]

    def rows_of(ref, start):
        return lambda row: ref[pl.ds(start + row, tiles, stride=ROWS), :]

    for number, (_, start) in enumerate(row_sources):
        description = describe(rows_of(came, start), origin)
        stage_features(row_stage[0], number * per, tiles, *description[:2])
        stage_target(row_stage[1:], number * per, tiles, description)
    for number, (_, start) in enumerate(col_sources):
        description = describe(rows_of(came, start), origin)
        stage_features(col_stage[0], number * per, tiles, *description[:2])
        stage_source(col_stage[1:], number * per, tiles, description)

    def prepare(step, carry):
        for number, (k, _) in enumerate(row_sources):
            tile = (my_col ^ k) * tiles + step
            staged = [ref[pl.ds(pl.multiple_of(number * per + step * ROWS, ROWS), ROWS), :] for ref in row_stage]
            row_feat[feat_at(tile), :] = features(staged[0], rows)
            left[wide_at(tile), :] = target_side(*staged[1:], rows)
        for number, (k, _) in enumerate(col_sources):
            tile = (my_row ^ k) * tiles + step
            staged = [ref[pl.ds(pl.multiple_of(number * per + step * ROWS, ROWS), ROWS), :] for ref in col_stage]
            col_feat[feat_at(tile), :] = features(staged[0], rows)
            right[term_at(tile), :] = source_side(*staged[1:], rows)
        return carry

    lax.fori_loop(0, tiles, prepare, 0, unroll=4)

    last = slots_ref.shape[1] - 1

    def multiply(slot, out):
        slot = jnp.minimum(slot, last)
        tgt, src = slots_ref[0, slot], slots_ref[1, slot]
        out[...] = jnp.dot(left[wide_at(tgt), :], right[term_at(src), :], preferred_element_type=jnp.float32)

    def add_up(slot, values):
        kept = jnp.clip(slot, 0, last)
        tgt, src = slots_ref[0, kept], slots_ref[1, kept]
        own = (tgt // tiles == my_col) & (src // tiles == my_row) & (tgt % tiles == src % tiles)
        alive = jnp.where((slot >= tiles) & (slot < count), 1.0, 0.0)
        react = jnp.where(own, 0.0, alive)
        to_target = alive * target_terms(col_feat[feat_at(src), :], values)
        to_source = react * source_terms(row_feat[feat_at(tgt), :], values)
        for k in range(2):
            row_sum[k][tile_at(tgt), :] += to_target[:, k * TILE : (k + 1) * TILE]
            col_sum[k][tile_at(src), :] += to_source[:, k * TILE : (k + 1) * TILE]

    for k in range(LEAD):
        multiply(tiles + k, products[k])
    loops = (count - tiles + STEPS - 1) // STEPS

    def visit(step, carry):
        for k in range(STEPS):
            slot = tiles + step * STEPS + k
            multiply(slot + LEAD, products[(k + LEAD) % STEPS])
            evaluate(products[k], pieces[k])
            add_up(slot - LEAD, pieces[(k - LEAD) % STEPS])
        return carry

    lax.fori_loop(0, loops, visit, 0)
    for k in range(LEAD):
        add_up(tiles + loops * STEPS - LEAD + k, pieces[STEPS - LEAD + k])

    row_results = [(k, row_outs[k], 0) for k in range(ncols)]
    col_results = [(k, col_outs[k // 2], k % 2 * per) for k in range(nrows)]
    number = 0
    for results, sources, sums, me in (
        (row_results, row_sources, row_sum, my_col),
        (col_results, col_sources, col_sum, my_row),
    ):
        starts = dict(sources) | {0: 0}
        for k, result, start in results:
            base = pl.multiple_of((me ^ k) * per, per)
            values = finish_block(rows_of(came, starts[k]), *(rows_of(ref, base) for ref in sums), origin)
            put_rows(done, number * per, tiles, numbered(0, values))
            result[start : start + per, :] = done[number * per : (number + 1) * per, :]
            number += 1


def halve_kernel(*refs):
    keep, send = refs[-2:]
    half = keep.shape[0]
    total = refs[0][...]
    for ref in refs[1:-2]:
        total = total + ref[...]
    keep[...] = total[:half, :]
    send[...] = total[half:, :]


def total_kernel(*refs):
    vel_ref, str_ref = refs[-2:]
    tiles = vel_ref.shape[1] // TILE
    for tile in range(tiles):
        at = slice(tile * ROWS, (tile + 1) * ROWS)
        total = refs[0][at, :]
        for ref in refs[1:-2]:
            total = total + ref[at, :]
        vel_ref[:, tile * TILE : (tile + 1) * TILE] = total[0:3, :]
        str_ref[:, tile * TILE : (tile + 1) * TILE] = total[3:6, :]


def shards(positions, strengths, cores, order, tile_counts, pair_slots, pair_count):
    tiles = tile_counts.shape[0]
    per_dev = tiles * TILE
    nrows = lax.axis_size("row")
    ncols = lax.axis_size("col")
    halves = nrows // 2
    assert nrows == 2 * halves and nrows & (nrows - 1) == 0 and ncols & (ncols - 1) == 0
    row_tiles, col_tiles = ncols * tiles, nrows * tiles
    smem = pl.BlockSpec(memory_space=pltpu.SMEM)
    vmem = pl.BlockSpec(memory_space=pltpu.VMEM)
    hbm = pl.BlockSpec(memory_space=pltpu.HBM)
    params = pltpu.CompilerParams(vmem_limit_bytes=VMEM_BYTES)

    def blocks(count):
        return jax.ShapeDtypeStruct((count * tiles * ROWS, TILE), jnp.float32)

    def in_hbm(value):
        return pltpu.with_memory_space_constraint(value, pltpu.HBM)

    inputs = (tile_counts, positions, strengths, cores.reshape(1, per_dev), order.reshape(1, per_dev), pair_slots)
    packed, slots = pl.pallas_call(
        pack_kernel,
        out_shape=[blocks(1), jax.ShapeDtypeStruct(pair_slots.shape, jnp.int32)],
        in_specs=[hbm] * len(inputs),
        out_specs=[vmem, smem],
        scratch_shapes=[
            pltpu.VMEM((ROWS, per_dev), jnp.float32),
            pltpu.VMEM((1, per_dev), jnp.int32),
            pltpu.SMEM(tile_counts.shape, jnp.int32),
            pltpu.SemaphoreType.DMA((len(inputs),)),
        ],
        compiler_params=params,
        name="pack",
    )(*map(in_hbm, inputs))

    def swap(value, axis, size, k):
        return lax.ppermute(value, axis, [(d, d ^ k) for d in range(size)])

    def strided(count):
        return pltpu.VMEM(((count * tiles + 1) * ROWS, TILE), jnp.float32)

    phases = [pltpu.VMEM((TILE, 4 * TILE), jnp.float32)] * STEPS + [pltpu.VMEM((TILE, 6 * TILE), jnp.bfloat16)] * STEPS
    own = pl.pallas_call(
        own_kernel,
        out_shape=[
            jax.ShapeDtypeStruct((per_dev, TERMS), jnp.bfloat16),
            jax.ShapeDtypeStruct((tiles * TERMS, 4 * TILE), jnp.bfloat16),
            jax.ShapeDtypeStruct((tiles * FEAT, TILE), jnp.bfloat16),
            jax.ShapeDtypeStruct((tiles * ROWS, 2 * TILE), jnp.float32),
            jax.ShapeDtypeStruct((ROWS, TILE), jnp.float32),
        ],
        in_specs=[vmem],
        out_specs=[vmem] * 5,
        scratch_shapes=phases + [strided(1)] * 8,
        compiler_params=params,
        cost_estimate=pl.CostEstimate(flops=tiles * 300 * TILE * TILE, bytes_accessed=2**21, transcendentals=0),
        name="own",
    )(packed)

    far = [swap(packed, "row", nrows, 2 * m) for m in range(1, halves)]
    from_row = [swap(packed, "col", ncols, k) for k in range(1, ncols)]
    joined = pl.pallas_call(
        join_kernel,
        out_shape=blocks(halves),
        in_specs=[vmem] * halves,
        out_specs=vmem,
        compiler_params=params,
        name="join",
    )(packed, *far)
    near = swap(joined, "row", nrows, 1)

    where = jnp.stack([lax.axis_index("row"), lax.axis_index("col"), pair_count[0]]).astype(jnp.int32)
    sums = pl.pallas_call(
        functools.partial(pair_kernel, nrows, ncols, tiles),
        out_shape=[blocks(1)] * ncols + [blocks(2)] * halves,
        in_specs=[smem] * 2 + [vmem] * (5 + ncols + halves),
        out_specs=[vmem] * (ncols + halves),
        scratch_shapes=[
            pltpu.VMEM((row_tiles * TILE, TERMS), jnp.bfloat16),
            pltpu.VMEM((col_tiles * TERMS, 4 * TILE), jnp.bfloat16),
            pltpu.VMEM((row_tiles * FEAT, TILE), jnp.bfloat16),
            pltpu.VMEM((col_tiles * FEAT, TILE), jnp.bfloat16),
            *[strided(ncols)] * 2,
            *[strided(nrows)] * 2,
            *[strided(ncols - 1)] * 3,
            *[strided(nrows - 1)] * 5,
            strided(ncols + nrows - 1),
            strided(ncols + nrows),
            *phases,
        ],
        compiler_params=params,
        name="pairs",
    )(where, slots, packed, *own, *from_row, *far, near)

    far_back = [swap(sums[ncols + m], "row", nrows, 2 * m) for m in range(1, halves)]
    row_back = [swap(sums[k], "col", ncols, k) for k in reversed(range(1, ncols))]
    keep, send = pl.pallas_call(
        halve_kernel,
        out_shape=[blocks(1)] * 2,
        in_specs=[vmem] * halves,
        out_specs=[vmem] * 2,
        compiler_params=params,
        name="halve",
    )(sums[ncols], *far_back)
    parts = [sums[0], keep, *row_back, swap(send, "row", nrows, 1)]
    velocity, stretching = pl.pallas_call(
        total_kernel,
        out_shape=[jax.ShapeDtypeStruct((3, per_dev), jnp.float32)] * 2,
        in_specs=[vmem] * len(parts),
        out_specs=[vmem, vmem],
        compiler_params=params,
        name="totals",
    )(*parts)
    return velocity, stretching


def solution(mesh):
    whole = ("groups", "row", "col")
    in_specs = (P(None, whole), P(None, whole), P(whole), P(whole), P(whole), P(None, whole), P(whole))
    out_specs = (P(None, whole), P(None, whole))
    return jax.shard_map(shards, mesh=mesh, in_specs=in_specs, out_specs=out_specs, check_vma=False)
```

```python
import functools
import math

import jax
import jax.numpy as jnp
from jax import lax
from jax.experimental import pallas as pl
from jax.experimental.pallas import tpu as pltpu
from jax.sharding import PartitionSpec as P

TILE = 128
ROWS = 8
STEPS = 8
LEAD = 2
FEAT = 32
TERMS = 64
VMEM_BYTES = 48 * 1024 * 1024

biot_factor = -1.0 / (4.0 * math.pi)


def row_ids(count=ROWS):
    return lax.broadcasted_iota(jnp.int32, (count, TILE), 0)


def roll_rows(value, shift):
    return pltpu.roll(value, shift % ROWS, 0)


def pack_kernel(
    counts_hbm, pos_hbm, str_hbm, core_hbm, order_hbm, slots_hbm,
    out_ref, slots_ref, stored, order_ref, counts_ref, arrived,
):
    tiles = order_ref.shape[1] // TILE
    pairs = (
        (pos_hbm, stored.at[0:3, :]),
        (str_hbm, stored.at[3:6, :]),
        (core_hbm, stored.at[6:7, :]),
        (order_hbm, order_ref),
        (counts_hbm, counts_ref),
        (slots_hbm, slots_ref),
    )
    copies = [pltpu.make_async_copy(src, dst, arrived.at[k]) for k, (src, dst) in enumerate(pairs)]
    for copy in copies:
        copy.start()
    stored[7:8, :] = jnp.zeros((1, stored.shape[1]), jnp.float32)
    for copy in copies:
        copy.wait()
    lane = lax.broadcasted_iota(jnp.int32, (ROWS, TILE), 1)
    rows = row_ids()
    is_strength = (rows >= 3) & (rows < 6)
    for tile in range(tiles):
        where_from = jnp.broadcast_to(order_ref[:, tile * TILE : (tile + 1) * TILE], (ROWS, TILE))
        inside = where_from & (TILE - 1)
        block = where_from >> 7
        value = jnp.zeros((ROWS, TILE), jnp.float32)
        for source in range(tiles):
            part = jnp.take_along_axis(stored[:, source * TILE : (source + 1) * TILE], inside, axis=1)
            value = jnp.where(block == source, part, value)
        live = lane < counts_ref[tile]
        value = jnp.where(is_strength & ~live, 0.0, value)
        value = jnp.where(rows == 7, live.astype(jnp.float32), value)
        out_ref[tile * ROWS : (tile + 1) * ROWS, :] = value


def split_three(value):
    first = value.astype(jnp.bfloat16).astype(jnp.float32)
    rest = value - first
    second = rest.astype(jnp.bfloat16).astype(jnp.float32)
    return first, second, rest - second


def split_two(value):
    high = value.astype(jnp.bfloat16)
    return high, (value - high.astype(jnp.float32)).astype(jnp.bfloat16)


def add_pieces(terms):
    return terms[0:ROWS, :] + (terms[ROWS : 2 * ROWS, :] + terms[2 * ROWS : 3 * ROWS, :])


def cross(left, right):
    return [left[1] * right[2] - left[2] * right[1], left[2] * right[0] - left[0] * right[2], left[0] * right[1] - left[1] * right[0]]


def describe(tile_row, origin):
    position = [tile_row(k) - origin[k : k + 1, :] for k in range(3)]
    strength = [tile_row(3 + k) for k in range(3)]
    core = tile_row(6)
    half = 0.5 * core * core
    coarse = [value.astype(jnp.bfloat16).astype(jnp.float32) for value in position]
    norm = coarse[0] * coarse[0] + coarse[1] * coarse[1] + coarse[2] * coarse[2]
    rest = [(value - near) * (value + near) for value, near in zip(position, coarse)]
    rest = rest[0] + rest[1] + rest[2] + half
    along = position[0] * strength[0] + position[1] * strength[1] + position[2] * strength[2]
    return position, strength, half, norm, rest, along


def put_rows(ref, start, tiles, values):
    for row, value in values.items():
        ref[pl.ds(start + row, tiles, stride=ROWS), :] = value


def negative(values):
    return [-value for value in values]


def numbered(first, values):
    return dict(enumerate(values, first))


def stage_features(ref, start, tiles, position, strength):
    put_rows(ref, start, tiles, numbered(0, strength + cross(position, strength)))


def stage_target(refs, start, tiles, description):
    position, strength, half, norm, rest, along = description
    put_rows(refs[0], start, tiles, numbered(0, position + strength))
    put_rows(refs[1], start, tiles, numbered(0, [norm, rest, along, half]))


def stage_source(refs, start, tiles, description):
    position, strength, half, norm, rest, along = description
    put_rows(refs[0], start, tiles, numbered(0, [-2.0 * value for value in position]) | {6: norm, 7: rest})
    put_rows(refs[1], start, tiles, numbered(3, negative(position)))
    put_rows(refs[2], start, tiles, numbered(0, negative(strength)) | {6: along})
    put_rows(refs[3], start, tiles, {6: half})


def features(tile, rows):
    value = jnp.where(rows < 6, tile, 0.0)
    return jnp.concatenate([*split_three(value), jnp.zeros_like(value)], axis=0).astype(jnp.bfloat16)


def target_side(shared, alone, rows):
    first, second, third = split_three(jnp.where(rows < 6, shared, 1.0))
    alone1, alone2, alone3 = split_three(jnp.where(rows < 4, alone, 0.0))
    both = jnp.where(rows < 4, alone1, roll_rows(alone2, 4))
    stacked = jnp.concatenate([first, both, first, first, second, second, third, alone3], axis=0)
    return stacked.astype(jnp.bfloat16).T


def source_side(dist, front, back, core, rows):
    zero = jnp.zeros_like(dist)
    one = jnp.ones_like(dist)
    values = (
        jnp.where((rows < 3) | (rows > 5), dist, 0.0),
        jnp.where((rows >= 3) & (rows < 6), front, 0.0),
        jnp.where((rows < 3) | (rows == 6), back, 0.0),
        jnp.where(rows == 6, core, 0.0),
    )
    pick = rows & 3
    picks = (jnp.where(pick < 2, one, zero), jnp.where(pick == 2, one, zero), zero, jnp.where(pick == 3, one, zero))
    blocks = []
    for value, picked in zip(values, picks):
        first, second, third = split_three(value)
        parts = [first, picked, second, third, first, second, first, picked]
        blocks.append(jnp.concatenate(parts, axis=0).astype(jnp.bfloat16))
    return jnp.concatenate(blocks, axis=1)


def finish_block(tile_row, smooth_row, grad_row, origin):
    position = [tile_row(k) - origin[k : k + 1, :] for k in range(3)]
    strength = [tile_row(3 + k) for k in range(3)]
    scale = biot_factor * tile_row(7)
    smooth = [smooth_row(k) for k in range(6)]
    grad = [grad_row(k) for k in range(6)]
    velocity = [turn - part for turn, part in zip(cross(position, smooth[:3]), smooth[3:])]
    lever = [turn - part for turn, part in zip(cross(position, grad[:3]), grad[3:])]
    stretch = [turn - 3.0 * part for turn, part in zip(cross(strength, smooth[:3]), lever)]
    return [scale * value for value in velocity + stretch]


def evaluate(products, pieces):
    for start in range(0, TILE, 16):
        at = slice(start, start + 16)
        dist, front, back, core = (products[at, k * TILE : (k + 1) * TILE] for k in range(4))
        inv = lax.rsqrt(dist)
        inv2 = inv * inv
        inv3 = inv2 * inv
        tail = core * (inv3 * inv2)
        smooth = inv3 + 1.5 * tail
        grad = inv2 * (smooth + tail)
        for k, value in enumerate((smooth, grad * front, grad * back)):
            high, low = split_two(value)
            pieces[at, 2 * k * TILE : (2 * k + 1) * TILE] = high
            pieces[at, (2 * k + 1) * TILE : (2 * k + 2) * TILE] = low


def tile_at(tile):
    return pl.ds(pl.multiple_of(tile * ROWS, ROWS), ROWS)


def term_at(tile):
    return pl.ds(pl.multiple_of(tile * TERMS, TERMS), TERMS)


def wide_at(tile):
    return pl.ds(pl.multiple_of(tile * TILE, TILE), TILE)


def feat_at(tile):
    return pl.ds(pl.multiple_of(tile * FEAT, FEAT), FEAT)


def target_terms(feat, values):
    smooth, front = values[:, : 2 * TILE], values[:, 2 * TILE : 4 * TILE]
    terms = lax.dot_general(
        jnp.concatenate([feat, feat], axis=1),
        jnp.concatenate([smooth, front], axis=0),
        (((1,), (1,)), ((), ())),
        preferred_element_type=jnp.float32,
    )
    return add_pieces(terms)


def source_terms(feat, values):
    high = jnp.concatenate([values[:, :TILE], values[:, 4 * TILE : 5 * TILE]], axis=1)
    low = jnp.concatenate([values[:, TILE : 2 * TILE], values[:, 5 * TILE :]], axis=1)
    both = jnp.concatenate([high, low], axis=0)
    terms = jnp.dot(jnp.concatenate([feat, feat], axis=1), both, preferred_element_type=jnp.float32)
    return add_pieces(terms)


def own_kernel(block, left, right, feat, sums, origin_ref, *scratch):
    products, pieces = scratch[:STEPS], scratch[STEPS : 2 * STEPS]
    stages, copied = scratch[2 * STEPS : -1], scratch[-1]
    copied[: block.shape[0], :] = block[...]
    tiles = block.shape[0] // ROWS
    rows = row_ids()
    total = block[0:ROWS, :]
    for tile in range(1, tiles):
        total = total + block[tile * ROWS : (tile + 1) * ROWS, :]
    origin = jnp.sum(total, axis=1, keepdims=True) * (1.0 / (tiles * TILE))
    origin = jnp.where(rows < 3, jnp.broadcast_to(origin, (ROWS, TILE)), 0.0)
    origin_ref[...] = origin
    description = describe(lambda row: copied[pl.ds(row, tiles, stride=ROWS), :], origin)
    stage_features(stages[0], 0, tiles, *description[:2])
    stage_target(stages[1:3], 0, tiles, description)
    stage_source(stages[3:], 0, tiles, description)
    for tile in range(tiles):
        staged = [ref[tile * ROWS : (tile + 1) * ROWS, :] for ref in stages]
        feat[tile * FEAT : (tile + 1) * FEAT, :] = features(staged[0], rows)
        left[tile * TILE : (tile + 1) * TILE, :] = target_side(*staged[1:3], rows)
        right[tile * TERMS : (tile + 1) * TERMS, :] = source_side(*staged[3:], rows)
    for step in range(tiles + 2 * LEAD):
        if step < tiles:
            target, source = left[step * TILE : (step + 1) * TILE, :], right[step * TERMS : (step + 1) * TERMS, :]
            products[step % STEPS][...] = jnp.dot(target, source, preferred_element_type=jnp.float32)
        if LEAD <= step < tiles + LEAD:
            evaluate(products[(step - LEAD) % STEPS], pieces[(step - LEAD) % STEPS])
        if step >= 2 * LEAD:
            tile = step - 2 * LEAD
            terms = target_terms(feat[tile * FEAT : (tile + 1) * FEAT, :], pieces[tile % STEPS])
            sums[tile * ROWS : (tile + 1) * ROWS, :] = terms


def join_kernel(*refs):
    out, start = refs[-1], 0
    for ref in refs[:-1]:
        out[start : start + ref.shape[0], :] = ref[...]
        start += ref.shape[0]


def pair_kernel(nrows, ncols, tiles, where_ref, slots_ref, *refs):
    own_block, own_left, own_right, own_feat, own_sums, origin_ref = refs[:6]
    refs = refs[6:]
    halves = nrows // 2
    row_ins, far_ins, near_in, refs = refs[: ncols - 1], refs[ncols - 1 : ncols + halves - 2], refs[ncols + halves - 2], refs[ncols + halves - 1 :]
    row_outs, col_outs, scratch = refs[:ncols], refs[ncols : ncols + halves], refs[ncols + halves :]
    left, right, row_feat, col_feat = scratch[:4]
    row_sum, col_sum = scratch[4:6], scratch[6:8]
    row_stage, col_stage = scratch[8:11], scratch[11:16]
    came, done = scratch[16:18]
    products, pieces = scratch[18 : 18 + STEPS], scratch[18 + STEPS :]
    per = tiles * ROWS
    rows = row_ids()
    my_row, my_col = where_ref[0], where_ref[1]
    count = where_ref[2]
    for number, ref in enumerate((own_block, *row_ins, *far_ins)):
        came[number * per : (number + 1) * per, :] = ref[...]
    near = ncols + halves - 1
    came[near * per : (near + halves) * per, :] = near_in[...]
    row_sources = [(k, k * per) for k in range(1, ncols)]
    col_sources = [(2 * m, (ncols - 1 + m) * per) for m in range(1, halves)]
    col_sources += [(2 * m + 1, (near + m) * per) for m in range(halves)]
    origin = origin_ref[...]

    for ref in (*row_sum, *col_sum):
        ref[...] = jnp.zeros_like(ref)
    for k in range(STEPS - LEAD, STEPS):
        pieces[k][...] = jnp.zeros_like(pieces[k])
    for feat, me in ((row_feat, my_col), (col_feat, my_row)):
        feat[pl.ds(pl.multiple_of(me * tiles * FEAT, tiles * FEAT), tiles * FEAT), :] = own_feat[...]
    for k, ref in enumerate(row_sum):
        ref[pl.ds(pl.multiple_of(my_col * per, per), per), :] = own_sums[:, k * TILE : (k + 1) * TILE]
    left[pl.ds(pl.multiple_of(my_col * tiles * TILE, tiles * TILE), tiles * TILE), :] = own_left[...]
    right[pl.ds(pl.multiple_of(my_row * tiles * TERMS, tiles * TERMS), tiles * TERMS), :] = own_right[...]

    def rows_of(ref, start):
        return lambda row: ref[pl.ds(start + row, tiles, stride=ROWS), :]

    for number, (_, start) in enumerate(row_sources):
        description = describe(rows_of(came, start), origin)
        stage_features(row_stage[0], number * per, tiles, *description[:2])
        stage_target(row_stage[1:], number * per, tiles, description)
    for number, (_, start) in enumerate(col_sources):
        description = describe(rows_of(came, start), origin)
        stage_features(col_stage[0], number * per, tiles, *description[:2])
        stage_source(col_stage[1:], number * per, tiles, description)

    def prepare(step, carry):
        for number, (k, _) in enumerate(row_sources):
            tile = (my_col ^ k) * tiles + step
            staged = [ref[pl.ds(pl.multiple_of(number * per + step * ROWS, ROWS), ROWS), :] for ref in row_stage]
            row_feat[feat_at(tile), :] = features(staged[0], rows)
            left[wide_at(tile), :] = target_side(*staged[1:], rows)
        for number, (k, _) in enumerate(col_sources):
            tile = (my_row ^ k) * tiles + step
            staged = [ref[pl.ds(pl.multiple_of(number * per + step * ROWS, ROWS), ROWS), :] for ref in col_stage]
            col_feat[feat_at(tile), :] = features(staged[0], rows)
            right[term_at(tile), :] = source_side(*staged[1:], rows)
        return carry

    lax.fori_loop(0, tiles, prepare, 0, unroll=8)

    last = slots_ref.shape[1] - 1

    def multiply(slot, out):
        slot = jnp.minimum(slot, last)
        tgt, src = slots_ref[0, slot], slots_ref[1, slot]
        out[...] = jnp.dot(left[wide_at(tgt), :], right[term_at(src), :], preferred_element_type=jnp.float32)

    def add_up(slot, values):
        kept = jnp.clip(slot, 0, last)
        tgt, src = slots_ref[0, kept], slots_ref[1, kept]
        own = (tgt // tiles == my_col) & (src // tiles == my_row) & (tgt % tiles == src % tiles)
        alive = jnp.where((slot >= tiles) & (slot < count), 1.0, 0.0)
        react = jnp.where(own, 0.0, alive)
        to_target = alive * target_terms(col_feat[feat_at(src), :], values)
        to_source = react * source_terms(row_feat[feat_at(tgt), :], values)
        for k in range(2):
            row_sum[k][tile_at(tgt), :] += to_target[:, k * TILE : (k + 1) * TILE]
            col_sum[k][tile_at(src), :] += to_source[:, k * TILE : (k + 1) * TILE]

    for k in range(LEAD):
        multiply(tiles + k, products[k])
    loops = (count - tiles + STEPS - 1) // STEPS

    def visit(step, carry):
        for k in range(STEPS):
            slot = tiles + step * STEPS + k
            multiply(slot + LEAD, products[(k + LEAD) % STEPS])
            evaluate(products[k], pieces[k])
            add_up(slot - LEAD, pieces[(k - LEAD) % STEPS])
        return carry

    lax.fori_loop(0, loops, visit, 0)
    for k in range(LEAD):
        add_up(tiles + loops * STEPS - LEAD + k, pieces[STEPS - LEAD + k])

    row_results = [(k, row_outs[k], 0) for k in range(ncols)]
    col_results = [(k, col_outs[k // 2], k % 2 * per) for k in range(nrows)]
    number = 0
    for results, sources, sums, me in (
        (row_results, row_sources, row_sum, my_col),
        (col_results, col_sources, col_sum, my_row),
    ):
        starts = dict(sources) | {0: 0}
        for k, result, start in results:
            base = pl.multiple_of((me ^ k) * per, per)
            values = finish_block(rows_of(came, starts[k]), *(rows_of(ref, base) for ref in sums), origin)
            put_rows(done, number * per, tiles, numbered(0, values))
            result[start : start + per, :] = done[number * per : (number + 1) * per, :]
            number += 1


def halve_kernel(*refs):
    keep, send = refs[-2:]
    half = keep.shape[0]
    total = refs[0][...]
    for ref in refs[1:-2]:
        total = total + ref[...]
    keep[...] = total[:half, :]
    send[...] = total[half:, :]


def total_kernel(*refs):
    vel_ref, str_ref = refs[-2:]
    tiles = vel_ref.shape[1] // TILE
    for tile in range(tiles):
        at = slice(tile * ROWS, (tile + 1) * ROWS)
        total = refs[0][at, :]
        for ref in refs[1:-2]:
            total = total + ref[at, :]
        vel_ref[:, tile * TILE : (tile + 1) * TILE] = total[0:3, :]
        str_ref[:, tile * TILE : (tile + 1) * TILE] = total[3:6, :]


def shards(positions, strengths, cores, order, tile_counts, pair_slots, pair_count):
    tiles = tile_counts.shape[0]
    per_dev = tiles * TILE
    nrows = lax.axis_size("row")
    ncols = lax.axis_size("col")
    halves = nrows // 2
    assert nrows == 2 * halves and nrows & (nrows - 1) == 0 and ncols & (ncols - 1) == 0
    row_tiles, col_tiles = ncols * tiles, nrows * tiles
    smem = pl.BlockSpec(memory_space=pltpu.SMEM)
    vmem = pl.BlockSpec(memory_space=pltpu.VMEM)
    hbm = pl.BlockSpec(memory_space=pltpu.HBM)
    params = pltpu.CompilerParams(vmem_limit_bytes=VMEM_BYTES)

    def blocks(count):
        return jax.ShapeDtypeStruct((count * tiles * ROWS, TILE), jnp.float32)

    def in_hbm(value):
        return pltpu.with_memory_space_constraint(value, pltpu.HBM)

    inputs = (tile_counts, positions, strengths, cores.reshape(1, per_dev), order.reshape(1, per_dev), pair_slots)
    packed, slots = pl.pallas_call(
        pack_kernel,
        out_shape=[blocks(1), jax.ShapeDtypeStruct(pair_slots.shape, jnp.int32)],
        in_specs=[hbm] * len(inputs),
        out_specs=[vmem, smem],
        scratch_shapes=[
            pltpu.VMEM((ROWS, per_dev), jnp.float32),
            pltpu.VMEM((1, per_dev), jnp.int32),
            pltpu.SMEM(tile_counts.shape, jnp.int32),
            pltpu.SemaphoreType.DMA((len(inputs),)),
        ],
        compiler_params=params,
        name="pack",
    )(*map(in_hbm, inputs))

    def swap(value, axis, size, k):
        return lax.ppermute(value, axis, [(d, d ^ k) for d in range(size)])

    def strided(count):
        return pltpu.VMEM(((count * tiles + 1) * ROWS, TILE), jnp.float32)

    phases = [pltpu.VMEM((TILE, 4 * TILE), jnp.float32)] * STEPS + [pltpu.VMEM((TILE, 6 * TILE), jnp.bfloat16)] * STEPS
    own = pl.pallas_call(
        own_kernel,
        out_shape=[
            jax.ShapeDtypeStruct((per_dev, TERMS), jnp.bfloat16),
            jax.ShapeDtypeStruct((tiles * TERMS, 4 * TILE), jnp.bfloat16),
            jax.ShapeDtypeStruct((tiles * FEAT, TILE), jnp.bfloat16),
            jax.ShapeDtypeStruct((tiles * ROWS, 2 * TILE), jnp.float32),
            jax.ShapeDtypeStruct((ROWS, TILE), jnp.float32),
        ],
        in_specs=[vmem],
        out_specs=[vmem] * 5,
        scratch_shapes=phases + [strided(1)] * 8,
        compiler_params=params,
        cost_estimate=pl.CostEstimate(flops=tiles * 300 * TILE * TILE, bytes_accessed=2**21, transcendentals=0),
        name="own",
    )(packed)

    far = [swap(packed, "row", nrows, 2 * m) for m in range(1, halves)]
    from_row = [swap(packed, "col", ncols, k) for k in range(1, ncols)]
    joined = pl.pallas_call(
        join_kernel,
        out_shape=blocks(halves),
        in_specs=[vmem] * halves,
        out_specs=vmem,
        compiler_params=params,
        name="join",
    )(packed, *far)
    near = swap(joined, "row", nrows, 1)

    where = jnp.stack([lax.axis_index("row"), lax.axis_index("col"), pair_count[0]]).astype(jnp.int32)
    sums = pl.pallas_call(
        functools.partial(pair_kernel, nrows, ncols, tiles),
        out_shape=[blocks(1)] * ncols + [blocks(2)] * halves,
        in_specs=[smem] * 2 + [vmem] * (5 + ncols + halves),
        out_specs=[vmem] * (ncols + halves),
        scratch_shapes=[
            pltpu.VMEM((row_tiles * TILE, TERMS), jnp.bfloat16),
            pltpu.VMEM((col_tiles * TERMS, 4 * TILE), jnp.bfloat16),
            pltpu.VMEM((row_tiles * FEAT, TILE), jnp.bfloat16),
            pltpu.VMEM((col_tiles * FEAT, TILE), jnp.bfloat16),
            *[strided(ncols)] * 2,
            *[strided(nrows)] * 2,
            *[strided(ncols - 1)] * 3,
            *[strided(nrows - 1)] * 5,
            strided(ncols + nrows - 1),
            strided(ncols + nrows),
            *phases,
        ],
        compiler_params=params,
        name="pairs",
    )(where, slots, packed, *own, *from_row, *far, near)

    far_back = [swap(sums[ncols + m], "row", nrows, 2 * m) for m in range(1, halves)]
    row_back = [swap(sums[k], "col", ncols, k) for k in reversed(range(1, ncols))]
    keep, send = pl.pallas_call(
        halve_kernel,
        out_shape=[blocks(1)] * 2,
        in_specs=[vmem] * halves,
        out_specs=[vmem] * 2,
        compiler_params=params,
        name="halve",
    )(sums[ncols], *far_back)
    parts = [sums[0], keep, *row_back, swap(send, "row", nrows, 1)]
    velocity, stretching = pl.pallas_call(
        total_kernel,
        out_shape=[jax.ShapeDtypeStruct((3, per_dev), jnp.float32)] * 2,
        in_specs=[vmem] * len(parts),
        out_specs=[vmem, vmem],
        compiler_params=params,
        name="totals",
    )(*parts)
    return velocity, stretching


def solution(mesh):
    whole = ("groups", "row", "col")
    in_specs = (P(None, whole), P(None, whole), P(whole), P(whole), P(whole), P(None, whole), P(whole))
    out_specs = (P(None, whole), P(None, whole))
    return jax.shard_map(shards, mesh=mesh, in_specs=in_specs, out_specs=out_specs, check_vma=False)
```

```python
import functools
import math

import jax
import jax.numpy as jnp
from jax import lax
from jax.experimental import pallas as pl
from jax.experimental.pallas import tpu as pltpu
from jax.sharding import PartitionSpec as P

TILE = 128
ROWS = 8
STEPS = 14
LEAD = 2
FEAT = 32
TERMS = 64
VMEM_BYTES = 48 * 1024 * 1024

biot_factor = -1.0 / (4.0 * math.pi)


def row_ids(count=ROWS):
    return lax.broadcasted_iota(jnp.int32, (count, TILE), 0)


def roll_rows(value, shift):
    return pltpu.roll(value, shift % ROWS, 0)


def pack_kernel(
    counts_hbm, pos_hbm, str_hbm, core_hbm, order_hbm, slots_hbm,
    out_ref, slots_ref, stored, order_ref, counts_ref, arrived,
):
    tiles = order_ref.shape[1] // TILE
    pairs = (
        (pos_hbm, stored.at[0:3, :]),
        (str_hbm, stored.at[3:6, :]),
        (core_hbm, stored.at[6:7, :]),
        (order_hbm, order_ref),
        (counts_hbm, counts_ref),
        (slots_hbm, slots_ref),
    )
    copies = [pltpu.make_async_copy(src, dst, arrived.at[k]) for k, (src, dst) in enumerate(pairs)]
    for copy in copies:
        copy.start()
    stored[7:8, :] = jnp.zeros((1, stored.shape[1]), jnp.float32)
    for copy in copies:
        copy.wait()
    lane = lax.broadcasted_iota(jnp.int32, (ROWS, TILE), 1)
    rows = row_ids()
    is_strength = (rows >= 3) & (rows < 6)
    for tile in range(tiles):
        where_from = jnp.broadcast_to(order_ref[:, tile * TILE : (tile + 1) * TILE], (ROWS, TILE))
        inside = where_from & (TILE - 1)
        block = where_from >> 7
        value = jnp.zeros((ROWS, TILE), jnp.float32)
        for source in range(tiles):
            part = jnp.take_along_axis(stored[:, source * TILE : (source + 1) * TILE], inside, axis=1)
            value = jnp.where(block == source, part, value)
        live = lane < counts_ref[tile]
        value = jnp.where(is_strength & ~live, 0.0, value)
        value = jnp.where(rows == 7, live.astype(jnp.float32), value)
        out_ref[tile * ROWS : (tile + 1) * ROWS, :] = value


def split_three(value):
    first = value.astype(jnp.bfloat16).astype(jnp.float32)
    rest = value - first
    second = rest.astype(jnp.bfloat16).astype(jnp.float32)
    return first, second, rest - second


def split_two(value):
    high = value.astype(jnp.bfloat16)
    return high, (value - high.astype(jnp.float32)).astype(jnp.bfloat16)


def add_pieces(terms):
    return terms[0:ROWS, :] + (terms[ROWS : 2 * ROWS, :] + terms[2 * ROWS : 3 * ROWS, :])


def cross(left, right):
    return [left[1] * right[2] - left[2] * right[1], left[2] * right[0] - left[0] * right[2], left[0] * right[1] - left[1] * right[0]]


def describe(tile_row, origin):
    position = [tile_row(k) - origin[k : k + 1, :] for k in range(3)]
    strength = [tile_row(3 + k) for k in range(3)]
    core = tile_row(6)
    half = 0.5 * core * core
    coarse = [value.astype(jnp.bfloat16).astype(jnp.float32) for value in position]
    norm = coarse[0] * coarse[0] + coarse[1] * coarse[1] + coarse[2] * coarse[2]
    rest = [(value - near) * (value + near) for value, near in zip(position, coarse)]
    rest = rest[0] + rest[1] + rest[2] + half
    along = position[0] * strength[0] + position[1] * strength[1] + position[2] * strength[2]
    return position, strength, half, norm, rest, along


def put_rows(ref, start, tiles, values):
    for row, value in values.items():
        ref[pl.ds(start + row, tiles, stride=ROWS), :] = value


def negative(values):
    return [-value for value in values]


def numbered(first, values):
    return dict(enumerate(values, first))


def stage_features(ref, start, tiles, position, strength):
    put_rows(ref, start, tiles, numbered(0, strength + cross(position, strength)))


def stage_target(refs, start, tiles, description):
    position, strength, half, norm, rest, along = description
    put_rows(refs[0], start, tiles, numbered(0, position + strength))
    put_rows(refs[1], start, tiles, numbered(0, [norm, rest, along, half]))


def stage_source(refs, start, tiles, description):
    position, strength, half, norm, rest, along = description
    put_rows(refs[0], start, tiles, numbered(0, [-2.0 * value for value in position]) | {6: norm, 7: rest})
    put_rows(refs[1], start, tiles, numbered(3, negative(position)))
    put_rows(refs[2], start, tiles, numbered(0, negative(strength)) | {6: along})
    put_rows(refs[3], start, tiles, {6: half})


def features(tile, rows):
    value = jnp.where(rows < 6, tile, 0.0)
    return jnp.concatenate([*split_three(value), jnp.zeros_like(value)], axis=0).astype(jnp.bfloat16)


def target_side(shared, alone, rows):
    first, second, third = split_three(jnp.where(rows < 6, shared, 1.0))
    alone1, alone2, alone3 = split_three(jnp.where(rows < 4, alone, 0.0))
    both = jnp.where(rows < 4, alone1, roll_rows(alone2, 4))
    stacked = jnp.concatenate([first, both, first, first, second, second, third, alone3], axis=0)
    return stacked.astype(jnp.bfloat16).T


def source_side(dist, front, back, core, rows):
    zero = jnp.zeros_like(dist)
    one = jnp.ones_like(dist)
    values = (
        jnp.where((rows < 3) | (rows > 5), dist, 0.0),
        jnp.where((rows >= 3) & (rows < 6), front, 0.0),
        jnp.where((rows < 3) | (rows == 6), back, 0.0),
        jnp.where(rows == 6, core, 0.0),
    )
    pick = rows & 3
    picks = (jnp.where(pick < 2, one, zero), jnp.where(pick == 2, one, zero), zero, jnp.where(pick == 3, one, zero))
    blocks = []
    for value, picked in zip(values, picks):
        first, second, third = split_three(value)
        parts = [first, picked, second, third, first, second, first, picked]
        blocks.append(jnp.concatenate(parts, axis=0).astype(jnp.bfloat16))
    return jnp.concatenate(blocks, axis=1)


def finish_block(tile_row, smooth_row, grad_row, origin):
    position = [tile_row(k) - origin[k : k + 1, :] for k in range(3)]
    strength = [tile_row(3 + k) for k in range(3)]
    scale = biot_factor * tile_row(7)
    smooth = [smooth_row(k) for k in range(6)]
    grad = [grad_row(k) for k in range(6)]
    velocity = [turn - part for turn, part in zip(cross(position, smooth[:3]), smooth[3:])]
    lever = [turn - part for turn, part in zip(cross(position, grad[:3]), grad[3:])]
    stretch = [turn - 3.0 * part for turn, part in zip(cross(strength, smooth[:3]), lever)]
    return [scale * value for value in velocity + stretch]


def evaluate(products, pieces):
    for start in range(0, TILE, 16):
        at = slice(start, start + 16)
        dist, front, back, core = (products[at, k * TILE : (k + 1) * TILE] for k in range(4))
        inv = lax.rsqrt(dist)
        inv2 = inv * inv
        inv3 = inv2 * inv
        tail = core * (inv3 * inv2)
        smooth = inv3 + 1.5 * tail
        grad = inv2 * (smooth + tail)
        for k, value in enumerate((smooth, grad * front, grad * back)):
            high, low = split_two(value)
            pieces[at, 2 * k * TILE : (2 * k + 1) * TILE] = high
            pieces[at, (2 * k + 1) * TILE : (2 * k + 2) * TILE] = low


def tile_at(tile):
    return pl.ds(pl.multiple_of(tile * ROWS, ROWS), ROWS)


def term_at(tile):
    return pl.ds(pl.multiple_of(tile * TERMS, TERMS), TERMS)


def wide_at(tile):
    return pl.ds(pl.multiple_of(tile * TILE, TILE), TILE)


def feat_at(tile):
    return pl.ds(pl.multiple_of(tile * FEAT, FEAT), FEAT)


def target_terms(feat, values):
    smooth, front = values[:, : 2 * TILE], values[:, 2 * TILE : 4 * TILE]
    terms = lax.dot_general(
        jnp.concatenate([feat, feat], axis=1),
        jnp.concatenate([smooth, front], axis=0),
        (((1,), (1,)), ((), ())),
        preferred_element_type=jnp.float32,
    )
    return add_pieces(terms)


def source_terms(feat, values):
    high = jnp.concatenate([values[:, :TILE], values[:, 4 * TILE : 5 * TILE]], axis=1)
    low = jnp.concatenate([values[:, TILE : 2 * TILE], values[:, 5 * TILE :]], axis=1)
    both = jnp.concatenate([high, low], axis=0)
    terms = jnp.dot(jnp.concatenate([feat, feat], axis=1), both, preferred_element_type=jnp.float32)
    return add_pieces(terms)


def own_kernel(block, left, right, feat, sums, origin_ref, *scratch):
    products, pieces = scratch[:STEPS], scratch[STEPS : 2 * STEPS]
    stages, copied = scratch[2 * STEPS : -1], scratch[-1]
    copied[: block.shape[0], :] = block[...]
    tiles = block.shape[0] // ROWS
    rows = row_ids()
    total = block[0:ROWS, :]
    for tile in range(1, tiles):
        total = total + block[tile * ROWS : (tile + 1) * ROWS, :]
    origin = jnp.sum(total, axis=1, keepdims=True) * (1.0 / (tiles * TILE))
    origin = jnp.where(rows < 3, jnp.broadcast_to(origin, (ROWS, TILE)), 0.0)
    origin_ref[...] = origin
    description = describe(lambda row: copied[pl.ds(row, tiles, stride=ROWS), :], origin)
    stage_features(stages[0], 0, tiles, *description[:2])
    stage_target(stages[1:3], 0, tiles, description)
    stage_source(stages[3:], 0, tiles, description)
    for tile in range(tiles):
        staged = [ref[tile * ROWS : (tile + 1) * ROWS, :] for ref in stages]
        feat[tile * FEAT : (tile + 1) * FEAT, :] = features(staged[0], rows)
        left[tile * TILE : (tile + 1) * TILE, :] = target_side(*staged[1:3], rows)
        right[tile * TERMS : (tile + 1) * TERMS, :] = source_side(*staged[3:], rows)
    for step in range(tiles + 2 * LEAD):
        if step < tiles:
            target, source = left[step * TILE : (step + 1) * TILE, :], right[step * TERMS : (step + 1) * TERMS, :]
            products[step % STEPS][...] = jnp.dot(target, source, preferred_element_type=jnp.float32)
        if LEAD <= step < tiles + LEAD:
            evaluate(products[(step - LEAD) % STEPS], pieces[(step - LEAD) % STEPS])
        if step >= 2 * LEAD:
            tile = step - 2 * LEAD
            terms = target_terms(feat[tile * FEAT : (tile + 1) * FEAT, :], pieces[tile % STEPS])
            sums[tile * ROWS : (tile + 1) * ROWS, :] = terms


def join_kernel(*refs):
    out, start = refs[-1], 0
    for ref in refs[:-1]:
        out[start : start + ref.shape[0], :] = ref[...]
        start += ref.shape[0]


def pair_kernel(nrows, ncols, tiles, where_ref, slots_ref, *refs):
    own_block, own_left, own_right, own_feat, own_sums, origin_ref = refs[:6]
    refs = refs[6:]
    halves = nrows // 2
    row_ins, far_ins, near_in, refs = refs[: ncols - 1], refs[ncols - 1 : ncols + halves - 2], refs[ncols + halves - 2], refs[ncols + halves - 1 :]
    row_outs, col_outs, scratch = refs[:ncols], refs[ncols : ncols + halves], refs[ncols + halves :]
    left, right, row_feat, col_feat = scratch[:4]
    row_sum, col_sum = scratch[4:6], scratch[6:8]
    row_stage, col_stage = scratch[8:11], scratch[11:16]
    came, done = scratch[16:18]
    products, pieces = scratch[18 : 18 + STEPS], scratch[18 + STEPS :]
    per = tiles * ROWS
    rows = row_ids()
    my_row, my_col = where_ref[0], where_ref[1]
    count = where_ref[2]
    for number, ref in enumerate((own_block, *row_ins, *far_ins)):
        came[number * per : (number + 1) * per, :] = ref[...]
    near = ncols + halves - 1
    came[near * per : (near + halves) * per, :] = near_in[...]
    row_sources = [(k, k * per) for k in range(1, ncols)]
    col_sources = [(2 * m, (ncols - 1 + m) * per) for m in range(1, halves)]
    col_sources += [(2 * m + 1, (near + m) * per) for m in range(halves)]
    origin = origin_ref[...]

    for ref in (*row_sum, *col_sum):
        ref[...] = jnp.zeros_like(ref)
    for k in range(STEPS - LEAD, STEPS):
        pieces[k][...] = jnp.zeros_like(pieces[k])
    for feat, me in ((row_feat, my_col), (col_feat, my_row)):
        feat[pl.ds(pl.multiple_of(me * tiles * FEAT, tiles * FEAT), tiles * FEAT), :] = own_feat[...]
    for k, ref in enumerate(row_sum):
        ref[pl.ds(pl.multiple_of(my_col * per, per), per), :] = own_sums[:, k * TILE : (k + 1) * TILE]
    left[pl.ds(pl.multiple_of(my_col * tiles * TILE, tiles * TILE), tiles * TILE), :] = own_left[...]
    right[pl.ds(pl.multiple_of(my_row * tiles * TERMS, tiles * TERMS), tiles * TERMS), :] = own_right[...]

    def rows_of(ref, start):
        return lambda row: ref[pl.ds(start + row, tiles, stride=ROWS), :]

    for number, (_, start) in enumerate(row_sources):
        description = describe(rows_of(came, start), origin)
        stage_features(row_stage[0], number * per, tiles, *description[:2])
        stage_target(row_stage[1:], number * per, tiles, description)
    for number, (_, start) in enumerate(col_sources):
        description = describe(rows_of(came, start), origin)
        stage_features(col_stage[0], number * per, tiles, *description[:2])
        stage_source(col_stage[1:], number * per, tiles, description)

    def prepare(step, carry):
        for number, (k, _) in enumerate(row_sources):
            tile = (my_col ^ k) * tiles + step
            staged = [ref[pl.ds(pl.multiple_of(number * per + step * ROWS, ROWS), ROWS), :] for ref in row_stage]
            row_feat[feat_at(tile), :] = features(staged[0], rows)
            left[wide_at(tile), :] = target_side(*staged[1:], rows)
        for number, (k, _) in enumerate(col_sources):
            tile = (my_row ^ k) * tiles + step
            staged = [ref[pl.ds(pl.multiple_of(number * per + step * ROWS, ROWS), ROWS), :] for ref in col_stage]
            col_feat[feat_at(tile), :] = features(staged[0], rows)
            right[term_at(tile), :] = source_side(*staged[1:], rows)
        return carry

    lax.fori_loop(0, tiles, prepare, 0, unroll=8)

    last = slots_ref.shape[1] - 1

    def multiply(slot, out):
        slot = jnp.minimum(slot, last)
        tgt, src = slots_ref[0, slot], slots_ref[1, slot]
        out[...] = jnp.dot(left[wide_at(tgt), :], right[term_at(src), :], preferred_element_type=jnp.float32)

    def add_up(slot, values):
        kept = jnp.clip(slot, 0, last)
        tgt, src = slots_ref[0, kept], slots_ref[1, kept]
        own = (tgt // tiles == my_col) & (src // tiles == my_row) & (tgt % tiles == src % tiles)
        alive = jnp.where((slot >= tiles) & (slot < count), 1.0, 0.0)
        react = jnp.where(own, 0.0, alive)
        to_target = alive * target_terms(col_feat[feat_at(src), :], values)
        to_source = react * source_terms(row_feat[feat_at(tgt), :], values)
        for k in range(2):
            row_sum[k][tile_at(tgt), :] += to_target[:, k * TILE : (k + 1) * TILE]
            col_sum[k][tile_at(src), :] += to_source[:, k * TILE : (k + 1) * TILE]

    for k in range(LEAD):
        multiply(tiles + k, products[k])
    loops = (count - tiles + STEPS - 1) // STEPS

    def visit(step, carry):
        for k in range(STEPS):
            slot = tiles + step * STEPS + k
            multiply(slot + LEAD, products[(k + LEAD) % STEPS])
            evaluate(products[k], pieces[k])
            add_up(slot - LEAD, pieces[(k - LEAD) % STEPS])
        return carry

    lax.fori_loop(0, loops, visit, 0)
    for k in range(LEAD):
        add_up(tiles + loops * STEPS - LEAD + k, pieces[STEPS - LEAD + k])

    row_results = [(k, row_outs[k], 0) for k in range(ncols)]
    col_results = [(k, col_outs[k // 2], k % 2 * per) for k in range(nrows)]
    number = 0
    for results, sources, sums, me in (
        (row_results, row_sources, row_sum, my_col),
        (col_results, col_sources, col_sum, my_row),
    ):
        starts = dict(sources) | {0: 0}
        for k, result, start in results:
            base = pl.multiple_of((me ^ k) * per, per)
            values = finish_block(rows_of(came, starts[k]), *(rows_of(ref, base) for ref in sums), origin)
            put_rows(done, number * per, tiles, numbered(0, values))
            result[start : start + per, :] = done[number * per : (number + 1) * per, :]
            number += 1


def halve_kernel(*refs):
    keep, send = refs[-2:]
    half = keep.shape[0]
    total = refs[0][...]
    for ref in refs[1:-2]:
        total = total + ref[...]
    keep[...] = total[:half, :]
    send[...] = total[half:, :]


def total_kernel(*refs):
    vel_ref, str_ref = refs[-2:]
    tiles = vel_ref.shape[1] // TILE
    for tile in range(tiles):
        at = slice(tile * ROWS, (tile + 1) * ROWS)
        total = refs[0][at, :]
        for ref in refs[1:-2]:
            total = total + ref[at, :]
        vel_ref[:, tile * TILE : (tile + 1) * TILE] = total[0:3, :]
        str_ref[:, tile * TILE : (tile + 1) * TILE] = total[3:6, :]


def shards(positions, strengths, cores, order, tile_counts, pair_slots, pair_count):
    tiles = tile_counts.shape[0]
    per_dev = tiles * TILE
    nrows = lax.axis_size("row")
    ncols = lax.axis_size("col")
    halves = nrows // 2
    assert nrows == 2 * halves and nrows & (nrows - 1) == 0 and ncols & (ncols - 1) == 0
    row_tiles, col_tiles = ncols * tiles, nrows * tiles
    smem = pl.BlockSpec(memory_space=pltpu.SMEM)
    vmem = pl.BlockSpec(memory_space=pltpu.VMEM)
    hbm = pl.BlockSpec(memory_space=pltpu.HBM)
    params = pltpu.CompilerParams(vmem_limit_bytes=VMEM_BYTES)

    def blocks(count):
        return jax.ShapeDtypeStruct((count * tiles * ROWS, TILE), jnp.float32)

    def in_hbm(value):
        return pltpu.with_memory_space_constraint(value, pltpu.HBM)

    inputs = (tile_counts, positions, strengths, cores.reshape(1, per_dev), order.reshape(1, per_dev), pair_slots)
    packed, slots = pl.pallas_call(
        pack_kernel,
        out_shape=[blocks(1), jax.ShapeDtypeStruct(pair_slots.shape, jnp.int32)],
        in_specs=[hbm] * len(inputs),
        out_specs=[vmem, smem],
        scratch_shapes=[
            pltpu.VMEM((ROWS, per_dev), jnp.float32),
            pltpu.VMEM((1, per_dev), jnp.int32),
            pltpu.SMEM(tile_counts.shape, jnp.int32),
            pltpu.SemaphoreType.DMA((len(inputs),)),
        ],
        compiler_params=params,
        name="pack",
    )(*map(in_hbm, inputs))

    def swap(value, axis, size, k):
        return lax.ppermute(value, axis, [(d, d ^ k) for d in range(size)])

    def strided(count):
        return pltpu.VMEM(((count * tiles + 1) * ROWS, TILE), jnp.float32)

    phases = [pltpu.VMEM((TILE, 4 * TILE), jnp.float32)] * STEPS + [pltpu.VMEM((TILE, 6 * TILE), jnp.bfloat16)] * STEPS
    own = pl.pallas_call(
        own_kernel,
        out_shape=[
            jax.ShapeDtypeStruct((per_dev, TERMS), jnp.bfloat16),
            jax.ShapeDtypeStruct((tiles * TERMS, 4 * TILE), jnp.bfloat16),
            jax.ShapeDtypeStruct((tiles * FEAT, TILE), jnp.bfloat16),
            jax.ShapeDtypeStruct((tiles * ROWS, 2 * TILE), jnp.float32),
            jax.ShapeDtypeStruct((ROWS, TILE), jnp.float32),
        ],
        in_specs=[vmem],
        out_specs=[vmem] * 5,
        scratch_shapes=phases + [strided(1)] * 8,
        compiler_params=params,
        cost_estimate=pl.CostEstimate(flops=tiles * 300 * TILE * TILE, bytes_accessed=2**21, transcendentals=0),
        name="own",
    )(packed)

    far = [swap(packed, "row", nrows, 2 * m) for m in range(1, halves)]
    from_row = [swap(packed, "col", ncols, k) for k in range(1, ncols)]
    joined = pl.pallas_call(
        join_kernel,
        out_shape=blocks(halves),
        in_specs=[vmem] * halves,
        out_specs=vmem,
        compiler_params=params,
        name="join",
    )(packed, *far)
    near = swap(joined, "row", nrows, 1)

    where = jnp.stack([lax.axis_index("row"), lax.axis_index("col"), pair_count[0]]).astype(jnp.int32)
    sums = pl.pallas_call(
        functools.partial(pair_kernel, nrows, ncols, tiles),
        out_shape=[blocks(1)] * ncols + [blocks(2)] * halves,
        in_specs=[smem] * 2 + [vmem] * (5 + ncols + halves),
        out_specs=[vmem] * (ncols + halves),
        scratch_shapes=[
            pltpu.VMEM((row_tiles * TILE, TERMS), jnp.bfloat16),
            pltpu.VMEM((col_tiles * TERMS, 4 * TILE), jnp.bfloat16),
            pltpu.VMEM((row_tiles * FEAT, TILE), jnp.bfloat16),
            pltpu.VMEM((col_tiles * FEAT, TILE), jnp.bfloat16),
            *[strided(ncols)] * 2,
            *[strided(nrows)] * 2,
            *[strided(ncols - 1)] * 3,
            *[strided(nrows - 1)] * 5,
            strided(ncols + nrows - 1),
            strided(ncols + nrows),
            *phases,
        ],
        compiler_params=params,
        name="pairs",
    )(where, slots, packed, *own, *from_row, *far, near)

    far_back = [swap(sums[ncols + m], "row", nrows, 2 * m) for m in range(1, halves)]
    row_back = [swap(sums[k], "col", ncols, k) for k in reversed(range(1, ncols))]
    keep, send = pl.pallas_call(
        halve_kernel,
        out_shape=[blocks(1)] * 2,
        in_specs=[vmem] * halves,
        out_specs=[vmem] * 2,
        compiler_params=params,
        name="halve",
    )(sums[ncols], *far_back)
    parts = [sums[0], keep, *row_back, swap(send, "row", nrows, 1)]
    velocity, stretching = pl.pallas_call(
        total_kernel,
        out_shape=[jax.ShapeDtypeStruct((3, per_dev), jnp.float32)] * 2,
        in_specs=[vmem] * len(parts),
        out_specs=[vmem, vmem],
        compiler_params=params,
        name="totals",
    )(*parts)
    return velocity, stretching


def solution(mesh):
    whole = ("groups", "row", "col")
    in_specs = (P(None, whole), P(None, whole), P(whole), P(whole), P(whole), P(None, whole), P(whole))
    out_specs = (P(None, whole), P(None, whole))
    return jax.shard_map(shards, mesh=mesh, in_specs=in_specs, out_specs=out_specs, check_vma=False)
```

```python
import functools
import math

import jax
import jax.numpy as jnp
from jax import lax
from jax.experimental import pallas as pl
from jax.experimental.pallas import tpu as pltpu
from jax.sharding import PartitionSpec as P

TILE = 128
ROWS = 8
STEPS = 28
LEAD = 2
FEAT = 32
TERMS = 64
VMEM_BYTES = 48 * 1024 * 1024

biot_factor = -1.0 / (4.0 * math.pi)


def row_ids(count=ROWS):
    return lax.broadcasted_iota(jnp.int32, (count, TILE), 0)


def roll_rows(value, shift):
    return pltpu.roll(value, shift % ROWS, 0)


def pack_kernel(
    counts_hbm, pos_hbm, str_hbm, core_hbm, order_hbm, slots_hbm,
    out_ref, slots_ref, stored, order_ref, counts_ref, arrived,
):
    tiles = order_ref.shape[1] // TILE
    pairs = (
        (pos_hbm, stored.at[0:3, :]),
        (str_hbm, stored.at[3:6, :]),
        (core_hbm, stored.at[6:7, :]),
        (order_hbm, order_ref),
        (counts_hbm, counts_ref),
        (slots_hbm, slots_ref),
    )
    copies = [pltpu.make_async_copy(src, dst, arrived.at[k]) for k, (src, dst) in enumerate(pairs)]
    for copy in copies:
        copy.start()
    stored[7:8, :] = jnp.zeros((1, stored.shape[1]), jnp.float32)
    for copy in copies:
        copy.wait()
    lane = lax.broadcasted_iota(jnp.int32, (ROWS, TILE), 1)
    rows = row_ids()
    is_strength = (rows >= 3) & (rows < 6)
    for tile in range(tiles):
        where_from = jnp.broadcast_to(order_ref[:, tile * TILE : (tile + 1) * TILE], (ROWS, TILE))
        inside = where_from & (TILE - 1)
        block = where_from >> 7
        value = jnp.zeros((ROWS, TILE), jnp.float32)
        for source in range(tiles):
            part = jnp.take_along_axis(stored[:, source * TILE : (source + 1) * TILE], inside, axis=1)
            value = jnp.where(block == source, part, value)
        live = lane < counts_ref[tile]
        value = jnp.where(is_strength & ~live, 0.0, value)
        value = jnp.where(rows == 7, live.astype(jnp.float32), value)
        out_ref[tile * ROWS : (tile + 1) * ROWS, :] = value


def split_three(value):
    first = value.astype(jnp.bfloat16).astype(jnp.float32)
    rest = value - first
    second = rest.astype(jnp.bfloat16).astype(jnp.float32)
    return first, second, rest - second


def split_two(value):
    high = value.astype(jnp.bfloat16)
    return high, (value - high.astype(jnp.float32)).astype(jnp.bfloat16)


def add_pieces(terms):
    return terms[0:ROWS, :] + (terms[ROWS : 2 * ROWS, :] + terms[2 * ROWS : 3 * ROWS, :])


def cross(left, right):
    return [left[1] * right[2] - left[2] * right[1], left[2] * right[0] - left[0] * right[2], left[0] * right[1] - left[1] * right[0]]


def describe(tile_row, origin):
    position = [tile_row(k) - origin[k : k + 1, :] for k in range(3)]
    strength = [tile_row(3 + k) for k in range(3)]
    core = tile_row(6)
    half = 0.5 * core * core
    coarse = [value.astype(jnp.bfloat16).astype(jnp.float32) for value in position]
    norm = coarse[0] * coarse[0] + coarse[1] * coarse[1] + coarse[2] * coarse[2]
    rest = [(value - near) * (value + near) for value, near in zip(position, coarse)]
    rest = rest[0] + rest[1] + rest[2] + half
    along = position[0] * strength[0] + position[1] * strength[1] + position[2] * strength[2]
    return position, strength, half, norm, rest, along


def put_rows(ref, start, tiles, values):
    for row, value in values.items():
        ref[pl.ds(start + row, tiles, stride=ROWS), :] = value


def negative(values):
    return [-value for value in values]


def numbered(first, values):
    return dict(enumerate(values, first))


def stage_features(ref, start, tiles, position, strength):
    put_rows(ref, start, tiles, numbered(0, strength + cross(position, strength)))


def stage_target(refs, start, tiles, description):
    position, strength, half, norm, rest, along = description
    put_rows(refs[0], start, tiles, numbered(0, position + strength))
    put_rows(refs[1], start, tiles, numbered(0, [norm, rest, along, half]))


def stage_source(refs, start, tiles, description):
    position, strength, half, norm, rest, along = description
    put_rows(refs[0], start, tiles, numbered(0, [-2.0 * value for value in position]) | {6: norm, 7: rest})
    put_rows(refs[1], start, tiles, numbered(3, negative(position)))
    put_rows(refs[2], start, tiles, numbered(0, negative(strength)) | {6: along})
    put_rows(refs[3], start, tiles, {6: half})


def features(tile, rows):
    value = jnp.where(rows < 6, tile, 0.0)
    return jnp.concatenate([*split_three(value), jnp.zeros_like(value)], axis=0).astype(jnp.bfloat16)


def target_side(shared, alone, rows):
    first, second, third = split_three(jnp.where(rows < 6, shared, 1.0))
    alone1, alone2, alone3 = split_three(jnp.where(rows < 4, alone, 0.0))
    both = jnp.where(rows < 4, alone1, roll_rows(alone2, 4))
    stacked = jnp.concatenate([first, both, first, first, second, second, third, alone3], axis=0)
    return stacked.astype(jnp.bfloat16).T


def source_side(dist, front, back, core, rows):
    zero = jnp.zeros_like(dist)
    one = jnp.ones_like(dist)
    values = (
        jnp.where((rows < 3) | (rows > 5), dist, 0.0),
        jnp.where((rows >= 3) & (rows < 6), front, 0.0),
        jnp.where((rows < 3) | (rows == 6), back, 0.0),
        jnp.where(rows == 6, core, 0.0),
    )
    pick = rows & 3
    picks = (jnp.where(pick < 2, one, zero), jnp.where(pick == 2, one, zero), zero, jnp.where(pick == 3, one, zero))
    blocks = []
    for value, picked in zip(values, picks):
        first, second, third = split_three(value)
        parts = [first, picked, second, third, first, second, first, picked]
        blocks.append(jnp.concatenate(parts, axis=0).astype(jnp.bfloat16))
    return jnp.concatenate(blocks, axis=1)


def finish_block(tile_row, smooth_row, grad_row, origin):
    position = [tile_row(k) - origin[k : k + 1, :] for k in range(3)]
    strength = [tile_row(3 + k) for k in range(3)]
    scale = biot_factor * tile_row(7)
    smooth = [smooth_row(k) for k in range(6)]
    grad = [grad_row(k) for k in range(6)]
    velocity = [turn - part for turn, part in zip(cross(position, smooth[:3]), smooth[3:])]
    lever = [turn - part for turn, part in zip(cross(position, grad[:3]), grad[3:])]
    stretch = [turn - 3.0 * part for turn, part in zip(cross(strength, smooth[:3]), lever)]
    return [scale * value for value in velocity + stretch]


def evaluate(products, pieces):
    for start in range(0, TILE, 16):
        at = slice(start, start + 16)
        dist, front, back, core = (products[at, k * TILE : (k + 1) * TILE] for k in range(4))
        inv = lax.rsqrt(dist)
        inv2 = inv * inv
        inv3 = inv2 * inv
        tail = core * (inv3 * inv2)
        smooth = inv3 + 1.5 * tail
        grad = inv2 * (smooth + tail)
        for k, value in enumerate((smooth, grad * front, grad * back)):
            high, low = split_two(value)
            pieces[at, 2 * k * TILE : (2 * k + 1) * TILE] = high
            pieces[at, (2 * k + 1) * TILE : (2 * k + 2) * TILE] = low


def tile_at(tile):
    return pl.ds(pl.multiple_of(tile * ROWS, ROWS), ROWS)


def term_at(tile):
    return pl.ds(pl.multiple_of(tile * TERMS, TERMS), TERMS)


def wide_at(tile):
    return pl.ds(pl.multiple_of(tile * TILE, TILE), TILE)


def feat_at(tile):
    return pl.ds(pl.multiple_of(tile * FEAT, FEAT), FEAT)


def target_terms(feat, values):
    smooth, front = values[:, : 2 * TILE], values[:, 2 * TILE : 4 * TILE]
    terms = lax.dot_general(
        jnp.concatenate([feat, feat], axis=1),
        jnp.concatenate([smooth, front], axis=0),
        (((1,), (1,)), ((), ())),
        preferred_element_type=jnp.float32,
    )
    return add_pieces(terms)


def source_terms(feat, values):
    high = jnp.concatenate([values[:, :TILE], values[:, 4 * TILE : 5 * TILE]], axis=1)
    low = jnp.concatenate([values[:, TILE : 2 * TILE], values[:, 5 * TILE :]], axis=1)
    both = jnp.concatenate([high, low], axis=0)
    terms = jnp.dot(jnp.concatenate([feat, feat], axis=1), both, preferred_element_type=jnp.float32)
    return add_pieces(terms)


def own_kernel(block, left, right, feat, sums, origin_ref, *scratch):
    products, pieces = scratch[:STEPS], scratch[STEPS : 2 * STEPS]
    stages, copied = scratch[2 * STEPS : -1], scratch[-1]
    copied[: block.shape[0], :] = block[...]
    tiles = block.shape[0] // ROWS
    rows = row_ids()
    total = block[0:ROWS, :]
    for tile in range(1, tiles):
        total = total + block[tile * ROWS : (tile + 1) * ROWS, :]
    origin = jnp.sum(total, axis=1, keepdims=True) * (1.0 / (tiles * TILE))
    origin = jnp.where(rows < 3, jnp.broadcast_to(origin, (ROWS, TILE)), 0.0)
    origin_ref[...] = origin
    description = describe(lambda row: copied[pl.ds(row, tiles, stride=ROWS), :], origin)
    stage_features(stages[0], 0, tiles, *description[:2])
    stage_target(stages[1:3], 0, tiles, description)
    stage_source(stages[3:], 0, tiles, description)
    for tile in range(tiles):
        staged = [ref[tile * ROWS : (tile + 1) * ROWS, :] for ref in stages]
        feat[tile * FEAT : (tile + 1) * FEAT, :] = features(staged[0], rows)
        left[tile * TILE : (tile + 1) * TILE, :] = target_side(*staged[1:3], rows)
        right[tile * TERMS : (tile + 1) * TERMS, :] = source_side(*staged[3:], rows)
    for step in range(tiles + 2 * LEAD):
        if step < tiles:
            target, source = left[step * TILE : (step + 1) * TILE, :], right[step * TERMS : (step + 1) * TERMS, :]
            products[step % STEPS][...] = jnp.dot(target, source, preferred_element_type=jnp.float32)
        if LEAD <= step < tiles + LEAD:
            evaluate(products[(step - LEAD) % STEPS], pieces[(step - LEAD) % STEPS])
        if step >= 2 * LEAD:
            tile = step - 2 * LEAD
            terms = target_terms(feat[tile * FEAT : (tile + 1) * FEAT, :], pieces[tile % STEPS])
            sums[tile * ROWS : (tile + 1) * ROWS, :] = terms


def join_kernel(*refs):
    out, start = refs[-1], 0
    for ref in refs[:-1]:
        out[start : start + ref.shape[0], :] = ref[...]
        start += ref.shape[0]


def pair_kernel(nrows, ncols, tiles, where_ref, slots_ref, *refs):
    own_block, own_left, own_right, own_feat, own_sums, origin_ref = refs[:6]
    refs = refs[6:]
    halves = nrows // 2
    row_ins, far_ins, near_in, refs = refs[: ncols - 1], refs[ncols - 1 : ncols + halves - 2], refs[ncols + halves - 2], refs[ncols + halves - 1 :]
    row_outs, col_outs, scratch = refs[:ncols], refs[ncols : ncols + halves], refs[ncols + halves :]
    left, right, row_feat, col_feat = scratch[:4]
    row_sum, col_sum = scratch[4:6], scratch[6:8]
    row_stage, col_stage = scratch[8:11], scratch[11:16]
    came, done = scratch[16:18]
    products, pieces = scratch[18 : 18 + STEPS], scratch[18 + STEPS :]
    per = tiles * ROWS
    rows = row_ids()
    my_row, my_col = where_ref[0], where_ref[1]
    count = where_ref[2]
    for number, ref in enumerate((own_block, *row_ins, *far_ins)):
        came[number * per : (number + 1) * per, :] = ref[...]
    near = ncols + halves - 1
    came[near * per : (near + halves) * per, :] = near_in[...]
    row_sources = [(k, k * per) for k in range(1, ncols)]
    col_sources = [(2 * m, (ncols - 1 + m) * per) for m in range(1, halves)]
    col_sources += [(2 * m + 1, (near + m) * per) for m in range(halves)]
    origin = origin_ref[...]

    for ref in (*row_sum, *col_sum):
        ref[...] = jnp.zeros_like(ref)
    for k in range(STEPS - LEAD, STEPS):
        pieces[k][...] = jnp.zeros_like(pieces[k])
    for feat, me in ((row_feat, my_col), (col_feat, my_row)):
        feat[pl.ds(pl.multiple_of(me * tiles * FEAT, tiles * FEAT), tiles * FEAT), :] = own_feat[...]
    for k, ref in enumerate(row_sum):
        ref[pl.ds(pl.multiple_of(my_col * per, per), per), :] = own_sums[:, k * TILE : (k + 1) * TILE]
    left[pl.ds(pl.multiple_of(my_col * tiles * TILE, tiles * TILE), tiles * TILE), :] = own_left[...]
    right[pl.ds(pl.multiple_of(my_row * tiles * TERMS, tiles * TERMS), tiles * TERMS), :] = own_right[...]

    def rows_of(ref, start):
        return lambda row: ref[pl.ds(start + row, tiles, stride=ROWS), :]

    for number, (_, start) in enumerate(row_sources):
        description = describe(rows_of(came, start), origin)
        stage_features(row_stage[0], number * per, tiles, *description[:2])
        stage_target(row_stage[1:], number * per, tiles, description)
    for number, (_, start) in enumerate(col_sources):
        description = describe(rows_of(came, start), origin)
        stage_features(col_stage[0], number * per, tiles, *description[:2])
        stage_source(col_stage[1:], number * per, tiles, description)

    def prepare(step, carry):
        for number, (k, _) in enumerate(row_sources):
            tile = (my_col ^ k) * tiles + step
            staged = [ref[pl.ds(pl.multiple_of(number * per + step * ROWS, ROWS), ROWS), :] for ref in row_stage]
            row_feat[feat_at(tile), :] = features(staged[0], rows)
            left[wide_at(tile), :] = target_side(*staged[1:], rows)
        for number, (k, _) in enumerate(col_sources):
            tile = (my_row ^ k) * tiles + step
            staged = [ref[pl.ds(pl.multiple_of(number * per + step * ROWS, ROWS), ROWS), :] for ref in col_stage]
            col_feat[feat_at(tile), :] = features(staged[0], rows)
            right[term_at(tile), :] = source_side(*staged[1:], rows)
        return carry

    lax.fori_loop(0, tiles, prepare, 0, unroll=8)

    last = slots_ref.shape[1] - 1

    def multiply(slot, out):
        slot = jnp.minimum(slot, last)
        tgt, src = slots_ref[0, slot], slots_ref[1, slot]
        out[...] = jnp.dot(left[wide_at(tgt), :], right[term_at(src), :], preferred_element_type=jnp.float32)

    def add_up(slot, values):
        kept = jnp.clip(slot, 0, last)
        tgt, src = slots_ref[0, kept], slots_ref[1, kept]
        own = (tgt // tiles == my_col) & (src // tiles == my_row) & (tgt % tiles == src % tiles)
        alive = jnp.where((slot >= tiles) & (slot < count), 1.0, 0.0)
        react = jnp.where(own, 0.0, alive)
        to_target = alive * target_terms(col_feat[feat_at(src), :], values)
        to_source = react * source_terms(row_feat[feat_at(tgt), :], values)
        for k in range(2):
            row_sum[k][tile_at(tgt), :] += to_target[:, k * TILE : (k + 1) * TILE]
            col_sum[k][tile_at(src), :] += to_source[:, k * TILE : (k + 1) * TILE]

    for k in range(LEAD):
        multiply(tiles + k, products[k])
    loops = (count - tiles + STEPS - 1) // STEPS

    def visit(step, carry):
        for k in range(STEPS):
            slot = tiles + step * STEPS + k
            multiply(slot + LEAD, products[(k + LEAD) % STEPS])
            evaluate(products[k], pieces[k])
            add_up(slot - LEAD, pieces[(k - LEAD) % STEPS])
        return carry

    lax.fori_loop(0, loops, visit, 0)
    for k in range(LEAD):
        add_up(tiles + loops * STEPS - LEAD + k, pieces[STEPS - LEAD + k])

    row_results = [(k, row_outs[k], 0) for k in range(ncols)]
    col_results = [(k, col_outs[k // 2], k % 2 * per) for k in range(nrows)]
    number = 0
    for results, sources, sums, me in (
        (row_results, row_sources, row_sum, my_col),
        (col_results, col_sources, col_sum, my_row),
    ):
        starts = dict(sources) | {0: 0}
        for k, result, start in results:
            base = pl.multiple_of((me ^ k) * per, per)
            values = finish_block(rows_of(came, starts[k]), *(rows_of(ref, base) for ref in sums), origin)
            put_rows(done, number * per, tiles, numbered(0, values))
            result[start : start + per, :] = done[number * per : (number + 1) * per, :]
            number += 1


def halve_kernel(*refs):
    keep, send = refs[-2:]
    half = keep.shape[0]
    total = refs[0][...]
    for ref in refs[1:-2]:
        total = total + ref[...]
    keep[...] = total[:half, :]
    send[...] = total[half:, :]


def total_kernel(*refs):
    vel_ref, str_ref = refs[-2:]
    tiles = vel_ref.shape[1] // TILE
    for tile in range(tiles):
        at = slice(tile * ROWS, (tile + 1) * ROWS)
        total = refs[0][at, :]
        for ref in refs[1:-2]:
            total = total + ref[at, :]
        vel_ref[:, tile * TILE : (tile + 1) * TILE] = total[0:3, :]
        str_ref[:, tile * TILE : (tile + 1) * TILE] = total[3:6, :]


def shards(positions, strengths, cores, order, tile_counts, pair_slots, pair_count):
    tiles = tile_counts.shape[0]
    per_dev = tiles * TILE
    nrows = lax.axis_size("row")
    ncols = lax.axis_size("col")
    halves = nrows // 2
    assert nrows == 2 * halves and nrows & (nrows - 1) == 0 and ncols & (ncols - 1) == 0
    row_tiles, col_tiles = ncols * tiles, nrows * tiles
    smem = pl.BlockSpec(memory_space=pltpu.SMEM)
    vmem = pl.BlockSpec(memory_space=pltpu.VMEM)
    hbm = pl.BlockSpec(memory_space=pltpu.HBM)
    params = pltpu.CompilerParams(vmem_limit_bytes=VMEM_BYTES)

    def blocks(count):
        return jax.ShapeDtypeStruct((count * tiles * ROWS, TILE), jnp.float32)

    def in_hbm(value):
        return pltpu.with_memory_space_constraint(value, pltpu.HBM)

    inputs = (tile_counts, positions, strengths, cores.reshape(1, per_dev), order.reshape(1, per_dev), pair_slots)
    packed, slots = pl.pallas_call(
        pack_kernel,
        out_shape=[blocks(1), jax.ShapeDtypeStruct(pair_slots.shape, jnp.int32)],
        in_specs=[hbm] * len(inputs),
        out_specs=[vmem, smem],
        scratch_shapes=[
            pltpu.VMEM((ROWS, per_dev), jnp.float32),
            pltpu.VMEM((1, per_dev), jnp.int32),
            pltpu.SMEM(tile_counts.shape, jnp.int32),
            pltpu.SemaphoreType.DMA((len(inputs),)),
        ],
        compiler_params=params,
        name="pack",
    )(*map(in_hbm, inputs))

    def swap(value, axis, size, k):
        return lax.ppermute(value, axis, [(d, d ^ k) for d in range(size)])

    def strided(count):
        return pltpu.VMEM(((count * tiles + 1) * ROWS, TILE), jnp.float32)

    phases = [pltpu.VMEM((TILE, 4 * TILE), jnp.float32)] * STEPS + [pltpu.VMEM((TILE, 6 * TILE), jnp.bfloat16)] * STEPS
    own = pl.pallas_call(
        own_kernel,
        out_shape=[
            jax.ShapeDtypeStruct((per_dev, TERMS), jnp.bfloat16),
            jax.ShapeDtypeStruct((tiles * TERMS, 4 * TILE), jnp.bfloat16),
            jax.ShapeDtypeStruct((tiles * FEAT, TILE), jnp.bfloat16),
            jax.ShapeDtypeStruct((tiles * ROWS, 2 * TILE), jnp.float32),
            jax.ShapeDtypeStruct((ROWS, TILE), jnp.float32),
        ],
        in_specs=[vmem],
        out_specs=[vmem] * 5,
        scratch_shapes=phases + [strided(1)] * 8,
        compiler_params=params,
        cost_estimate=pl.CostEstimate(flops=tiles * 300 * TILE * TILE, bytes_accessed=2**21, transcendentals=0),
        name="own",
    )(packed)

    far = [swap(packed, "row", nrows, 2 * m) for m in range(1, halves)]
    from_row = [swap(packed, "col", ncols, k) for k in range(1, ncols)]
    joined = pl.pallas_call(
        join_kernel,
        out_shape=blocks(halves),
        in_specs=[vmem] * halves,
        out_specs=vmem,
        compiler_params=params,
        name="join",
    )(packed, *far)
    near = swap(joined, "row", nrows, 1)

    where = jnp.stack([lax.axis_index("row"), lax.axis_index("col"), pair_count[0]]).astype(jnp.int32)
    sums = pl.pallas_call(
        functools.partial(pair_kernel, nrows, ncols, tiles),
        out_shape=[blocks(1)] * ncols + [blocks(2)] * halves,
        in_specs=[smem] * 2 + [vmem] * (5 + ncols + halves),
        out_specs=[vmem] * (ncols + halves),
        scratch_shapes=[
            pltpu.VMEM((row_tiles * TILE, TERMS), jnp.bfloat16),
            pltpu.VMEM((col_tiles * TERMS, 4 * TILE), jnp.bfloat16),
            pltpu.VMEM((row_tiles * FEAT, TILE), jnp.bfloat16),
            pltpu.VMEM((col_tiles * FEAT, TILE), jnp.bfloat16),
            *[strided(ncols)] * 2,
            *[strided(nrows)] * 2,
            *[strided(ncols - 1)] * 3,
            *[strided(nrows - 1)] * 5,
            strided(ncols + nrows - 1),
            strided(ncols + nrows),
            *phases,
        ],
        compiler_params=params,
        name="pairs",
    )(where, slots, packed, *own, *from_row, *far, near)

    far_back = [swap(sums[ncols + m], "row", nrows, 2 * m) for m in range(1, halves)]
    row_back = [swap(sums[k], "col", ncols, k) for k in reversed(range(1, ncols))]
    keep, send = pl.pallas_call(
        halve_kernel,
        out_shape=[blocks(1)] * 2,
        in_specs=[vmem] * halves,
        out_specs=[vmem] * 2,
        compiler_params=params,
        name="halve",
    )(sums[ncols], *far_back)
    parts = [sums[0], keep, *row_back, swap(send, "row", nrows, 1)]
    velocity, stretching = pl.pallas_call(
        total_kernel,
        out_shape=[jax.ShapeDtypeStruct((3, per_dev), jnp.float32)] * 2,
        in_specs=[vmem] * len(parts),
        out_specs=[vmem, vmem],
        compiler_params=params,
        name="totals",
    )(*parts)
    return velocity, stretching


def solution(mesh):
    whole = ("groups", "row", "col")
    in_specs = (P(None, whole), P(None, whole), P(whole), P(whole), P(whole), P(None, whole), P(whole))
    out_specs = (P(None, whole), P(None, whole))
    return jax.shard_map(shards, mesh=mesh, in_specs=in_specs, out_specs=out_specs, check_vma=False)
```

```python
import functools
import math

import jax
import jax.numpy as jnp
from jax import lax
from jax.experimental import pallas as pl
from jax.experimental.pallas import tpu as pltpu
from jax.sharding import PartitionSpec as P

TILE = 128
ROWS = 8
STEPS = 28
LEAD = 2
FEAT = 32
TERMS = 64
VMEM_BYTES = 48 * 1024 * 1024

biot_factor = -1.0 / (4.0 * math.pi)


def row_ids(count=ROWS):
    return lax.broadcasted_iota(jnp.int32, (count, TILE), 0)


def roll_rows(value, shift):
    return pltpu.roll(value, shift % ROWS, 0)


def pack_kernel(
    counts_hbm, pos_hbm, str_hbm, core_hbm, order_hbm, slots_hbm,
    out_ref, slots_ref, stored, pos_ref, str_ref, core_ref, order_ref, counts_ref, arrived,
):
    tiles = order_ref.shape[1] // TILE
    pairs = (
        (pos_hbm, pos_ref),
        (str_hbm, str_ref),
        (core_hbm, core_ref),
        (order_hbm, order_ref),
        (counts_hbm, counts_ref),
        (slots_hbm, slots_ref),
    )
    copies = [pltpu.make_async_copy(src, dst, arrived.at[k]) for k, (src, dst) in enumerate(pairs)]
    for copy in copies:
        copy.start()
    stored[7:8, :] = jnp.zeros((1, stored.shape[1]), jnp.float32)
    for copy in copies:
        copy.wait()
    stored[0:3, :] = pos_ref[...]
    stored[3:6, :] = str_ref[...]
    stored[6:7, :] = core_ref[...]
    lane = lax.broadcasted_iota(jnp.int32, (ROWS, TILE), 1)
    rows = row_ids()
    is_strength = (rows >= 3) & (rows < 6)
    for tile in range(tiles):
        where_from = jnp.broadcast_to(order_ref[:, tile * TILE : (tile + 1) * TILE], (ROWS, TILE))
        inside = where_from & (TILE - 1)
        block = where_from >> 7
        value = jnp.zeros((ROWS, TILE), jnp.float32)
        for source in range(tiles):
            lanes = stored[:, source * TILE : (source + 1) * TILE]
            part = jnp.take_along_axis(lanes, inside, axis=1, mode="promise_in_bounds")
            value = jnp.where(block == source, part, value)
        live = lane < counts_ref[tile]
        value = jnp.where(is_strength & ~live, 0.0, value)
        value = jnp.where(rows == 7, live.astype(jnp.float32), value)
        out_ref[tile * ROWS : (tile + 1) * ROWS, :] = value


def split_three(value):
    first = value.astype(jnp.bfloat16).astype(jnp.float32)
    rest = value - first
    second = rest.astype(jnp.bfloat16).astype(jnp.float32)
    return first, second, rest - second


def split_two(value):
    high = value.astype(jnp.bfloat16)
    return high, (value - high.astype(jnp.float32)).astype(jnp.bfloat16)


def add_pieces(terms):
    return terms[0:ROWS, :] + (terms[ROWS : 2 * ROWS, :] + terms[2 * ROWS : 3 * ROWS, :])


def cross(left, right):
    return [left[1] * right[2] - left[2] * right[1], left[2] * right[0] - left[0] * right[2], left[0] * right[1] - left[1] * right[0]]


def describe(tile_row, origin):
    position = [tile_row(k) - origin[k : k + 1, :] for k in range(3)]
    strength = [tile_row(3 + k) for k in range(3)]
    core = tile_row(6)
    half = 0.5 * core * core
    coarse = [value.astype(jnp.bfloat16).astype(jnp.float32) for value in position]
    norm = coarse[0] * coarse[0] + coarse[1] * coarse[1] + coarse[2] * coarse[2]
    rest = [(value - near) * (value + near) for value, near in zip(position, coarse)]
    rest = rest[0] + rest[1] + rest[2] + half
    along = position[0] * strength[0] + position[1] * strength[1] + position[2] * strength[2]
    return position, strength, half, norm, rest, along


def put_rows(ref, start, tiles, values):
    for row, value in values.items():
        ref[pl.ds(start + row, tiles, stride=ROWS), :] = value


def negative(values):
    return [-value for value in values]


def numbered(first, values):
    return dict(enumerate(values, first))


def stage_features(ref, start, tiles, position, strength):
    put_rows(ref, start, tiles, numbered(0, strength + cross(position, strength)))


def stage_target(refs, start, tiles, description):
    position, strength, half, norm, rest, along = description
    put_rows(refs[0], start, tiles, numbered(0, position + strength))
    put_rows(refs[1], start, tiles, numbered(0, [norm, rest, along, half]))


def stage_source(refs, start, tiles, description):
    position, strength, half, norm, rest, along = description
    put_rows(refs[0], start, tiles, numbered(0, [-2.0 * value for value in position]) | {6: norm, 7: rest})
    put_rows(refs[1], start, tiles, numbered(3, negative(position)))
    put_rows(refs[2], start, tiles, numbered(0, negative(strength)) | {6: along})
    put_rows(refs[3], start, tiles, {6: half})


def features(tile, rows):
    value = jnp.where(rows < 6, tile, 0.0)
    return jnp.concatenate([*split_three(value), jnp.zeros_like(value)], axis=0).astype(jnp.bfloat16)


def target_side(shared, alone, rows):
    first, second, third = split_three(jnp.where(rows < 6, shared, 1.0))
    alone1, alone2, alone3 = split_three(jnp.where(rows < 4, alone, 0.0))
    both = jnp.where(rows < 4, alone1, roll_rows(alone2, 4))
    stacked = jnp.concatenate([first, both, first, first, second, second, third, alone3], axis=0)
    return stacked.astype(jnp.bfloat16).T


def source_side(dist, front, back, core, rows):
    zero = jnp.zeros_like(dist)
    one = jnp.ones_like(dist)
    values = (
        jnp.where((rows < 3) | (rows > 5), dist, 0.0),
        jnp.where((rows >= 3) & (rows < 6), front, 0.0),
        jnp.where((rows < 3) | (rows == 6), back, 0.0),
        jnp.where(rows == 6, core, 0.0),
    )
    pick = rows & 3
    picks = (jnp.where(pick < 2, one, zero), jnp.where(pick == 2, one, zero), zero, jnp.where(pick == 3, one, zero))
    blocks = []
    for value, picked in zip(values, picks):
        first, second, third = split_three(value)
        parts = [first, picked, second, third, first, second, first, picked]
        blocks.append(jnp.concatenate(parts, axis=0).astype(jnp.bfloat16))
    return jnp.concatenate(blocks, axis=1)


def finish_block(tile_row, smooth_row, grad_row, origin):
    position = [tile_row(k) - origin[k : k + 1, :] for k in range(3)]
    strength = [tile_row(3 + k) for k in range(3)]
    scale = biot_factor * tile_row(7)
    smooth = [smooth_row(k) for k in range(6)]
    grad = [grad_row(k) for k in range(6)]
    velocity = [turn - part for turn, part in zip(cross(position, smooth[:3]), smooth[3:])]
    lever = [turn - part for turn, part in zip(cross(position, grad[:3]), grad[3:])]
    stretch = [turn - 3.0 * part for turn, part in zip(cross(strength, smooth[:3]), lever)]
    return [scale * value for value in velocity + stretch]


def evaluate(products, pieces):
    for start in range(0, TILE, 16):
        at = slice(start, start + 16)
        dist, front, back, core = (products[at, k * TILE : (k + 1) * TILE] for k in range(4))
        inv = lax.rsqrt(dist)
        inv2 = inv * inv
        inv3 = inv2 * inv
        tail = core * (inv3 * inv2)
        smooth = inv3 + 1.5 * tail
        grad = inv2 * (smooth + tail)
        for k, value in enumerate((smooth, grad * front, grad * back)):
            high, low = split_two(value)
            pieces[at, 2 * k * TILE : (2 * k + 1) * TILE] = high
            pieces[at, (2 * k + 1) * TILE : (2 * k + 2) * TILE] = low


def tile_at(tile):
    return pl.ds(pl.multiple_of(tile * ROWS, ROWS), ROWS)


def term_at(tile):
    return pl.ds(pl.multiple_of(tile * TERMS, TERMS), TERMS)


def wide_at(tile):
    return pl.ds(pl.multiple_of(tile * TILE, TILE), TILE)


def feat_at(tile):
    return pl.ds(pl.multiple_of(tile * FEAT, FEAT), FEAT)


def target_terms(feat, values):
    smooth, front = values[:, : 2 * TILE], values[:, 2 * TILE : 4 * TILE]
    terms = lax.dot_general(
        jnp.concatenate([feat, feat], axis=1),
        jnp.concatenate([smooth, front], axis=0),
        (((1,), (1,)), ((), ())),
        preferred_element_type=jnp.float32,
    )
    return add_pieces(terms)


def source_terms(feat, values):
    high = jnp.concatenate([values[:, :TILE], values[:, 4 * TILE : 5 * TILE]], axis=1)
    low = jnp.concatenate([values[:, TILE : 2 * TILE], values[:, 5 * TILE :]], axis=1)
    both = jnp.concatenate([high, low], axis=0)
    terms = jnp.dot(jnp.concatenate([feat, feat], axis=1), both, preferred_element_type=jnp.float32)
    return add_pieces(terms)


def own_kernel(block, left, right, feat, sums, origin_ref, *scratch):
    products, pieces = scratch[:STEPS], scratch[STEPS : 2 * STEPS]
    stages, copied = scratch[2 * STEPS : -1], scratch[-1]
    copied[: block.shape[0], :] = block[...]
    tiles = block.shape[0] // ROWS
    rows = row_ids()
    total = block[0:ROWS, :]
    for tile in range(1, tiles):
        total = total + block[tile * ROWS : (tile + 1) * ROWS, :]
    origin = jnp.sum(total, axis=1, keepdims=True) * (1.0 / (tiles * TILE))
    origin = jnp.where(rows < 3, jnp.broadcast_to(origin, (ROWS, TILE)), 0.0)
    origin_ref[...] = origin
    description = describe(lambda row: copied[pl.ds(row, tiles, stride=ROWS), :], origin)
    stage_features(stages[0], 0, tiles, *description[:2])
    stage_target(stages[1:3], 0, tiles, description)
    stage_source(stages[3:], 0, tiles, description)
    for tile in range(tiles):
        staged = [ref[tile * ROWS : (tile + 1) * ROWS, :] for ref in stages]
        feat[tile * FEAT : (tile + 1) * FEAT, :] = features(staged[0], rows)
        left[tile * TILE : (tile + 1) * TILE, :] = target_side(*staged[1:3], rows)
        right[tile * TERMS : (tile + 1) * TERMS, :] = source_side(*staged[3:], rows)
    for step in range(tiles + 2 * LEAD):
        if step < tiles:
            target, source = left[step * TILE : (step + 1) * TILE, :], right[step * TERMS : (step + 1) * TERMS, :]
            products[step % STEPS][...] = jnp.dot(target, source, preferred_element_type=jnp.float32)
        if LEAD <= step < tiles + LEAD:
            evaluate(products[(step - LEAD) % STEPS], pieces[(step - LEAD) % STEPS])
        if step >= 2 * LEAD:
            tile = step - 2 * LEAD
            terms = target_terms(feat[tile * FEAT : (tile + 1) * FEAT, :], pieces[tile % STEPS])
            sums[tile * ROWS : (tile + 1) * ROWS, :] = terms


def join_kernel(*refs):
    out, start = refs[-1], 0
    for ref in refs[:-1]:
        out[start : start + ref.shape[0], :] = ref[...]
        start += ref.shape[0]


def pair_kernel(nrows, ncols, tiles, where_ref, slots_ref, *refs):
    own_block, own_left, own_right, own_feat, own_sums, origin_ref = refs[:6]
    refs = refs[6:]
    halves = nrows // 2
    row_ins, far_ins, near_in, refs = refs[: ncols - 1], refs[ncols - 1 : ncols + halves - 2], refs[ncols + halves - 2], refs[ncols + halves - 1 :]
    row_outs, col_outs, scratch = refs[:ncols], refs[ncols : ncols + halves], refs[ncols + halves :]
    left, right, row_feat, col_feat = scratch[:4]
    row_sum, col_sum = scratch[4:6], scratch[6:8]
    row_stage, col_stage = scratch[8:11], scratch[11:16]
    came, done = scratch[16:18]
    products, pieces = scratch[18 : 18 + STEPS], scratch[18 + STEPS :]
    per = tiles * ROWS
    rows = row_ids()
    my_row, my_col = where_ref[0], where_ref[1]
    count = where_ref[2]
    for number, ref in enumerate((own_block, *row_ins, *far_ins)):
        came[number * per : (number + 1) * per, :] = ref[...]
    near = ncols + halves - 1
    came[near * per : (near + halves) * per, :] = near_in[...]
    row_sources = [(k, k * per) for k in range(1, ncols)]
    col_sources = [(2 * m, (ncols - 1 + m) * per) for m in range(1, halves)]
    col_sources += [(2 * m + 1, (near + m) * per) for m in range(halves)]
    origin = origin_ref[...]

    for ref in (*row_sum, *col_sum):
        ref[...] = jnp.zeros_like(ref)
    for k in range(STEPS - LEAD, STEPS):
        pieces[k][...] = jnp.zeros_like(pieces[k])
    for feat, me in ((row_feat, my_col), (col_feat, my_row)):
        feat[pl.ds(pl.multiple_of(me * tiles * FEAT, tiles * FEAT), tiles * FEAT), :] = own_feat[...]
    for k, ref in enumerate(row_sum):
        ref[pl.ds(pl.multiple_of(my_col * per, per), per), :] = own_sums[:, k * TILE : (k + 1) * TILE]
    left[pl.ds(pl.multiple_of(my_col * tiles * TILE, tiles * TILE), tiles * TILE), :] = own_left[...]
    right[pl.ds(pl.multiple_of(my_row * tiles * TERMS, tiles * TERMS), tiles * TERMS), :] = own_right[...]

    def rows_of(ref, start):
        return lambda row: ref[pl.ds(start + row, tiles, stride=ROWS), :]

    for number, (_, start) in enumerate(row_sources):
        description = describe(rows_of(came, start), origin)
        stage_features(row_stage[0], number * per, tiles, *description[:2])
        stage_target(row_stage[1:], number * per, tiles, description)
    for number, (_, start) in enumerate(col_sources):
        description = describe(rows_of(came, start), origin)
        stage_features(col_stage[0], number * per, tiles, *description[:2])
        stage_source(col_stage[1:], number * per, tiles, description)

    def prepare(step, carry):
        for number, (k, _) in enumerate(row_sources):
            tile = (my_col ^ k) * tiles + step
            staged = [ref[pl.ds(pl.multiple_of(number * per + step * ROWS, ROWS), ROWS), :] for ref in row_stage]
            row_feat[feat_at(tile), :] = features(staged[0], rows)
            left[wide_at(tile), :] = target_side(*staged[1:], rows)
        for number, (k, _) in enumerate(col_sources):
            tile = (my_row ^ k) * tiles + step
            staged = [ref[pl.ds(pl.multiple_of(number * per + step * ROWS, ROWS), ROWS), :] for ref in col_stage]
            col_feat[feat_at(tile), :] = features(staged[0], rows)
            right[term_at(tile), :] = source_side(*staged[1:], rows)
        return carry

    lax.fori_loop(0, tiles, prepare, 0, unroll=8)

    last = slots_ref.shape[1] - 1

    def multiply(slot, out):
        slot = jnp.minimum(slot, last)
        tgt, src = slots_ref[0, slot], slots_ref[1, slot]
        out[...] = jnp.dot(left[wide_at(tgt), :], right[term_at(src), :], preferred_element_type=jnp.float32)

    def add_up(slot, values):
        kept = jnp.clip(slot, 0, last)
        tgt, src = slots_ref[0, kept], slots_ref[1, kept]
        own = (tgt // tiles == my_col) & (src // tiles == my_row) & (tgt % tiles == src % tiles)
        alive = jnp.where((slot >= tiles) & (slot < count), 1.0, 0.0)
        react = jnp.where(own, 0.0, alive)
        to_target = alive * target_terms(col_feat[feat_at(src), :], values)
        to_source = react * source_terms(row_feat[feat_at(tgt), :], values)
        for k in range(2):
            row_sum[k][tile_at(tgt), :] += to_target[:, k * TILE : (k + 1) * TILE]
            col_sum[k][tile_at(src), :] += to_source[:, k * TILE : (k + 1) * TILE]

    for k in range(LEAD):
        multiply(tiles + k, products[k])
    loops = (count - tiles + STEPS - 1) // STEPS

    def visit(step, carry):
        for k in range(STEPS):
            slot = tiles + step * STEPS + k
            multiply(slot + LEAD, products[(k + LEAD) % STEPS])
            evaluate(products[k], pieces[k])
            add_up(slot - LEAD, pieces[(k - LEAD) % STEPS])
        return carry

    lax.fori_loop(0, loops, visit, 0)
    for k in range(LEAD):
        add_up(tiles + loops * STEPS - LEAD + k, pieces[STEPS - LEAD + k])

    row_results = [(k, row_outs[k], 0) for k in range(ncols)]
    col_results = [(k, col_outs[k // 2], k % 2 * per) for k in range(nrows)]
    number = 0
    for results, sources, sums, me in (
        (row_results, row_sources, row_sum, my_col),
        (col_results, col_sources, col_sum, my_row),
    ):
        starts = dict(sources) | {0: 0}
        for k, result, start in results:
            base = pl.multiple_of((me ^ k) * per, per)
            values = finish_block(rows_of(came, starts[k]), *(rows_of(ref, base) for ref in sums), origin)
            put_rows(done, number * per, tiles, numbered(0, values))
            result[start : start + per, :] = done[number * per : (number + 1) * per, :]
            number += 1


def halve_kernel(*refs):
    keep, send = refs[-2:]
    half = keep.shape[0]
    total = refs[0][...]
    for ref in refs[1:-2]:
        total = total + ref[...]
    keep[...] = total[:half, :]
    send[...] = total[half:, :]


def total_kernel(*refs):
    vel_ref, str_ref = refs[-2:]
    tiles = vel_ref.shape[1] // TILE
    for tile in range(tiles):
        at = slice(tile * ROWS, (tile + 1) * ROWS)
        total = refs[0][at, :]
        for ref in refs[1:-2]:
            total = total + ref[at, :]
        vel_ref[:, tile * TILE : (tile + 1) * TILE] = total[0:3, :]
        str_ref[:, tile * TILE : (tile + 1) * TILE] = total[3:6, :]


def shards(positions, strengths, cores, order, tile_counts, pair_slots, pair_count):
    tiles = tile_counts.shape[0]
    per_dev = tiles * TILE
    nrows = lax.axis_size("row")
    ncols = lax.axis_size("col")
    halves = nrows // 2
    assert nrows == 2 * halves and nrows & (nrows - 1) == 0 and ncols & (ncols - 1) == 0
    row_tiles, col_tiles = ncols * tiles, nrows * tiles
    smem = pl.BlockSpec(memory_space=pltpu.SMEM)
    vmem = pl.BlockSpec(memory_space=pltpu.VMEM)
    hbm = pl.BlockSpec(memory_space=pltpu.HBM)
    params = pltpu.CompilerParams(vmem_limit_bytes=VMEM_BYTES)

    def blocks(count):
        return jax.ShapeDtypeStruct((count * tiles * ROWS, TILE), jnp.float32)

    def in_hbm(value):
        return pltpu.with_memory_space_constraint(value, pltpu.HBM)

    inputs = (tile_counts, positions, strengths, cores.reshape(1, per_dev), order.reshape(1, per_dev), pair_slots)
    packed, slots = pl.pallas_call(
        pack_kernel,
        out_shape=[blocks(1), jax.ShapeDtypeStruct(pair_slots.shape, jnp.int32)],
        in_specs=[hbm] * len(inputs),
        out_specs=[vmem, smem],
        scratch_shapes=[
            pltpu.VMEM((ROWS, per_dev), jnp.float32),
            *[pltpu.VMEM(value.shape, value.dtype) for value in inputs[1:5]],
            pltpu.SMEM(tile_counts.shape, jnp.int32),
            pltpu.SemaphoreType.DMA((len(inputs),)),
        ],
        compiler_params=params,
        name="pack",
    )(*map(in_hbm, inputs))

    def swap(value, axis, size, k):
        return lax.ppermute(value, axis, [(d, d ^ k) for d in range(size)])

    def strided(count):
        return pltpu.VMEM(((count * tiles + 1) * ROWS, TILE), jnp.float32)

    phases = [pltpu.VMEM((TILE, 4 * TILE), jnp.float32)] * STEPS + [pltpu.VMEM((TILE, 6 * TILE), jnp.bfloat16)] * STEPS
    own = pl.pallas_call(
        own_kernel,
        out_shape=[
            jax.ShapeDtypeStruct((per_dev, TERMS), jnp.bfloat16),
            jax.ShapeDtypeStruct((tiles * TERMS, 4 * TILE), jnp.bfloat16),
            jax.ShapeDtypeStruct((tiles * FEAT, TILE), jnp.bfloat16),
            jax.ShapeDtypeStruct((tiles * ROWS, 2 * TILE), jnp.float32),
            jax.ShapeDtypeStruct((ROWS, TILE), jnp.float32),
        ],
        in_specs=[vmem],
        out_specs=[vmem] * 5,
        scratch_shapes=phases + [strided(1)] * 8,
        compiler_params=params,
        cost_estimate=pl.CostEstimate(flops=tiles * 300 * TILE * TILE, bytes_accessed=2**21, transcendentals=0),
        name="own",
    )(packed)

    far = [swap(packed, "row", nrows, 2 * m) for m in range(1, halves)]
    from_row = [swap(packed, "col", ncols, k) for k in range(1, ncols)]
    joined = pl.pallas_call(
        join_kernel,
        out_shape=blocks(halves),
        in_specs=[vmem] * halves,
        out_specs=vmem,
        compiler_params=params,
        name="join",
    )(packed, *far)
    near = swap(joined, "row", nrows, 1)

    where = jnp.stack([lax.axis_index("row"), lax.axis_index("col"), pair_count[0]]).astype(jnp.int32)
    sums = pl.pallas_call(
        functools.partial(pair_kernel, nrows, ncols, tiles),
        out_shape=[blocks(1)] * ncols + [blocks(2)] * halves,
        in_specs=[smem] * 2 + [vmem] * (5 + ncols + halves),
        out_specs=[vmem] * (ncols + halves),
        scratch_shapes=[
            pltpu.VMEM((row_tiles * TILE, TERMS), jnp.bfloat16),
            pltpu.VMEM((col_tiles * TERMS, 4 * TILE), jnp.bfloat16),
            pltpu.VMEM((row_tiles * FEAT, TILE), jnp.bfloat16),
            pltpu.VMEM((col_tiles * FEAT, TILE), jnp.bfloat16),
            *[strided(ncols)] * 2,
            *[strided(nrows)] * 2,
            *[strided(ncols - 1)] * 3,
            *[strided(nrows - 1)] * 5,
            strided(ncols + nrows - 1),
            strided(ncols + nrows),
            *phases,
        ],
        compiler_params=params,
        name="pairs",
    )(where, slots, packed, *own, *from_row, *far, near)

    far_back = [swap(sums[ncols + m], "row", nrows, 2 * m) for m in range(1, halves)]
    row_back = [swap(sums[k], "col", ncols, k) for k in reversed(range(1, ncols))]
    keep, send = pl.pallas_call(
        halve_kernel,
        out_shape=[blocks(1)] * 2,
        in_specs=[vmem] * halves,
        out_specs=[vmem] * 2,
        compiler_params=params,
        name="halve",
    )(sums[ncols], *far_back)
    parts = [sums[0], keep, *row_back, swap(send, "row", nrows, 1)]
    velocity, stretching = pl.pallas_call(
        total_kernel,
        out_shape=[jax.ShapeDtypeStruct((3, per_dev), jnp.float32)] * 2,
        in_specs=[vmem] * len(parts),
        out_specs=[vmem, vmem],
        compiler_params=params,
        name="totals",
    )(*parts)
    return velocity, stretching


def solution(mesh):
    whole = ("groups", "row", "col")
    in_specs = (P(None, whole), P(None, whole), P(whole), P(whole), P(whole), P(None, whole), P(whole))
    out_specs = (P(None, whole), P(None, whole))
    return jax.shard_map(shards, mesh=mesh, in_specs=in_specs, out_specs=out_specs, check_vma=False)
```

```python
import functools
import math

import jax
import jax.numpy as jnp
from jax import lax
from jax.experimental import pallas as pl
from jax.experimental.pallas import tpu as pltpu
from jax.sharding import PartitionSpec as P

TILE = 128
ROWS = 8
STEPS = 28
LEAD = 2
FEAT = 32
TERMS = 64
VMEM_BYTES = 48 * 1024 * 1024

biot_factor = -1.0 / (4.0 * math.pi)


def row_ids(count=ROWS):
    return lax.broadcasted_iota(jnp.int32, (count, TILE), 0)


def roll_rows(value, shift):
    return pltpu.roll(value, shift % ROWS, 0)


def pack_kernel(
    counts_hbm, pos_hbm, str_hbm, core_hbm, order_hbm, slots_hbm,
    out_ref, slots_ref, stored, order_ref, counts_ref, arrived,
):
    tiles = order_ref.shape[1] // TILE
    pairs = (
        (pos_hbm, stored.at[0:3, :]),
        (str_hbm, stored.at[3:6, :]),
        (core_hbm, stored.at[6:7, :]),
        (order_hbm, order_ref),
        (counts_hbm, counts_ref),
        (slots_hbm, slots_ref),
    )
    copies = [pltpu.make_async_copy(src, dst, arrived.at[k]) for k, (src, dst) in enumerate(pairs)]
    for copy in copies:
        copy.start()
    stored[7:8, :] = jnp.zeros((1, stored.shape[1]), jnp.float32)
    for copy in copies:
        copy.wait()
    lane = lax.broadcasted_iota(jnp.int32, (ROWS, TILE), 1)
    rows = row_ids()
    is_strength = (rows >= 3) & (rows < 6)
    for tile in range(tiles):
        where_from = jnp.broadcast_to(order_ref[:, tile * TILE : (tile + 1) * TILE], (ROWS, TILE))
        inside = where_from & (TILE - 1)
        block = where_from >> 7
        value = jnp.zeros((ROWS, TILE), jnp.float32)
        for source in range(tiles):
            part = jnp.take_along_axis(stored[:, source * TILE : (source + 1) * TILE], inside, axis=1)
            value = jnp.where(block == source, part, value)
        live = lane < counts_ref[tile]
        value = jnp.where(is_strength & ~live, 0.0, value)
        value = jnp.where(rows == 7, live.astype(jnp.float32), value)
        out_ref[tile * ROWS : (tile + 1) * ROWS, :] = value


def split_three(value):
    first = value.astype(jnp.bfloat16).astype(jnp.float32)
    rest = value - first
    second = rest.astype(jnp.bfloat16).astype(jnp.float32)
    return first, second, rest - second


def split_two(value):
    high = value.astype(jnp.bfloat16)
    return high, (value - high.astype(jnp.float32)).astype(jnp.bfloat16)


def add_pieces(terms):
    return terms[0:ROWS, :] + (terms[ROWS : 2 * ROWS, :] + terms[2 * ROWS : 3 * ROWS, :])


def cross(left, right):
    return [left[1] * right[2] - left[2] * right[1], left[2] * right[0] - left[0] * right[2], left[0] * right[1] - left[1] * right[0]]


def describe(tile_row, origin):
    position = [tile_row(k) - origin[k : k + 1, :] for k in range(3)]
    strength = [tile_row(3 + k) for k in range(3)]
    core = tile_row(6)
    half = 0.5 * core * core
    coarse = [value.astype(jnp.bfloat16).astype(jnp.float32) for value in position]
    norm = coarse[0] * coarse[0] + coarse[1] * coarse[1] + coarse[2] * coarse[2]
    rest = [(value - near) * (value + near) for value, near in zip(position, coarse)]
    rest = rest[0] + rest[1] + rest[2] + half
    along = position[0] * strength[0] + position[1] * strength[1] + position[2] * strength[2]
    return position, strength, half, norm, rest, along


def put_rows(ref, start, tiles, values):
    for row, value in values.items():
        ref[pl.ds(start + row, tiles, stride=ROWS), :] = value


def negative(values):
    return [-value for value in values]


def numbered(first, values):
    return dict(enumerate(values, first))


def stage_features(ref, start, tiles, position, strength):
    put_rows(ref, start, tiles, numbered(0, strength + cross(position, strength)))


def stage_target(refs, start, tiles, description):
    position, strength, half, norm, rest, along = description
    put_rows(refs[0], start, tiles, numbered(0, position + strength))
    put_rows(refs[1], start, tiles, numbered(0, [norm, rest, along, half]))


def stage_source(refs, start, tiles, description):
    position, strength, half, norm, rest, along = description
    put_rows(refs[0], start, tiles, numbered(0, [-2.0 * value for value in position]) | {6: norm, 7: rest})
    put_rows(refs[1], start, tiles, numbered(3, negative(position)))
    put_rows(refs[2], start, tiles, numbered(0, negative(strength)) | {6: along})
    put_rows(refs[3], start, tiles, {6: half})


def features(tile, rows):
    value = jnp.where(rows < 6, tile, 0.0)
    return jnp.concatenate([*split_three(value), jnp.zeros_like(value)], axis=0).astype(jnp.bfloat16)


def target_side(shared, alone, rows):
    first, second, third = split_three(jnp.where(rows < 6, shared, 1.0))
    alone1, alone2, alone3 = split_three(jnp.where(rows < 4, alone, 0.0))
    both = jnp.where(rows < 4, alone1, roll_rows(alone2, 4))
    stacked = jnp.concatenate([first, both, first, first, second, second, third, alone3], axis=0)
    return stacked.astype(jnp.bfloat16).T


def source_side(dist, front, back, core, rows):
    zero = jnp.zeros_like(dist)
    one = jnp.ones_like(dist)
    values = (
        jnp.where((rows < 3) | (rows > 5), dist, 0.0),
        jnp.where((rows >= 3) & (rows < 6), front, 0.0),
        jnp.where((rows < 3) | (rows == 6), back, 0.0),
        jnp.where(rows == 6, core, 0.0),
    )
    pick = rows & 3
    picks = (jnp.where(pick < 2, one, zero), jnp.where(pick == 2, one, zero), zero, jnp.where(pick == 3, one, zero))
    blocks = []
    for value, picked in zip(values, picks):
        first, second, third = split_three(value)
        parts = [first, picked, second, third, first, second, first, picked]
        blocks.append(jnp.concatenate(parts, axis=0).astype(jnp.bfloat16))
    return jnp.concatenate(blocks, axis=1)


def finish_block(tile_row, smooth_row, grad_row, origin):
    position = [tile_row(k) - origin[k : k + 1, :] for k in range(3)]
    strength = [tile_row(3 + k) for k in range(3)]
    scale = biot_factor * tile_row(7)
    smooth = [smooth_row(k) for k in range(6)]
    grad = [grad_row(k) for k in range(6)]
    velocity = [turn - part for turn, part in zip(cross(position, smooth[:3]), smooth[3:])]
    lever = [turn - part for turn, part in zip(cross(position, grad[:3]), grad[3:])]
    stretch = [turn - 3.0 * part for turn, part in zip(cross(strength, smooth[:3]), lever)]
    return [scale * value for value in velocity + stretch]


def evaluate(products, pieces):
    for start in range(0, TILE, 16):
        at = slice(start, start + 16)
        dist, front, back, core = (products[at, k * TILE : (k + 1) * TILE] for k in range(4))
        inv = lax.rsqrt(dist)
        inv2 = inv * inv
        inv3 = inv2 * inv
        tail = core * (inv3 * inv2)
        smooth = inv3 + 1.5 * tail
        grad = inv2 * (smooth + tail)
        for k, value in enumerate((smooth, grad * front, grad * back)):
            high, low = split_two(value)
            pieces[at, 2 * k * TILE : (2 * k + 1) * TILE] = high
            pieces[at, (2 * k + 1) * TILE : (2 * k + 2) * TILE] = low


def tile_at(tile):
    return pl.ds(pl.multiple_of(tile * ROWS, ROWS), ROWS)


def term_at(tile):
    return pl.ds(pl.multiple_of(tile * TERMS, TERMS), TERMS)


def wide_at(tile):
    return pl.ds(pl.multiple_of(tile * TILE, TILE), TILE)


def feat_at(tile):
    return pl.ds(pl.multiple_of(tile * FEAT, FEAT), FEAT)


def target_terms(feat, values):
    smooth, front = values[:, : 2 * TILE], values[:, 2 * TILE : 4 * TILE]
    terms = lax.dot_general(
        jnp.concatenate([feat, feat], axis=1),
        jnp.concatenate([smooth, front], axis=0),
        (((1,), (1,)), ((), ())),
        preferred_element_type=jnp.float32,
    )
    return add_pieces(terms)


def source_terms(feat, values):
    high = jnp.concatenate([values[:, :TILE], values[:, 4 * TILE : 5 * TILE]], axis=1)
    low = jnp.concatenate([values[:, TILE : 2 * TILE], values[:, 5 * TILE :]], axis=1)
    both = jnp.concatenate([high, low], axis=0)
    terms = jnp.dot(jnp.concatenate([feat, feat], axis=1), both, preferred_element_type=jnp.float32)
    return add_pieces(terms)


def own_kernel(block, left, right, feat, sums, origin_ref, *scratch):
    products, pieces = scratch[:STEPS], scratch[STEPS : 2 * STEPS]
    stages, copied = scratch[2 * STEPS : -1], scratch[-1]
    copied[: block.shape[0], :] = block[...]
    tiles = block.shape[0] // ROWS
    rows = row_ids()
    total = block[0:ROWS, :]
    for tile in range(1, tiles):
        total = total + block[tile * ROWS : (tile + 1) * ROWS, :]
    origin = jnp.sum(total, axis=1, keepdims=True) * (1.0 / (tiles * TILE))
    origin = jnp.where(rows < 3, jnp.broadcast_to(origin, (ROWS, TILE)), 0.0)
    origin_ref[...] = origin
    description = describe(lambda row: copied[pl.ds(row, tiles, stride=ROWS), :], origin)
    stage_features(stages[0], 0, tiles, *description[:2])
    stage_target(stages[1:3], 0, tiles, description)
    stage_source(stages[3:], 0, tiles, description)
    for tile in range(tiles):
        staged = [ref[tile * ROWS : (tile + 1) * ROWS, :] for ref in stages]
        feat[tile * FEAT : (tile + 1) * FEAT, :] = features(staged[0], rows)
        left[tile * TILE : (tile + 1) * TILE, :] = target_side(*staged[1:3], rows)
        right[tile * TERMS : (tile + 1) * TERMS, :] = source_side(*staged[3:], rows)
    for step in range(tiles + 2 * LEAD):
        if step < tiles:
            target, source = left[step * TILE : (step + 1) * TILE, :], right[step * TERMS : (step + 1) * TERMS, :]
            products[step % STEPS][...] = jnp.dot(target, source, preferred_element_type=jnp.float32)
        if LEAD <= step < tiles + LEAD:
            evaluate(products[(step - LEAD) % STEPS], pieces[(step - LEAD) % STEPS])
        if step >= 2 * LEAD:
            tile = step - 2 * LEAD
            terms = target_terms(feat[tile * FEAT : (tile + 1) * FEAT, :], pieces[tile % STEPS])
            sums[tile * ROWS : (tile + 1) * ROWS, :] = terms


def join_kernel(*refs):
    out, start = refs[-1], 0
    for ref in refs[:-1]:
        out[start : start + ref.shape[0], :] = ref[...]
        start += ref.shape[0]


def pair_kernel(nrows, ncols, tiles, where_ref, slots_ref, *refs):
    own_block, own_left, own_right, own_feat, own_sums, origin_ref = refs[:6]
    refs = refs[6:]
    halves = nrows // 2
    row_ins, far_ins, near_in, refs = refs[: ncols - 1], refs[ncols - 1 : ncols + halves - 2], refs[ncols + halves - 2], refs[ncols + halves - 1 :]
    row_outs, col_outs, scratch = refs[:ncols], refs[ncols : ncols + halves], refs[ncols + halves :]
    left, right, row_feat, col_feat = scratch[:4]
    row_sum, col_sum = scratch[4:6], scratch[6:8]
    row_stage, col_stage = scratch[8:11], scratch[11:16]
    came, done = scratch[16:18]
    products, pieces = scratch[18 : 18 + STEPS], scratch[18 + STEPS :]
    per = tiles * ROWS
    rows = row_ids()
    my_row, my_col = where_ref[0], where_ref[1]
    count = where_ref[2]
    for number, ref in enumerate((own_block, *row_ins, *far_ins)):
        came[number * per : (number + 1) * per, :] = ref[...]
    near = ncols + halves - 1
    came[near * per : (near + halves) * per, :] = near_in[...]
    row_sources = [(k, k * per) for k in range(1, ncols)]
    col_sources = [(2 * m, (ncols - 1 + m) * per) for m in range(1, halves)]
    col_sources += [(2 * m + 1, (near + m) * per) for m in range(halves)]
    origin = origin_ref[...]

    for ref in (*row_sum, *col_sum):
        ref[...] = jnp.zeros_like(ref)
    for k in range(STEPS - LEAD, STEPS):
        pieces[k][...] = jnp.zeros_like(pieces[k])
    for feat, me in ((row_feat, my_col), (col_feat, my_row)):
        feat[pl.ds(pl.multiple_of(me * tiles * FEAT, tiles * FEAT), tiles * FEAT), :] = own_feat[...]
    for k, ref in enumerate(row_sum):
        ref[pl.ds(pl.multiple_of(my_col * per, per), per), :] = own_sums[:, k * TILE : (k + 1) * TILE]
    left[pl.ds(pl.multiple_of(my_col * tiles * TILE, tiles * TILE), tiles * TILE), :] = own_left[...]
    right[pl.ds(pl.multiple_of(my_row * tiles * TERMS, tiles * TERMS), tiles * TERMS), :] = own_right[...]

    def rows_of(ref, start):
        return lambda row: ref[pl.ds(start + row, tiles, stride=ROWS), :]

    for number, (_, start) in enumerate(row_sources):
        description = describe(rows_of(came, start), origin)
        stage_features(row_stage[0], number * per, tiles, *description[:2])
        stage_target(row_stage[1:], number * per, tiles, description)
    for number, (_, start) in enumerate(col_sources):
        description = describe(rows_of(came, start), origin)
        stage_features(col_stage[0], number * per, tiles, *description[:2])
        stage_source(col_stage[1:], number * per, tiles, description)

    def prepare(step, carry):
        for number, (k, _) in enumerate(row_sources):
            tile = (my_col ^ k) * tiles + step
            staged = [ref[pl.ds(pl.multiple_of(number * per + step * ROWS, ROWS), ROWS), :] for ref in row_stage]
            row_feat[feat_at(tile), :] = features(staged[0], rows)
            left[wide_at(tile), :] = target_side(*staged[1:], rows)
        for number, (k, _) in enumerate(col_sources):
            tile = (my_row ^ k) * tiles + step
            staged = [ref[pl.ds(pl.multiple_of(number * per + step * ROWS, ROWS), ROWS), :] for ref in col_stage]
            col_feat[feat_at(tile), :] = features(staged[0], rows)
            right[term_at(tile), :] = source_side(*staged[1:], rows)
        return carry

    lax.fori_loop(0, tiles, prepare, 0, unroll=8)

    last = slots_ref.shape[1] - 1

    def multiply(slot, out):
        slot = jnp.minimum(slot, last)
        tgt, src = slots_ref[0, slot], slots_ref[1, slot]
        out[...] = jnp.dot(left[wide_at(tgt), :], right[term_at(src), :], preferred_element_type=jnp.float32)

    def add_up(slot, values):
        kept = jnp.clip(slot, 0, last)
        tgt, src = slots_ref[0, kept], slots_ref[1, kept]
        own = (tgt // tiles == my_col) & (src // tiles == my_row) & (tgt % tiles == src % tiles)
        alive = jnp.where((slot >= tiles) & (slot < count), 1.0, 0.0)
        react = jnp.where(own, 0.0, alive)
        to_target = alive * target_terms(col_feat[feat_at(src), :], values)
        to_source = react * source_terms(row_feat[feat_at(tgt), :], values)
        for k in range(2):
            row_sum[k][tile_at(tgt), :] += to_target[:, k * TILE : (k + 1) * TILE]
            col_sum[k][tile_at(src), :] += to_source[:, k * TILE : (k + 1) * TILE]

    for k in range(LEAD):
        multiply(tiles + k, products[k])
    loops = (count - tiles + STEPS - 1) // STEPS

    def visit(step, carry):
        for k in range(STEPS):
            slot = tiles + step * STEPS + k
            add_up(slot - LEAD, pieces[(k - LEAD) % STEPS])
            multiply(slot + LEAD, products[(k + LEAD) % STEPS])
            evaluate(products[k], pieces[k])
        return carry

    lax.fori_loop(0, loops, visit, 0)
    for k in range(LEAD):
        add_up(tiles + loops * STEPS - LEAD + k, pieces[STEPS - LEAD + k])

    row_results = [(k, row_outs[k], 0) for k in range(ncols)]
    col_results = [(k, col_outs[k // 2], k % 2 * per) for k in range(nrows)]
    number = 0
    for results, sources, sums, me in (
        (row_results, row_sources, row_sum, my_col),
        (col_results, col_sources, col_sum, my_row),
    ):
        starts = dict(sources) | {0: 0}
        for k, result, start in results:
            base = pl.multiple_of((me ^ k) * per, per)
            values = finish_block(rows_of(came, starts[k]), *(rows_of(ref, base) for ref in sums), origin)
            put_rows(done, number * per, tiles, numbered(0, values))
            result[start : start + per, :] = done[number * per : (number + 1) * per, :]
            number += 1


def halve_kernel(*refs):
    keep, send = refs[-2:]
    half = keep.shape[0]
    total = refs[0][...]
    for ref in refs[1:-2]:
        total = total + ref[...]
    keep[...] = total[:half, :]
    send[...] = total[half:, :]


def total_kernel(*refs):
    vel_ref, str_ref = refs[-2:]
    tiles = vel_ref.shape[1] // TILE
    for tile in range(tiles):
        at = slice(tile * ROWS, (tile + 1) * ROWS)
        total = refs[0][at, :]
        for ref in refs[1:-2]:
            total = total + ref[at, :]
        vel_ref[:, tile * TILE : (tile + 1) * TILE] = total[0:3, :]
        str_ref[:, tile * TILE : (tile + 1) * TILE] = total[3:6, :]


def shards(positions, strengths, cores, order, tile_counts, pair_slots, pair_count):
    tiles = tile_counts.shape[0]
    per_dev = tiles * TILE
    nrows = lax.axis_size("row")
    ncols = lax.axis_size("col")
    halves = nrows // 2
    assert nrows == 2 * halves and nrows & (nrows - 1) == 0 and ncols & (ncols - 1) == 0
    row_tiles, col_tiles = ncols * tiles, nrows * tiles
    smem = pl.BlockSpec(memory_space=pltpu.SMEM)
    vmem = pl.BlockSpec(memory_space=pltpu.VMEM)
    hbm = pl.BlockSpec(memory_space=pltpu.HBM)
    params = pltpu.CompilerParams(vmem_limit_bytes=VMEM_BYTES)

    def blocks(count):
        return jax.ShapeDtypeStruct((count * tiles * ROWS, TILE), jnp.float32)

    def in_hbm(value):
        return pltpu.with_memory_space_constraint(value, pltpu.HBM)

    inputs = (tile_counts, positions, strengths, cores.reshape(1, per_dev), order.reshape(1, per_dev), pair_slots)
    packed, slots = pl.pallas_call(
        pack_kernel,
        out_shape=[blocks(1), jax.ShapeDtypeStruct(pair_slots.shape, jnp.int32)],
        in_specs=[hbm] * len(inputs),
        out_specs=[vmem, smem],
        scratch_shapes=[
            pltpu.VMEM((ROWS, per_dev), jnp.float32),
            pltpu.VMEM((1, per_dev), jnp.int32),
            pltpu.SMEM(tile_counts.shape, jnp.int32),
            pltpu.SemaphoreType.DMA((len(inputs),)),
        ],
        compiler_params=params,
        name="pack",
    )(*map(in_hbm, inputs))

    def swap(value, axis, size, k):
        return lax.ppermute(value, axis, [(d, d ^ k) for d in range(size)])

    def strided(count):
        return pltpu.VMEM(((count * tiles + 1) * ROWS, TILE), jnp.float32)

    phases = [pltpu.VMEM((TILE, 4 * TILE), jnp.float32)] * STEPS + [pltpu.VMEM((TILE, 6 * TILE), jnp.bfloat16)] * STEPS
    own = pl.pallas_call(
        own_kernel,
        out_shape=[
            jax.ShapeDtypeStruct((per_dev, TERMS), jnp.bfloat16),
            jax.ShapeDtypeStruct((tiles * TERMS, 4 * TILE), jnp.bfloat16),
            jax.ShapeDtypeStruct((tiles * FEAT, TILE), jnp.bfloat16),
            jax.ShapeDtypeStruct((tiles * ROWS, 2 * TILE), jnp.float32),
            jax.ShapeDtypeStruct((ROWS, TILE), jnp.float32),
        ],
        in_specs=[vmem],
        out_specs=[vmem] * 5,
        scratch_shapes=phases + [strided(1)] * 8,
        compiler_params=params,
        cost_estimate=pl.CostEstimate(flops=tiles * 300 * TILE * TILE, bytes_accessed=2**21, transcendentals=0),
        name="own",
    )(packed)

    far = [swap(packed, "row", nrows, 2 * m) for m in range(1, halves)]
    from_row = [swap(packed, "col", ncols, k) for k in range(1, ncols)]
    joined = pl.pallas_call(
        join_kernel,
        out_shape=blocks(halves),
        in_specs=[vmem] * halves,
        out_specs=vmem,
        compiler_params=params,
        name="join",
    )(packed, *far)
    near = swap(joined, "row", nrows, 1)

    where = jnp.stack([lax.axis_index("row"), lax.axis_index("col"), pair_count[0]]).astype(jnp.int32)
    sums = pl.pallas_call(
        functools.partial(pair_kernel, nrows, ncols, tiles),
        out_shape=[blocks(1)] * ncols + [blocks(2)] * halves,
        in_specs=[smem] * 2 + [vmem] * (5 + ncols + halves),
        out_specs=[vmem] * (ncols + halves),
        scratch_shapes=[
            pltpu.VMEM((row_tiles * TILE, TERMS), jnp.bfloat16),
            pltpu.VMEM((col_tiles * TERMS, 4 * TILE), jnp.bfloat16),
            pltpu.VMEM((row_tiles * FEAT, TILE), jnp.bfloat16),
            pltpu.VMEM((col_tiles * FEAT, TILE), jnp.bfloat16),
            *[strided(ncols)] * 2,
            *[strided(nrows)] * 2,
            *[strided(ncols - 1)] * 3,
            *[strided(nrows - 1)] * 5,
            strided(ncols + nrows - 1),
            strided(ncols + nrows),
            *phases,
        ],
        compiler_params=params,
        name="pairs",
    )(where, slots, packed, *own, *from_row, *far, near)

    far_back = [swap(sums[ncols + m], "row", nrows, 2 * m) for m in range(1, halves)]
    row_back = [swap(sums[k], "col", ncols, k) for k in reversed(range(1, ncols))]
    keep, send = pl.pallas_call(
        halve_kernel,
        out_shape=[blocks(1)] * 2,
        in_specs=[vmem] * halves,
        out_specs=[vmem] * 2,
        compiler_params=params,
        name="halve",
    )(sums[ncols], *far_back)
    parts = [sums[0], keep, *row_back, swap(send, "row", nrows, 1)]
    velocity, stretching = pl.pallas_call(
        total_kernel,
        out_shape=[jax.ShapeDtypeStruct((3, per_dev), jnp.float32)] * 2,
        in_specs=[vmem] * len(parts),
        out_specs=[vmem, vmem],
        compiler_params=params,
        name="totals",
    )(*parts)
    return velocity, stretching


def solution(mesh):
    whole = ("groups", "row", "col")
    in_specs = (P(None, whole), P(None, whole), P(whole), P(whole), P(whole), P(None, whole), P(whole))
    out_specs = (P(None, whole), P(None, whole))
    return jax.shard_map(shards, mesh=mesh, in_specs=in_specs, out_specs=out_specs, check_vma=False)
```

```python
import functools
import math

import jax
import jax.numpy as jnp
from jax import lax
from jax.experimental import pallas as pl
from jax.experimental.pallas import tpu as pltpu
from jax.sharding import PartitionSpec as P

TILE = 128
ROWS = 8
STEPS = 28
LEAD = 1
FEAT = 32
TERMS = 64
VMEM_BYTES = 48 * 1024 * 1024

biot_factor = -1.0 / (4.0 * math.pi)


def row_ids(count=ROWS):
    return lax.broadcasted_iota(jnp.int32, (count, TILE), 0)


def roll_rows(value, shift):
    return pltpu.roll(value, shift % ROWS, 0)


def pack_kernel(
    counts_hbm, pos_hbm, str_hbm, core_hbm, order_hbm, slots_hbm,
    out_ref, slots_ref, stored, order_ref, counts_ref, arrived,
):
    tiles = order_ref.shape[1] // TILE
    pairs = (
        (pos_hbm, stored.at[0:3, :]),
        (str_hbm, stored.at[3:6, :]),
        (core_hbm, stored.at[6:7, :]),
        (order_hbm, order_ref),
        (counts_hbm, counts_ref),
        (slots_hbm, slots_ref),
    )
    copies = [pltpu.make_async_copy(src, dst, arrived.at[k]) for k, (src, dst) in enumerate(pairs)]
    for copy in copies:
        copy.start()
    stored[7:8, :] = jnp.zeros((1, stored.shape[1]), jnp.float32)
    for copy in copies:
        copy.wait()
    lane = lax.broadcasted_iota(jnp.int32, (ROWS, TILE), 1)
    rows = row_ids()
    is_strength = (rows >= 3) & (rows < 6)
    for tile in range(tiles):
        where_from = jnp.broadcast_to(order_ref[:, tile * TILE : (tile + 1) * TILE], (ROWS, TILE))
        inside = where_from & (TILE - 1)
        block = where_from >> 7
        value = jnp.zeros((ROWS, TILE), jnp.float32)
        for source in range(tiles):
            part = jnp.take_along_axis(stored[:, source * TILE : (source + 1) * TILE], inside, axis=1)
            value = jnp.where(block == source, part, value)
        live = lane < counts_ref[tile]
        value = jnp.where(is_strength & ~live, 0.0, value)
        value = jnp.where(rows == 7, live.astype(jnp.float32), value)
        out_ref[tile * ROWS : (tile + 1) * ROWS, :] = value


def split_three(value):
    first = value.astype(jnp.bfloat16).astype(jnp.float32)
    rest = value - first
    second = rest.astype(jnp.bfloat16).astype(jnp.float32)
    return first, second, rest - second


def split_two(value):
    high = value.astype(jnp.bfloat16)
    return high, (value - high.astype(jnp.float32)).astype(jnp.bfloat16)


def add_pieces(terms):
    return terms[0:ROWS, :] + (terms[ROWS : 2 * ROWS, :] + terms[2 * ROWS : 3 * ROWS, :])


def cross(left, right):
    return [left[1] * right[2] - left[2] * right[1], left[2] * right[0] - left[0] * right[2], left[0] * right[1] - left[1] * right[0]]


def describe(tile_row, origin):
    position = [tile_row(k) - origin[k : k + 1, :] for k in range(3)]
    strength = [tile_row(3 + k) for k in range(3)]
    core = tile_row(6)
    half = 0.5 * core * core
    coarse = [value.astype(jnp.bfloat16).astype(jnp.float32) for value in position]
    norm = coarse[0] * coarse[0] + coarse[1] * coarse[1] + coarse[2] * coarse[2]
    rest = [(value - near) * (value + near) for value, near in zip(position, coarse)]
    rest = rest[0] + rest[1] + rest[2] + half
    along = position[0] * strength[0] + position[1] * strength[1] + position[2] * strength[2]
    return position, strength, half, norm, rest, along


def put_rows(ref, start, tiles, values):
    for row, value in values.items():
        ref[pl.ds(start + row, tiles, stride=ROWS), :] = value


def negative(values):
    return [-value for value in values]


def numbered(first, values):
    return dict(enumerate(values, first))


def stage_features(ref, start, tiles, position, strength):
    put_rows(ref, start, tiles, numbered(0, strength + cross(position, strength)))


def stage_target(refs, start, tiles, description):
    position, strength, half, norm, rest, along = description
    put_rows(refs[0], start, tiles, numbered(0, position + strength))
    put_rows(refs[1], start, tiles, numbered(0, [norm, rest, along, half]))


def stage_source(refs, start, tiles, description):
    position, strength, half, norm, rest, along = description
    put_rows(refs[0], start, tiles, numbered(0, [-2.0 * value for value in position]) | {6: norm, 7: rest})
    put_rows(refs[1], start, tiles, numbered(3, negative(position)))
    put_rows(refs[2], start, tiles, numbered(0, negative(strength)) | {6: along})
    put_rows(refs[3], start, tiles, {6: half})


def features(tile, rows):
    value = jnp.where(rows < 6, tile, 0.0)
    return jnp.concatenate([*split_three(value), jnp.zeros_like(value)], axis=0).astype(jnp.bfloat16)


def target_side(shared, alone, rows):
    first, second, third = split_three(jnp.where(rows < 6, shared, 1.0))
    alone1, alone2, alone3 = split_three(jnp.where(rows < 4, alone, 0.0))
    both = jnp.where(rows < 4, alone1, roll_rows(alone2, 4))
    stacked = jnp.concatenate([first, both, first, first, second, second, third, alone3], axis=0)
    return stacked.astype(jnp.bfloat16).T


def source_side(dist, front, back, core, rows):
    zero = jnp.zeros_like(dist)
    one = jnp.ones_like(dist)
    values = (
        jnp.where((rows < 3) | (rows > 5), dist, 0.0),
        jnp.where((rows >= 3) & (rows < 6), front, 0.0),
        jnp.where((rows < 3) | (rows == 6), back, 0.0),
        jnp.where(rows == 6, core, 0.0),
    )
    pick = rows & 3
    picks = (jnp.where(pick < 2, one, zero), jnp.where(pick == 2, one, zero), zero, jnp.where(pick == 3, one, zero))
    blocks = []
    for value, picked in zip(values, picks):
        first, second, third = split_three(value)
        parts = [first, picked, second, third, first, second, first, picked]
        blocks.append(jnp.concatenate(parts, axis=0).astype(jnp.bfloat16))
    return jnp.concatenate(blocks, axis=1)


def finish_block(tile_row, smooth_row, grad_row, origin):
    position = [tile_row(k) - origin[k : k + 1, :] for k in range(3)]
    strength = [tile_row(3 + k) for k in range(3)]
    scale = biot_factor * tile_row(7)
    smooth = [smooth_row(k) for k in range(6)]
    grad = [grad_row(k) for k in range(6)]
    velocity = [turn - part for turn, part in zip(cross(position, smooth[:3]), smooth[3:])]
    lever = [turn - part for turn, part in zip(cross(position, grad[:3]), grad[3:])]
    stretch = [turn - 3.0 * part for turn, part in zip(cross(strength, smooth[:3]), lever)]
    return [scale * value for value in velocity + stretch]


def evaluate(products, pieces):
    for start in range(0, TILE, 16):
        at = slice(start, start + 16)
        dist, front, back, core = (products[at, k * TILE : (k + 1) * TILE] for k in range(4))
        inv = lax.rsqrt(dist)
        inv2 = inv * inv
        inv3 = inv2 * inv
        tail = core * (inv3 * inv2)
        smooth = inv3 + 1.5 * tail
        grad = inv2 * (smooth + tail)
        for k, value in enumerate((smooth, grad * front, grad * back)):
            high, low = split_two(value)
            pieces[at, 2 * k * TILE : (2 * k + 1) * TILE] = high
            pieces[at, (2 * k + 1) * TILE : (2 * k + 2) * TILE] = low


def tile_at(tile):
    return pl.ds(pl.multiple_of(tile * ROWS, ROWS), ROWS)


def term_at(tile):
    return pl.ds(pl.multiple_of(tile * TERMS, TERMS), TERMS)


def wide_at(tile):
    return pl.ds(pl.multiple_of(tile * TILE, TILE), TILE)


def feat_at(tile):
    return pl.ds(pl.multiple_of(tile * FEAT, FEAT), FEAT)


def target_terms(feat, values):
    smooth, front = values[:, : 2 * TILE], values[:, 2 * TILE : 4 * TILE]
    terms = lax.dot_general(
        jnp.concatenate([feat, feat], axis=1),
        jnp.concatenate([smooth, front], axis=0),
        (((1,), (1,)), ((), ())),
        preferred_element_type=jnp.float32,
    )
    return add_pieces(terms)


def source_terms(feat, values):
    high = jnp.concatenate([values[:, :TILE], values[:, 4 * TILE : 5 * TILE]], axis=1)
    low = jnp.concatenate([values[:, TILE : 2 * TILE], values[:, 5 * TILE :]], axis=1)
    both = jnp.concatenate([high, low], axis=0)
    terms = jnp.dot(jnp.concatenate([feat, feat], axis=1), both, preferred_element_type=jnp.float32)
    return add_pieces(terms)


def own_kernel(block, left, right, feat, sums, origin_ref, *scratch):
    products, pieces = scratch[:STEPS], scratch[STEPS : 2 * STEPS]
    stages, copied = scratch[2 * STEPS : -1], scratch[-1]
    copied[: block.shape[0], :] = block[...]
    tiles = block.shape[0] // ROWS
    rows = row_ids()
    total = block[0:ROWS, :]
    for tile in range(1, tiles):
        total = total + block[tile * ROWS : (tile + 1) * ROWS, :]
    origin = jnp.sum(total, axis=1, keepdims=True) * (1.0 / (tiles * TILE))
    origin = jnp.where(rows < 3, jnp.broadcast_to(origin, (ROWS, TILE)), 0.0)
    origin_ref[...] = origin
    description = describe(lambda row: copied[pl.ds(row, tiles, stride=ROWS), :], origin)
    stage_features(stages[0], 0, tiles, *description[:2])
    stage_target(stages[1:3], 0, tiles, description)
    stage_source(stages[3:], 0, tiles, description)
    for tile in range(tiles):
        staged = [ref[tile * ROWS : (tile + 1) * ROWS, :] for ref in stages]
        feat[tile * FEAT : (tile + 1) * FEAT, :] = features(staged[0], rows)
        left[tile * TILE : (tile + 1) * TILE, :] = target_side(*staged[1:3], rows)
        right[tile * TERMS : (tile + 1) * TERMS, :] = source_side(*staged[3:], rows)
    for step in range(tiles + 2 * LEAD):
        if step < tiles:
            target, source = left[step * TILE : (step + 1) * TILE, :], right[step * TERMS : (step + 1) * TERMS, :]
            products[step % STEPS][...] = jnp.dot(target, source, preferred_element_type=jnp.float32)
        if LEAD <= step < tiles + LEAD:
            evaluate(products[(step - LEAD) % STEPS], pieces[(step - LEAD) % STEPS])
        if step >= 2 * LEAD:
            tile = step - 2 * LEAD
            terms = target_terms(feat[tile * FEAT : (tile + 1) * FEAT, :], pieces[tile % STEPS])
            sums[tile * ROWS : (tile + 1) * ROWS, :] = terms


def join_kernel(*refs):
    out, start = refs[-1], 0
    for ref in refs[:-1]:
        out[start : start + ref.shape[0], :] = ref[...]
        start += ref.shape[0]


def pair_kernel(nrows, ncols, tiles, where_ref, slots_ref, *refs):
    own_block, own_left, own_right, own_feat, own_sums, origin_ref = refs[:6]
    refs = refs[6:]
    halves = nrows // 2
    row_ins, far_ins, near_in, refs = refs[: ncols - 1], refs[ncols - 1 : ncols + halves - 2], refs[ncols + halves - 2], refs[ncols + halves - 1 :]
    row_outs, col_outs, scratch = refs[:ncols], refs[ncols : ncols + halves], refs[ncols + halves :]
    left, right, row_feat, col_feat = scratch[:4]
    row_sum, col_sum = scratch[4:6], scratch[6:8]
    row_stage, col_stage = scratch[8:11], scratch[11:16]
    came, done = scratch[16:18]
    products, pieces = scratch[18 : 18 + STEPS], scratch[18 + STEPS :]
    per = tiles * ROWS
    rows = row_ids()
    my_row, my_col = where_ref[0], where_ref[1]
    count = where_ref[2]
    for number, ref in enumerate((own_block, *row_ins, *far_ins)):
        came[number * per : (number + 1) * per, :] = ref[...]
    near = ncols + halves - 1
    came[near * per : (near + halves) * per, :] = near_in[...]
    row_sources = [(k, k * per) for k in range(1, ncols)]
    col_sources = [(2 * m, (ncols - 1 + m) * per) for m in range(1, halves)]
    col_sources += [(2 * m + 1, (near + m) * per) for m in range(halves)]
    origin = origin_ref[...]

    for ref in (*row_sum, *col_sum):
        ref[...] = jnp.zeros_like(ref)
    for k in range(STEPS - LEAD, STEPS):
        pieces[k][...] = jnp.zeros_like(pieces[k])
    for feat, me in ((row_feat, my_col), (col_feat, my_row)):
        feat[pl.ds(pl.multiple_of(me * tiles * FEAT, tiles * FEAT), tiles * FEAT), :] = own_feat[...]
    for k, ref in enumerate(row_sum):
        ref[pl.ds(pl.multiple_of(my_col * per, per), per), :] = own_sums[:, k * TILE : (k + 1) * TILE]
    left[pl.ds(pl.multiple_of(my_col * tiles * TILE, tiles * TILE), tiles * TILE), :] = own_left[...]
    right[pl.ds(pl.multiple_of(my_row * tiles * TERMS, tiles * TERMS), tiles * TERMS), :] = own_right[...]

    def rows_of(ref, start):
        return lambda row: ref[pl.ds(start + row, tiles, stride=ROWS), :]

    for number, (_, start) in enumerate(row_sources):
        description = describe(rows_of(came, start), origin)
        stage_features(row_stage[0], number * per, tiles, *description[:2])
        stage_target(row_stage[1:], number * per, tiles, description)
    for number, (_, start) in enumerate(col_sources):
        description = describe(rows_of(came, start), origin)
        stage_features(col_stage[0], number * per, tiles, *description[:2])
        stage_source(col_stage[1:], number * per, tiles, description)

    def prepare(step, carry):
        for number, (k, _) in enumerate(row_sources):
            tile = (my_col ^ k) * tiles + step
            staged = [ref[pl.ds(pl.multiple_of(number * per + step * ROWS, ROWS), ROWS), :] for ref in row_stage]
            row_feat[feat_at(tile), :] = features(staged[0], rows)
            left[wide_at(tile), :] = target_side(*staged[1:], rows)
        for number, (k, _) in enumerate(col_sources):
            tile = (my_row ^ k) * tiles + step
            staged = [ref[pl.ds(pl.multiple_of(number * per + step * ROWS, ROWS), ROWS), :] for ref in col_stage]
            col_feat[feat_at(tile), :] = features(staged[0], rows)
            right[term_at(tile), :] = source_side(*staged[1:], rows)
        return carry

    lax.fori_loop(0, tiles, prepare, 0, unroll=8)

    last = slots_ref.shape[1] - 1

    def multiply(slot, out):
        slot = jnp.minimum(slot, last)
        tgt, src = slots_ref[0, slot], slots_ref[1, slot]
        out[...] = jnp.dot(left[wide_at(tgt), :], right[term_at(src), :], preferred_element_type=jnp.float32)

    def add_up(slot, values):
        kept = jnp.clip(slot, 0, last)
        tgt, src = slots_ref[0, kept], slots_ref[1, kept]
        own = (tgt // tiles == my_col) & (src // tiles == my_row) & (tgt % tiles == src % tiles)
        alive = jnp.where((slot >= tiles) & (slot < count), 1.0, 0.0)
        react = jnp.where(own, 0.0, alive)
        to_target = alive * target_terms(col_feat[feat_at(src), :], values)
        to_source = react * source_terms(row_feat[feat_at(tgt), :], values)
        for k in range(2):
            row_sum[k][tile_at(tgt), :] += to_target[:, k * TILE : (k + 1) * TILE]
            col_sum[k][tile_at(src), :] += to_source[:, k * TILE : (k + 1) * TILE]

    for k in range(LEAD):
        multiply(tiles + k, products[k])
    loops = (count - tiles + STEPS - 1) // STEPS

    def visit(step, carry):
        for k in range(STEPS):
            slot = tiles + step * STEPS + k
            add_up(slot - LEAD, pieces[(k - LEAD) % STEPS])
            multiply(slot + LEAD, products[(k + LEAD) % STEPS])
            evaluate(products[k], pieces[k])
        return carry

    lax.fori_loop(0, loops, visit, 0)
    for k in range(LEAD):
        add_up(tiles + loops * STEPS - LEAD + k, pieces[STEPS - LEAD + k])

    row_results = [(k, row_outs[k], 0) for k in range(ncols)]
    col_results = [(k, col_outs[k // 2], k % 2 * per) for k in range(nrows)]
    number = 0
    for results, sources, sums, me in (
        (row_results, row_sources, row_sum, my_col),
        (col_results, col_sources, col_sum, my_row),
    ):
        starts = dict(sources) | {0: 0}
        for k, result, start in results:
            base = pl.multiple_of((me ^ k) * per, per)
            values = finish_block(rows_of(came, starts[k]), *(rows_of(ref, base) for ref in sums), origin)
            put_rows(done, number * per, tiles, numbered(0, values))
            result[start : start + per, :] = done[number * per : (number + 1) * per, :]
            number += 1


def halve_kernel(*refs):
    keep, send = refs[-2:]
    half = keep.shape[0]
    total = refs[0][...]
    for ref in refs[1:-2]:
        total = total + ref[...]
    keep[...] = total[:half, :]
    send[...] = total[half:, :]


def total_kernel(*refs):
    vel_ref, str_ref = refs[-2:]
    tiles = vel_ref.shape[1] // TILE
    for tile in range(tiles):
        at = slice(tile * ROWS, (tile + 1) * ROWS)
        total = refs[0][at, :]
        for ref in refs[1:-2]:
            total = total + ref[at, :]
        vel_ref[:, tile * TILE : (tile + 1) * TILE] = total[0:3, :]
        str_ref[:, tile * TILE : (tile + 1) * TILE] = total[3:6, :]


def shards(positions, strengths, cores, order, tile_counts, pair_slots, pair_count):
    tiles = tile_counts.shape[0]
    per_dev = tiles * TILE
    nrows = lax.axis_size("row")
    ncols = lax.axis_size("col")
    halves = nrows // 2
    assert nrows == 2 * halves and nrows & (nrows - 1) == 0 and ncols & (ncols - 1) == 0
    row_tiles, col_tiles = ncols * tiles, nrows * tiles
    smem = pl.BlockSpec(memory_space=pltpu.SMEM)
    vmem = pl.BlockSpec(memory_space=pltpu.VMEM)
    hbm = pl.BlockSpec(memory_space=pltpu.HBM)
    params = pltpu.CompilerParams(vmem_limit_bytes=VMEM_BYTES)

    def blocks(count):
        return jax.ShapeDtypeStruct((count * tiles * ROWS, TILE), jnp.float32)

    def in_hbm(value):
        return pltpu.with_memory_space_constraint(value, pltpu.HBM)

    inputs = (tile_counts, positions, strengths, cores.reshape(1, per_dev), order.reshape(1, per_dev), pair_slots)
    packed, slots = pl.pallas_call(
        pack_kernel,
        out_shape=[blocks(1), jax.ShapeDtypeStruct(pair_slots.shape, jnp.int32)],
        in_specs=[hbm] * len(inputs),
        out_specs=[vmem, smem],
        scratch_shapes=[
            pltpu.VMEM((ROWS, per_dev), jnp.float32),
            pltpu.VMEM((1, per_dev), jnp.int32),
            pltpu.SMEM(tile_counts.shape, jnp.int32),
            pltpu.SemaphoreType.DMA((len(inputs),)),
        ],
        compiler_params=params,
        name="pack",
    )(*map(in_hbm, inputs))

    def swap(value, axis, size, k):
        return lax.ppermute(value, axis, [(d, d ^ k) for d in range(size)])

    def strided(count):
        return pltpu.VMEM(((count * tiles + 1) * ROWS, TILE), jnp.float32)

    phases = [pltpu.VMEM((TILE, 4 * TILE), jnp.float32)] * STEPS + [pltpu.VMEM((TILE, 6 * TILE), jnp.bfloat16)] * STEPS
    own = pl.pallas_call(
        own_kernel,
        out_shape=[
            jax.ShapeDtypeStruct((per_dev, TERMS), jnp.bfloat16),
            jax.ShapeDtypeStruct((tiles * TERMS, 4 * TILE), jnp.bfloat16),
            jax.ShapeDtypeStruct((tiles * FEAT, TILE), jnp.bfloat16),
            jax.ShapeDtypeStruct((tiles * ROWS, 2 * TILE), jnp.float32),
            jax.ShapeDtypeStruct((ROWS, TILE), jnp.float32),
        ],
        in_specs=[vmem],
        out_specs=[vmem] * 5,
        scratch_shapes=phases + [strided(1)] * 8,
        compiler_params=params,
        cost_estimate=pl.CostEstimate(flops=tiles * 300 * TILE * TILE, bytes_accessed=2**21, transcendentals=0),
        name="own",
    )(packed)

    far = [swap(packed, "row", nrows, 2 * m) for m in range(1, halves)]
    from_row = [swap(packed, "col", ncols, k) for k in range(1, ncols)]
    joined = pl.pallas_call(
        join_kernel,
        out_shape=blocks(halves),
        in_specs=[vmem] * halves,
        out_specs=vmem,
        compiler_params=params,
        name="join",
    )(packed, *far)
    near = swap(joined, "row", nrows, 1)

    where = jnp.stack([lax.axis_index("row"), lax.axis_index("col"), pair_count[0]]).astype(jnp.int32)
    sums = pl.pallas_call(
        functools.partial(pair_kernel, nrows, ncols, tiles),
        out_shape=[blocks(1)] * ncols + [blocks(2)] * halves,
        in_specs=[smem] * 2 + [vmem] * (5 + ncols + halves),
        out_specs=[vmem] * (ncols + halves),
        scratch_shapes=[
            pltpu.VMEM((row_tiles * TILE, TERMS), jnp.bfloat16),
            pltpu.VMEM((col_tiles * TERMS, 4 * TILE), jnp.bfloat16),
            pltpu.VMEM((row_tiles * FEAT, TILE), jnp.bfloat16),
            pltpu.VMEM((col_tiles * FEAT, TILE), jnp.bfloat16),
            *[strided(ncols)] * 2,
            *[strided(nrows)] * 2,
            *[strided(ncols - 1)] * 3,
            *[strided(nrows - 1)] * 5,
            strided(ncols + nrows - 1),
            strided(ncols + nrows),
            *phases,
        ],
        compiler_params=params,
        name="pairs",
    )(where, slots, packed, *own, *from_row, *far, near)

    far_back = [swap(sums[ncols + m], "row", nrows, 2 * m) for m in range(1, halves)]
    row_back = [swap(sums[k], "col", ncols, k) for k in reversed(range(1, ncols))]
    keep, send = pl.pallas_call(
        halve_kernel,
        out_shape=[blocks(1)] * 2,
        in_specs=[vmem] * halves,
        out_specs=[vmem] * 2,
        compiler_params=params,
        name="halve",
    )(sums[ncols], *far_back)
    parts = [sums[0], keep, *row_back, swap(send, "row", nrows, 1)]
    velocity, stretching = pl.pallas_call(
        total_kernel,
        out_shape=[jax.ShapeDtypeStruct((3, per_dev), jnp.float32)] * 2,
        in_specs=[vmem] * len(parts),
        out_specs=[vmem, vmem],
        compiler_params=params,
        name="totals",
    )(*parts)
    return velocity, stretching


def solution(mesh):
    whole = ("groups", "row", "col")
    in_specs = (P(None, whole), P(None, whole), P(whole), P(whole), P(whole), P(None, whole), P(whole))
    out_specs = (P(None, whole), P(None, whole))
    return jax.shard_map(shards, mesh=mesh, in_specs=in_specs, out_specs=out_specs, check_vma=False)
```

```python
import functools
import math

import jax
import jax.numpy as jnp
from jax import lax
from jax.experimental import pallas as pl
from jax.experimental.pallas import tpu as pltpu
from jax.sharding import PartitionSpec as P

TILE = 128
ROWS = 8
STEPS = 28
LEAD = 3
FEAT = 32
TERMS = 64
VMEM_BYTES = 48 * 1024 * 1024

biot_factor = -1.0 / (4.0 * math.pi)


def row_ids(count=ROWS):
    return lax.broadcasted_iota(jnp.int32, (count, TILE), 0)


def roll_rows(value, shift):
    return pltpu.roll(value, shift % ROWS, 0)


def pack_kernel(
    counts_hbm, pos_hbm, str_hbm, core_hbm, order_hbm, slots_hbm,
    out_ref, slots_ref, stored, order_ref, counts_ref, arrived,
):
    tiles = order_ref.shape[1] // TILE
    pairs = (
        (pos_hbm, stored.at[0:3, :]),
        (str_hbm, stored.at[3:6, :]),
        (core_hbm, stored.at[6:7, :]),
        (order_hbm, order_ref),
        (counts_hbm, counts_ref),
        (slots_hbm, slots_ref),
    )
    copies = [pltpu.make_async_copy(src, dst, arrived.at[k]) for k, (src, dst) in enumerate(pairs)]
    for copy in copies:
        copy.start()
    stored[7:8, :] = jnp.zeros((1, stored.shape[1]), jnp.float32)
    for copy in copies:
        copy.wait()
    lane = lax.broadcasted_iota(jnp.int32, (ROWS, TILE), 1)
    rows = row_ids()
    is_strength = (rows >= 3) & (rows < 6)
    for tile in range(tiles):
        where_from = jnp.broadcast_to(order_ref[:, tile * TILE : (tile + 1) * TILE], (ROWS, TILE))
        inside = where_from & (TILE - 1)
        block = where_from >> 7
        value = jnp.zeros((ROWS, TILE), jnp.float32)
        for source in range(tiles):
            part = jnp.take_along_axis(stored[:, source * TILE : (source + 1) * TILE], inside, axis=1)
            value = jnp.where(block == source, part, value)
        live = lane < counts_ref[tile]
        value = jnp.where(is_strength & ~live, 0.0, value)
        value = jnp.where(rows == 7, live.astype(jnp.float32), value)
        out_ref[tile * ROWS : (tile + 1) * ROWS, :] = value


def split_three(value):
    first = value.astype(jnp.bfloat16).astype(jnp.float32)
    rest = value - first
    second = rest.astype(jnp.bfloat16).astype(jnp.float32)
    return first, second, rest - second


def split_two(value):
    high = value.astype(jnp.bfloat16)
    return high, (value - high.astype(jnp.float32)).astype(jnp.bfloat16)


def add_pieces(terms):
    return terms[0:ROWS, :] + (terms[ROWS : 2 * ROWS, :] + terms[2 * ROWS : 3 * ROWS, :])


def cross(left, right):
    return [left[1] * right[2] - left[2] * right[1], left[2] * right[0] - left[0] * right[2], left[0] * right[1] - left[1] * right[0]]


def describe(tile_row, origin):
    position = [tile_row(k) - origin[k : k + 1, :] for k in range(3)]
    strength = [tile_row(3 + k) for k in range(3)]
    core = tile_row(6)
    half = 0.5 * core * core
    coarse = [value.astype(jnp.bfloat16).astype(jnp.float32) for value in position]
    norm = coarse[0] * coarse[0] + coarse[1] * coarse[1] + coarse[2] * coarse[2]
    rest = [(value - near) * (value + near) for value, near in zip(position, coarse)]
    rest = rest[0] + rest[1] + rest[2] + half
    along = position[0] * strength[0] + position[1] * strength[1] + position[2] * strength[2]
    return position, strength, half, norm, rest, along


def put_rows(ref, start, tiles, values):
    for row, value in values.items():
        ref[pl.ds(start + row, tiles, stride=ROWS), :] = value


def negative(values):
    return [-value for value in values]


def numbered(first, values):
    return dict(enumerate(values, first))


def stage_features(ref, start, tiles, position, strength):
    put_rows(ref, start, tiles, numbered(0, strength + cross(position, strength)))


def stage_target(refs, start, tiles, description):
    position, strength, half, norm, rest, along = description
    put_rows(refs[0], start, tiles, numbered(0, position + strength))
    put_rows(refs[1], start, tiles, numbered(0, [norm, rest, along, half]))


def stage_source(refs, start, tiles, description):
    position, strength, half, norm, rest, along = description
    put_rows(refs[0], start, tiles, numbered(0, [-2.0 * value for value in position]) | {6: norm, 7: rest})
    put_rows(refs[1], start, tiles, numbered(3, negative(position)))
    put_rows(refs[2], start, tiles, numbered(0, negative(strength)) | {6: along})
    put_rows(refs[3], start, tiles, {6: half})


def features(tile, rows):
    value = jnp.where(rows < 6, tile, 0.0)
    return jnp.concatenate([*split_three(value), jnp.zeros_like(value)], axis=0).astype(jnp.bfloat16)


def target_side(shared, alone, rows):
    first, second, third = split_three(jnp.where(rows < 6, shared, 1.0))
    alone1, alone2, alone3 = split_three(jnp.where(rows < 4, alone, 0.0))
    both = jnp.where(rows < 4, alone1, roll_rows(alone2, 4))
    stacked = jnp.concatenate([first, both, first, first, second, second, third, alone3], axis=0)
    return stacked.astype(jnp.bfloat16).T


def source_side(dist, front, back, core, rows):
    zero = jnp.zeros_like(dist)
    one = jnp.ones_like(dist)
    values = (
        jnp.where((rows < 3) | (rows > 5), dist, 0.0),
        jnp.where((rows >= 3) & (rows < 6), front, 0.0),
        jnp.where((rows < 3) | (rows == 6), back, 0.0),
        jnp.where(rows == 6, core, 0.0),
    )
    pick = rows & 3
    picks = (jnp.where(pick < 2, one, zero), jnp.where(pick == 2, one, zero), zero, jnp.where(pick == 3, one, zero))
    blocks = []
    for value, picked in zip(values, picks):
        first, second, third = split_three(value)
        parts = [first, picked, second, third, first, second, first, picked]
        blocks.append(jnp.concatenate(parts, axis=0).astype(jnp.bfloat16))
    return jnp.concatenate(blocks, axis=1)


def finish_block(tile_row, smooth_row, grad_row, origin):
    position = [tile_row(k) - origin[k : k + 1, :] for k in range(3)]
    strength = [tile_row(3 + k) for k in range(3)]
    scale = biot_factor * tile_row(7)
    smooth = [smooth_row(k) for k in range(6)]
    grad = [grad_row(k) for k in range(6)]
    velocity = [turn - part for turn, part in zip(cross(position, smooth[:3]), smooth[3:])]
    lever = [turn - part for turn, part in zip(cross(position, grad[:3]), grad[3:])]
    stretch = [turn - 3.0 * part for turn, part in zip(cross(strength, smooth[:3]), lever)]
    return [scale * value for value in velocity + stretch]


def evaluate(products, pieces):
    for start in range(0, TILE, 16):
        at = slice(start, start + 16)
        dist, front, back, core = (products[at, k * TILE : (k + 1) * TILE] for k in range(4))
        inv = lax.rsqrt(dist)
        inv2 = inv * inv
        inv3 = inv2 * inv
        tail = core * (inv3 * inv2)
        smooth = inv3 + 1.5 * tail
        grad = inv2 * (smooth + tail)
        for k, value in enumerate((smooth, grad * front, grad * back)):
            high, low = split_two(value)
            pieces[at, 2 * k * TILE : (2 * k + 1) * TILE] = high
            pieces[at, (2 * k + 1) * TILE : (2 * k + 2) * TILE] = low


def tile_at(tile):
    return pl.ds(pl.multiple_of(tile * ROWS, ROWS), ROWS)


def term_at(tile):
    return pl.ds(pl.multiple_of(tile * TERMS, TERMS), TERMS)


def wide_at(tile):
    return pl.ds(pl.multiple_of(tile * TILE, TILE), TILE)


def feat_at(tile):
    return pl.ds(pl.multiple_of(tile * FEAT, FEAT), FEAT)


def target_terms(feat, values):
    smooth, front = values[:, : 2 * TILE], values[:, 2 * TILE : 4 * TILE]
    terms = lax.dot_general(
        jnp.concatenate([feat, feat], axis=1),
        jnp.concatenate([smooth, front], axis=0),
        (((1,), (1,)), ((), ())),
        preferred_element_type=jnp.float32,
    )
    return add_pieces(terms)


def source_terms(feat, values):
    high = jnp.concatenate([values[:, :TILE], values[:, 4 * TILE : 5 * TILE]], axis=1)
    low = jnp.concatenate([values[:, TILE : 2 * TILE], values[:, 5 * TILE :]], axis=1)
    both = jnp.concatenate([high, low], axis=0)
    terms = jnp.dot(jnp.concatenate([feat, feat], axis=1), both, preferred_element_type=jnp.float32)
    return add_pieces(terms)


def own_kernel(block, left, right, feat, sums, origin_ref, *scratch):
    products, pieces = scratch[:STEPS], scratch[STEPS : 2 * STEPS]
    stages, copied = scratch[2 * STEPS : -1], scratch[-1]
    copied[: block.shape[0], :] = block[...]
    tiles = block.shape[0] // ROWS
    rows = row_ids()
    total = block[0:ROWS, :]
    for tile in range(1, tiles):
        total = total + block[tile * ROWS : (tile + 1) * ROWS, :]
    origin = jnp.sum(total, axis=1, keepdims=True) * (1.0 / (tiles * TILE))
    origin = jnp.where(rows < 3, jnp.broadcast_to(origin, (ROWS, TILE)), 0.0)
    origin_ref[...] = origin
    description = describe(lambda row: copied[pl.ds(row, tiles, stride=ROWS), :], origin)
    stage_features(stages[0], 0, tiles, *description[:2])
    stage_target(stages[1:3], 0, tiles, description)
    stage_source(stages[3:], 0, tiles, description)
    for tile in range(tiles):
        staged = [ref[tile * ROWS : (tile + 1) * ROWS, :] for ref in stages]
        feat[tile * FEAT : (tile + 1) * FEAT, :] = features(staged[0], rows)
        left[tile * TILE : (tile + 1) * TILE, :] = target_side(*staged[1:3], rows)
        right[tile * TERMS : (tile + 1) * TERMS, :] = source_side(*staged[3:], rows)
    for step in range(tiles + 2 * LEAD):
        if step < tiles:
            target, source = left[step * TILE : (step + 1) * TILE, :], right[step * TERMS : (step + 1) * TERMS, :]
            products[step % STEPS][...] = jnp.dot(target, source, preferred_element_type=jnp.float32)
        if LEAD <= step < tiles + LEAD:
            evaluate(products[(step - LEAD) % STEPS], pieces[(step - LEAD) % STEPS])
        if step >= 2 * LEAD:
            tile = step - 2 * LEAD
            terms = target_terms(feat[tile * FEAT : (tile + 1) * FEAT, :], pieces[tile % STEPS])
            sums[tile * ROWS : (tile + 1) * ROWS, :] = terms


def join_kernel(*refs):
    out, start = refs[-1], 0
    for ref in refs[:-1]:
        out[start : start + ref.shape[0], :] = ref[...]
        start += ref.shape[0]


def pair_kernel(nrows, ncols, tiles, where_ref, slots_ref, *refs):
    own_block, own_left, own_right, own_feat, own_sums, origin_ref = refs[:6]
    refs = refs[6:]
    halves = nrows // 2
    row_ins, far_ins, near_in, refs = refs[: ncols - 1], refs[ncols - 1 : ncols + halves - 2], refs[ncols + halves - 2], refs[ncols + halves - 1 :]
    row_outs, col_outs, scratch = refs[:ncols], refs[ncols : ncols + halves], refs[ncols + halves :]
    left, right, row_feat, col_feat = scratch[:4]
    row_sum, col_sum = scratch[4:6], scratch[6:8]
    row_stage, col_stage = scratch[8:11], scratch[11:16]
    came, done = scratch[16:18]
    products, pieces = scratch[18 : 18 + STEPS], scratch[18 + STEPS :]
    per = tiles * ROWS
    rows = row_ids()
    my_row, my_col = where_ref[0], where_ref[1]
    count = where_ref[2]
    for number, ref in enumerate((own_block, *row_ins, *far_ins)):
        came[number * per : (number + 1) * per, :] = ref[...]
    near = ncols + halves - 1
    came[near * per : (near + halves) * per, :] = near_in[...]
    row_sources = [(k, k * per) for k in range(1, ncols)]
    col_sources = [(2 * m, (ncols - 1 + m) * per) for m in range(1, halves)]
    col_sources += [(2 * m + 1, (near + m) * per) for m in range(halves)]
    origin = origin_ref[...]

    for ref in (*row_sum, *col_sum):
        ref[...] = jnp.zeros_like(ref)
    for k in range(STEPS - LEAD, STEPS):
        pieces[k][...] = jnp.zeros_like(pieces[k])
    for feat, me in ((row_feat, my_col), (col_feat, my_row)):
        feat[pl.ds(pl.multiple_of(me * tiles * FEAT, tiles * FEAT), tiles * FEAT), :] = own_feat[...]
    for k, ref in enumerate(row_sum):
        ref[pl.ds(pl.multiple_of(my_col * per, per), per), :] = own_sums[:, k * TILE : (k + 1) * TILE]
    left[pl.ds(pl.multiple_of(my_col * tiles * TILE, tiles * TILE), tiles * TILE), :] = own_left[...]
    right[pl.ds(pl.multiple_of(my_row * tiles * TERMS, tiles * TERMS), tiles * TERMS), :] = own_right[...]

    def rows_of(ref, start):
        return lambda row: ref[pl.ds(start + row, tiles, stride=ROWS), :]

    for number, (_, start) in enumerate(row_sources):
        description = describe(rows_of(came, start), origin)
        stage_features(row_stage[0], number * per, tiles, *description[:2])
        stage_target(row_stage[1:], number * per, tiles, description)
    for number, (_, start) in enumerate(col_sources):
        description = describe(rows_of(came, start), origin)
        stage_features(col_stage[0], number * per, tiles, *description[:2])
        stage_source(col_stage[1:], number * per, tiles, description)

    def prepare(step, carry):
        for number, (k, _) in enumerate(row_sources):
            tile = (my_col ^ k) * tiles + step
            staged = [ref[pl.ds(pl.multiple_of(number * per + step * ROWS, ROWS), ROWS), :] for ref in row_stage]
            row_feat[feat_at(tile), :] = features(staged[0], rows)
            left[wide_at(tile), :] = target_side(*staged[1:], rows)
        for number, (k, _) in enumerate(col_sources):
            tile = (my_row ^ k) * tiles + step
            staged = [ref[pl.ds(pl.multiple_of(number * per + step * ROWS, ROWS), ROWS), :] for ref in col_stage]
            col_feat[feat_at(tile), :] = features(staged[0], rows)
            right[term_at(tile), :] = source_side(*staged[1:], rows)
        return carry

    lax.fori_loop(0, tiles, prepare, 0, unroll=8)

    last = slots_ref.shape[1] - 1

    def multiply(slot, out):
        slot = jnp.minimum(slot, last)
        tgt, src = slots_ref[0, slot], slots_ref[1, slot]
        out[...] = jnp.dot(left[wide_at(tgt), :], right[term_at(src), :], preferred_element_type=jnp.float32)

    def add_up(slot, values):
        kept = jnp.clip(slot, 0, last)
        tgt, src = slots_ref[0, kept], slots_ref[1, kept]
        own = (tgt // tiles == my_col) & (src // tiles == my_row) & (tgt % tiles == src % tiles)
        alive = jnp.where((slot >= tiles) & (slot < count), 1.0, 0.0)
        react = jnp.where(own, 0.0, alive)
        to_target = alive * target_terms(col_feat[feat_at(src), :], values)
        to_source = react * source_terms(row_feat[feat_at(tgt), :], values)
        for k in range(2):
            row_sum[k][tile_at(tgt), :] += to_target[:, k * TILE : (k + 1) * TILE]
            col_sum[k][tile_at(src), :] += to_source[:, k * TILE : (k + 1) * TILE]

    for k in range(LEAD):
        multiply(tiles + k, products[k])
    loops = (count - tiles + STEPS - 1) // STEPS

    def visit(step, carry):
        for k in range(STEPS):
            slot = tiles + step * STEPS + k
            add_up(slot - LEAD, pieces[(k - LEAD) % STEPS])
            multiply(slot + LEAD, products[(k + LEAD) % STEPS])
            evaluate(products[k], pieces[k])
        return carry

    lax.fori_loop(0, loops, visit, 0)
    for k in range(LEAD):
        add_up(tiles + loops * STEPS - LEAD + k, pieces[STEPS - LEAD + k])

    row_results = [(k, row_outs[k], 0) for k in range(ncols)]
    col_results = [(k, col_outs[k // 2], k % 2 * per) for k in range(nrows)]
    number = 0
    for results, sources, sums, me in (
        (row_results, row_sources, row_sum, my_col),
        (col_results, col_sources, col_sum, my_row),
    ):
        starts = dict(sources) | {0: 0}
        for k, result, start in results:
            base = pl.multiple_of((me ^ k) * per, per)
            values = finish_block(rows_of(came, starts[k]), *(rows_of(ref, base) for ref in sums), origin)
            put_rows(done, number * per, tiles, numbered(0, values))
            result[start : start + per, :] = done[number * per : (number + 1) * per, :]
            number += 1


def halve_kernel(*refs):
    keep, send = refs[-2:]
    half = keep.shape[0]
    total = refs[0][...]
    for ref in refs[1:-2]:
        total = total + ref[...]
    keep[...] = total[:half, :]
    send[...] = total[half:, :]


def total_kernel(*refs):
    vel_ref, str_ref = refs[-2:]
    tiles = vel_ref.shape[1] // TILE
    for tile in range(tiles):
        at = slice(tile * ROWS, (tile + 1) * ROWS)
        total = refs[0][at, :]
        for ref in refs[1:-2]:
            total = total + ref[at, :]
        vel_ref[:, tile * TILE : (tile + 1) * TILE] = total[0:3, :]
        str_ref[:, tile * TILE : (tile + 1) * TILE] = total[3:6, :]


def shards(positions, strengths, cores, order, tile_counts, pair_slots, pair_count):
    tiles = tile_counts.shape[0]
    per_dev = tiles * TILE
    nrows = lax.axis_size("row")
    ncols = lax.axis_size("col")
    halves = nrows // 2
    assert nrows == 2 * halves and nrows & (nrows - 1) == 0 and ncols & (ncols - 1) == 0
    row_tiles, col_tiles = ncols * tiles, nrows * tiles
    smem = pl.BlockSpec(memory_space=pltpu.SMEM)
    vmem = pl.BlockSpec(memory_space=pltpu.VMEM)
    hbm = pl.BlockSpec(memory_space=pltpu.HBM)
    params = pltpu.CompilerParams(vmem_limit_bytes=VMEM_BYTES)

    def blocks(count):
        return jax.ShapeDtypeStruct((count * tiles * ROWS, TILE), jnp.float32)

    def in_hbm(value):
        return pltpu.with_memory_space_constraint(value, pltpu.HBM)

    inputs = (tile_counts, positions, strengths, cores.reshape(1, per_dev), order.reshape(1, per_dev), pair_slots)
    packed, slots = pl.pallas_call(
        pack_kernel,
        out_shape=[blocks(1), jax.ShapeDtypeStruct(pair_slots.shape, jnp.int32)],
        in_specs=[hbm] * len(inputs),
        out_specs=[vmem, smem],
        scratch_shapes=[
            pltpu.VMEM((ROWS, per_dev), jnp.float32),
            pltpu.VMEM((1, per_dev), jnp.int32),
            pltpu.SMEM(tile_counts.shape, jnp.int32),
            pltpu.SemaphoreType.DMA((len(inputs),)),
        ],
        compiler_params=params,
        name="pack",
    )(*map(in_hbm, inputs))

    def swap(value, axis, size, k):
        return lax.ppermute(value, axis, [(d, d ^ k) for d in range(size)])

    def strided(count):
        return pltpu.VMEM(((count * tiles + 1) * ROWS, TILE), jnp.float32)

    phases = [pltpu.VMEM((TILE, 4 * TILE), jnp.float32)] * STEPS + [pltpu.VMEM((TILE, 6 * TILE), jnp.bfloat16)] * STEPS
    own = pl.pallas_call(
        own_kernel,
        out_shape=[
            jax.ShapeDtypeStruct((per_dev, TERMS), jnp.bfloat16),
            jax.ShapeDtypeStruct((tiles * TERMS, 4 * TILE), jnp.bfloat16),
            jax.ShapeDtypeStruct((tiles * FEAT, TILE), jnp.bfloat16),
            jax.ShapeDtypeStruct((tiles * ROWS, 2 * TILE), jnp.float32),
            jax.ShapeDtypeStruct((ROWS, TILE), jnp.float32),
        ],
        in_specs=[vmem],
        out_specs=[vmem] * 5,
        scratch_shapes=phases + [strided(1)] * 8,
        compiler_params=params,
        cost_estimate=pl.CostEstimate(flops=tiles * 300 * TILE * TILE, bytes_accessed=2**21, transcendentals=0),
        name="own",
    )(packed)

    far = [swap(packed, "row", nrows, 2 * m) for m in range(1, halves)]
    from_row = [swap(packed, "col", ncols, k) for k in range(1, ncols)]
    joined = pl.pallas_call(
        join_kernel,
        out_shape=blocks(halves),
        in_specs=[vmem] * halves,
        out_specs=vmem,
        compiler_params=params,
        name="join",
    )(packed, *far)
    near = swap(joined, "row", nrows, 1)

    where = jnp.stack([lax.axis_index("row"), lax.axis_index("col"), pair_count[0]]).astype(jnp.int32)
    sums = pl.pallas_call(
        functools.partial(pair_kernel, nrows, ncols, tiles),
        out_shape=[blocks(1)] * ncols + [blocks(2)] * halves,
        in_specs=[smem] * 2 + [vmem] * (5 + ncols + halves),
        out_specs=[vmem] * (ncols + halves),
        scratch_shapes=[
            pltpu.VMEM((row_tiles * TILE, TERMS), jnp.bfloat16),
            pltpu.VMEM((col_tiles * TERMS, 4 * TILE), jnp.bfloat16),
            pltpu.VMEM((row_tiles * FEAT, TILE), jnp.bfloat16),
            pltpu.VMEM((col_tiles * FEAT, TILE), jnp.bfloat16),
            *[strided(ncols)] * 2,
            *[strided(nrows)] * 2,
            *[strided(ncols - 1)] * 3,
            *[strided(nrows - 1)] * 5,
            strided(ncols + nrows - 1),
            strided(ncols + nrows),
            *phases,
        ],
        compiler_params=params,
        name="pairs",
    )(where, slots, packed, *own, *from_row, *far, near)

    far_back = [swap(sums[ncols + m], "row", nrows, 2 * m) for m in range(1, halves)]
    row_back = [swap(sums[k], "col", ncols, k) for k in reversed(range(1, ncols))]
    keep, send = pl.pallas_call(
        halve_kernel,
        out_shape=[blocks(1)] * 2,
        in_specs=[vmem] * halves,
        out_specs=[vmem] * 2,
        compiler_params=params,
        name="halve",
    )(sums[ncols], *far_back)
    parts = [sums[0], keep, *row_back, swap(send, "row", nrows, 1)]
    velocity, stretching = pl.pallas_call(
        total_kernel,
        out_shape=[jax.ShapeDtypeStruct((3, per_dev), jnp.float32)] * 2,
        in_specs=[vmem] * len(parts),
        out_specs=[vmem, vmem],
        compiler_params=params,
        name="totals",
    )(*parts)
    return velocity, stretching


def solution(mesh):
    whole = ("groups", "row", "col")
    in_specs = (P(None, whole), P(None, whole), P(whole), P(whole), P(whole), P(None, whole), P(whole))
    out_specs = (P(None, whole), P(None, whole))
    return jax.shard_map(shards, mesh=mesh, in_specs=in_specs, out_specs=out_specs, check_vma=False)
```
